32 devices in a mesh: rep: 8 (over y, x, core), shard: 4 (over z).
Axes of the slice: x: 2, y: 2, z: 4, core: 2. Of those that a mesh axis runs over, the one named last changes fastest.
Arguments:
- tokens: bfloat16 [5120, 1536], P(('rep', 'shard')), may hold values from -6 to 6
- segment_ids: int32 [8, 640], P('rep'), may hold values from 0 to 2, never falling along the last dimension, each value on 1 to 512 neighbouring positions
- first_gain: bfloat16 [1536], P('shard'), may hold values from 0.5 to 1.5
- input_weight: bfloat16 [1536, 2048], P('shard'), may hold values from -0.15625 to 0.15625
- input_bias: bfloat16 [2048], P('shard'), may hold values from -0.625 to 0.625
- output_weight: bfloat16 [1536, 1536], P('shard'), may hold values from -0.875 to 0.875
- second_gain: bfloat16 [1536], P('shard'), may hold values from 0.5 to 1.5
- gate_weight: bfloat16 [1536, 8960], P('shard'), may hold values from -0.15625 to 0.15625
- up_weight: bfloat16 [1536, 8960], P('shard'), may hold values from -0.15625 to 0.15625
- down_weight: bfloat16 [8960, 1536], P('shard'), may hold values from -0.0625 to 0.0625
- output_cotangent: bfloat16 [5120, 1536], P(('rep', 'shard')), may hold values from -6 to 6
Outputs:
- block_out: bfloat16 [5120, 1536], P(('rep', 'shard'))
- tokens_gradient: bfloat16 [5120, 1536], P(('rep', 'shard'))
- first_gain_gradient: float32 [1536], P('shard')
- input_weight_gradient: float32 [1536, 2048], P('shard')
- input_bias_gradient: float32 [1792], P('shard')
- value_bias_gradient: float32 [256], P('shard')
- output_weight_gradient: float32 [1536, 1536], P('shard')
- second_gain_gradient: float32 [1536], P('shard')
- gate_weight_gradient: float32 [1536, 8960], P('shard')
- up_weight_gradient: float32 [1536, 8960], P('shard')
- down_weight_gradient: float32 [8960, 1536], P('shard')
The draws below stay inside these ranges and needn't reach their ends.
Inputs may be any that keep to these rules, and one draw needn't show every extreme that they name: `segment_ids`: in every row the numbers never fall and each of 0 to 2 appears; a sequence has 1 to 512 tokens, and in every row one has exactly 512.
All inputs are finite; a program needn't handle non-finite values.
Results may differ from the reference program's by a relative error of at most 0.02.
Values may be sent and summed in bfloat16 or wider, within the bound.
No kernel may reach another device: no remote copies, remote signals or barrier semaphores. Data moves between devices by JAX's collectives and lax.ppermute only.
A program may use at most 448 MiB of HBM per device.

```python
import math
from functools import partial
import jax
import jax.numpy as jnp
import numpy as np
from jax import lax

D = 1536
FF = 8960
QH = 12
KVH = 2
HD = 128
SEQS = 3
QW = 1536
KW = 256
GROUP_TOK = 640
GROUPS = 8
TOKENS = 5120
SEQ_MOST = 512


def level_of(own_key, shape, cuts, smallest, high):
    level, own = 1.0, jax.random.fold_in(own_key, 6)
    for axis_at, shards_of in cuts:
        draws = jnp.exp(jax.random.uniform(jax.random.fold_in(own, axis_at), (shards_of,), jnp.float32, smallest / len(cuts), high / len(cuts)))
        level = level * jnp.repeat(draws, shape[axis_at] // shards_of).reshape([-1 if axis == axis_at else 1 for axis in range(len(shape))])
    return level


def profile(count, total, limit, skew):
    loads = [(1 << 20) // math.isqrt(standing ** skew) + 1 for standing in range(2, count + 1)]
    spare, given = total - limit - (count - 1), [1] * (count - 1)
    while spare > 0:
        movable = [i for i in range(count - 1) if given[i] < limit]
        mass, left = sum([loads[i] for i in movable]), spare
        for i in movable:
            addition = min(limit - given[i], max(1, left * loads[i] // mass), spare)
            given[i] = given[i] + addition
            spare = spare - addition
    return np.array([limit] + given)


def uneven(key, number_of, total, bound, slope):
    if number_of == 2:
        one = jax.random.randint(key, (), max(1, total - bound), min(bound, total - 1) + 1)
        return jnp.stack([one, total - one])
    tallies = jnp.asarray(profile(number_of, total, bound, slope), jnp.int32)
    twos = (number_of - 1) // 2
    donor, sink = tallies[1:1 + 2 * twos:2], tallies[2:2 + 2 * twos:2]
    room = jnp.minimum(donor - 1, bound - sink)
    passed = jax.random.randint(jax.random.fold_in(key, 1), (twos,), 0, 1 << 20) % (room + 1)
    tallies = tallies.at[1:1 + 2 * twos:2].set(donor - passed).at[2:2 + 2 * twos:2].set(sink + passed)
    return tallies[jax.random.permutation(jax.random.fold_in(key, 2), number_of)]


def noise(rng, dims, deviation, reach, shards=(), held_as=jnp.bfloat16):
    result = deviation * jax.random.normal(rng, dims, jnp.float32)
    if shards:
        result = result * level_of(rng, dims, shards, -0.22, 0.18)
    return jnp.clip(result, -reach, reach).astype(held_as)


def setup_inputs(seed: int = 0) -> dict:
    seeds = jax.random.split(jax.random.key(seed), 12)
    tokens = noise(seeds[0], (TOKENS, D), 1.0, 6.0, ((0, 32),))
    segment_ids = jax.vmap(lambda own: jnp.searchsorted(jnp.cumsum(uneven(own, SEQS, GROUP_TOK, SEQ_MOST, 1)), jnp.arange(GROUP_TOK), side="right"))(jax.random.split(seeds[1], GROUPS)).reshape((GROUPS, GROUP_TOK)).astype(jnp.int32)
    first_gain = jnp.clip(1.0 + 0.1 * jax.random.normal(seeds[2], (D,), jnp.float32), 0.5, 1.5).astype(jnp.bfloat16)
    input_weight = noise(seeds[3], (D, QW + 2 * KW), D ** -0.5, 0.15625, ((0, 4),))
    input_bias = noise(seeds[4], (QW + 2 * KW,), 0.1, 0.625, ((0, 4),))
    output_weight = noise(seeds[5], (QW, D), (D // 32) ** -0.5, 0.875, ((0, 4),))
    second_gain = jnp.clip(1.0 + 0.1 * jax.random.normal(seeds[6], (D,), jnp.float32), 0.5, 1.5).astype(jnp.bfloat16)
    gate_weight = noise(seeds[7], (D, FF), D ** -0.5, 0.15625, ((0, 4),))
    up_weight = noise(seeds[8], (D, FF), D ** -0.5, 0.15625, ((0, 4),))
    down_weight = noise(seeds[9], (FF, D), FF ** -0.5, 0.0625, ((0, 4),))
    output_cotangent = noise(seeds[10], (TOKENS, D), 1.0, 6.0, ((0, 32),))
    return {"tokens": tokens, "segment_ids": segment_ids, "first_gain": first_gain, "input_weight": input_weight, "input_bias": input_bias, "output_weight": output_weight, "second_gain": second_gain, "gate_weight": gate_weight, "up_weight": up_weight, "down_weight": down_weight, "output_cotangent": output_cotangent}


EPSILON = 1e-06
LOG_THETA = math.log(1000000.0)
MASKED = -1e+30

@jax.custom_vjp
def low(v):
    return lax.optimization_barrier(v.astype(jnp.bfloat16)).astype(jnp.float32)

@jax.custom_vjp
def low_back(v):
    return v

def low_keep(v):
    return (low(v), None)

def low_pass(kept, grad):
    return (grad,)

def back_keep(v):
    return (v, None)

def back_low(kept, grad):
    return (low(grad),)
low.defvjp(low_keep, low_pass)
low_back.defvjp(back_keep, back_low)

def rope_tables(places, head_width):
    half_width = head_width // 2
    frequency = jnp.exp(jnp.arange(half_width, dtype=jnp.float32) * (-2.0 * LOG_THETA / head_width))
    angles = places.astype(jnp.float32)[:, None] * frequency[None, :]
    angles = jnp.concatenate([angles, angles], axis=-1)
    return (jnp.cos(angles), jnp.sin(angles))

def positions(segments):
    labels = jnp.arange(SEQS, dtype=jnp.int32)
    starts = lax.optimization_barrier(jnp.sum((segments[None, :] < labels[:, None]).astype(jnp.int32), axis=1))
    own_start = lax.optimization_barrier(jnp.sum(jnp.where(segments[:, None] == labels[None, :], starts[None, :], 0), axis=1))
    return jnp.arange(segments.shape[0], dtype=jnp.int32) - own_start

def rotate(field_rows, cosine_table, sine_table):
    half_width = field_rows.shape[-1] // 2
    turned = jnp.concatenate([-field_rows[..., half_width:], field_rows[..., :half_width]], axis=-1)
    return field_rows * cosine_table[:, None, :] + turned * sine_table[:, None, :]

def layer_pass(wide_rows, segments, gain_one, input_matrix, input_shift, output_matrix, gain_two, gate_matrix, up_matrix, down_matrix):
    highest = lax.Precision.HIGHEST
    length = wide_rows.shape[0]
    score_scale = 1.0 / math.sqrt(HD)
    inverse_one = lax.rsqrt(lax.optimization_barrier(jnp.mean(wide_rows * wide_rows, axis=-1, keepdims=True)) + EPSILON)
    normed_one = low(wide_rows * inverse_one * gain_one)
    projected = low_back(jnp.dot(normed_one, input_matrix, precision=highest) + input_shift)
    cosine_table, sine_table = rope_tables(positions(segments), HD)
    queries = low(rotate(projected[:, :QW].reshape(length, QH, HD), cosine_table, sine_table))
    key_rows = low(rotate(projected[:, QW:QW + KW].reshape(length, KVH, HD), cosine_table, sine_table))
    value_rows = low(projected[:, QW + KW:].reshape(length, KVH, HD))
    indices = jnp.arange(length, dtype=jnp.int32)
    allowed = (segments[:, None] == segments[None, :]) & (indices[None, :] <= indices[:, None])
    per_group = QH // KVH
    head_queries = jnp.transpose(queries, (1, 0, 2))
    head_keys = jnp.repeat(jnp.transpose(key_rows, (1, 0, 2)), per_group, axis=0)
    head_values = jnp.repeat(jnp.transpose(value_rows, (1, 0, 2)), per_group, axis=0)

    def one_head(inputs):
        query_rows, keys_here, values_here = inputs
        scores = low_back(jnp.dot(query_rows, keys_here.T, precision=highest) * score_scale)
        scores = jnp.where(allowed, scores, MASKED)
        log_total = jax.nn.logsumexp(scores, axis=-1, keepdims=True)
        shares = low(jnp.exp(scores - log_total))
        return jnp.dot(shares, values_here, precision=highest)
    attended = lax.map(jax.checkpoint(one_head), (head_queries, head_keys, head_values))
    attended = low(low_back(jnp.transpose(attended, (1, 0, 2)).reshape(length, QW)))
    hidden = wide_rows + low_back(jnp.dot(attended, output_matrix, precision=highest))
    inverse_two = lax.rsqrt(lax.optimization_barrier(jnp.mean(hidden * hidden, axis=-1, keepdims=True)) + EPSILON)
    normed_two = low(hidden * inverse_two * gain_two)
    gate_linear = low_back(jnp.dot(normed_two, gate_matrix, precision=highest))
    up_linear = low_back(jnp.dot(normed_two, up_matrix, precision=highest))
    inner_act = low(jax.nn.silu(gate_linear) * up_linear)
    return hidden + jnp.dot(inner_act, down_matrix, precision=highest)

def forward(segment_ids, wide_tokens, gain_one, input_matrix, input_shift, output_matrix, gain_two, gate_matrix, up_matrix, down_matrix):
    blocks = wide_tokens.reshape(GROUPS, GROUP_TOK, D)

    def group_step(unused, inputs):
        return (unused, jax.checkpoint(layer_pass)(inputs[0], inputs[1], gain_one, input_matrix, input_shift, output_matrix, gain_two, gate_matrix, up_matrix, down_matrix))
    unused, results = lax.scan(group_step, jnp.zeros((), jnp.float32), (blocks, segment_ids))
    return results.reshape(GROUPS * GROUP_TOK, D)

def reference(tokens, segment_ids, first_gain, input_weight, input_bias, output_weight, second_gain, gate_weight, up_weight, down_weight, output_cotangent):
    block_out, pullback = jax.vjp(partial(forward, segment_ids), tokens.astype(jnp.float32), first_gain.astype(jnp.float32), input_weight.astype(jnp.float32), input_bias.astype(jnp.float32), output_weight.astype(jnp.float32), second_gain.astype(jnp.float32), gate_weight.astype(jnp.float32), up_weight.astype(jnp.float32), down_weight.astype(jnp.float32))
    gradients = pullback(output_cotangent.astype(jnp.float32))
    bias_split = QW + KW
    return (block_out.astype(jnp.bfloat16), gradients[0].astype(jnp.bfloat16), gradients[1], gradients[2], gradients[3][:bias_split], gradients[3][bias_split:], gradients[4], gradients[5], gradients[6], gradients[7], gradients[8])
```

```python
import math

import jax
import jax.numpy as jnp
from jax import lax
from jax.sharding import PartitionSpec as P

QH = 12
KVH = 2
HD = 128
SEQS = 3


EPSILON = 1e-06
LOG_THETA = math.log(1000000.0)
MASKED = -1e30


def rope_tables(places, head_width):
    half_width = head_width // 2
    frequency = jnp.exp(jnp.arange(half_width, dtype=jnp.float32) * (-2.0 * LOG_THETA / head_width))
    angles = places.astype(jnp.float32)[:, None] * frequency[None, :]
    angles = jnp.concatenate([angles, angles], axis=-1)
    return (jnp.cos(angles), jnp.sin(angles))


def positions(segments):
    labels = jnp.arange(SEQS, dtype=jnp.int32)
    starts = jnp.sum((segments[None, :] < labels[:, None]).astype(jnp.int32), axis=1)
    own_start = jnp.sum(jnp.where(segments[:, None] == labels[None, :], starts[None, :], 0), axis=1)
    return jnp.arange(segments.shape[0], dtype=jnp.int32) - own_start


def rotate(field_rows, cosine_table, sine_table):
    half_width = field_rows.shape[-1] // 2
    turned = jnp.concatenate([-field_rows[..., half_width:], field_rows[..., :half_width]], axis=-1)
    return field_rows * cosine_table[:, None, :] + turned * sine_table[:, None, :]


def rotate_back(gradient, cosine_table, sine_table):
    half_width = gradient.shape[-1] // 2
    moved_part = gradient * sine_table[:, None, :]
    turned = jnp.concatenate([moved_part[..., half_width:], -moved_part[..., :half_width]], axis=-1)
    return gradient * cosine_table[:, None, :] + turned


def transposed_times(left_side, right_side):
    return lax.dot_general(
        left_side, right_side, (((0,), (0,)), ((), ())), preferred_element_type=jnp.float32
    )


def times_transposed(left_side, right_side):
    return lax.dot_general(
        left_side, right_side, (((1,), (1,)), ((), ())), preferred_element_type=jnp.float32
    )


def norm_back(normed_gradient, unit_rows, inverse_rms, gain_row):
    scaled = normed_gradient * gain_row
    return inverse_rms * (scaled - unit_rows * jnp.mean(scaled * unit_rows, axis=-1, keepdims=True))


class Line:
    def __init__(self, name, size, place, pairs, crossed=False):
        self.name, self.size, self.place, self.pairs = name, size, place, pairs
        self.crossed = crossed

    def shift(self, value, step):
        return lax.ppermute(value, self.name, self.pairs(step % self.size))

    def behind(self, step):
        return lax.rem(self.place + (self.size - step % self.size), self.size)

    def ahead(self, step):
        return lax.rem(self.place + step % self.size, self.size)


def make_lines(reps, shards):
    inner = 2 if reps % 4 == 0 else 1
    outer = reps // (2 * inner)
    square = inner == outer

    def split(index):
        core, b, a = index % 2, (index // 2) % inner, index // (2 * inner)
        return core, b, a

    def join(core, b, a):
        return (a * inner + b) * 2 + core

    def first_pairs(step):
        pairs = []
        for index in range(reps):
            core, b, a = split(index)
            if square and core == 0:
                pairs.append((index, join(core, (b + step) % inner, a)))
            else:
                pairs.append((index, join(core, b, (a + step) % outer)))
        return pairs

    def second_pairs(step):
        pairs = []
        for index in range(reps):
            core, b, a = split(index)
            if square and core == 0:
                pairs.append((index, join(core, b, (a + step) % outer)))
            else:
                pairs.append((index, join(core, (b + step) % inner, a)))
        return pairs

    def core_pairs(step):
        pairs = []
        for index in range(reps):
            core, b, a = split(index)
            pairs.append((index, join((core + step) % 2, b, a)))
        return pairs

    def shard_pairs(step):
        return [(index, (index + step) % shards) for index in range(shards)]

    core, b, a = split(lax.axis_index("rep"))
    first, second = (jnp.where(core == 0, b, a), jnp.where(core == 0, a, b)) if square else (a, b)
    return (
        Line("shard", shards, lax.axis_index("shard"), shard_pairs),
        Line("rep", 2, core, core_pairs, square),
        Line("rep", outer, first, first_pairs),
        Line("rep", inner, second, second_pairs),
    )


def pick(array, index, axis):
    return lax.dynamic_index_in_dim(array, index, axis, keepdims=False)


def put(array, piece, index, axis):
    return lax.dynamic_update_index_in_dim(array, piece, index, axis)


def stack_by_place(pieces, line, axis=0):
    shape = list(pieces[0].shape)
    shape.insert(axis, line.size)
    held = jnp.zeros(shape, pieces[0].dtype)
    for step, piece in enumerate(pieces):
        held = put(held, piece, line.behind(step), axis)
    return held


def gather_line(value, line):
    return [value] + [line.shift(value, step) for step in range(1, line.size)]


def sum_line(blocks, line, axis):
    total = pick(blocks, line.place, axis).astype(jnp.float32)
    for step in range(1, line.size):
        total = total + line.shift(pick(blocks, line.ahead(step), axis), step).astype(jnp.float32)
    return total.astype(blocks.dtype)


def gather_rep(piece, core, first, second):
    held = [(0, 0, piece)]
    for step in range(1, second.size):
        held.append((0, step, second.shift(piece, step)))
    for step in range(1, first.size):
        held += [(step, at, first.shift(value, step)) for zero, at, value in held if zero == 0]
    placed = [
        (core.place, first.behind(one), second.behind(two), value) for one, two, value in held
    ]
    there, here = (second, first) if core.crossed else (first, second)
    for one, two, value in held:
        placed.append(
            (core.behind(1), there.behind(one), here.behind(two), core.shift(value, 1))
        )
    return [((c * first.size + f) * second.size + s, value) for c, f, s, value in placed]


def sum_rep(blocks, axis, core, first, second):
    shape = blocks.shape
    blocks = blocks.reshape(shape[:axis] + (2, first.size, second.size) + shape[axis + 1 :])
    for line in (core, first, second):
        blocks = sum_line(blocks, line, axis)
    return blocks


def on_device(
    tokens,
    segment_ids,
    first_gain,
    input_weight,
    input_bias,
    output_weight,
    second_gain,
    gate_weight,
    up_weight,
    down_weight,
    output_cotangent,
):
    bf16, f32 = jnp.bfloat16, jnp.float32
    shards, reps = lax.axis_size("shard"), lax.axis_size("rep")
    shard, core, first, second = make_lines(reps, shards)
    rep_place = (core.place * first.size + first.place) * second.size + second.place
    own_rows, width = tokens.shape
    segments = segment_ids[0]
    per_group = QH // KVH
    query_width = QH * HD
    pair_width = KVH * HD
    score_scale = 1.0 / math.sqrt(HD)
    first_row = shard.place * own_rows
    part_rows = input_weight.shape[0] // reps
    hidden_units = gate_weight.shape[1]
    block_units = hidden_units // shards

    def gather_weight(weight):
        piece = pick(weight.reshape(reps, part_rows, weight.shape[1]), rep_place, 0)
        column = stack_by_place(gather_line(piece, shard), shard)
        whole = jnp.zeros((shards, reps, part_rows, weight.shape[1]), weight.dtype)
        for place, value in gather_rep(column, core, first, second):
            whole = put(whole, value, place, 1)
        return whole.reshape(width, weight.shape[1])

    def gather_column_blocks(weights):
        pieces = jnp.stack(
            [
                pick(weight.reshape(reps, part_rows, hidden_units), rep_place, 0)
                .reshape(part_rows, shards, block_units)
                .transpose(1, 0, 2)
                for weight in weights
            ],
            axis=1,
        )
        rows = [pick(pieces, shard.place, 0)] + [
            shard.shift(pick(pieces, shard.ahead(step), 0), step) for step in range(1, shards)
        ]
        column = stack_by_place(rows, shard, 1)
        wholes = [jnp.zeros((shards, reps, part_rows, block_units), bf16) for _ in weights]
        for place, value in gather_rep(column, core, first, second):
            wholes = [put(whole, value[at], place, 1) for at, whole in enumerate(wholes)]
        return [whole.reshape(width, block_units) for whole in wholes]

    input_matrix = gather_weight(input_weight)
    shard_vectors = jnp.concatenate([first_gain, second_gain, input_bias])
    vector_rows = stack_by_place(gather_line(shard_vectors, shard), shard)
    own_gain = first_gain.shape[0]
    gain_one = vector_rows[:, :own_gain].reshape(width).astype(f32)
    gain_two = vector_rows[:, own_gain : 2 * own_gain].reshape(width).astype(f32)
    shift_row = vector_rows[:, 2 * own_gain :].reshape(-1).astype(f32)

    places = positions(segments)
    own_segments = lax.dynamic_slice_in_dim(segments, first_row, own_rows)
    cosine_table, sine_table = rope_tables(
        lax.dynamic_slice_in_dim(places, first_row, own_rows), HD
    )
    wide_tokens = tokens.astype(f32)
    inverse_one = lax.rsqrt(jnp.mean(wide_tokens * wide_tokens, axis=-1, keepdims=True) + EPSILON)
    unit_one = wide_tokens * inverse_one
    normed_one = (unit_one * gain_one).astype(bf16)
    output_matrix = gather_weight(output_weight)
    gate_matrix, up_matrix = gather_column_blocks([gate_weight, up_weight])

    projected = jnp.dot(normed_one, input_matrix, preferred_element_type=f32) + shift_row
    queries = rotate(
        projected[:, :query_width].reshape(own_rows, QH, HD), cosine_table, sine_table
    ).astype(bf16)
    key_part = rotate(
        projected[:, query_width : query_width + pair_width].reshape(own_rows, KVH, HD),
        cosine_table,
        sine_table,
    )
    own_pairs = jnp.concatenate(
        [key_part.reshape(own_rows, pair_width), projected[:, query_width + pair_width :]], axis=1
    ).astype(bf16)
    pairs = jnp.concatenate(gather_line(own_pairs, shard), axis=0)
    group_rows = pairs.shape[0]
    row_index = jnp.arange(own_rows, dtype=jnp.int32)
    key_index = jnp.concatenate([shard.behind(step) * own_rows + row_index for step in range(shards)])
    key_segments = jnp.concatenate(
        [
            lax.dynamic_slice_in_dim(segments, shard.behind(step) * own_rows, own_rows)
            for step in range(shards)
        ]
    )
    query_index = first_row + row_index
    allowed = (own_segments[:, None] == key_segments[None, :]) & (
        key_index[None, :] <= query_index[:, None]
    )
    grouped_queries = queries.reshape(own_rows, KVH, per_group, HD)
    keys = pairs[:, :pair_width].reshape(group_rows, KVH, HD)
    values = pairs[:, pair_width:].reshape(group_rows, KVH, HD)
    raw_scores = (
        jnp.einsum("tkgd,jkd->kgtj", grouped_queries, keys, preferred_element_type=f32)
        * score_scale
    )
    masked = jnp.where(allowed[None, None], raw_scores, MASKED)
    top_score = jnp.max(masked, axis=-1, keepdims=True)
    log_norm = top_score + jnp.log(jnp.sum(jnp.exp(masked - top_score), axis=-1, keepdims=True))
    shares = jnp.where(allowed[None, None], jnp.exp(masked - log_norm), 0.0)
    shares_low = shares.astype(bf16)
    attention_low = (
        jnp.einsum("kgtj,jkd->tkgd", shares_low, values, preferred_element_type=f32)
        .reshape(own_rows, query_width)
        .astype(bf16)
    )
    hidden = wide_tokens + jnp.dot(attention_low, output_matrix, preferred_element_type=f32)
    inverse_two = lax.rsqrt(jnp.mean(hidden * hidden, axis=-1, keepdims=True) + EPSILON)
    unit_two = hidden * inverse_two
    normed_two = (unit_two * gain_two).astype(bf16)

    cotangents = jnp.concatenate(gather_line(output_cotangent, shard), axis=0)
    group_normed = jnp.concatenate(gather_line(normed_two, shard), axis=0)

    def sum_rows(rows):
        blocks = rows.reshape(shards, own_rows, width)
        total = blocks[0]
        for step in range(1, shards):
            total = total + shard.shift(blocks[step].astype(bf16), shards - step).astype(f32)
        return total

    gate_linear = jnp.dot(group_normed, gate_matrix, preferred_element_type=f32)
    up_linear = jnp.dot(group_normed, up_matrix, preferred_element_type=f32)
    gate_sigmoid = jax.nn.sigmoid(gate_linear)
    gate_output = gate_linear * gate_sigmoid
    inner_act = (gate_output * up_linear).astype(bf16)
    inner_gradient = times_transposed(cotangents, down_weight)

    down_blocks = transposed_times(inner_act, cotangents).astype(bf16)
    down_piece = sum_rep(
        down_blocks.reshape(reps, block_units // reps, width), 0, core, first, second
    )

    gate_gradient_rows = (
        inner_gradient * up_linear * gate_sigmoid * (1.0 + gate_linear * (1.0 - gate_sigmoid))
    ).astype(bf16)
    up_gradient_rows = (inner_gradient * gate_output).astype(bf16)
    normed_two_gradient = sum_rows(
        times_transposed(gate_gradient_rows, gate_matrix)
        + times_transposed(up_gradient_rows, up_matrix)
    )

    def column_gradient(gradient_rows):
        partial = transposed_times(group_normed, gradient_rows).astype(bf16)
        piece = sum_rep(
            partial.reshape(shards, reps, part_rows, block_units), 1, core, first, second
        )
        rows = [pick(piece, shard.place, 0)] + [
            shard.shift(pick(piece, shard.ahead(step), 0), step) for step in range(1, shards)
        ]
        return (
            stack_by_place(rows, shard).transpose(1, 0, 2).reshape(part_rows, shards * block_units)
        )

    def spread(piece):
        rows = piece.shape[0]
        whole = jnp.zeros((reps,) + piece.shape, f32)
        for place, value in gather_rep(piece, core, first, second):
            whole = put(whole, value.astype(f32), place, 0)
        return whole.reshape(reps * rows, piece.shape[1])

    gate_piece = column_gradient(gate_gradient_rows)
    up_piece = column_gradient(up_gradient_rows)
    down_total = spread(down_piece)
    gate_total = spread(gate_piece)
    up_total = spread(up_piece)
    block_out = (
        hidden + sum_rows(jnp.dot(inner_act, down_weight, preferred_element_type=f32))
    ).astype(bf16)

    gain_two_gradient = jnp.sum(normed_two_gradient * unit_two, axis=0)
    hidden_gradient = output_cotangent.astype(f32) + norm_back(
        normed_two_gradient, unit_two, inverse_two, gain_two
    )
    branch_gradient = hidden_gradient.astype(bf16)

    def row_gradient(partial):
        columns = partial.shape[1]
        piece = sum_rep(
            partial.astype(bf16).reshape(shards, reps, part_rows, columns), 1, core, first, second
        )
        return spread(sum_line(piece, shard, 0))

    output_total = row_gradient(transposed_times(attention_low, branch_gradient))
    attention_gradient = times_transposed(branch_gradient, output_matrix).astype(bf16)
    grouped_gradient = attention_gradient.reshape(own_rows, KVH, per_group, HD)
    share_gradient = jnp.einsum(
        "tkgd,jkd->kgtj", grouped_gradient, values, preferred_element_type=f32
    )
    share_dot = jnp.sum(shares * share_gradient, axis=-1, keepdims=True)
    score_gradient = (shares * (share_gradient - share_dot)).astype(bf16)
    query_gradient = jnp.einsum(
        "kgtj,jkd->tkgd", score_gradient, keys, preferred_element_type=f32
    )
    key_gradient = (
        jnp.einsum("kgtj,tkgd->jkd", score_gradient, grouped_queries, preferred_element_type=f32)
        * score_scale
    )
    value_gradient = jnp.einsum(
        "kgtj,tkgd->jkd", shares_low, grouped_gradient, preferred_element_type=f32
    )
    pair_blocks = jnp.concatenate(
        [
            key_gradient.reshape(group_rows, pair_width),
            value_gradient.reshape(group_rows, pair_width),
        ],
        axis=1,
    ).reshape(shards, own_rows, 2 * pair_width)
    pair_gradients = pair_blocks[0]
    for step in range(1, shards):
        pair_gradients = pair_gradients + shard.shift(
            pair_blocks[step].astype(bf16), shards - step
        ).astype(f32)
    query_back = rotate_back(
        (query_gradient * score_scale).reshape(own_rows, QH, HD), cosine_table, sine_table
    ).reshape(own_rows, query_width)
    key_back = rotate_back(
        pair_gradients[:, :pair_width].reshape(own_rows, KVH, HD), cosine_table, sine_table
    ).reshape(own_rows, pair_width)
    projected_gradient = jnp.concatenate(
        [query_back, key_back, pair_gradients[:, pair_width:]], axis=1
    ).astype(bf16)
    input_total = row_gradient(transposed_times(normed_one, projected_gradient))
    bias_gradient = jnp.sum(projected_gradient.astype(f32), axis=0)
    bias_split = query_width + pair_width
    normed_one_gradient = times_transposed(projected_gradient, input_matrix)
    gain_one_gradient = jnp.sum(normed_one_gradient * unit_one, axis=0)
    tokens_gradient = (
        hidden_gradient + norm_back(normed_one_gradient, unit_one, inverse_one, gain_one)
    ).astype(bf16)

    small_parts = (
        gain_one_gradient,
        gain_two_gradient,
        bias_gradient[:bias_split],
        bias_gradient[bias_split:],
    )
    small_rows = jnp.concatenate([part.reshape(shards, -1) for part in small_parts], axis=1)
    small = sum_line(small_rows, shard, 0)
    for line in (core, first, second):
        total = small
        for step in range(1, line.size):
            total = total + line.shift(small, step)
        small = total
    small_totals, at = [], 0
    for part in small_parts:
        size = part.shape[0] // shards
        small_totals.append(small[at : at + size])
        at += size
    return (
        block_out,
        tokens_gradient,
        small_totals[0],
        input_total,
        small_totals[2],
        small_totals[3],
        output_total,
        small_totals[1],
        gate_total,
        up_total,
        down_total,
    )


def solution(mesh):
    placed = (
        P(("rep", "shard"), None),
        P("rep", None),
        P("shard"),
        P("shard", None),
        P("shard"),
        P("shard", None),
        P("shard"),
        P("shard", None),
        P("shard", None),
        P("shard", None),
        P(("rep", "shard"), None),
    )
    return jax.shard_map(
        on_device,
        mesh=mesh,
        in_specs=placed,
        out_specs=(
            P(("rep", "shard"), None),
            P(("rep", "shard"), None),
            P("shard"),
            P("shard", None),
            P("shard"),
            P("shard"),
            P("shard", None),
            P("shard"),
            P("shard", None),
            P("shard", None),
            P("shard", None),
        ),
        check_vma=False,
    )
```

```python
import math

import jax
import jax.numpy as jnp
from jax import lax
from jax.experimental import pallas as pl
from jax.experimental.pallas import tpu as pltpu
from jax.sharding import PartitionSpec as P

QH = 12
KVH = 2
HD = 128
SEQS = 3


EPSILON = 1e-06
LOG_THETA = math.log(1000000.0)
MASKED = -1e30
VMEM_LIMIT = 56 * 1024 * 1024
TILE = 512


def rope_tables(places, head_width):
    half_width = head_width // 2
    frequency = jnp.exp(jnp.arange(half_width, dtype=jnp.float32) * (-2.0 * LOG_THETA / head_width))
    angles = places.astype(jnp.float32)[:, None] * frequency[None, :]
    angles = jnp.concatenate([angles, angles], axis=-1)
    return (jnp.cos(angles), jnp.sin(angles))


def positions(segments):
    labels = jnp.arange(SEQS, dtype=jnp.int32)
    starts = jnp.sum((segments[None, :] < labels[:, None]).astype(jnp.int32), axis=1)
    own_start = jnp.sum(jnp.where(segments[:, None] == labels[None, :], starts[None, :], 0), axis=1)
    return jnp.arange(segments.shape[0], dtype=jnp.int32) - own_start


def rotate(field_rows, cosine_table, sine_table):
    half_width = field_rows.shape[-1] // 2
    turned = jnp.concatenate([-field_rows[..., half_width:], field_rows[..., :half_width]], axis=-1)
    return field_rows * cosine_table[:, None, :] + turned * sine_table[:, None, :]


def rotate_back(gradient, cosine_table, sine_table):
    half_width = gradient.shape[-1] // 2
    moved_part = gradient * sine_table[:, None, :]
    turned = jnp.concatenate([moved_part[..., half_width:], -moved_part[..., :half_width]], axis=-1)
    return gradient * cosine_table[:, None, :] + turned


def transposed_times(left_side, right_side):
    return lax.dot_general(
        left_side, right_side, (((0,), (0,)), ((), ())), preferred_element_type=jnp.float32
    )


def times_transposed(left_side, right_side):
    return lax.dot_general(
        left_side, right_side, (((1,), (1,)), ((), ())), preferred_element_type=jnp.float32
    )


def norm_back(normed_gradient, unit_rows, inverse_rms, gain_row):
    scaled = normed_gradient * gain_row
    return inverse_rms * (scaled - unit_rows * jnp.mean(scaled * unit_rows, axis=-1, keepdims=True))


class Line:
    def __init__(self, name, size, place, pairs, crossed=False):
        self.name, self.size, self.place, self.pairs = name, size, place, pairs
        self.crossed = crossed

    def shift(self, value, step):
        return lax.ppermute(value, self.name, self.pairs(step % self.size))

    def behind(self, step):
        return lax.rem(self.place + (self.size - step % self.size), self.size)

    def ahead(self, step):
        return lax.rem(self.place + step % self.size, self.size)


def make_lines(reps, shards):
    inner = 2 if reps % 4 == 0 else 1
    outer = reps // (2 * inner)
    square = inner == outer

    def split(index):
        core, b, a = index % 2, (index // 2) % inner, index // (2 * inner)
        return core, b, a

    def join(core, b, a):
        return (a * inner + b) * 2 + core

    def first_pairs(step):
        pairs = []
        for index in range(reps):
            core, b, a = split(index)
            if square and core == 0:
                pairs.append((index, join(core, (b + step) % inner, a)))
            else:
                pairs.append((index, join(core, b, (a + step) % outer)))
        return pairs

    def second_pairs(step):
        pairs = []
        for index in range(reps):
            core, b, a = split(index)
            if square and core == 0:
                pairs.append((index, join(core, b, (a + step) % outer)))
            else:
                pairs.append((index, join(core, (b + step) % inner, a)))
        return pairs

    def core_pairs(step):
        pairs = []
        for index in range(reps):
            core, b, a = split(index)
            pairs.append((index, join((core + step) % 2, b, a)))
        return pairs

    def shard_pairs(step):
        return [(index, (index + step) % shards) for index in range(shards)]

    core, b, a = split(lax.axis_index("rep"))
    first, second = (jnp.where(core == 0, b, a), jnp.where(core == 0, a, b)) if square else (a, b)
    return (
        Line("shard", shards, lax.axis_index("shard"), shard_pairs),
        Line("rep", 2, core, core_pairs, square),
        Line("rep", outer, first, first_pairs),
        Line("rep", inner, second, second_pairs),
    )


def pick(array, index, axis):
    return lax.dynamic_index_in_dim(array, index, axis, keepdims=False)


def put(array, piece, index, axis):
    return lax.dynamic_update_index_in_dim(array, piece, index, axis)


def in_place_order(pieces, line):
    ordered = []
    for place in range(line.size):
        chosen = pieces[0]
        for step in range(1, line.size):
            chosen = jnp.where(line.behind(step) == place, pieces[step], chosen)
        ordered.append(chosen)
    return ordered


def tie(*arrays):
    return lax.optimization_barrier(arrays)


def gather_line(value, line):
    return [value] + [line.shift(value, step) for step in range(1, line.size)]


def send_sums(blocks, line, axis):
    return [line.shift(pick(blocks, line.ahead(step), axis), step) for step in range(1, line.size)]


def add_sums(blocks, line, axis, arrived):
    total = pick(blocks, line.place, axis).astype(jnp.float32)
    for block in arrived:
        total = total + block.astype(jnp.float32)
    return total.astype(blocks.dtype)


class Spread:
    def __init__(self, piece, core, first, second):
        self.lines = core, first, second
        self.held = [(0, 0, piece)]
        for step in range(1, second.size):
            self.held.append((0, step, second.shift(piece, step)))
        for step in range(1, first.size):
            self.held.append((step, 0, first.shift(piece, step)))

    def arrived(self):
        return [value for one, two, value in self.held[1:]]

    def replace(self, values):
        self.held = self.held[:1] + [
            (one, two, value) for (one, two, old), value in zip(self.held[1:], values)
        ]

    def further(self):
        core, first, second = self.lines
        for step in range(1, first.size):
            for one, two, value in [entry for entry in self.held if entry[0] == 0 and entry[1]]:
                self.held.append((step, two, first.shift(value, step)))

    def finish(self):
        core, first, second = self.lines
        placed = [
            (core.place, first.behind(one), second.behind(two), value)
            for one, two, value in self.held
        ]
        there, here = (second, first) if core.crossed else (first, second)
        for one, two, value in self.held:
            placed.append(
                (core.behind(1), there.behind(one), here.behind(two), core.shift(value, 1))
            )
        places = [(c * first.size + f) * second.size + s for c, f, s, value in placed]
        return jnp.stack(places).astype(jnp.int32), [value for c, f, s, value in placed]


def place_blocks(order, places, pieces):
    reps, shards = len(pieces), pieces[0].shape[0]
    block = pieces[0].shape[1:]

    def body(order_ref, places_ref, *refs):
        sources, (out_ref, held, in_sems, out_sems) = refs[:reps], refs[reps:]
        loads = [
            [
                pltpu.make_async_copy(
                    sources[r].at[k], held.at[k, places_ref[r]], in_sems.at[r, k]
                )
                for r in range(reps)
            ]
            for k in range(shards)
        ]
        stores = [
            pltpu.make_async_copy(held.at[k], out_ref.at[order_ref[k]], out_sems.at[k])
            for k in range(shards)
        ]
        for k in range(shards):
            for r in range(reps):
                loads[k][r].start()
        for k in range(shards):
            for r in range(reps):
                loads[k][r].wait()
            stores[k].start()
        for store in stores:
            store.wait()

    return pl.pallas_call(
        body,
        out_shape=jax.ShapeDtypeStruct((shards, reps) + block, pieces[0].dtype),
        in_specs=[pl.BlockSpec(memory_space=pltpu.SMEM)] * 2
        + [pl.BlockSpec(memory_space=pl.ANY)] * reps,
        out_specs=pl.BlockSpec(memory_space=pl.ANY),
        scratch_shapes=[
            pltpu.VMEM((shards, reps) + block, pieces[0].dtype),
            pltpu.SemaphoreType.DMA((reps, shards)),
            pltpu.SemaphoreType.DMA((shards,)),
        ],
        compiler_params=pltpu.CompilerParams(vmem_limit_bytes=VMEM_LIMIT),
        name="place_blocks",
    )(order, places, *pieces)


def widen_pieces(places, pieces):
    reps = len(pieces)
    rows, columns = pieces[0].shape
    strip = next(size for size in (16, 8, rows) if rows % size == 0)

    def body(places_ref, *refs):
        sources, (out_ref, narrow, wide, in_sems, out_sems) = refs[:reps], refs[reps:]
        loads = [
            pltpu.make_async_copy(sources[r], narrow.at[r], in_sems.at[r]) for r in range(reps)
        ]
        stores = [
            pltpu.make_async_copy(wide.at[r], out_ref.at[places_ref[r]], out_sems.at[r])
            for r in range(reps)
        ]
        for load in loads:
            load.start()
        for r in range(reps):
            loads[r].wait()

            def convert(at, carry):
                cut = pl.ds(pl.multiple_of(at * strip, strip), strip)
                wide[r, cut, :] = narrow[r, cut, :].astype(jnp.float32)
                return carry

            lax.fori_loop(0, rows // strip, convert, 0)
            stores[r].start()
        for store in stores:
            store.wait()

    return pl.pallas_call(
        body,
        out_shape=jax.ShapeDtypeStruct((reps, rows, columns), jnp.float32),
        in_specs=[pl.BlockSpec(memory_space=pltpu.SMEM)]
        + [pl.BlockSpec(memory_space=pl.ANY)] * reps,
        out_specs=pl.BlockSpec(memory_space=pl.ANY),
        scratch_shapes=[
            pltpu.VMEM((reps, rows, columns), jnp.bfloat16),
            pltpu.VMEM((reps, rows, columns), jnp.float32),
            pltpu.SemaphoreType.DMA((reps,)),
            pltpu.SemaphoreType.DMA((reps,)),
        ],
        compiler_params=pltpu.CompilerParams(vmem_limit_bytes=VMEM_LIMIT),
        name="widen_pieces",
    )(places, *pieces).reshape(reps * rows, columns)


def resident(shape):
    return pl.BlockSpec(shape, lambda i: (0, 0), pipeline_mode=pl.Buffered(1))


def cost(flops):
    return pl.CostEstimate(flops=flops, bytes_accessed=0, transcendentals=0)


def feed_forward(rows, cotangents, gate_matrix, up_matrix, down_matrix):
    count, width = rows.shape
    units = gate_matrix.shape[1]

    def body(rows_ref, cotangents_ref, gate_ref, up_ref, down_ref, inner_ref, d_gate_ref, d_up_ref):
        gate = jnp.dot(rows_ref[...], gate_ref[...], preferred_element_type=jnp.float32)
        up = jnp.dot(rows_ref[...], up_ref[...], preferred_element_type=jnp.float32)
        sigmoid = jax.nn.sigmoid(gate)
        silu = gate * sigmoid
        inner_ref[...] = (silu * up).astype(jnp.bfloat16)
        d_inner = times_transposed(cotangents_ref[...], down_ref[...])
        d_up_ref[...] = (d_inner * silu).astype(jnp.bfloat16)
        d_gate_ref[...] = (d_inner * up * sigmoid * (1.0 + gate * (1.0 - sigmoid))).astype(
            jnp.bfloat16
        )

    columns = pl.BlockSpec((width, TILE), lambda i: (0, i))
    results = pl.BlockSpec((count, TILE), lambda i: (0, i))
    return pl.pallas_call(
        body,
        grid=(pl.cdiv(units, TILE),),
        out_shape=[jax.ShapeDtypeStruct((count, units), jnp.bfloat16)] * 3,
        in_specs=[
            resident((count, width)),
            resident((count, width)),
            columns,
            columns,
            pl.BlockSpec((TILE, width), lambda i: (i, 0)),
        ],
        out_specs=[results] * 3,
        compiler_params=pltpu.CompilerParams(vmem_limit_bytes=VMEM_LIMIT),
        cost_estimate=cost(2 * count * width * units),
        name="feed_forward",
    )(rows, cotangents, gate_matrix, up_matrix, down_matrix)


def split_gradient(left, right, groups, core_place):
    count, rows = left.shape
    columns = right.shape[1]
    half = rows // (2 * groups)

    def body(core_ref, left_ref, right_ref, other_ref, own_ref, turned):
        @pl.when(pl.program_id(0) == 0)
        def turn():
            turned[...] = left_ref[...].T

        core = core_ref[0]
        for out_ref, which in ((other_ref, 1 - core), (own_ref, core)):
            for group in range(groups):
                at = pl.multiple_of((2 * group + which) * half, 16)
                out_ref[group * half : (group + 1) * half, :] = jnp.dot(
                    turned[pl.ds(at, half), :], right_ref[...], preferred_element_type=jnp.float32
                ).astype(jnp.bfloat16)

    results = pl.BlockSpec((rows // 2, TILE), lambda i: (0, i))
    return pl.pallas_call(
        body,
        grid=(pl.cdiv(columns, TILE),),
        out_shape=[jax.ShapeDtypeStruct((rows // 2, columns), jnp.bfloat16)] * 2,
        in_specs=[
            pl.BlockSpec(memory_space=pltpu.SMEM),
            resident((count, rows)),
            pl.BlockSpec((count, TILE), lambda i: (0, i)),
        ],
        out_specs=[results] * 2,
        scratch_shapes=[pltpu.VMEM((rows, count), jnp.bfloat16)],
        compiler_params=pltpu.CompilerParams(vmem_limit_bytes=VMEM_LIMIT),
        cost_estimate=cost(count * rows * columns),
        name="split_gradient",
    )(core_place.reshape(1).astype(jnp.int32), left, right)


def rows_product(lefts, rights, turned, blocks):
    count, depth = lefts[0].shape
    columns = rights[0].shape[0 if turned else 1]
    pairs, part = len(lefts), count // blocks

    def body(*refs):
        total = None
        for left_ref, right_ref in zip(refs[:pairs], refs[pairs : 2 * pairs]):
            if turned:
                product = times_transposed(left_ref[...], right_ref[...])
            else:
                product = jnp.dot(
                    left_ref[...], right_ref[...], preferred_element_type=jnp.float32
                )
            total = product if total is None else total + product
        for block in range(blocks):
            refs[2 * pairs + block][...] = total[block * part : (block + 1) * part].astype(
                jnp.bfloat16
            )

    right_spec = (
        pl.BlockSpec((TILE, depth), lambda i: (i, 0))
        if turned
        else pl.BlockSpec((depth, TILE), lambda i: (0, i))
    )
    return pl.pallas_call(
        body,
        grid=(pl.cdiv(columns, TILE),),
        out_shape=[jax.ShapeDtypeStruct((part, columns), jnp.bfloat16)] * blocks,
        in_specs=[resident((count, depth))] * pairs + [right_spec] * pairs,
        out_specs=[pl.BlockSpec((part, TILE), lambda i: (0, i))] * blocks,
        compiler_params=pltpu.CompilerParams(vmem_limit_bytes=VMEM_LIMIT),
        cost_estimate=cost(pairs * count * depth * columns),
        name="rows_product",
    )(*lefts, *rights)


def on_device(
    tokens,
    segment_ids,
    first_gain,
    input_weight,
    input_bias,
    output_weight,
    second_gain,
    gate_weight,
    up_weight,
    down_weight,
    output_cotangent,
):
    bf16, f32 = jnp.bfloat16, jnp.float32
    shards, reps = lax.axis_size("shard"), lax.axis_size("rep")
    shard, core, first, second = make_lines(reps, shards)
    rep_place = (core.place * first.size + first.place) * second.size + second.place
    own_rows, width = tokens.shape
    segments = segment_ids[0]
    per_group = QH // KVH
    query_width = QH * HD
    pair_width = KVH * HD
    score_scale = 1.0 / math.sqrt(HD)
    first_row = shard.place * own_rows
    part_rows = input_weight.shape[0] // reps
    hidden_units = gate_weight.shape[1]
    block_units = hidden_units // shards

    z_order = jnp.stack([shard.behind(step) for step in range(shards)]).astype(jnp.int32)

    def weight_piece(weight):
        return pick(weight.reshape(reps, part_rows, weight.shape[1]), rep_place, 0)

    def column_pieces(weights):
        return jnp.stack(
            [
                weight_piece(weight).reshape(part_rows, shards, block_units).transpose(1, 0, 2)
                for weight in weights
            ],
            axis=1,
        )

    input_rows = gather_line(weight_piece(input_weight), shard)
    shard_vectors = jnp.concatenate([first_gain, second_gain, input_bias])
    vector_rows = jnp.stack(in_place_order(gather_line(shard_vectors, shard), shard))
    own_gain = first_gain.shape[0]
    gain_one = vector_rows[:, :own_gain].reshape(width).astype(f32)
    gain_two = vector_rows[:, own_gain : 2 * own_gain].reshape(width).astype(f32)
    shift_row = vector_rows[:, 2 * own_gain :].reshape(-1).astype(f32)

    output_piece, gate_weight, up_weight, *input_rows = tie(
        weight_piece(output_weight), gate_weight, up_weight, *input_rows
    )
    output_rows = gather_line(output_piece, shard)
    input_spread = Spread(jnp.stack(input_rows), core, first, second)
    columns = column_pieces([gate_weight, up_weight])
    columns, *output_rows = tie(columns, *output_rows)
    column_rows = [pick(columns, shard.place, 0)] + [
        shard.shift(pick(columns, shard.ahead(step), 0), step) for step in range(1, shards)
    ]
    input_spread.further()
    input_matrix = place_blocks(z_order, *input_spread.finish()).reshape(width, -1)

    places = positions(segments)
    own_segments = lax.dynamic_slice_in_dim(segments, first_row, own_rows)
    cosine_table, sine_table = rope_tables(
        lax.dynamic_slice_in_dim(places, first_row, own_rows), HD
    )
    wide_tokens = tokens.astype(f32)
    inverse_one = lax.rsqrt(jnp.mean(wide_tokens * wide_tokens, axis=-1, keepdims=True) + EPSILON)
    unit_one = wide_tokens * inverse_one
    normed_one = (unit_one * gain_one).astype(bf16)
    output_column, input_matrix = tie(jnp.stack(output_rows), input_matrix)
    output_spread = Spread(output_column, core, first, second)
    projected = jnp.dot(normed_one, input_matrix, preferred_element_type=f32) + shift_row
    queries = rotate(
        projected[:, :query_width].reshape(own_rows, QH, HD), cosine_table, sine_table
    ).astype(bf16)
    key_part = rotate(
        projected[:, query_width : query_width + pair_width].reshape(own_rows, KVH, HD),
        cosine_table,
        sine_table,
    )
    own_pairs = jnp.concatenate(
        [key_part.reshape(own_rows, pair_width), projected[:, query_width + pair_width :]], axis=1
    ).astype(bf16)
    pair_rows = gather_line(own_pairs, shard)
    output_spread.further()
    output_matrix = place_blocks(z_order, *output_spread.finish()).reshape(width, width)
    gate_up_column, output_matrix = tie(jnp.stack(column_rows, axis=1), output_matrix)
    gate_up_spread = Spread(gate_up_column, core, first, second)
    gate_up_spread.further()
    gate_up_places, gate_up_pieces = gate_up_spread.finish()
    gate_matrix, up_matrix = (
        place_blocks(z_order, gate_up_places, [piece[at] for piece in gate_up_pieces]).reshape(
            width, block_units
        )
        for at in range(2)
    )
    output_cotangent, *pair_rows = tie(output_cotangent, *pair_rows)
    cotangents = jnp.concatenate(gather_line(output_cotangent, shard), axis=0)
    pairs = jnp.concatenate(pair_rows, axis=0)
    group_rows = pairs.shape[0]
    row_index = jnp.arange(own_rows, dtype=jnp.int32)
    key_index = jnp.concatenate([shard.behind(step) * own_rows + row_index for step in range(shards)])
    key_segments = jnp.concatenate(
        [
            lax.dynamic_slice_in_dim(segments, shard.behind(step) * own_rows, own_rows)
            for step in range(shards)
        ]
    )
    query_index = first_row + row_index
    allowed = (own_segments[:, None] == key_segments[None, :]) & (
        key_index[None, :] <= query_index[:, None]
    )
    grouped_queries = queries.reshape(own_rows, KVH, per_group, HD)
    keys = pairs[:, :pair_width].reshape(group_rows, KVH, HD)
    values = pairs[:, pair_width:].reshape(group_rows, KVH, HD)
    raw_scores = (
        jnp.einsum("tkgd,jkd->kgtj", grouped_queries, keys, preferred_element_type=f32)
        * score_scale
    )
    masked = jnp.where(allowed[None, None], raw_scores, MASKED)
    top_score = jnp.max(masked, axis=-1, keepdims=True)
    log_norm = top_score + jnp.log(jnp.sum(jnp.exp(masked - top_score), axis=-1, keepdims=True))
    shares = jnp.where(allowed[None, None], jnp.exp(masked - log_norm), 0.0)
    shares_low = shares.astype(bf16)
    attention_low = (
        jnp.einsum("kgtj,jkd->tkgd", shares_low, values, preferred_element_type=f32)
        .reshape(own_rows, query_width)
        .astype(bf16)
    )
    hidden = wide_tokens + jnp.dot(attention_low, output_matrix, preferred_element_type=f32)
    inverse_two = lax.rsqrt(jnp.mean(hidden * hidden, axis=-1, keepdims=True) + EPSILON)
    unit_two = hidden * inverse_two
    normed_two = (unit_two * gain_two).astype(bf16)

    group_normed = jnp.concatenate(gather_line(normed_two, shard), axis=0)

    def send_rows(rows):
        return [
            shard.shift(rows[step].astype(bf16), shards - step) for step in range(1, shards)
        ]

    def add_rows(own, arrived):
        total = own.astype(f32)
        for block in arrived:
            total = total + block.astype(f32)
        return total

    def by_columns(piece):
        rows = [pick(piece, shard.place, 0)] + send_sums(piece, shard, 0)
        return jnp.concatenate(in_place_order(rows, shard), axis=1)

    plane = (first.size, second.size)

    def add_half(own, arrived, shape):
        return (own.astype(f32) + arrived.astype(f32)).astype(bf16).reshape(shape)

    by_rows = (shards,) + plane + (part_rows, block_units)
    by_units = plane + (block_units // reps, width)

    inner_act, gate_gradient_rows, up_gradient_rows = feed_forward(
        group_normed, cotangents, gate_matrix, up_matrix, down_weight
    )

    down_sent, down_own = split_gradient(inner_act, cotangents, 1, core.place)
    gate_gradient_rows, up_gradient_rows, down_own = tie(
        gate_gradient_rows, up_gradient_rows, down_own
    )
    down_arrived = core.shift(down_sent, 1)
    normed_own, *normed_partial = rows_product(
        (gate_gradient_rows, up_gradient_rows), (gate_matrix, up_matrix), True, shards
    )
    normed_arrived = send_rows([None] + normed_partial)

    down_arrived, normed_own = tie(down_arrived, normed_own)
    down_sum = add_half(down_own, down_arrived, by_units)
    group_normed, down_sum = tie(group_normed, down_sum)
    down_first = send_sums(down_sum, first, 0)
    gate_sent, gate_own = split_gradient(group_normed, gate_gradient_rows, shards, core.place)
    up_gradient_rows, gate_own = tie(up_gradient_rows, gate_own)
    gate_arrived = core.shift(gate_sent, 1)
    up_sent, up_own = split_gradient(group_normed, up_gradient_rows, shards, core.place)
    gate_arrived, up_own = tie(gate_arrived, up_own)
    up_arrived = core.shift(up_sent, 1)
    gate_sum = add_half(gate_own, gate_arrived, by_rows)
    *down_first, gate_sum = tie(*down_first, gate_sum)
    gate_first = send_sums(gate_sum, first, 1)
    down_sum = add_sums(down_sum, first, 0, down_first)
    up_arrived, down_sum = tie(up_arrived, down_sum)
    down_second = send_sums(down_sum, second, 0)
    up_sum = add_half(up_own, up_arrived, by_rows)
    *gate_first, up_sum = tie(*gate_first, up_sum)
    up_first = send_sums(up_sum, first, 1)
    gate_sum = add_sums(gate_sum, first, 1, gate_first)
    *down_second, gate_sum = tie(*down_second, gate_sum)
    gate_second = send_sums(gate_sum, second, 1)
    down_piece = add_sums(down_sum, second, 0, down_second)

    *normed_arrived, down_piece = tie(*normed_arrived, down_piece)
    down_spread = Spread(down_piece, core, first, second)
    normed_two_gradient = add_rows(normed_own, normed_arrived)
    gain_two_gradient = jnp.sum(normed_two_gradient * unit_two, axis=0)
    hidden_gradient = output_cotangent.astype(f32) + norm_back(
        normed_two_gradient, unit_two, inverse_two, gain_two
    )
    branch_gradient = hidden_gradient.astype(bf16)
    *up_first, branch_gradient = tie(*up_first, branch_gradient)
    up_sum = add_sums(up_sum, first, 1, up_first)

    attention_gradient = times_transposed(branch_gradient, output_matrix).astype(bf16)
    *gate_second, attention_gradient, up_sum = tie(*gate_second, attention_gradient, up_sum)
    up_second = send_sums(up_sum, second, 1)
    gate_sum = add_sums(gate_sum, second, 1, gate_second)
    gate_piece = by_columns(gate_sum)

    grouped_gradient = attention_gradient.reshape(own_rows, KVH, per_group, HD)
    share_gradient = jnp.einsum(
        "tkgd,jkd->kgtj", grouped_gradient, values, preferred_element_type=f32
    )
    share_dot = jnp.sum(shares * share_gradient, axis=-1, keepdims=True)
    score_gradient = (shares * (share_gradient - share_dot)).astype(bf16)
    query_gradient = jnp.einsum(
        "kgtj,jkd->tkgd", score_gradient, keys, preferred_element_type=f32
    )
    key_gradient = (
        jnp.einsum("kgtj,tkgd->jkd", score_gradient, grouped_queries, preferred_element_type=f32)
        * score_scale
    )
    value_gradient = jnp.einsum(
        "kgtj,tkgd->jkd", shares_low, grouped_gradient, preferred_element_type=f32
    )
    pair_blocks = jnp.concatenate(
        [
            key_gradient.reshape(group_rows, pair_width),
            value_gradient.reshape(group_rows, pair_width),
        ],
        axis=1,
    ).reshape(shards, own_rows, 2 * pair_width)
    pair_own = pair_blocks[0]
    pair_arrived = send_rows(pair_blocks)

    *down_moved, pair_own = tie(*down_spread.arrived(), pair_own)
    down_spread.replace(down_moved)
    down_spread.further()
    output_sent, output_own = split_gradient(
        attention_low, branch_gradient, shards, core.place
    )
    output_arrived = core.shift(output_sent, 1)
    *up_second, gate_piece, pair_own = tie(*up_second, gate_piece, pair_own)
    gate_spread = Spread(gate_piece, core, first, second)
    up_sum = add_sums(up_sum, second, 1, up_second)
    up_piece = by_columns(up_sum)
    output_arrived, up_sum, output_own = tie(output_arrived, up_sum, output_own)
    output_sum = add_half(output_own, output_arrived, (shards,) + plane + (part_rows, width))
    output_first = send_sums(output_sum, first, 1)

    *pair_arrived, output_sum = tie(*pair_arrived, output_sum)
    pair_gradients = add_rows(pair_own, pair_arrived)
    query_back = rotate_back(
        (query_gradient * score_scale).reshape(own_rows, QH, HD), cosine_table, sine_table
    ).reshape(own_rows, query_width)
    key_back = rotate_back(
        pair_gradients[:, :pair_width].reshape(own_rows, KVH, HD), cosine_table, sine_table
    ).reshape(own_rows, pair_width)
    projected_gradient = jnp.concatenate(
        [query_back, key_back, pair_gradients[:, pair_width:]], axis=1
    ).astype(bf16)
    *down_moved, projected_gradient = tie(*down_spread.arrived(), projected_gradient)
    down_spread.replace(down_moved)
    down_places, down_pieces = down_spread.finish()
    input_sent, input_own = split_gradient(normed_one, projected_gradient, shards, core.place)
    input_arrived = core.shift(input_sent, 1)
    up_spread = Spread(up_piece, core, first, second)

    *gate_moved, input_own = tie(*gate_spread.arrived(), input_own)
    gate_spread.replace(gate_moved)
    gate_spread.further()
    *output_first, input_own = tie(*output_first, input_own)
    output_sum = add_sums(output_sum, first, 1, output_first)
    output_second = send_sums(output_sum, second, 1)
    bias_gradient = jnp.sum(projected_gradient.astype(f32), axis=0)
    bias_split = query_width + pair_width
    normed_one_gradient = times_transposed(projected_gradient, input_matrix)
    normed_one_gradient, input_arrived, input_own = tie(
        normed_one_gradient, input_arrived, input_own
    )
    input_sum = add_half(
        input_own, input_arrived, (shards,) + plane + (part_rows, projected_gradient.shape[1])
    )
    input_first = send_sums(input_sum, first, 1)
    gain_one_gradient = jnp.sum(normed_one_gradient * unit_one, axis=0)
    tokens_gradient = (
        hidden_gradient + norm_back(normed_one_gradient, unit_one, inverse_one, gain_one)
    ).astype(bf16)

    inner_act, input_sum = tie(inner_act, input_sum)
    block_own, *block_partial = rows_product((inner_act,), (down_weight,), False, shards)
    block_arrived = send_rows([None] + block_partial)
    down_total = widen_pieces(down_places, down_pieces)
    *input_first, down_total, block_own = tie(*input_first, down_total, block_own)
    input_sum = add_sums(input_sum, first, 1, input_first)
    input_second = send_sums(input_sum, second, 1)
    *output_second, input_sum = tie(*output_second, input_sum)
    output_sum = add_sums(output_sum, second, 1, output_second)
    output_piece = add_sums(output_sum, shard, 0, send_sums(output_sum, shard, 0))
    *gate_moved, input_sum = tie(*gate_spread.arrived(), input_sum)
    gate_spread.replace(gate_moved)
    gate_places, gate_pieces = gate_spread.finish()
    *input_second, output_sum = tie(*input_second, output_sum)
    input_sum = add_sums(input_sum, second, 1, input_second)
    input_shard = send_sums(input_sum, shard, 0)
    *up_moved, input_sum = tie(*up_spread.arrived(), input_sum)
    up_spread.replace(up_moved)
    up_spread.further()
    gate_total = widen_pieces(gate_places, gate_pieces)
    output_spread = Spread(output_piece, core, first, second)
    output_spread.further()
    up_places, up_pieces = up_spread.finish()
    block_out = add_rows(hidden, [block_own] + block_arrived).astype(bf16)
    output_total = widen_pieces(*output_spread.finish())
    input_shard, gate_total, block_out = (
        lambda *parts: (parts[:-2], parts[-2], parts[-1])
    )(*tie(*input_shard, gate_total, block_out))
    input_piece = add_sums(input_sum, shard, 0, input_shard)
    input_spread = Spread(input_piece, core, first, second)
    input_spread.further()
    up_total = widen_pieces(up_places, up_pieces)
    input_total = widen_pieces(*input_spread.finish())

    small_parts = (
        gain_one_gradient,
        gain_two_gradient,
        bias_gradient[:bias_split],
        bias_gradient[bias_split:],
    )
    small_rows = jnp.concatenate([part.reshape(shards, -1) for part in small_parts], axis=1)
    small = add_sums(small_rows, shard, 0, send_sums(small_rows, shard, 0))
    for line in (core, first, second):
        total = small
        for step in range(1, line.size):
            total = total + line.shift(small, step)
        small = total
    small_totals, at = [], 0
    for part in small_parts:
        size = part.shape[0] // shards
        small_totals.append(small[at : at + size])
        at += size
    return (
        block_out,
        tokens_gradient,
        small_totals[0],
        input_total,
        small_totals[2],
        small_totals[3],
        output_total,
        small_totals[1],
        gate_total,
        up_total,
        down_total,
    )


def solution(mesh):
    placed = (
        P(("rep", "shard"), None),
        P("rep", None),
        P("shard"),
        P("shard", None),
        P("shard"),
        P("shard", None),
        P("shard"),
        P("shard", None),
        P("shard", None),
        P("shard", None),
        P(("rep", "shard"), None),
    )
    return jax.shard_map(
        on_device,
        mesh=mesh,
        in_specs=placed,
        out_specs=(
            P(("rep", "shard"), None),
            P(("rep", "shard"), None),
            P("shard"),
            P("shard", None),
            P("shard"),
            P("shard"),
            P("shard", None),
            P("shard"),
            P("shard", None),
            P("shard", None),
            P("shard", None),
        ),
        check_vma=False,
    )
```

```python
import math

import jax
import jax.numpy as jnp
from jax import lax
from jax.experimental import pallas as pl
from jax.experimental.pallas import tpu as pltpu
from jax.sharding import PartitionSpec as P

QH = 12
KVH = 2
HD = 128
SEQS = 3


EPSILON = 1e-06
LOG_THETA = math.log(1000000.0)
MASKED = -1e30
VMEM_LIMIT = 56 * 1024 * 1024
TILE = 512
COST = pl.CostEstimate(flops=1, bytes_accessed=1, transcendentals=0)


def rope_tables(places, head_width):
    half_width = head_width // 2
    frequency = jnp.exp(jnp.arange(half_width, dtype=jnp.float32) * (-2.0 * LOG_THETA / head_width))
    angles = places.astype(jnp.float32)[:, None] * frequency[None, :]
    angles = jnp.concatenate([angles, angles], axis=-1)
    return (jnp.cos(angles), jnp.sin(angles))


def positions(segments):
    labels = jnp.arange(SEQS, dtype=jnp.int32)
    starts = jnp.sum((segments[None, :] < labels[:, None]).astype(jnp.int32), axis=1)
    own_start = jnp.sum(jnp.where(segments[:, None] == labels[None, :], starts[None, :], 0), axis=1)
    return jnp.arange(segments.shape[0], dtype=jnp.int32) - own_start


def rotate(field_rows, cosine_table, sine_table):
    half_width = field_rows.shape[-1] // 2
    turned = jnp.concatenate([-field_rows[..., half_width:], field_rows[..., :half_width]], axis=-1)
    return field_rows * cosine_table[:, None, :] + turned * sine_table[:, None, :]


def transposed_times(left_side, right_side):
    return lax.dot_general(
        left_side, right_side, (((0,), (0,)), ((), ())), preferred_element_type=jnp.float32
    )


def times_transposed(left_side, right_side):
    return lax.dot_general(
        left_side, right_side, (((1,), (1,)), ((), ())), preferred_element_type=jnp.float32
    )


def norm_back(normed_gradient, unit_rows, inverse_rms, gain_row):
    scaled = normed_gradient * gain_row
    return inverse_rms * (scaled - unit_rows * jnp.mean(scaled * unit_rows, axis=-1, keepdims=True))


class Line:
    def __init__(self, name, size, place, pairs, crossed=False):
        self.name, self.size, self.place, self.pairs = name, size, place, pairs
        self.crossed = crossed

    def shift(self, value, step):
        return lax.ppermute(value, self.name, self.pairs(step % self.size))

    def behind(self, step):
        return lax.rem(self.place + (self.size - step % self.size), self.size)

    def ahead(self, step):
        return lax.rem(self.place + step % self.size, self.size)


def make_lines(reps, shards):
    inner = 2 if reps % 4 == 0 else 1
    outer = reps // (2 * inner)
    square = inner == outer

    def split(index):
        core, b, a = index % 2, (index // 2) % inner, index // (2 * inner)
        return core, b, a

    def join(core, b, a):
        return (a * inner + b) * 2 + core

    def first_pairs(step):
        pairs = []
        for index in range(reps):
            core, b, a = split(index)
            if square and core == 0:
                pairs.append((index, join(core, (b + step) % inner, a)))
            else:
                pairs.append((index, join(core, b, (a + step) % outer)))
        return pairs

    def second_pairs(step):
        pairs = []
        for index in range(reps):
            core, b, a = split(index)
            if square and core == 0:
                pairs.append((index, join(core, b, (a + step) % outer)))
            else:
                pairs.append((index, join(core, (b + step) % inner, a)))
        return pairs

    def core_pairs(step):
        pairs = []
        for index in range(reps):
            core, b, a = split(index)
            pairs.append((index, join((core + step) % 2, b, a)))
        return pairs

    def shard_pairs(step):
        return [(index, (index + step) % shards) for index in range(shards)]

    core, b, a = split(lax.axis_index("rep"))
    first, second = (jnp.where(core == 0, b, a), jnp.where(core == 0, a, b)) if square else (a, b)
    return (
        Line("shard", shards, lax.axis_index("shard"), shard_pairs),
        Line("rep", 2, core, core_pairs, square),
        Line("rep", outer, first, first_pairs),
        Line("rep", inner, second, second_pairs),
    )


def pick(array, index, axis):
    return lax.dynamic_index_in_dim(array, index, axis, keepdims=False)


def put(array, piece, index, axis):
    return lax.dynamic_update_index_in_dim(array, piece, index, axis)


def in_place_order(pieces, line):
    ordered = []
    for place in range(line.size):
        chosen = pieces[0]
        for step in range(1, line.size):
            chosen = jnp.where(line.behind(step) == place, pieces[step], chosen)
        ordered.append(chosen)
    return ordered


def tie(*arrays):
    return lax.optimization_barrier(arrays)


def gather_line(value, line):
    return [value] + [line.shift(value, step) for step in range(1, line.size)]


class Clock:
    def __init__(self):
        self.token = jnp.zeros((8, 128), jnp.float32)

    def __call__(self, *arrays):
        self.token, *arrays = tie(self.token, *arrays)
        return arrays


def total_of(terms):
    total = terms[0].astype(jnp.float32)
    for term in terms[1:]:
        total = total + term.astype(jnp.float32)
    return total


class Halving:
    def __init__(self, clock, terms, axis):
        self.clock, self.terms, self.axis = clock, terms, axis

    def send(self, line):
        self.moving = [
            line.shift(
                total_of([pick(term, line.ahead(step), self.axis) for term in self.terms]).astype(
                    jnp.bfloat16
                ),
                step,
            )
            for step in range(1, line.size)
        ]
        self.terms = [pick(term, line.place, self.axis) for term in self.terms]

    def receive(self):
        self.terms = self.terms + self.clock(*self.moving)


class Spread:
    def __init__(self, clock, piece, core, first, second):
        self.clock, self.lines = clock, (core, first, second)
        self.own = piece
        self.across = {(0, two): second.shift(piece, two) for two in range(1, second.size)}
        self.along = {(one, 0): first.shift(piece, one) for one in range(1, first.size)}
        self.here = {(0, 0): piece}
        self.there = {(0, 0): core.shift(piece, 1)}

    def arrive(self, group):
        for key, value in zip(group, self.clock(*group.values())):
            self.here[key] = value
            self.there[key] = self.lines[0].shift(value, 1)

    def further(self):
        self.arrive(self.across)
        self.beyond = {
            (one, two): self.lines[1].shift(self.here[0, two], one)
            for one in range(1, self.lines[1].size)
            for two in range(1, self.lines[2].size)
        }

    def over(self):
        self.arrive(self.along)
        self.arrive(self.beyond)

    def finish(self):
        core, first, second = self.lines
        placed = [
            (core.place, first.behind(one), second.behind(two), value)
            for (one, two), value in self.here.items()
        ]
        far, near = (second, first) if core.crossed else (first, second)
        others = self.clock(*self.there.values())
        for (one, two), value in zip(self.there, others):
            placed.append((core.behind(1), far.behind(one), near.behind(two), value))
        places = [(c * first.size + f) * second.size + s for c, f, s, value in placed]
        return jnp.stack(places).astype(jnp.int32), [value for c, f, s, value in placed]


def place_blocks(order, places, pieces):
    reps = len(pieces)
    groups, shards = pieces[0].shape[:2]
    block = pieces[0].shape[2:]
    whole = (shards, reps) + block

    def body(order_ref, places_ref, *refs):
        sources, outs, (held, in_sems, out_sems) = (
            refs[:reps],
            refs[reps : reps + groups],
            refs[reps + groups :],
        )
        slabs = [(g, k) for g in range(groups) for k in range(shards)]

        def load(g, k, r):
            return pltpu.make_async_copy(
                sources[r].at[g, k], held.at[g, k, places_ref[r]], in_sems.at[g, k, r]
            )

        def store(g, k):
            return pltpu.make_async_copy(
                held.at[g, k], outs[g].at[order_ref[k]], out_sems.at[g, k]
            )

        for g, k in slabs:
            for r in range(reps):
                load(g, k, r).start()
        for g, k in slabs:
            for r in range(reps):
                load(g, k, r).wait()
            store(g, k).start()
        for g, k in slabs:
            store(g, k).wait()

    return pl.pallas_call(
        body,
        out_shape=[jax.ShapeDtypeStruct(whole, pieces[0].dtype)] * groups,
        in_specs=[pl.BlockSpec(memory_space=pltpu.SMEM)] * 2
        + [pl.BlockSpec(memory_space=pl.ANY)] * reps,
        out_specs=[pl.BlockSpec(memory_space=pl.ANY)] * groups,
        scratch_shapes=[
            pltpu.VMEM((groups,) + whole, pieces[0].dtype),
            pltpu.SemaphoreType.DMA((groups, shards, reps)),
            pltpu.SemaphoreType.DMA((groups, shards)),
        ],
        compiler_params=pltpu.CompilerParams(vmem_limit_bytes=VMEM_LIMIT),
        cost_estimate=COST,
        name="place_blocks",
    )(order, places, *pieces)


def widen_pieces(places, pieces):
    reps = len(pieces)
    rows, columns = pieces[0].shape
    strip = next(size for size in (16, 8, rows) if rows % size == 0)

    def body(places_ref, *refs):
        sources, (out_ref, narrow, wide, in_sems, out_sems) = refs[:reps], refs[reps:]
        loads = [
            pltpu.make_async_copy(sources[r], narrow.at[r], in_sems.at[r]) for r in range(reps)
        ]
        stores = [
            pltpu.make_async_copy(wide.at[r], out_ref.at[places_ref[r]], out_sems.at[r])
            for r in range(reps)
        ]
        for load in loads:
            load.start()
        for r in range(reps):
            loads[r].wait()

            def convert(at, carry):
                cut = pl.ds(pl.multiple_of(at * strip, strip), strip)
                wide[r, cut, :] = narrow[r, cut, :].astype(jnp.float32)
                return carry

            lax.fori_loop(0, rows // strip, convert, 0)
            stores[r].start()
        for store in stores:
            store.wait()

    return pl.pallas_call(
        body,
        out_shape=jax.ShapeDtypeStruct((reps, rows, columns), jnp.float32),
        in_specs=[pl.BlockSpec(memory_space=pltpu.SMEM)]
        + [pl.BlockSpec(memory_space=pl.ANY)] * reps,
        out_specs=pl.BlockSpec(memory_space=pl.ANY),
        scratch_shapes=[
            pltpu.VMEM((reps, rows, columns), jnp.bfloat16),
            pltpu.VMEM((reps, rows, columns), jnp.float32),
            pltpu.SemaphoreType.DMA((reps,)),
            pltpu.SemaphoreType.DMA((reps,)),
        ],
        compiler_params=pltpu.CompilerParams(vmem_limit_bytes=VMEM_LIMIT),
        cost_estimate=COST,
        name="widen_pieces",
    )(places, *pieces).reshape(reps * rows, columns)


def resident(shape):
    return pl.BlockSpec(shape, lambda i: (0, 0), pipeline_mode=pl.Buffered(1))


def feed_forward(rows, cotangents, gate_matrix, up_matrix, down_matrix):
    count, width = rows.shape
    units = gate_matrix.shape[1]

    def body(rows_ref, cotangents_ref, gate_ref, up_ref, down_ref, inner_ref, d_gate_ref, d_up_ref):
        gate = jnp.dot(rows_ref[...], gate_ref[...], preferred_element_type=jnp.float32)
        up = jnp.dot(rows_ref[...], up_ref[...], preferred_element_type=jnp.float32)
        sigmoid = jax.nn.sigmoid(gate)
        silu = gate * sigmoid
        inner_ref[...] = (silu * up).astype(jnp.bfloat16)
        d_inner = times_transposed(cotangents_ref[...], down_ref[...])
        d_up_ref[...] = (d_inner * silu).astype(jnp.bfloat16)
        d_gate_ref[...] = (d_inner * up * sigmoid * (1.0 + gate * (1.0 - sigmoid))).astype(
            jnp.bfloat16
        )

    columns = pl.BlockSpec((width, TILE), lambda i: (0, i))
    results = pl.BlockSpec((count, TILE), lambda i: (0, i))
    return pl.pallas_call(
        body,
        grid=(pl.cdiv(units, TILE),),
        out_shape=[jax.ShapeDtypeStruct((count, units), jnp.bfloat16)] * 3,
        in_specs=[
            resident((count, width)),
            resident((count, width)),
            columns,
            columns,
            pl.BlockSpec((TILE, width), lambda i: (i, 0)),
        ],
        out_specs=[results] * 3,
        compiler_params=pltpu.CompilerParams(vmem_limit_bytes=VMEM_LIMIT),
        cost_estimate=COST,
        name="feed_forward",
    )(rows, cotangents, gate_matrix, up_matrix, down_matrix)


def split_gradient(left, right, groups, core_place):
    count, rows = left.shape
    columns = right.shape[1]
    half = rows // (2 * groups)

    def body(core_ref, left_ref, right_ref, other_ref, own_ref, turned):
        @pl.when(pl.program_id(0) == 0)
        def turn():
            whole = left_ref[...].T
            for group in range(groups):
                for which in range(2):
                    at = (2 * group + which) * half
                    turned[which, group * half : (group + 1) * half, :] = whole[at : at + half]

        core = core_ref[0]
        for out_ref, which in ((other_ref, 1 - core), (own_ref, core)):
            product = jnp.dot(turned[which], right_ref[...], preferred_element_type=jnp.float32)
            for group in range(groups):
                out_ref[group] = product[group * half : (group + 1) * half].astype(jnp.bfloat16)

    return pl.pallas_call(
        body,
        grid=(pl.cdiv(columns, TILE),),
        out_shape=[jax.ShapeDtypeStruct((groups, half, columns), jnp.bfloat16)] * 2,
        in_specs=[
            pl.BlockSpec(memory_space=pltpu.SMEM),
            resident((count, rows)),
            pl.BlockSpec((count, TILE), lambda i: (0, i)),
        ],
        out_specs=[pl.BlockSpec((groups, half, TILE), lambda i: (0, 0, i))] * 2,
        scratch_shapes=[pltpu.VMEM((2, rows // 2, count), jnp.bfloat16)],
        compiler_params=pltpu.CompilerParams(vmem_limit_bytes=VMEM_LIMIT),
        cost_estimate=COST,
        name="split_gradient",
    )(core_place.reshape(1).astype(jnp.int32), left, right)


def rows_product(lefts, rights, turned, blocks):
    count, depth = lefts[0].shape
    columns = rights[0].shape[0 if turned else 1]
    pairs, part = len(lefts), count // blocks

    def body(*refs):
        total = None
        for left_ref, right_ref in zip(refs[:pairs], refs[pairs : 2 * pairs]):
            if turned:
                product = times_transposed(left_ref[...], right_ref[...])
            else:
                product = jnp.dot(
                    left_ref[...], right_ref[...], preferred_element_type=jnp.float32
                )
            total = product if total is None else total + product
        for block in range(blocks):
            refs[2 * pairs + block][...] = total[block * part : (block + 1) * part].astype(
                jnp.bfloat16
            )

    right_spec = (
        pl.BlockSpec((TILE, depth), lambda i: (i, 0))
        if turned
        else pl.BlockSpec((depth, TILE), lambda i: (0, i))
    )
    return pl.pallas_call(
        body,
        grid=(pl.cdiv(columns, TILE),),
        out_shape=[jax.ShapeDtypeStruct((part, columns), jnp.bfloat16)] * blocks,
        in_specs=[resident((count, depth))] * pairs + [right_spec] * pairs,
        out_specs=[pl.BlockSpec((part, TILE), lambda i: (0, i))] * blocks,
        compiler_params=pltpu.CompilerParams(vmem_limit_bytes=VMEM_LIMIT),
        cost_estimate=COST,
        name="rows_product",
    )(*lefts, *rights)


def kept_bias(row_segments, row_index, key_segments, key_index):
    kept = (row_segments == key_segments) & (key_index <= row_index)
    return jnp.where(kept, 0.0, MASKED)


def in_vmem(count):
    return [pl.BlockSpec(memory_space=pltpu.VMEM)] * count


def attention_forward(projected, cosine, signed_sine, pairs, rows, keys):
    count = projected.shape[0]
    per_group = QH // KVH
    scale = 1.0 / math.sqrt(HD)
    shape = (KVH, per_group * count, HD)

    def body(projected_ref, cosine_ref, sine_ref, pairs_ref, rows_ref, keys_ref, queries_ref, out_ref):
        bias = kept_bias(rows_ref[:, 0:1], rows_ref[:, 1:2], keys_ref[0:1, :], keys_ref[1:2, :])
        for k in range(KVH):
            for h in range(per_group):
                at = (k * per_group + h) * HD
                field = projected_ref[:, at : at + HD]
                queries_ref[k, h * count : (h + 1) * count, :] = (
                    field * cosine_ref[...] + pltpu.roll(field, HD // 2, 1) * sine_ref[...]
                ).astype(jnp.bfloat16)
            keys_here = pairs_ref[:, k * HD : (k + 1) * HD]
            values_here = pairs_ref[:, (KVH + k) * HD : (KVH + k + 1) * HD]
            scores = times_transposed(queries_ref[k], keys_here) * scale + bias
            powers = jnp.exp(scores - jnp.max(scores, axis=1, keepdims=True))
            shares = powers * (1.0 / jnp.sum(powers, axis=1, keepdims=True))
            result = jnp.dot(
                shares.astype(jnp.bfloat16), values_here, preferred_element_type=jnp.float32
            ).astype(jnp.bfloat16)
            for h in range(per_group):
                at = (k * per_group + h) * HD
                out_ref[:, at : at + HD] = result[h * count : (h + 1) * count]

    return pl.pallas_call(
        body,
        out_shape=[
            jax.ShapeDtypeStruct(shape, jnp.bfloat16),
            jax.ShapeDtypeStruct((count, QH * HD), jnp.bfloat16),
        ],
        in_specs=in_vmem(6),
        out_specs=in_vmem(2),
        compiler_params=pltpu.CompilerParams(vmem_limit_bytes=VMEM_LIMIT),
        cost_estimate=COST,
        name="attention_forward",
    )(projected, cosine, signed_sine, pairs, rows, keys)


def attention_backward(queries, gradient, pairs, cosine, signed_sine, rows, keys, blocks):
    count = gradient.shape[0]
    per_group = QH // KVH
    scale = 1.0 / math.sqrt(HD)
    group_rows = pairs.shape[0]
    part = group_rows // blocks

    def body(queries_ref, gradient_ref, pairs_ref, cosine_ref, sine_ref, rows_ref, keys_ref, d_ref, *outs):
        block_refs, stacked = outs[:blocks], outs[blocks]
        bias = kept_bias(rows_ref[0:1, :], rows_ref[1:2, :], keys_ref[:, 0:1], keys_ref[:, 1:2])
        for k in range(KVH):
            for h in range(per_group):
                at = (k * per_group + h) * HD
                stacked[h * count : (h + 1) * count, :] = gradient_ref[:, at : at + HD]
            keys_here = pairs_ref[:, k * HD : (k + 1) * HD]
            values_here = pairs_ref[:, (KVH + k) * HD : (KVH + k + 1) * HD]
            scores = times_transposed(keys_here, queries_ref[k]) * scale + bias
            powers = jnp.exp(scores - jnp.max(scores, axis=0, keepdims=True))
            shares = powers * (1.0 / jnp.sum(powers, axis=0, keepdims=True))
            d_shares = times_transposed(values_here, stacked[...])
            dots = jnp.sum(shares * d_shares, axis=0, keepdims=True)
            d_scores = (shares * (d_shares - dots)).astype(jnp.bfloat16)
            d_keys = jnp.dot(d_scores, queries_ref[k], preferred_element_type=jnp.float32) * scale
            d_values = jnp.dot(
                shares.astype(jnp.bfloat16), stacked[...], preferred_element_type=jnp.float32
            )
            for block in range(blocks):
                cut = slice(block * part, (block + 1) * part)
                block_refs[block][:, k * HD : (k + 1) * HD] = d_keys[cut].astype(jnp.bfloat16)
                block_refs[block][:, (KVH + k) * HD : (KVH + k + 1) * HD] = d_values[cut].astype(
                    jnp.bfloat16
                )
            d_queries = transposed_times(d_scores, keys_here) * scale
            for h in range(per_group):
                at = (k * per_group + h) * HD
                field = d_queries[h * count : (h + 1) * count]
                d_ref[:, at : at + HD] = (
                    field * cosine_ref[...] - pltpu.roll(field, HD // 2, 1) * sine_ref[...]
                ).astype(jnp.bfloat16)

    return pl.pallas_call(
        body,
        out_shape=[jax.ShapeDtypeStruct((count, QH * HD), jnp.bfloat16)]
        + [jax.ShapeDtypeStruct((part, 2 * KVH * HD), jnp.bfloat16)] * blocks,
        in_specs=in_vmem(7),
        out_specs=in_vmem(1 + blocks),
        scratch_shapes=[pltpu.VMEM((per_group * count, HD), jnp.bfloat16)],
        compiler_params=pltpu.CompilerParams(vmem_limit_bytes=VMEM_LIMIT),
        cost_estimate=COST,
        name="attention_backward",
    )(queries, gradient, pairs, cosine, signed_sine, rows, keys)


def join_projected(d_queries, pair_terms, cosine, signed_sine):
    count, query_width = d_queries.shape
    pair_width = KVH * HD
    terms = len(pair_terms)

    def body(d_queries_ref, cosine_ref, sine_ref, *refs):
        term_refs, out_ref, sum_ref = refs[:terms], refs[terms], refs[terms + 1]
        out_ref[:, :query_width] = d_queries_ref[...]
        for at in range(0, 2 * pair_width, HD):
            field = total_of([term[:, at : at + HD] for term in term_refs])
            if at < pair_width:
                field = field * cosine_ref[...] - pltpu.roll(field, HD // 2, 1) * sine_ref[...]
            out_ref[:, query_width + at : query_width + at + HD] = field.astype(jnp.bfloat16)
        sum_ref[...] = jnp.sum(out_ref[...].astype(jnp.float32), axis=0, keepdims=True)

    return pl.pallas_call(
        body,
        out_shape=[
            jax.ShapeDtypeStruct((count, query_width + 2 * pair_width), jnp.bfloat16),
            jax.ShapeDtypeStruct((1, query_width + 2 * pair_width), jnp.float32),
        ],
        in_specs=in_vmem(3 + terms),
        out_specs=in_vmem(2),
        cost_estimate=COST,
        name="join_projected",
    )(d_queries, cosine, signed_sine, *pair_terms)


def on_device(
    tokens,
    segment_ids,
    first_gain,
    input_weight,
    input_bias,
    output_weight,
    second_gain,
    gate_weight,
    up_weight,
    down_weight,
    output_cotangent,
):
    bf16, f32 = jnp.bfloat16, jnp.float32
    shards, reps = lax.axis_size("shard"), lax.axis_size("rep")
    shard, core, first, second = make_lines(reps, shards)
    plane = (first.size, second.size)
    rep_place = (core.place * first.size + first.place) * second.size + second.place
    own_rows, width = tokens.shape
    segments = segment_ids[0]
    per_group = QH // KVH
    query_width = QH * HD
    pair_width = KVH * HD
    first_row = shard.place * own_rows
    part_rows = input_weight.shape[0] // reps
    hidden_units = gate_weight.shape[1]
    block_units = hidden_units // shards
    by_rows = (shards,) + plane + (part_rows,)
    clock = Clock()
    z_order = jnp.stack([shard.behind(step) for step in range(shards)]).astype(jnp.int32)

    def weight_piece(weight):
        return pick(weight.reshape(reps, part_rows, weight.shape[1]), rep_place, 0)

    def column_piece(weight):
        return weight_piece(weight).reshape(part_rows, shards, block_units).transpose(1, 0, 2)

    def spread(piece):
        return Spread(clock, piece, core, first, second)

    def send_rows(rows):
        return [shard.shift(row, shards - step) for step, row in enumerate(rows, 1)]

    def place_sends(blocks):
        return [pick(blocks, shard.place, 0)] + [
            shard.shift(pick(blocks, shard.ahead(step), 0), step) for step in range(1, shards)
        ]

    shard_vectors = jnp.concatenate([first_gain, second_gain, input_bias])
    vector_moving = gather_line(shard_vectors, shard)
    input_moving = gather_line(weight_piece(input_weight), shard)
    input_rows = clock(*input_moving)
    input_spread = spread(jnp.stack(input_rows)[None])
    output_piece, gate_weight, up_weight = clock(
        weight_piece(output_weight), gate_weight, up_weight
    )
    output_moving = gather_line(output_piece, shard)
    (columns,) = clock(jnp.stack([column_piece(gate_weight), column_piece(up_weight)], axis=1))
    column_moving = place_sends(columns)
    vector_rows = jnp.stack(in_place_order(clock(*vector_moving), shard))
    own_gain = first_gain.shape[0]
    gain_one = vector_rows[:, :own_gain].reshape(width).astype(f32)
    gain_two = vector_rows[:, own_gain : 2 * own_gain].reshape(width).astype(f32)
    shift_row = vector_rows[:, 2 * own_gain :].reshape(-1).astype(f32)

    places = positions(segments)
    cosine_table, sine_table = rope_tables(
        lax.dynamic_slice_in_dim(places, first_row, own_rows), HD
    )
    signed_sine = jnp.concatenate(
        [-sine_table[:, : HD // 2], sine_table[:, HD // 2 :]], axis=1
    )
    own_segments = lax.dynamic_slice_in_dim(segments, first_row, own_rows)
    row_index = jnp.arange(own_rows, dtype=jnp.int32)
    key_index = jnp.concatenate([shard.behind(step) * own_rows + row_index for step in range(shards)])
    key_segments = jnp.concatenate(
        [
            lax.dynamic_slice_in_dim(segments, shard.behind(step) * own_rows, own_rows)
            for step in range(shards)
        ]
    )
    key_marks = jnp.stack([key_segments, key_index])
    row_marks = jnp.tile(jnp.stack([own_segments, first_row + row_index]), (1, per_group))

    wide_tokens = tokens.astype(f32)
    inverse_one = lax.rsqrt(jnp.mean(wide_tokens * wide_tokens, axis=-1, keepdims=True) + EPSILON)
    unit_one = wide_tokens * inverse_one
    (normed_one,) = clock((unit_one * gain_one).astype(bf16))

    input_spread.further()
    input_spread.over()
    output_spread = spread(jnp.stack(clock(*output_moving))[None])
    (input_matrix,) = place_blocks(z_order, *input_spread.finish())
    (input_matrix,) = clock(input_matrix.reshape(width, -1))
    projected = jnp.dot(normed_one, input_matrix, preferred_element_type=f32) + shift_row
    key_part = rotate(
        projected[:, query_width : query_width + pair_width].reshape(own_rows, KVH, HD),
        cosine_table,
        sine_table,
    )
    (own_pairs,) = clock(
        jnp.concatenate(
            [key_part.reshape(own_rows, pair_width), projected[:, query_width + pair_width :]],
            axis=1,
        ).astype(bf16)
    )
    pair_moving = gather_line(own_pairs, shard)
    output_spread.further()
    output_spread.over()
    pairs = jnp.concatenate(clock(*pair_moving), axis=0)
    (output_cotangent,) = clock(output_cotangent)
    cotangent_moving = gather_line(output_cotangent, shard)
    queries, attention_low = attention_forward(
        projected, cosine_table, signed_sine, pairs, row_marks.T, key_marks
    )
    (output_matrix,) = place_blocks(z_order, *output_spread.finish())
    output_matrix, attention_low = clock(output_matrix.reshape(width, width), attention_low)
    hidden = wide_tokens + jnp.dot(attention_low, output_matrix, preferred_element_type=f32)
    inverse_two = lax.rsqrt(jnp.mean(hidden * hidden, axis=-1, keepdims=True) + EPSILON)
    unit_two = hidden * inverse_two
    (normed_two,) = clock((unit_two * gain_two).astype(bf16))
    normed_moving = gather_line(normed_two, shard)
    gate_up_spread = spread(jnp.stack(clock(*column_moving), axis=1))
    gate_up_spread.further()
    gate_up_spread.over()
    gate_matrix, up_matrix = place_blocks(z_order, *gate_up_spread.finish())
    gate_matrix, up_matrix = clock(
        gate_matrix.reshape(width, block_units), up_matrix.reshape(width, block_units)
    )
    cotangents = jnp.concatenate(clock(*cotangent_moving), axis=0)
    group_normed = jnp.concatenate(clock(*normed_moving), axis=0)

    inner_act, d_gate, d_up = clock(
        *feed_forward(group_normed, cotangents, gate_matrix, up_matrix, down_weight)
    )

    def start_halving(left, right, groups, shape, axis):
        sent, own = clock(*split_gradient(left, right, groups, core.place))
        halving = Halving(clock, [own.reshape(shape)], axis)
        halving.moving = [core.shift(sent, 1).reshape(shape)]
        return halving

    down = start_halving(
        inner_act, cotangents, 1, plane + (block_units // reps, width), 0
    )
    normed_own, *normed_partial = clock(
        *rows_product((d_gate, d_up), (gate_matrix, up_matrix), True, shards)
    )
    normed_arriving = send_rows(normed_partial)
    down.receive()
    down.send(first)
    gate = start_halving(group_normed, d_gate, shards, by_rows + (block_units,), 1)
    up = start_halving(group_normed, d_up, shards, by_rows + (block_units,), 1)
    gate.receive()
    gate.send(first)
    down.receive()
    down.send(second)
    up.receive()
    up.send(first)
    gate.receive()
    gate.send(second)
    down.receive()
    down_spread = spread(total_of(down.terms).astype(bf16))

    normed_two_gradient = total_of([normed_own] + clock(*normed_arriving))
    gain_two_gradient = jnp.sum(normed_two_gradient * unit_two, axis=0)
    hidden_gradient = output_cotangent.astype(f32) + norm_back(
        normed_two_gradient, unit_two, inverse_two, gain_two
    )
    (branch_gradient,) = clock(hidden_gradient.astype(bf16))
    up.receive()
    up.send(second)
    (attention_gradient,) = clock(times_transposed(branch_gradient, output_matrix).astype(bf16))
    d_queries, pair_own, *pair_partial = clock(
        *attention_backward(
            queries,
            attention_gradient,
            pairs,
            cosine_table,
            signed_sine,
            row_marks,
            key_marks.T,
            shards,
        )
    )
    pair_arriving = send_rows(pair_partial)
    output = start_halving(attention_low, branch_gradient, shards, by_rows + (width,), 1)
    down_spread.further()
    gate.receive()
    gate_moving = place_sends(total_of(gate.terms).astype(bf16))
    output.receive()
    output.send(first)
    up.receive()
    up_moving = place_sends(total_of(up.terms).astype(bf16))
    pair_terms = [pair_own] + clock(*pair_arriving)
    projected_gradient, bias_sum = clock(
        *join_projected(d_queries, pair_terms, cosine_table, signed_sine)
    )
    projected = start_halving(
        normed_one, projected_gradient, shards, by_rows + (projected_gradient.shape[1],), 1
    )
    down_spread.over()

    def side_by_side(moving):
        rows = clock(*moving)
        return jnp.concatenate(in_place_order(rows, shard), axis=1)

    gate_spread = spread(side_by_side(gate_moving))
    projected.receive()
    projected.send(first)
    normed_one_gradient = times_transposed(projected_gradient, input_matrix)
    gain_one_gradient = jnp.sum(normed_one_gradient * unit_one, axis=0)
    (tokens_gradient,) = clock(
        (
            hidden_gradient + norm_back(normed_one_gradient, unit_one, inverse_one, gain_one)
        ).astype(bf16)
    )
    bias_gradient = bias_sum[0]
    bias_split = query_width + pair_width
    small_parts = (
        gain_one_gradient,
        gain_two_gradient,
        bias_gradient[:bias_split],
        bias_gradient[bias_split:],
    )
    (small_rows,) = clock(
        jnp.concatenate([part.reshape(shards, -1) for part in small_parts], axis=1)
    )
    small_moving = place_sends(small_rows)
    block_own, *block_partial = clock(*rows_product((inner_act,), (down_weight,), False, shards))
    block_arriving = send_rows(block_partial)
    up_spread = spread(side_by_side(up_moving))
    output.receive()
    output.send(second)
    gate_spread.further()
    projected.receive()
    projected.send(second)
    small = total_of(clock(*small_moving))
    small_moving = [core.shift(small, 1)]
    down_total, *small_moving = clock(widen_pieces(*down_spread.finish()), *small_moving)
    small = total_of([small] + small_moving)
    small_moving = [first.shift(small, step) for step in range(1, first.size)]
    output.receive()
    output_moving = place_sends(total_of(output.terms).astype(bf16))
    gate_spread.over()
    projected.receive()
    projected_moving = place_sends(total_of(projected.terms).astype(bf16))
    small = total_of([small] + clock(*small_moving))
    small_moving = [second.shift(small, step) for step in range(1, second.size)]
    up_spread.further()
    output_spread = spread(total_of(clock(*output_moving)).astype(bf16))
    (gate_total,) = clock(widen_pieces(*gate_spread.finish()))
    input_spread = spread(total_of(clock(*projected_moving)).astype(bf16))
    up_spread.over()
    output_spread.further()
    input_spread.further()
    small = total_of([small] + clock(*small_moving))
    (block_out,) = clock(total_of([hidden, block_own] + clock(*block_arriving)).astype(bf16))
    (up_total,) = clock(widen_pieces(*up_spread.finish()))
    output_spread.over()
    input_spread.over()
    (output_total,) = clock(widen_pieces(*output_spread.finish()))
    (input_total,) = clock(widen_pieces(*input_spread.finish()))

    small = small + clock.token[0, 0]
    small_totals, at = [], 0
    for part in small_parts:
        size = part.shape[0] // shards
        small_totals.append(small[at : at + size])
        at += size
    return (
        block_out,
        tokens_gradient,
        small_totals[0],
        input_total,
        small_totals[2],
        small_totals[3],
        output_total,
        small_totals[1],
        gate_total,
        up_total,
        down_total,
    )


def solution(mesh):
    placed = (
        P(("rep", "shard"), None),
        P("rep", None),
        P("shard"),
        P("shard", None),
        P("shard"),
        P("shard", None),
        P("shard"),
        P("shard", None),
        P("shard", None),
        P("shard", None),
        P(("rep", "shard"), None),
    )
    return jax.shard_map(
        on_device,
        mesh=mesh,
        in_specs=placed,
        out_specs=(
            P(("rep", "shard"), None),
            P(("rep", "shard"), None),
            P("shard"),
            P("shard", None),
            P("shard"),
            P("shard"),
            P("shard", None),
            P("shard"),
            P("shard", None),
            P("shard", None),
            P("shard", None),
        ),
        check_vma=False,
    )
```

```python
import math

import jax
import jax.numpy as jnp
from jax import lax
from jax.experimental import pallas as pl
from jax.experimental.pallas import tpu as pltpu
from jax.sharding import PartitionSpec as P

QH = 12
KVH = 2
HD = 128
SEQS = 3


EPSILON = 1e-06
LOG_THETA = math.log(1000000.0)
MASKED = -1e30
VMEM_LIMIT = 56 * 1024 * 1024
TILE = 512
COST = pl.CostEstimate(flops=1, bytes_accessed=1, transcendentals=0)


def rope_tables(places, head_width):
    half_width = head_width // 2
    frequency = jnp.exp(jnp.arange(half_width, dtype=jnp.float32) * (-2.0 * LOG_THETA / head_width))
    angles = places.astype(jnp.float32)[:, None] * frequency[None, :]
    angles = jnp.concatenate([angles, angles], axis=-1)
    return (jnp.cos(angles), jnp.sin(angles))


def positions(segments):
    labels = jnp.arange(SEQS, dtype=jnp.int32)
    starts = jnp.sum((segments[None, :] < labels[:, None]).astype(jnp.int32), axis=1)
    own_start = jnp.sum(jnp.where(segments[:, None] == labels[None, :], starts[None, :], 0), axis=1)
    return jnp.arange(segments.shape[0], dtype=jnp.int32) - own_start


def rotate(field_rows, cosine_table, sine_table):
    half_width = field_rows.shape[-1] // 2
    turned = jnp.concatenate([-field_rows[..., half_width:], field_rows[..., :half_width]], axis=-1)
    return field_rows * cosine_table[:, None, :] + turned * sine_table[:, None, :]


def transposed_times(left_side, right_side):
    return lax.dot_general(
        left_side, right_side, (((0,), (0,)), ((), ())), preferred_element_type=jnp.float32
    )


def times_transposed(left_side, right_side):
    return lax.dot_general(
        left_side, right_side, (((1,), (1,)), ((), ())), preferred_element_type=jnp.float32
    )


def norm_back(normed_gradient, unit_rows, inverse_rms, gain_row):
    scaled = normed_gradient * gain_row
    return inverse_rms * (scaled - unit_rows * jnp.mean(scaled * unit_rows, axis=-1, keepdims=True))


class Line:
    def __init__(self, name, size, place, pairs, crossed=False):
        self.name, self.size, self.place, self.pairs = name, size, place, pairs
        self.crossed = crossed

    def shift(self, value, step):
        return lax.ppermute(value, self.name, self.pairs(step % self.size))

    def behind(self, step):
        return lax.rem(self.place + (self.size - step % self.size), self.size)

    def ahead(self, step):
        return lax.rem(self.place + step % self.size, self.size)


def make_lines(reps, shards):
    inner = 2 if reps % 4 == 0 else 1
    outer = reps // (2 * inner)
    square = inner == outer

    def split(index):
        core, b, a = index % 2, (index // 2) % inner, index // (2 * inner)
        return core, b, a

    def join(core, b, a):
        return (a * inner + b) * 2 + core

    def first_pairs(step):
        pairs = []
        for index in range(reps):
            core, b, a = split(index)
            if square and core == 0:
                pairs.append((index, join(core, (b + step) % inner, a)))
            else:
                pairs.append((index, join(core, b, (a + step) % outer)))
        return pairs

    def second_pairs(step):
        pairs = []
        for index in range(reps):
            core, b, a = split(index)
            if square and core == 0:
                pairs.append((index, join(core, b, (a + step) % outer)))
            else:
                pairs.append((index, join(core, (b + step) % inner, a)))
        return pairs

    def core_pairs(step):
        pairs = []
        for index in range(reps):
            core, b, a = split(index)
            pairs.append((index, join((core + step) % 2, b, a)))
        return pairs

    def shard_pairs(step):
        return [(index, (index + step) % shards) for index in range(shards)]

    core, b, a = split(lax.axis_index("rep"))
    first, second = (jnp.where(core == 0, b, a), jnp.where(core == 0, a, b)) if square else (a, b)
    return (
        Line("shard", shards, lax.axis_index("shard"), shard_pairs),
        Line("rep", 2, core, core_pairs, square),
        Line("rep", outer, first, first_pairs),
        Line("rep", inner, second, second_pairs),
    )


def pick(array, index, axis):
    return lax.dynamic_index_in_dim(array, index, axis, keepdims=False)


def put(array, piece, index, axis):
    return lax.dynamic_update_index_in_dim(array, piece, index, axis)


def in_place_order(pieces, line):
    ordered = []
    for place in range(line.size):
        chosen = pieces[0]
        for step in range(1, line.size):
            chosen = jnp.where(line.behind(step) == place, pieces[step], chosen)
        ordered.append(chosen)
    return ordered


def tie(*arrays):
    return lax.optimization_barrier(arrays)


def gather_line(value, line):
    return [value] + [line.shift(value, step) for step in range(1, line.size)]


class Clock:
    def __init__(self):
        self.token = jnp.zeros((8, 128), jnp.float32)

    def __call__(self, *arrays):
        self.token, *arrays = tie(self.token, *arrays)
        return arrays

    def run(self, step, *arrays):
        return self(*step(*self(*arrays)))


def total_of(terms):
    total = terms[0].astype(jnp.float32)
    for term in terms[1:]:
        total = total + term.astype(jnp.float32)
    return total


def add_chosen(chosen, *terms):
    count = len(terms)
    groups, places, rows, columns = terms[0].shape
    chosen = jnp.stack([jnp.stack(line) for line in chosen]).astype(jnp.int32)
    slots = chosen.shape[1]

    def body(chosen_ref, *refs):
        refs[count][...] = total_of([ref[...] for ref in refs[:count]]).astype(jnp.bfloat16)

    return pl.pallas_call(
        body,
        out_shape=jax.ShapeDtypeStruct((groups, slots, rows, columns), jnp.bfloat16),
        grid_spec=pltpu.PrefetchScalarGridSpec(
            num_scalar_prefetch=1,
            grid=(groups, slots),
            in_specs=[
                pl.BlockSpec(
                    (1, 1, rows, columns), lambda z, j, at, t=t: (z, at[t, j], 0, 0)
                )
                for t in range(count)
            ],
            out_specs=pl.BlockSpec((1, 1, rows, columns), lambda z, j, at: (z, j, 0, 0)),
        ),
        compiler_params=pltpu.CompilerParams(vmem_limit_bytes=VMEM_LIMIT),
        cost_estimate=COST,
        name="add_chosen",
    )(chosen, *terms)


class Halving:
    def __init__(self, clock, sent, own, core, first, second):
        self.clock, self.first, self.second = clock, first, second
        self.own = own
        self.moving = [core.shift(sent, 1)]

    def chosen(self, one, two):
        return one * self.second.size + two

    def along_first(self):
        (arrived,) = self.clock(*self.moving)
        self.halves = [self.own, arrived]
        self.moving = []
        for step in range(1, self.first.size):
            one = self.first.ahead(step)
            slots = [self.chosen(one, two) for two in range(self.second.size)]
            (block,) = self.clock(add_chosen([slots] * 2, *self.halves))
            self.moving.append(self.first.shift(block, step))

    def along_second(self):
        self.quarters = self.clock(*self.moving)
        self.moving = []
        for step in range(1, self.second.size):
            two = self.second.ahead(step)
            slots = [[self.chosen(self.first.place, two)]] * 2 + [[two]] * len(self.quarters)
            (block,) = self.clock(add_chosen(slots, *self.halves, *self.quarters))
            self.moving.append(self.second.shift(block, step))

    def finish(self):
        eighths = self.clock(*self.moving)
        two = self.second.place
        zero = jnp.zeros((), jnp.int32)
        slots = (
            [[self.chosen(self.first.place, two)]] * 2
            + [[two]] * len(self.quarters)
            + [[zero]] * len(eighths)
        )
        (block,) = self.clock(add_chosen(slots, *self.halves, *self.quarters, *eighths))
        return block[:, 0]


class Spread:
    def __init__(self, clock, piece, core, first, second):
        self.clock, self.lines = clock, (core, first, second)
        self.across = {(0, two): second.shift(piece, two) for two in range(1, second.size)}
        self.along = {(one, 0): first.shift(piece, one) for one in range(1, first.size)}
        self.here = {(0, 0): piece}
        self.there = {(0, 0): core.shift(piece, 1)}

    def waits(self):
        if hasattr(self, "beyond"):
            return list(self.beyond.values())
        return list(self.across.values()) + list(self.along.values())

    def arrive(self, group, values):
        for key, value in zip(group, values):
            self.here[key] = value
            self.there[key] = self.lines[0].shift(value, 1)

    def further(self, *values):
        values = values or self.clock(*self.waits())
        self.arrive(list(self.across) + list(self.along), values)
        self.beyond = {
            (one, two): self.lines[1].shift(self.here[0, two], one)
            for one in range(1, self.lines[1].size)
            for two in range(1, self.lines[2].size)
        }

    def over(self, *values):
        values = values or self.clock(*self.waits())
        self.arrive(self.beyond, values)

    def finish(self):
        core, first, second = self.lines
        placed = [
            (core.place, first.behind(one), second.behind(two), value)
            for (one, two), value in self.here.items()
        ]
        far, near = (second, first) if core.crossed else (first, second)
        others = self.clock(*self.there.values())
        for (one, two), value in zip(self.there, others):
            placed.append((core.behind(1), far.behind(one), near.behind(two), value))
        places = [(c * first.size + f) * second.size + s for c, f, s, value in placed]
        return jnp.stack(places).astype(jnp.int32), [value for c, f, s, value in placed]


def place_blocks(order, places, *pieces):
    reps = len(pieces)
    groups, shards = pieces[0].shape[:2]
    block = pieces[0].shape[2:]
    whole = (shards, reps) + block

    def body(order_ref, places_ref, *refs):
        sources, outs, (held, in_sems, out_sems) = (
            refs[:reps],
            refs[reps : reps + groups],
            refs[reps + groups :],
        )
        slabs = [(g, k) for g in range(groups) for k in range(shards)]

        def load(g, k, r):
            return pltpu.make_async_copy(
                sources[r].at[g, k], held.at[g, k, places_ref[r]], in_sems.at[g, k, r]
            )

        def store(g, k):
            return pltpu.make_async_copy(
                held.at[g, k], outs[g].at[order_ref[k]], out_sems.at[g, k]
            )

        for g, k in slabs:
            for r in range(reps):
                load(g, k, r).start()
        for g, k in slabs:
            for r in range(reps):
                load(g, k, r).wait()
            store(g, k).start()
        for g, k in slabs:
            store(g, k).wait()

    return pl.pallas_call(
        body,
        out_shape=[jax.ShapeDtypeStruct(whole, pieces[0].dtype)] * groups,
        in_specs=[pl.BlockSpec(memory_space=pltpu.SMEM)] * 2
        + [pl.BlockSpec(memory_space=pl.ANY)] * reps,
        out_specs=[pl.BlockSpec(memory_space=pl.ANY)] * groups,
        scratch_shapes=[
            pltpu.VMEM((groups,) + whole, pieces[0].dtype),
            pltpu.SemaphoreType.DMA((groups, shards, reps)),
            pltpu.SemaphoreType.DMA((groups, shards)),
        ],
        compiler_params=pltpu.CompilerParams(vmem_limit_bytes=VMEM_LIMIT),
        cost_estimate=COST,
        name="place_blocks",
    )(order, places, *pieces)


def widen_pieces(places, *pieces):
    reps = len(pieces)
    rows, columns = pieces[0].shape
    strip = next(size for size in (16, 8, rows) if rows % size == 0)

    def body(places_ref, *refs):
        sources, (out_ref, narrow, wide, in_sems, out_sems) = refs[:reps], refs[reps:]
        loads = [
            pltpu.make_async_copy(sources[r], narrow.at[r], in_sems.at[r]) for r in range(reps)
        ]
        stores = [
            pltpu.make_async_copy(wide.at[r], out_ref.at[places_ref[r]], out_sems.at[r])
            for r in range(reps)
        ]
        for load in loads:
            load.start()
        for r in range(reps):
            loads[r].wait()

            def convert(at, carry):
                cut = pl.ds(pl.multiple_of(at * strip, strip), strip)
                wide[r, cut, :] = narrow[r, cut, :].astype(jnp.float32)
                return carry

            lax.fori_loop(0, rows // strip, convert, 0)
            stores[r].start()
        for store in stores:
            store.wait()

    result = pl.pallas_call(
        body,
        out_shape=jax.ShapeDtypeStruct((reps, rows, columns), jnp.float32),
        in_specs=[pl.BlockSpec(memory_space=pltpu.SMEM)]
        + [pl.BlockSpec(memory_space=pl.ANY)] * reps,
        out_specs=pl.BlockSpec(memory_space=pl.ANY),
        scratch_shapes=[
            pltpu.VMEM((reps, rows, columns), jnp.bfloat16),
            pltpu.VMEM((reps, rows, columns), jnp.float32),
            pltpu.SemaphoreType.DMA((reps,)),
            pltpu.SemaphoreType.DMA((reps,)),
        ],
        compiler_params=pltpu.CompilerParams(vmem_limit_bytes=VMEM_LIMIT),
        cost_estimate=COST,
        name="widen_pieces",
    )(places, *pieces)
    return (result.reshape(reps * rows, columns),)


def resident(shape):
    return pl.BlockSpec(shape, lambda i: (0, 0), pipeline_mode=pl.Buffered(1))


def feed_forward(rows, cotangents, gate_matrix, up_matrix, down_matrix):
    count, width = rows.shape
    units = gate_matrix.shape[1]

    def body(rows_ref, cotangents_ref, gate_ref, up_ref, down_ref, inner_ref, d_gate_ref, d_up_ref):
        gate = jnp.dot(rows_ref[...], gate_ref[...], preferred_element_type=jnp.float32)
        up = jnp.dot(rows_ref[...], up_ref[...], preferred_element_type=jnp.float32)
        sigmoid = jax.nn.sigmoid(gate)
        silu = gate * sigmoid
        inner_ref[...] = (silu * up).astype(jnp.bfloat16)
        d_inner = times_transposed(cotangents_ref[...], down_ref[...])
        d_up_ref[...] = (d_inner * silu).astype(jnp.bfloat16)
        d_gate_ref[...] = (d_inner * up * sigmoid * (1.0 + gate * (1.0 - sigmoid))).astype(
            jnp.bfloat16
        )

    columns = pl.BlockSpec((width, TILE), lambda i: (0, i))
    results = pl.BlockSpec((count, TILE), lambda i: (0, i))
    return pl.pallas_call(
        body,
        grid=(pl.cdiv(units, TILE),),
        out_shape=[jax.ShapeDtypeStruct((count, units), jnp.bfloat16)] * 3,
        in_specs=[
            resident((count, width)),
            resident((count, width)),
            columns,
            columns,
            pl.BlockSpec((TILE, width), lambda i: (i, 0)),
        ],
        out_specs=[results] * 3,
        compiler_params=pltpu.CompilerParams(vmem_limit_bytes=VMEM_LIMIT),
        cost_estimate=COST,
        name="feed_forward",
    )(rows, cotangents, gate_matrix, up_matrix, down_matrix)


def split_gradient(left, right, groups, core_place):
    count, rows = left.shape
    columns = right.shape[1]
    half = rows // (2 * groups)

    def body(core_ref, left_ref, right_ref, other_ref, own_ref, turned):
        @pl.when(pl.program_id(0) == 0)
        def turn():
            whole = left_ref[...].T
            for group in range(groups):
                for which in range(2):
                    at = (2 * group + which) * half
                    turned[which, group * half : (group + 1) * half, :] = whole[at : at + half]

        core = core_ref[0]
        for out_ref, which in ((other_ref, 1 - core), (own_ref, core)):
            product = jnp.dot(turned[which], right_ref[...], preferred_element_type=jnp.float32)
            for group in range(groups):
                out_ref[group] = product[group * half : (group + 1) * half].astype(jnp.bfloat16)

    return pl.pallas_call(
        body,
        grid=(pl.cdiv(columns, TILE),),
        out_shape=[jax.ShapeDtypeStruct((groups, half, columns), jnp.bfloat16)] * 2,
        in_specs=[
            pl.BlockSpec(memory_space=pltpu.SMEM),
            resident((count, rows)),
            pl.BlockSpec((count, TILE), lambda i: (0, i)),
        ],
        out_specs=[pl.BlockSpec((groups, half, TILE), lambda i: (0, 0, i))] * 2,
        scratch_shapes=[pltpu.VMEM((2, rows // 2, count), jnp.bfloat16)],
        compiler_params=pltpu.CompilerParams(vmem_limit_bytes=VMEM_LIMIT),
        cost_estimate=COST,
        name="split_gradient",
    )(core_place.reshape(1).astype(jnp.int32), left, right)


def rows_product(lefts, rights, turned, blocks):
    count, depth = lefts[0].shape
    columns = rights[0].shape[0 if turned else 1]
    pairs, part = len(lefts), count // blocks

    def body(*refs):
        total = None
        for left_ref, right_ref in zip(refs[:pairs], refs[pairs : 2 * pairs]):
            if turned:
                product = times_transposed(left_ref[...], right_ref[...])
            else:
                product = jnp.dot(
                    left_ref[...], right_ref[...], preferred_element_type=jnp.float32
                )
            total = product if total is None else total + product
        for block in range(blocks):
            refs[2 * pairs + block][...] = total[block * part : (block + 1) * part].astype(
                jnp.bfloat16
            )

    right_spec = (
        pl.BlockSpec((TILE, depth), lambda i: (i, 0))
        if turned
        else pl.BlockSpec((depth, TILE), lambda i: (0, i))
    )
    return pl.pallas_call(
        body,
        grid=(pl.cdiv(columns, TILE),),
        out_shape=[jax.ShapeDtypeStruct((part, columns), jnp.bfloat16)] * blocks,
        in_specs=[resident((count, depth))] * pairs + [right_spec] * pairs,
        out_specs=[pl.BlockSpec((part, TILE), lambda i: (0, i))] * blocks,
        compiler_params=pltpu.CompilerParams(vmem_limit_bytes=VMEM_LIMIT),
        cost_estimate=COST,
        name="rows_product",
    )(*lefts, *rights)


def kept_bias(row_segments, row_index, key_segments, key_index):
    kept = (row_segments == key_segments) & (key_index <= row_index)
    return jnp.where(kept, 0.0, MASKED)


def in_vmem(count):
    return [pl.BlockSpec(memory_space=pltpu.VMEM)] * count


def attention_forward(projected, cosine, signed_sine, pairs, rows, keys):
    count = projected.shape[0]
    per_group = QH // KVH
    scale = 1.0 / math.sqrt(HD)
    shape = (KVH, per_group * count, HD)

    def body(projected_ref, cosine_ref, sine_ref, pairs_ref, rows_ref, keys_ref, queries_ref, out_ref):
        bias = kept_bias(rows_ref[:, 0:1], rows_ref[:, 1:2], keys_ref[0:1, :], keys_ref[1:2, :])
        for k in range(KVH):
            for h in range(per_group):
                at = (k * per_group + h) * HD
                field = projected_ref[:, at : at + HD]
                queries_ref[k, h * count : (h + 1) * count, :] = (
                    field * cosine_ref[...] + pltpu.roll(field, HD // 2, 1) * sine_ref[...]
                ).astype(jnp.bfloat16)
            keys_here = pairs_ref[:, k * HD : (k + 1) * HD]
            values_here = pairs_ref[:, (KVH + k) * HD : (KVH + k + 1) * HD]
            scores = times_transposed(queries_ref[k], keys_here) * scale + bias
            powers = jnp.exp(scores - jnp.max(scores, axis=1, keepdims=True))
            shares = powers * (1.0 / jnp.sum(powers, axis=1, keepdims=True))
            result = jnp.dot(
                shares.astype(jnp.bfloat16), values_here, preferred_element_type=jnp.float32
            ).astype(jnp.bfloat16)
            for h in range(per_group):
                at = (k * per_group + h) * HD
                out_ref[:, at : at + HD] = result[h * count : (h + 1) * count]

    return pl.pallas_call(
        body,
        out_shape=[
            jax.ShapeDtypeStruct(shape, jnp.bfloat16),
            jax.ShapeDtypeStruct((count, QH * HD), jnp.bfloat16),
        ],
        in_specs=in_vmem(6),
        out_specs=in_vmem(2),
        compiler_params=pltpu.CompilerParams(vmem_limit_bytes=VMEM_LIMIT),
        cost_estimate=COST,
        name="attention_forward",
    )(projected, cosine, signed_sine, pairs, rows, keys)


def attention_backward(queries, gradient, pairs, cosine, signed_sine, rows, keys, blocks):
    count = gradient.shape[0]
    per_group = QH // KVH
    scale = 1.0 / math.sqrt(HD)
    group_rows = pairs.shape[0]
    part = group_rows // blocks

    def body(queries_ref, gradient_ref, pairs_ref, cosine_ref, sine_ref, rows_ref, keys_ref, d_ref, *outs):
        block_refs, stacked = outs[:blocks], outs[blocks]
        bias = kept_bias(rows_ref[0:1, :], rows_ref[1:2, :], keys_ref[:, 0:1], keys_ref[:, 1:2])
        for k in range(KVH):
            for h in range(per_group):
                at = (k * per_group + h) * HD
                stacked[h * count : (h + 1) * count, :] = gradient_ref[:, at : at + HD]
            keys_here = pairs_ref[:, k * HD : (k + 1) * HD]
            values_here = pairs_ref[:, (KVH + k) * HD : (KVH + k + 1) * HD]
            scores = times_transposed(keys_here, queries_ref[k]) * scale + bias
            powers = jnp.exp(scores - jnp.max(scores, axis=0, keepdims=True))
            shares = powers * (1.0 / jnp.sum(powers, axis=0, keepdims=True))
            d_shares = times_transposed(values_here, stacked[...])
            dots = jnp.sum(shares * d_shares, axis=0, keepdims=True)
            d_scores = (shares * (d_shares - dots)).astype(jnp.bfloat16)
            d_keys = jnp.dot(d_scores, queries_ref[k], preferred_element_type=jnp.float32) * scale
            d_values = jnp.dot(
                shares.astype(jnp.bfloat16), stacked[...], preferred_element_type=jnp.float32
            )
            for block in range(blocks):
                cut = slice(block * part, (block + 1) * part)
                block_refs[block][:, k * HD : (k + 1) * HD] = d_keys[cut].astype(jnp.bfloat16)
                block_refs[block][:, (KVH + k) * HD : (KVH + k + 1) * HD] = d_values[cut].astype(
                    jnp.bfloat16
                )
            d_queries = transposed_times(d_scores, keys_here) * scale
            for h in range(per_group):
                at = (k * per_group + h) * HD
                field = d_queries[h * count : (h + 1) * count]
                d_ref[:, at : at + HD] = (
                    field * cosine_ref[...] - pltpu.roll(field, HD // 2, 1) * sine_ref[...]
                ).astype(jnp.bfloat16)

    return pl.pallas_call(
        body,
        out_shape=[jax.ShapeDtypeStruct((count, QH * HD), jnp.bfloat16)]
        + [jax.ShapeDtypeStruct((part, 2 * KVH * HD), jnp.bfloat16)] * blocks,
        in_specs=in_vmem(7),
        out_specs=in_vmem(1 + blocks),
        scratch_shapes=[pltpu.VMEM((per_group * count, HD), jnp.bfloat16)],
        compiler_params=pltpu.CompilerParams(vmem_limit_bytes=VMEM_LIMIT),
        cost_estimate=COST,
        name="attention_backward",
    )(queries, gradient, pairs, cosine, signed_sine, rows, keys)


def join_projected(d_queries, pair_terms, cosine, signed_sine):
    count, query_width = d_queries.shape
    pair_width = KVH * HD
    terms = len(pair_terms)

    def body(d_queries_ref, cosine_ref, sine_ref, *refs):
        term_refs, out_ref, sum_ref = refs[:terms], refs[terms], refs[terms + 1]
        out_ref[:, :query_width] = d_queries_ref[...]
        for at in range(0, 2 * pair_width, HD):
            field = total_of([term[:, at : at + HD] for term in term_refs])
            if at < pair_width:
                field = field * cosine_ref[...] - pltpu.roll(field, HD // 2, 1) * sine_ref[...]
            out_ref[:, query_width + at : query_width + at + HD] = field.astype(jnp.bfloat16)
        sum_ref[...] = jnp.sum(out_ref[...].astype(jnp.float32), axis=0, keepdims=True)

    return pl.pallas_call(
        body,
        out_shape=[
            jax.ShapeDtypeStruct((count, query_width + 2 * pair_width), jnp.bfloat16),
            jax.ShapeDtypeStruct((1, query_width + 2 * pair_width), jnp.float32),
        ],
        in_specs=in_vmem(3 + terms),
        out_specs=in_vmem(2),
        cost_estimate=COST,
        name="join_projected",
    )(d_queries, cosine, signed_sine, *pair_terms)


def on_device(
    tokens,
    segment_ids,
    first_gain,
    input_weight,
    input_bias,
    output_weight,
    second_gain,
    gate_weight,
    up_weight,
    down_weight,
    output_cotangent,
):
    bf16, f32 = jnp.bfloat16, jnp.float32
    shards, reps = lax.axis_size("shard"), lax.axis_size("rep")
    shard, core, first, second = make_lines(reps, shards)
    rep_place = (core.place * first.size + first.place) * second.size + second.place
    own_rows, width = tokens.shape
    segments = segment_ids[0]
    per_group = QH // KVH
    query_width = QH * HD
    pair_width = KVH * HD
    first_row = shard.place * own_rows
    part_rows = input_weight.shape[0] // reps
    hidden_units = gate_weight.shape[1]
    block_units = hidden_units // shards
    clock = Clock()
    z_order = jnp.stack([shard.behind(step) for step in range(shards)]).astype(jnp.int32)

    def weight_piece(weight):
        return pick(weight.reshape(reps, part_rows, weight.shape[1]), rep_place, 0)

    def column_piece(weight):
        return weight_piece(weight).reshape(part_rows, shards, block_units).transpose(1, 0, 2)

    def spread(piece):
        return Spread(clock, piece, core, first, second)

    def flat_of(spread_pieces):
        at, pieces = spread_pieces.finish()
        return [at] + pieces

    def send_rows(rows):
        return [shard.shift(row, shards - step) for step, row in enumerate(rows, 1)]

    def place_sends(blocks):
        return [pick(blocks, shard.place, 0)] + [
            shard.shift(pick(blocks, shard.ahead(step), 0), step) for step in range(1, shards)
        ]

    shard_vectors = jnp.concatenate([first_gain, second_gain, input_bias])
    vector_moving = gather_line(shard_vectors, shard)
    input_moving = gather_line(weight_piece(input_weight), shard)
    columns = [column_piece(gate_weight), column_piece(up_weight)]
    output_piece = weight_piece(output_weight)
    arrived = clock(*vector_moving, *input_moving, *columns, output_piece)
    vectors, input_rows = arrived[:shards], arrived[shards : 2 * shards]
    *columns, output_piece = arrived[2 * shards :]

    input_spread = spread(jnp.stack(input_rows)[None])
    output_moving = gather_line(output_piece, shard)
    cotangent_arrived = [output_cotangent, shard.shift(output_cotangent, 1)]
    vector_rows = jnp.stack(in_place_order(vectors, shard))
    own_gain = first_gain.shape[0]
    gain_one = vector_rows[:, :own_gain].reshape(width).astype(f32)
    gain_two = vector_rows[:, own_gain : 2 * own_gain].reshape(width).astype(f32)
    shift_row = vector_rows[:, 2 * own_gain :].reshape(-1).astype(f32)
    places = positions(segments)
    cosine_table, sine_table = rope_tables(
        lax.dynamic_slice_in_dim(places, first_row, own_rows), HD
    )
    signed_sine = jnp.concatenate(
        [-sine_table[:, : HD // 2], sine_table[:, HD // 2 :]], axis=1
    )
    own_segments = lax.dynamic_slice_in_dim(segments, first_row, own_rows)
    row_index = jnp.arange(own_rows, dtype=jnp.int32)
    key_index = jnp.concatenate([shard.behind(step) * own_rows + row_index for step in range(shards)])
    key_segments = jnp.concatenate(
        [
            lax.dynamic_slice_in_dim(segments, shard.behind(step) * own_rows, own_rows)
            for step in range(shards)
        ]
    )
    key_marks = jnp.stack([key_segments, key_index])
    row_marks = jnp.tile(jnp.stack([own_segments, first_row + row_index]), (1, per_group))
    wide_tokens = tokens.astype(f32)
    inverse_one = lax.rsqrt(jnp.mean(wide_tokens * wide_tokens, axis=-1, keepdims=True) + EPSILON)
    unit_one = wide_tokens * inverse_one
    normed_one = (unit_one * gain_one).astype(bf16)
    (
        normed_one,
        cosine_table,
        sine_table,
        signed_sine,
        key_marks,
        row_marks,
    ) = clock(normed_one, cosine_table, sine_table, signed_sine, key_marks, row_marks)

    def together(*groups):
        flat = clock(*[array for group in groups for array in group])
        parts, at = [], 0
        for group in groups:
            parts.append(flat[at : at + len(group)])
            at += len(group)
        return parts

    arrived, output_rows, (moved,) = together(
        input_spread.waits(), output_moving, cotangent_arrived[1:]
    )
    cotangent_arrived[1] = moved
    input_spread.further(*arrived)
    output_spread = spread(jnp.stack(output_rows)[None])
    gate_moving = place_sends(columns[0])
    arrived, output_arrived, gate_rows = together(
        input_spread.waits(), output_spread.waits(), gate_moving
    )
    input_spread.over(*arrived)
    output_spread.further(*output_arrived)
    input_places, input_pieces = input_spread.finish()
    gate_spread = spread(jnp.stack(gate_rows)[None])
    up_moving = place_sends(columns[1])
    (input_matrix,) = clock.run(place_blocks, z_order, input_places, *input_pieces)
    input_matrix = input_matrix.reshape(width, -1)
    projected = jnp.dot(normed_one, input_matrix, preferred_element_type=f32) + shift_row
    key_part = rotate(
        projected[:, query_width : query_width + pair_width].reshape(own_rows, KVH, HD),
        cosine_table,
        sine_table,
    )
    (own_pairs,) = clock(
        jnp.concatenate(
            [key_part.reshape(own_rows, pair_width), projected[:, query_width + pair_width :]],
            axis=1,
        ).astype(bf16)
    )
    pair_moving = gather_line(own_pairs, shard)
    pair_rows, output_arrived, gate_arrived, up_rows = together(
        pair_moving, output_spread.waits(), gate_spread.waits(), up_moving
    )
    pairs = jnp.concatenate(pair_rows, axis=0)
    output_spread.over(*output_arrived)
    gate_spread.further(*gate_arrived)
    up_spread = spread(jnp.stack(up_rows)[None])
    last = shards - 1
    cotangent_arrived += [None] * (shards - 2)
    if last > 1:
        cotangent_arrived[last] = shard.shift(output_cotangent, last)
    queries, attention_low = clock.run(
        attention_forward, projected, cosine_table, signed_sine, pairs, row_marks.T, key_marks
    )
    output_places, output_pieces = output_spread.finish()
    (output_matrix,) = clock.run(place_blocks, z_order, output_places, *output_pieces)
    output_matrix = output_matrix.reshape(width, width)
    hidden = wide_tokens + jnp.dot(attention_low, output_matrix, preferred_element_type=f32)
    inverse_two = lax.rsqrt(jnp.mean(hidden * hidden, axis=-1, keepdims=True) + EPSILON)
    unit_two = hidden * inverse_two
    (normed_two,) = clock((unit_two * gain_two).astype(bf16))
    normed_arrived = gather_line(normed_two, shard)
    for step in range(2, last):
        cotangent_arrived[step] = shard.shift(output_cotangent, step)
    gate_arrived, up_arrived = together(gate_spread.waits(), up_spread.waits())
    gate_spread.over(*gate_arrived)
    up_spread.further(*up_arrived)
    edge = [1] if last == 1 else [1, last]
    up_arrived, normed_edge, (moved,) = together(
        up_spread.waits(), [normed_arrived[step] for step in edge], [cotangent_arrived[last]]
    )
    up_spread.over(*up_arrived)
    cotangent_arrived[last] = moved
    for step, value in zip(edge, normed_edge):
        normed_arrived[step] = value
    gate_places, gate_pieces = gate_spread.finish()
    (gate_matrix,) = clock.run(place_blocks, z_order, gate_places, *gate_pieces)
    up_places, up_pieces = up_spread.finish()
    (up_matrix,) = clock.run(place_blocks, z_order, up_places, *up_pieces)
    gate_matrix = gate_matrix.reshape(width, block_units)
    up_matrix = up_matrix.reshape(width, block_units)
    normed_arrived, cotangent_arrived = together(normed_arrived, cotangent_arrived)
    cotangents = jnp.concatenate(cotangent_arrived, axis=0)
    group_normed = jnp.concatenate(normed_arrived, axis=0)

    inner_act, d_gate, d_up = clock.run(
        feed_forward, group_normed, cotangents, gate_matrix, up_matrix, down_weight
    )

    def start_halving(left, right, groups):
        sent, own = clock.run(
            lambda left, right: split_gradient(left, right, groups, core.place), left, right
        )
        shape = (groups, first.size * second.size, -1, right.shape[1])
        return Halving(clock, sent.reshape(shape), own.reshape(shape), core, first, second)

    def side_by_side(moving):
        rows = clock(*moving)
        return clock(jnp.concatenate(in_place_order(rows, shard), axis=1))[0]

    down = start_halving(inner_act, cotangents, 1)
    normed_own, *normed_partial = clock.run(
        lambda *operands: rows_product(operands[:2], operands[2:], True, shards),
        d_gate,
        d_up,
        gate_matrix,
        up_matrix,
    )
    normed_arriving = send_rows(normed_partial)
    down.along_first()
    gate = start_halving(group_normed, d_gate, shards)
    up = start_halving(group_normed, d_up, shards)
    gate.along_first()
    down.along_second()
    up.along_first()
    gate.along_second()
    down_spread = spread(down.finish()[0])

    normed_two_gradient = total_of([normed_own] + clock(*normed_arriving))
    gain_two_gradient = jnp.sum(normed_two_gradient * unit_two, axis=0)
    hidden_gradient = output_cotangent.astype(f32) + norm_back(
        normed_two_gradient, unit_two, inverse_two, gain_two
    )
    (branch_gradient,) = clock(hidden_gradient.astype(bf16))
    (attention_gradient,) = clock(times_transposed(branch_gradient, output_matrix).astype(bf16))
    d_queries, pair_own, *pair_partial = clock.run(
        lambda *operands: attention_backward(*operands, shards),
        queries,
        attention_gradient,
        pairs,
        cosine_table,
        signed_sine,
        row_marks,
        key_marks.T,
    )
    pair_arriving = send_rows(pair_partial)
    up.along_second()
    output = start_halving(attention_low, branch_gradient, shards)
    gate_moving = place_sends(gate.finish())
    output.along_first()
    down_spread.further()
    up_moving = place_sends(up.finish())
    pair_terms = [pair_own] + clock(*pair_arriving)
    projected_gradient, bias_sum = clock.run(
        lambda *operands: join_projected(operands[0], operands[3:], *operands[1:3]),
        d_queries,
        cosine_table,
        signed_sine,
        *pair_terms,
    )
    projected = start_halving(normed_one, projected_gradient, shards)
    gate_spread = spread(side_by_side(gate_moving))
    projected.along_first()
    block_own, *block_partial = clock.run(
        lambda left, right: rows_product((left,), (right,), False, shards), inner_act, down_weight
    )
    output.along_second()
    down_spread.over()
    up_piece = side_by_side(up_moving)
    block_arriving = send_rows(block_partial)
    projected.along_second()
    up_spread = spread(up_piece)
    gate_spread.further()
    projected_gradient, hidden_gradient = clock(projected_gradient, hidden_gradient)
    normed_one_gradient = times_transposed(projected_gradient, input_matrix)
    gain_one_gradient = jnp.sum(normed_one_gradient * unit_one, axis=0)
    (tokens_gradient,) = clock(
        (
            hidden_gradient + norm_back(normed_one_gradient, unit_one, inverse_one, gain_one)
        ).astype(bf16)
    )
    bias_gradient = bias_sum[0]
    bias_split = query_width + pair_width
    small_parts = (
        gain_one_gradient,
        gain_two_gradient,
        bias_gradient[:bias_split],
        bias_gradient[bias_split:],
    )
    (small_rows,) = clock(
        jnp.concatenate([part.reshape(shards, -1) for part in small_parts], axis=1)
    )
    small_moving = place_sends(small_rows)
    output_moving = place_sends(output.finish())
    projected_moving = place_sends(projected.finish())
    gate_spread.over()
    (down_total,) = clock.run(widen_pieces, *flat_of(down_spread))
    small = total_of(clock(*small_moving))
    small_moving = [core.shift(small, 1)]
    output_spread = spread(clock(total_of(clock(*output_moving)).astype(bf16))[0])
    input_spread = spread(clock(total_of(clock(*projected_moving)).astype(bf16))[0])
    up_spread.further()
    small = total_of([small] + clock(*small_moving))
    small_moving = [first.shift(small, step) for step in range(1, first.size)]
    (gate_total,) = clock.run(widen_pieces, *flat_of(gate_spread))
    output_spread.further()
    input_spread.further()
    up_spread.over()
    small = total_of([small] + clock(*small_moving))
    small_moving = [second.shift(small, step) for step in range(1, second.size)]
    (block_out,) = clock(total_of([hidden, block_own] + clock(*block_arriving)).astype(bf16))
    output_spread.over()
    input_spread.over()
    (up_total,) = clock.run(widen_pieces, *flat_of(up_spread))
    small = total_of([small] + clock(*small_moving))
    (output_total,) = clock.run(widen_pieces, *flat_of(output_spread))
    (input_total,) = clock.run(widen_pieces, *flat_of(input_spread))

    small = small + clock.token[0, 0]
    small_totals, at = [], 0
    for part in small_parts:
        size = part.shape[0] // shards
        small_totals.append(small[at : at + size])
        at += size
    return (
        block_out,
        tokens_gradient,
        small_totals[0],
        input_total,
        small_totals[2],
        small_totals[3],
        output_total,
        small_totals[1],
        gate_total,
        up_total,
        down_total,
    )


def solution(mesh):
    placed = (
        P(("rep", "shard"), None),
        P("rep", None),
        P("shard"),
        P("shard", None),
        P("shard"),
        P("shard", None),
        P("shard"),
        P("shard", None),
        P("shard", None),
        P("shard", None),
        P(("rep", "shard"), None),
    )
    return jax.shard_map(
        on_device,
        mesh=mesh,
        in_specs=placed,
        out_specs=(
            P(("rep", "shard"), None),
            P(("rep", "shard"), None),
            P("shard"),
            P("shard", None),
            P("shard"),
            P("shard"),
            P("shard", None),
            P("shard"),
            P("shard", None),
            P("shard", None),
            P("shard", None),
        ),
        check_vma=False,
    )
```

```python
import math

import jax
import jax.numpy as jnp
from jax import lax
from jax.experimental import pallas as pl
from jax.experimental.pallas import tpu as pltpu
from jax.sharding import PartitionSpec as P

QH = 12
KVH = 2
HD = 128
SEQS = 3


EPSILON = 1e-06
LOG_THETA = math.log(1000000.0)
MASKED = -1e30
VMEM_LIMIT = 56 * 1024 * 1024
TILE = 512
COST = pl.CostEstimate(flops=1, bytes_accessed=1, transcendentals=0)


def rope_tables(places, head_width):
    half_width = head_width // 2
    frequency = jnp.exp(jnp.arange(half_width, dtype=jnp.float32) * (-2.0 * LOG_THETA / head_width))
    angles = places.astype(jnp.float32)[:, None] * frequency[None, :]
    angles = jnp.concatenate([angles, angles], axis=-1)
    return (jnp.cos(angles), jnp.sin(angles))


def positions(segments):
    labels = jnp.arange(SEQS, dtype=jnp.int32)
    starts = jnp.sum((segments[None, :] < labels[:, None]).astype(jnp.int32), axis=1)
    own_start = jnp.sum(jnp.where(segments[:, None] == labels[None, :], starts[None, :], 0), axis=1)
    return jnp.arange(segments.shape[0], dtype=jnp.int32) - own_start


def rotate(field_rows, cosine_table, sine_table):
    half_width = field_rows.shape[-1] // 2
    turned = jnp.concatenate([-field_rows[..., half_width:], field_rows[..., :half_width]], axis=-1)
    return field_rows * cosine_table[:, None, :] + turned * sine_table[:, None, :]


def transposed_times(left_side, right_side):
    return lax.dot_general(
        left_side, right_side, (((0,), (0,)), ((), ())), preferred_element_type=jnp.float32
    )


def times_transposed(left_side, right_side):
    return lax.dot_general(
        left_side, right_side, (((1,), (1,)), ((), ())), preferred_element_type=jnp.float32
    )


def norm_back(normed_gradient, unit_rows, inverse_rms, gain_row):
    scaled = normed_gradient * gain_row
    return inverse_rms * (scaled - unit_rows * jnp.mean(scaled * unit_rows, axis=-1, keepdims=True))


class Line:
    def __init__(self, name, size, place, pairs, crossed=False):
        self.name, self.size, self.place, self.pairs = name, size, place, pairs
        self.crossed = crossed

    def shift(self, value, step):
        return lax.ppermute(value, self.name, self.pairs(step % self.size))

    def behind(self, step):
        return lax.rem(self.place + (self.size - step % self.size), self.size)

    def ahead(self, step):
        return lax.rem(self.place + step % self.size, self.size)


def make_lines(reps, shards):
    inner = 2 if reps % 4 == 0 else 1
    outer = reps // (2 * inner)
    square = inner == outer

    def split(index):
        core, b, a = index % 2, (index // 2) % inner, index // (2 * inner)
        return core, b, a

    def join(core, b, a):
        return (a * inner + b) * 2 + core

    def first_pairs(step):
        pairs = []
        for index in range(reps):
            core, b, a = split(index)
            if square and core == 0:
                pairs.append((index, join(core, (b + step) % inner, a)))
            else:
                pairs.append((index, join(core, b, (a + step) % outer)))
        return pairs

    def second_pairs(step):
        pairs = []
        for index in range(reps):
            core, b, a = split(index)
            if square and core == 0:
                pairs.append((index, join(core, b, (a + step) % outer)))
            else:
                pairs.append((index, join(core, (b + step) % inner, a)))
        return pairs

    def core_pairs(step):
        pairs = []
        for index in range(reps):
            core, b, a = split(index)
            pairs.append((index, join((core + step) % 2, b, a)))
        return pairs

    def shard_pairs(step):
        return [(index, (index + step) % shards) for index in range(shards)]

    core, b, a = split(lax.axis_index("rep"))
    first, second = (jnp.where(core == 0, b, a), jnp.where(core == 0, a, b)) if square else (a, b)
    return (
        Line("shard", shards, lax.axis_index("shard"), shard_pairs),
        Line("rep", 2, core, core_pairs, square),
        Line("rep", outer, first, first_pairs),
        Line("rep", inner, second, second_pairs),
    )


def rep_places(reps):
    inner = 2 if reps % 4 == 0 else 1
    outer = reps // (2 * inner)
    places = []
    for index in range(reps):
        core, b, a = index % 2, (index // 2) % inner, index // (2 * inner)
        one, two = (b, a) if inner == outer and core == 0 else (a, b)
        places.append((core * outer + one) * inner + two)
    return places


def pick(array, index, axis):
    return lax.dynamic_index_in_dim(array, index, axis, keepdims=False)


def put(array, piece, index, axis):
    return lax.dynamic_update_index_in_dim(array, piece, index, axis)


def in_place_order(pieces, line):
    ordered = []
    for place in range(line.size):
        chosen = pieces[0]
        for step in range(1, line.size):
            chosen = jnp.where(line.behind(step) == place, pieces[step], chosen)
        ordered.append(chosen)
    return ordered


def tie(*arrays):
    return lax.optimization_barrier(arrays)


def gather_line(value, line):
    return [value] + [line.shift(value, step) for step in range(1, line.size)]


class Clock:
    def __init__(self):
        self.token = jnp.zeros((8, 128), jnp.float32)

    def __call__(self, *arrays):
        self.token, *arrays = tie(self.token, *arrays)
        return arrays

    def run(self, step, *arrays):
        return self(*step(*self(*arrays)))


def total_of(terms):
    total = terms[0].astype(jnp.float32)
    for term in terms[1:]:
        total = total + term.astype(jnp.float32)
    return total


def add_chosen(chosen, *terms):
    count = len(terms)
    groups, places, rows, columns = terms[0].shape
    chosen = jnp.stack([jnp.stack(line) for line in chosen]).astype(jnp.int32)
    slots = chosen.shape[1]

    def body(chosen_ref, *refs):
        refs[count][...] = total_of([ref[...] for ref in refs[:count]]).astype(jnp.bfloat16)

    return pl.pallas_call(
        body,
        out_shape=jax.ShapeDtypeStruct((groups, slots, rows, columns), jnp.bfloat16),
        grid_spec=pltpu.PrefetchScalarGridSpec(
            num_scalar_prefetch=1,
            grid=(groups, slots),
            in_specs=[
                pl.BlockSpec(
                    (1, 1, rows, columns), lambda z, j, at, t=t: (z, at[t, j], 0, 0)
                )
                for t in range(count)
            ],
            out_specs=pl.BlockSpec((1, 1, rows, columns), lambda z, j, at: (z, j, 0, 0)),
        ),
        compiler_params=pltpu.CompilerParams(vmem_limit_bytes=VMEM_LIMIT),
        cost_estimate=COST,
        name="add_chosen",
    )(chosen, *terms)


class Halving:
    def __init__(self, clock, sent, own, core, first, second):
        self.clock, self.first, self.second = clock, first, second
        self.own = own
        self.moving = [core.shift(sent, 1)]

    def chosen(self, one, two):
        return one * self.second.size + two

    def along_first(self):
        (arrived,) = self.clock(*self.moving)
        self.halves = [self.own, arrived]
        self.moving = []
        for step in range(1, self.first.size):
            one = self.first.ahead(step)
            slots = [self.chosen(one, two) for two in range(self.second.size)]
            (block,) = self.clock(add_chosen([slots] * 2, *self.halves))
            self.moving.append(self.first.shift(block, step))

    def along_second(self):
        self.quarters = self.clock(*self.moving)
        self.moving = []
        for step in range(1, self.second.size):
            two = self.second.ahead(step)
            slots = [[self.chosen(self.first.place, two)]] * 2 + [[two]] * len(self.quarters)
            (block,) = self.clock(add_chosen(slots, *self.halves, *self.quarters))
            self.moving.append(self.second.shift(block, step))

    def finish(self):
        eighths = self.clock(*self.moving)
        two = self.second.place
        zero = jnp.zeros((), jnp.int32)
        slots = (
            [[self.chosen(self.first.place, two)]] * 2
            + [[two]] * len(self.quarters)
            + [[zero]] * len(eighths)
        )
        (block,) = self.clock(add_chosen(slots, *self.halves, *self.quarters, *eighths))
        return block[:, 0]


class Spread:
    def __init__(self, clock, piece, core, first, second):
        self.clock, self.lines = clock, (core, first, second)
        self.across = {(0, two): second.shift(piece, two) for two in range(1, second.size)}
        self.along = {(one, 0): first.shift(piece, one) for one in range(1, first.size)}
        self.here = {(0, 0): piece}

    def waits(self):
        if hasattr(self, "there"):
            return [self.there]
        if hasattr(self, "beyond"):
            return list(self.beyond.values())
        return list(self.across.values()) + list(self.along.values())

    def further(self, *values):
        values = values or self.clock(*self.waits())
        self.here.update(zip(list(self.across) + list(self.along), values))
        self.beyond = {
            (one, two): self.lines[1].shift(self.here[0, two], one)
            for one in range(1, self.lines[1].size)
            for two in range(1, self.lines[2].size)
        }

    def over(self, *values):
        values = values or self.clock(*self.waits())
        self.here.update(zip(self.beyond, values))
        (stacked,) = self.clock(jnp.stack(list(self.here.values())))
        self.there = self.lines[0].shift(stacked, 1)

    def finish(self, *values):
        core, first, second = self.lines
        (others,) = values or self.clock(*self.waits())
        placed = [(core.place, first.behind(one), second.behind(two)) for one, two in self.here]
        far, near = (second, first) if core.crossed else (first, second)
        placed += [(core.behind(1), far.behind(one), near.behind(two)) for one, two in self.here]
        places = [(c * first.size + f) * second.size + s for c, f, s in placed]
        return [jnp.stack(places).astype(jnp.int32), others] + list(self.here.values())


def piece_of(r, sources):
    return sources[r] if r < len(sources) - 1 else sources[-1].at[r - len(sources) + 1]


def place_blocks(order, places, others, *pieces):
    reps = 2 * len(pieces)
    groups, shards = pieces[0].shape[:2]
    block = pieces[0].shape[2:]

    def body(order_ref, places_ref, *refs):
        sources, rest = refs[: len(pieces) + 1], refs[len(pieces) + 1 :]
        move_blocks(
            lambda g, k, r: piece_of(r, sources).at[g, k],
            lambda r: places_ref[r],
            order_ref,
            rest[:groups],
            *rest[groups:],
        )

    return blocks_call(body, 2, len(pieces) + 1, groups, shards, reps, block)(
        order, places, *pieces, others
    )


def place_gathered(order, gathered):
    reps, shards, groups = gathered.shape[:3]

    def body(order_ref, source, *rest):
        move_blocks(
            lambda g, k, r: source.at[r, k, g], lambda r: r, order_ref, rest[:groups], *rest[groups:]
        )

    return blocks_call(body, 1, 1, groups, shards, reps, gathered.shape[3:])(order, gathered)


def move_blocks(source_of, place_of, order_ref, outs, held, in_sems, out_sems):
    groups, shards, reps = in_sems.shape
    slabs = [(g, k) for g in range(groups) for k in range(shards)]

    def load(g, k, r):
        return pltpu.make_async_copy(
            source_of(g, k, r), held.at[g, k, place_of(r)], in_sems.at[g, k, r]
        )

    def store(g, k):
        return pltpu.make_async_copy(held.at[g, k], outs[g].at[order_ref[k]], out_sems.at[g, k])

    for g, k in slabs:
        for r in range(reps):
            load(g, k, r).start()
    for g, k in slabs:
        for r in range(reps):
            load(g, k, r).wait()
        store(g, k).start()
    for g, k in slabs:
        store(g, k).wait()


def blocks_call(body, scalars, sources, groups, shards, reps, block):
    whole = (shards, reps) + block
    return pl.pallas_call(
        body,
        out_shape=[jax.ShapeDtypeStruct(whole, jnp.bfloat16)] * groups,
        in_specs=[pl.BlockSpec(memory_space=pltpu.SMEM)] * scalars
        + [pl.BlockSpec(memory_space=pl.ANY)] * sources,
        out_specs=[pl.BlockSpec(memory_space=pl.ANY)] * groups,
        scratch_shapes=[
            pltpu.VMEM((groups,) + whole, jnp.bfloat16),
            pltpu.SemaphoreType.DMA((groups, shards, reps)),
            pltpu.SemaphoreType.DMA((groups, shards)),
        ],
        compiler_params=pltpu.CompilerParams(vmem_limit_bytes=VMEM_LIMIT),
        cost_estimate=COST,
        name="place_blocks",
    )


def widen_pieces(places, others, *pieces):
    reps = 2 * len(pieces)
    rows, columns = pieces[0].shape
    strip = next(size for size in (16, 8, rows) if rows % size == 0)

    def body(places_ref, *refs):
        sources = refs[: len(pieces) + 1]
        out_ref, narrow, wide, in_sems, out_sems = refs[len(pieces) + 1 :]
        loads = [
            pltpu.make_async_copy(piece_of(r, sources), narrow.at[r], in_sems.at[r])
            for r in range(reps)
        ]
        stores = [
            pltpu.make_async_copy(wide.at[r], out_ref.at[places_ref[r]], out_sems.at[r])
            for r in range(reps)
        ]
        for load in loads:
            load.start()
        for r in range(reps):
            loads[r].wait()

            def convert(at, carry):
                cut = pl.ds(pl.multiple_of(at * strip, strip), strip)
                wide[r, cut, :] = narrow[r, cut, :].astype(jnp.float32)
                return carry

            lax.fori_loop(0, rows // strip, convert, 0)
            stores[r].start()
        for store in stores:
            store.wait()

    result = pl.pallas_call(
        body,
        out_shape=jax.ShapeDtypeStruct((reps, rows, columns), jnp.float32),
        in_specs=[pl.BlockSpec(memory_space=pltpu.SMEM)]
        + [pl.BlockSpec(memory_space=pl.ANY)] * (len(pieces) + 1),
        out_specs=pl.BlockSpec(memory_space=pl.ANY),
        scratch_shapes=[
            pltpu.VMEM((reps, rows, columns), jnp.bfloat16),
            pltpu.VMEM((reps, rows, columns), jnp.float32),
            pltpu.SemaphoreType.DMA((reps,)),
            pltpu.SemaphoreType.DMA((reps,)),
        ],
        compiler_params=pltpu.CompilerParams(vmem_limit_bytes=VMEM_LIMIT),
        cost_estimate=COST,
        name="widen_pieces",
    )(places, *pieces, others)
    return (result.reshape(reps * rows, columns),)


def resident(shape):
    return pl.BlockSpec(shape, lambda i: (0, 0), pipeline_mode=pl.Buffered(1))


def feed_forward(rows, cotangents, gate_matrix, up_matrix, down_matrix):
    count, width = rows.shape
    units = gate_matrix.shape[1]

    def body(rows_ref, cotangents_ref, gate_ref, up_ref, down_ref, inner_ref, d_gate_ref, d_up_ref):
        gate = jnp.dot(rows_ref[...], gate_ref[...], preferred_element_type=jnp.float32)
        up = jnp.dot(rows_ref[...], up_ref[...], preferred_element_type=jnp.float32)
        sigmoid = jax.nn.sigmoid(gate)
        silu = gate * sigmoid
        inner_ref[...] = (silu * up).astype(jnp.bfloat16)
        d_inner = times_transposed(cotangents_ref[...], down_ref[...])
        d_up_ref[...] = (d_inner * silu).astype(jnp.bfloat16)
        d_gate_ref[...] = (d_inner * up * sigmoid * (1.0 + gate * (1.0 - sigmoid))).astype(
            jnp.bfloat16
        )

    columns = pl.BlockSpec((width, TILE), lambda i: (0, i))
    results = pl.BlockSpec((count, TILE), lambda i: (0, i))
    return pl.pallas_call(
        body,
        grid=(pl.cdiv(units, TILE),),
        out_shape=[jax.ShapeDtypeStruct((count, units), jnp.bfloat16)] * 3,
        in_specs=[
            resident((count, width)),
            resident((count, width)),
            columns,
            columns,
            pl.BlockSpec((TILE, width), lambda i: (i, 0)),
        ],
        out_specs=[results] * 3,
        compiler_params=pltpu.CompilerParams(vmem_limit_bytes=VMEM_LIMIT),
        cost_estimate=COST,
        name="feed_forward",
    )(rows, cotangents, gate_matrix, up_matrix, down_matrix)


def split_gradient(left, right, groups, core_place):
    count, rows = left.shape
    columns = right.shape[1]
    half = rows // (2 * groups)

    def body(core_ref, left_ref, right_ref, other_ref, own_ref, turned):
        @pl.when(pl.program_id(0) == 0)
        def turn():
            whole = left_ref[...].T
            for group in range(groups):
                for which in range(2):
                    at = (2 * group + which) * half
                    turned[which, group * half : (group + 1) * half, :] = whole[at : at + half]

        core = core_ref[0]
        for out_ref, which in ((other_ref, 1 - core), (own_ref, core)):
            product = jnp.dot(turned[which], right_ref[...], preferred_element_type=jnp.float32)
            for group in range(groups):
                out_ref[group] = product[group * half : (group + 1) * half].astype(jnp.bfloat16)

    return pl.pallas_call(
        body,
        grid=(pl.cdiv(columns, TILE),),
        out_shape=[jax.ShapeDtypeStruct((groups, half, columns), jnp.bfloat16)] * 2,
        in_specs=[
            pl.BlockSpec(memory_space=pltpu.SMEM),
            resident((count, rows)),
            pl.BlockSpec((count, TILE), lambda i: (0, i)),
        ],
        out_specs=[pl.BlockSpec((groups, half, TILE), lambda i: (0, 0, i))] * 2,
        scratch_shapes=[pltpu.VMEM((2, rows // 2, count), jnp.bfloat16)],
        compiler_params=pltpu.CompilerParams(vmem_limit_bytes=VMEM_LIMIT),
        cost_estimate=COST,
        name="split_gradient",
    )(core_place.reshape(1).astype(jnp.int32), left, right)


def ordered_gradient(left, right, shards, order):
    reps = len(order)
    count, rows = left.shape
    columns = right.shape[1]
    part = rows // (shards * reps)

    def body(left_ref, right_ref, out_ref, turned):
        @pl.when(pl.program_id(0) == 0)
        def turn():
            turned[...] = left_ref[...].T

        product = jnp.dot(turned[...], right_ref[...], preferred_element_type=jnp.float32)
        for z in range(shards):
            for r in range(reps):
                at = (z * reps + order[r]) * part
                out_ref[r, z] = product[at : at + part].astype(jnp.bfloat16)

    return pl.pallas_call(
        body,
        grid=(pl.cdiv(columns, TILE),),
        out_shape=[jax.ShapeDtypeStruct((reps, shards, part, columns), jnp.bfloat16)],
        in_specs=[
            resident((count, rows)),
            pl.BlockSpec((count, TILE), lambda i: (0, i)),
        ],
        out_specs=[pl.BlockSpec((reps, shards, part, TILE), lambda i: (0, 0, 0, i))],
        scratch_shapes=[pltpu.VMEM((rows, count), jnp.bfloat16)],
        compiler_params=pltpu.CompilerParams(vmem_limit_bytes=VMEM_LIMIT),
        cost_estimate=COST,
        name="ordered_gradient",
    )(left, right)


def rows_product(lefts, rights, turned, blocks):
    count, depth = lefts[0].shape
    columns = rights[0].shape[0 if turned else 1]
    pairs, part = len(lefts), count // blocks

    def body(*refs):
        total = None
        for left_ref, right_ref in zip(refs[:pairs], refs[pairs : 2 * pairs]):
            if turned:
                product = times_transposed(left_ref[...], right_ref[...])
            else:
                product = jnp.dot(
                    left_ref[...], right_ref[...], preferred_element_type=jnp.float32
                )
            total = product if total is None else total + product
        for block in range(blocks):
            refs[2 * pairs + block][...] = total[block * part : (block + 1) * part].astype(
                jnp.bfloat16
            )

    right_spec = (
        pl.BlockSpec((TILE, depth), lambda i: (i, 0))
        if turned
        else pl.BlockSpec((depth, TILE), lambda i: (0, i))
    )
    return pl.pallas_call(
        body,
        grid=(pl.cdiv(columns, TILE),),
        out_shape=[jax.ShapeDtypeStruct((part, columns), jnp.bfloat16)] * blocks,
        in_specs=[resident((count, depth))] * pairs + [right_spec] * pairs,
        out_specs=[pl.BlockSpec((part, TILE), lambda i: (0, i))] * blocks,
        compiler_params=pltpu.CompilerParams(vmem_limit_bytes=VMEM_LIMIT),
        cost_estimate=COST,
        name="rows_product",
    )(*lefts, *rights)


def kept_bias(row_segments, row_index, key_segments, key_index):
    kept = (row_segments == key_segments) & (key_index <= row_index)
    return jnp.where(kept, 0.0, MASKED)


def in_vmem(count):
    return [pl.BlockSpec(memory_space=pltpu.VMEM)] * count


def attention_forward(projected, cosine, signed_sine, pairs, rows, keys):
    count = projected.shape[0]
    per_group = QH // KVH
    scale = 1.0 / math.sqrt(HD)
    shape = (KVH, per_group * count, HD)

    def body(projected_ref, cosine_ref, sine_ref, pairs_ref, rows_ref, keys_ref, queries_ref, out_ref):
        bias = kept_bias(rows_ref[:, 0:1], rows_ref[:, 1:2], keys_ref[0:1, :], keys_ref[1:2, :])
        for k in range(KVH):
            for h in range(per_group):
                at = (k * per_group + h) * HD
                field = projected_ref[:, at : at + HD]
                queries_ref[k, h * count : (h + 1) * count, :] = (
                    field * cosine_ref[...] + pltpu.roll(field, HD // 2, 1) * sine_ref[...]
                ).astype(jnp.bfloat16)
            keys_here = pairs_ref[:, k * HD : (k + 1) * HD]
            values_here = pairs_ref[:, (KVH + k) * HD : (KVH + k + 1) * HD]
            scores = times_transposed(queries_ref[k], keys_here) * scale + bias
            powers = jnp.exp(scores - jnp.max(scores, axis=1, keepdims=True))
            shares = powers * (1.0 / jnp.sum(powers, axis=1, keepdims=True))
            result = jnp.dot(
                shares.astype(jnp.bfloat16), values_here, preferred_element_type=jnp.float32
            ).astype(jnp.bfloat16)
            for h in range(per_group):
                at = (k * per_group + h) * HD
                out_ref[:, at : at + HD] = result[h * count : (h + 1) * count]

    return pl.pallas_call(
        body,
        out_shape=[
            jax.ShapeDtypeStruct(shape, jnp.bfloat16),
            jax.ShapeDtypeStruct((count, QH * HD), jnp.bfloat16),
        ],
        in_specs=in_vmem(6),
        out_specs=in_vmem(2),
        compiler_params=pltpu.CompilerParams(vmem_limit_bytes=VMEM_LIMIT),
        cost_estimate=COST,
        name="attention_forward",
    )(projected, cosine, signed_sine, pairs, rows, keys)


def attention_backward(queries, gradient, pairs, cosine, signed_sine, rows, keys, blocks):
    count = gradient.shape[0]
    per_group = QH // KVH
    scale = 1.0 / math.sqrt(HD)
    group_rows = pairs.shape[0]
    part = group_rows // blocks

    def body(queries_ref, gradient_ref, pairs_ref, cosine_ref, sine_ref, rows_ref, keys_ref, d_ref, *outs):
        block_refs, stacked = outs[:blocks], outs[blocks]
        bias = kept_bias(rows_ref[0:1, :], rows_ref[1:2, :], keys_ref[:, 0:1], keys_ref[:, 1:2])
        for k in range(KVH):
            for h in range(per_group):
                at = (k * per_group + h) * HD
                stacked[h * count : (h + 1) * count, :] = gradient_ref[:, at : at + HD]
            keys_here = pairs_ref[:, k * HD : (k + 1) * HD]
            values_here = pairs_ref[:, (KVH + k) * HD : (KVH + k + 1) * HD]
            scores = times_transposed(keys_here, queries_ref[k]) * scale + bias
            powers = jnp.exp(scores - jnp.max(scores, axis=0, keepdims=True))
            shares = powers * (1.0 / jnp.sum(powers, axis=0, keepdims=True))
            d_shares = times_transposed(values_here, stacked[...])
            dots = jnp.sum(shares * d_shares, axis=0, keepdims=True)
            d_scores = (shares * (d_shares - dots)).astype(jnp.bfloat16)
            d_keys = jnp.dot(d_scores, queries_ref[k], preferred_element_type=jnp.float32) * scale
            d_values = jnp.dot(
                shares.astype(jnp.bfloat16), stacked[...], preferred_element_type=jnp.float32
            )
            for block in range(blocks):
                cut = slice(block * part, (block + 1) * part)
                block_refs[block][:, k * HD : (k + 1) * HD] = d_keys[cut].astype(jnp.bfloat16)
                block_refs[block][:, (KVH + k) * HD : (KVH + k + 1) * HD] = d_values[cut].astype(
                    jnp.bfloat16
                )
            d_queries = transposed_times(d_scores, keys_here) * scale
            for h in range(per_group):
                at = (k * per_group + h) * HD
                field = d_queries[h * count : (h + 1) * count]
                d_ref[:, at : at + HD] = (
                    field * cosine_ref[...] - pltpu.roll(field, HD // 2, 1) * sine_ref[...]
                ).astype(jnp.bfloat16)

    return pl.pallas_call(
        body,
        out_shape=[jax.ShapeDtypeStruct((count, QH * HD), jnp.bfloat16)]
        + [jax.ShapeDtypeStruct((part, 2 * KVH * HD), jnp.bfloat16)] * blocks,
        in_specs=in_vmem(7),
        out_specs=in_vmem(1 + blocks),
        scratch_shapes=[pltpu.VMEM((per_group * count, HD), jnp.bfloat16)],
        compiler_params=pltpu.CompilerParams(vmem_limit_bytes=VMEM_LIMIT),
        cost_estimate=COST,
        name="attention_backward",
    )(queries, gradient, pairs, cosine, signed_sine, rows, keys)


def join_projected(d_queries, pair_terms, cosine, signed_sine):
    count, query_width = d_queries.shape
    pair_width = KVH * HD
    terms = len(pair_terms)

    def body(d_queries_ref, cosine_ref, sine_ref, *refs):
        term_refs, out_ref, sum_ref = refs[:terms], refs[terms], refs[terms + 1]
        out_ref[:, :query_width] = d_queries_ref[...]
        for at in range(0, 2 * pair_width, HD):
            field = total_of([term[:, at : at + HD] for term in term_refs])
            if at < pair_width:
                field = field * cosine_ref[...] - pltpu.roll(field, HD // 2, 1) * sine_ref[...]
            out_ref[:, query_width + at : query_width + at + HD] = field.astype(jnp.bfloat16)
        sum_ref[...] = jnp.sum(out_ref[...].astype(jnp.float32), axis=0, keepdims=True)

    return pl.pallas_call(
        body,
        out_shape=[
            jax.ShapeDtypeStruct((count, query_width + 2 * pair_width), jnp.bfloat16),
            jax.ShapeDtypeStruct((1, query_width + 2 * pair_width), jnp.float32),
        ],
        in_specs=in_vmem(3 + terms),
        out_specs=in_vmem(2),
        cost_estimate=COST,
        name="join_projected",
    )(d_queries, cosine, signed_sine, *pair_terms)


def on_device(
    tokens,
    segment_ids,
    first_gain,
    input_weight,
    input_bias,
    output_weight,
    second_gain,
    gate_weight,
    up_weight,
    down_weight,
    output_cotangent,
):
    bf16, f32 = jnp.bfloat16, jnp.float32
    shards, reps = lax.axis_size("shard"), lax.axis_size("rep")
    shard, core, first, second = make_lines(reps, shards)
    rep_place = (core.place * first.size + first.place) * second.size + second.place
    own_rows, width = tokens.shape
    segments = segment_ids[0]
    per_group = QH // KVH
    query_width = QH * HD
    pair_width = KVH * HD
    first_row = shard.place * own_rows
    part_rows = input_weight.shape[0] // reps
    hidden_units = gate_weight.shape[1]
    block_units = hidden_units // shards
    clock = Clock()
    z_order = jnp.stack([shard.behind(step) for step in range(shards)]).astype(jnp.int32)

    def weight_piece(weight, place):
        return pick(weight.reshape(reps, part_rows, weight.shape[1]), place, 0)

    def column_piece(weight, place):
        return weight_piece(weight, place).reshape(part_rows, shards, block_units).transpose(1, 0, 2)

    def spread(piece):
        return Spread(clock, piece, core, first, second)

    def send_rows(rows):
        return [shard.shift(row, shards - step) for step, row in enumerate(rows, 1)]

    def place_sends(blocks):
        return [pick(blocks, shard.place, 0)] + [
            shard.shift(pick(blocks, shard.ahead(step), 0), step) for step in range(1, shards)
        ]

    def together(*groups):
        flat = clock(*[array for group in groups for array in group])
        parts, at = [], 0
        for group in groups:
            parts.append(flat[at : at + len(group)])
            at += len(group)
        return parts

    rep_index = lax.axis_index("rep")
    input_matrix = lax.all_gather(
        weight_piece(input_weight, rep_index), ("shard", "rep"), axis=0, tiled=True
    )
    shard_vectors = jnp.concatenate([first_gain, second_gain, input_bias])
    vector_moving = gather_line(shard_vectors, shard)
    output_piece = weight_piece(output_weight, rep_place)
    vectors, (output_piece,) = together(vector_moving, [output_piece])
    output_moving = gather_line(output_piece, shard)
    vector_rows = jnp.stack(in_place_order(vectors, shard))
    own_gain = first_gain.shape[0]
    gain_one = vector_rows[:, :own_gain].reshape(width).astype(f32)
    gain_two = vector_rows[:, own_gain : 2 * own_gain].reshape(width).astype(f32)
    shift_row = vector_rows[:, 2 * own_gain :].reshape(-1).astype(f32)
    columns = jnp.stack(
        [column_piece(gate_weight, rep_index), column_piece(up_weight, rep_index)], axis=1
    )
    output_rows, (columns,) = together(output_moving, [columns])
    output_spread = spread(jnp.stack(output_rows)[None])
    column_moving = place_sends(columns)

    places = positions(segments)
    cosine_table, sine_table = rope_tables(
        lax.dynamic_slice_in_dim(places, first_row, own_rows), HD
    )
    signed_sine = jnp.concatenate(
        [-sine_table[:, : HD // 2], sine_table[:, HD // 2 :]], axis=1
    )
    own_segments = lax.dynamic_slice_in_dim(segments, first_row, own_rows)
    row_index = jnp.arange(own_rows, dtype=jnp.int32)
    key_index = jnp.concatenate([shard.behind(step) * own_rows + row_index for step in range(shards)])
    key_segments = jnp.concatenate(
        [
            lax.dynamic_slice_in_dim(segments, shard.behind(step) * own_rows, own_rows)
            for step in range(shards)
        ]
    )
    key_marks = jnp.stack([key_segments, key_index])
    row_marks = jnp.tile(jnp.stack([own_segments, first_row + row_index]), (1, per_group))
    wide_tokens = tokens.astype(f32)
    inverse_one = lax.rsqrt(jnp.mean(wide_tokens * wide_tokens, axis=-1, keepdims=True) + EPSILON)
    unit_one = wide_tokens * inverse_one
    normed_one = (unit_one * gain_one).astype(bf16)
    (
        normed_one,
        cosine_table,
        sine_table,
        signed_sine,
        key_marks,
        row_marks,
    ) = clock(normed_one, cosine_table, sine_table, signed_sine, key_marks, row_marks)
    output_spread.further()
    output_arrived, column_rows = together(output_spread.waits(), column_moving)
    output_spread.over(*output_arrived)
    gate_up = lax.all_gather(jnp.stack(column_rows)[None], "rep", axis=0, tiled=True)
    (output_matrix,) = clock.run(place_blocks, z_order, *output_spread.finish())
    output_matrix = output_matrix.reshape(width, width)

    cotangent_arrived = [output_cotangent] + [None] * (shards - 1)
    far = list(range(2, shards - 1))
    near = sorted({1, shards - 1})
    for step in far:
        cotangent_arrived[step] = shard.shift(output_cotangent, step)
    (input_matrix,) = clock(input_matrix)
    projected = jnp.dot(normed_one, input_matrix, preferred_element_type=f32) + shift_row
    key_part = rotate(
        projected[:, query_width : query_width + pair_width].reshape(own_rows, KVH, HD),
        cosine_table,
        sine_table,
    )
    (own_pairs,) = clock(
        jnp.concatenate(
            [key_part.reshape(own_rows, pair_width), projected[:, query_width + pair_width :]],
            axis=1,
        ).astype(bf16)
    )
    pair_rows, moved = together(
        gather_line(own_pairs, shard), [cotangent_arrived[step] for step in far]
    )
    for step, value in zip(far, moved):
        cotangent_arrived[step] = value
    pairs = jnp.concatenate(pair_rows, axis=0)
    for step in near:
        cotangent_arrived[step] = shard.shift(output_cotangent, step)
    queries, attention_low = clock.run(
        attention_forward, projected, cosine_table, signed_sine, pairs, row_marks.T, key_marks
    )
    hidden = wide_tokens + jnp.dot(attention_low, output_matrix, preferred_element_type=f32)
    inverse_two = lax.rsqrt(jnp.mean(hidden * hidden, axis=-1, keepdims=True) + EPSILON)
    unit_two = hidden * inverse_two
    (normed_two,) = clock((unit_two * gain_two).astype(bf16))
    normed_arrived, cotangent_arrived = together(gather_line(normed_two, shard), cotangent_arrived)
    cotangents = jnp.concatenate(cotangent_arrived, axis=0)
    group_normed = jnp.concatenate(normed_arrived, axis=0)
    gate_matrix, up_matrix = clock.run(place_gathered, z_order, gate_up)
    gate_matrix = gate_matrix.reshape(width, block_units)
    up_matrix = up_matrix.reshape(width, block_units)

    inner_act, d_gate, d_up = clock.run(
        feed_forward, group_normed, cotangents, gate_matrix, up_matrix, down_weight
    )

    def start_halving(left, right, groups):
        sent, own = clock.run(
            lambda left, right: split_gradient(left, right, groups, core.place), left, right
        )
        shape = (groups, first.size * second.size, -1, right.shape[1])
        return Halving(clock, sent.reshape(shape), own.reshape(shape), core, first, second)

    def side_by_side(rows):
        return clock(jnp.concatenate(in_place_order(rows, shard), axis=1))[0]

    def sum_over_rep(blocks):
        return lax.psum_scatter(blocks, "rep", scatter_dimension=0, tiled=True)

    (down_blocks,) = clock.run(
        lambda left, right: ordered_gradient(left, right, 1, list(range(reps))), inner_act, cotangents
    )
    down_piece = sum_over_rep(down_blocks.reshape(block_units, width))
    normed_own, *normed_partial = clock.run(
        lambda *operands: rows_product(operands[:2], operands[2:], True, shards),
        d_gate,
        d_up,
        gate_matrix,
        up_matrix,
    )
    normed_arriving = send_rows(normed_partial)
    up = start_halving(group_normed, d_up, shards)
    (gate_blocks,) = clock.run(
        lambda left, right: ordered_gradient(left, right, shards, rep_places(reps)), group_normed, d_gate
    )
    up.along_first()
    (down_piece,) = clock(down_piece)
    gate_piece = sum_over_rep(gate_blocks.reshape(width, block_units))
    up.along_second()

    normed_two_gradient = total_of([normed_own] + clock(*normed_arriving))
    gain_two_gradient = jnp.sum(normed_two_gradient * unit_two, axis=0)
    hidden_gradient = output_cotangent.astype(f32) + norm_back(
        normed_two_gradient, unit_two, inverse_two, gain_two
    )
    (branch_gradient,) = clock(hidden_gradient.astype(bf16))
    (attention_gradient,) = clock(times_transposed(branch_gradient, output_matrix).astype(bf16))
    d_queries, pair_own, *pair_partial = clock.run(
        lambda *operands: attention_backward(*operands, shards),
        queries,
        attention_gradient,
        pairs,
        cosine_table,
        signed_sine,
        row_marks,
        key_marks.T,
    )
    pair_arriving = send_rows(pair_partial)
    output = start_halving(attention_low, branch_gradient, shards)
    up_blocks = up.finish()
    output.along_first()
    block_own, *block_partial = clock.run(
        lambda left, right: rows_product((left,), (right,), False, shards), inner_act, down_weight
    )
    pair_terms = [pair_own] + clock(*pair_arriving)
    up_moving = place_sends(up_blocks)
    projected_gradient, bias_sum = clock.run(
        lambda *operands: join_projected(operands[0], operands[3:], *operands[1:3]),
        d_queries,
        cosine_table,
        signed_sine,
        *pair_terms,
    )
    projected = start_halving(normed_one, projected_gradient, shards)
    output.along_second()
    projected.along_first()
    up_rows = clock(*up_moving)
    up_spread = spread(side_by_side(up_rows))
    output_blocks = output.finish()
    projected_gradient, hidden_gradient = clock(projected_gradient, hidden_gradient)
    normed_one_gradient = times_transposed(projected_gradient, input_matrix)
    gain_one_gradient = jnp.sum(normed_one_gradient * unit_one, axis=0)
    (tokens_gradient,) = clock(
        (
            hidden_gradient + norm_back(normed_one_gradient, unit_one, inverse_one, gain_one)
        ).astype(bf16)
    )
    bias_gradient = bias_sum[0]
    bias_split = query_width + pair_width
    small_parts = (
        gain_one_gradient,
        gain_two_gradient,
        bias_gradient[:bias_split],
        bias_gradient[bias_split:],
    )
    (small,) = clock(
        jnp.concatenate([part.reshape(shards, -1) for part in small_parts], axis=1)
    )
    projected.along_second()
    up_spread.further()
    output_moving = place_sends(output_blocks)
    input_blocks = projected.finish()
    output_sum = clock(total_of(clock(*output_moving)).astype(bf16))[0]
    input_moving = place_sends(input_blocks)
    up_spread.over()
    input_sum = clock(total_of(clock(*input_moving)).astype(bf16))[0]
    (gate_piece,) = clock(gate_piece)
    down_spread = lax.all_gather(down_piece, "rep", axis=0, tiled=True)
    gate_moving = place_sends(gate_piece.reshape(shards, part_rows, block_units))
    (up_total,) = clock.run(widen_pieces, *up_spread.finish())
    gate_rows = clock(*gate_moving)
    gate_spread = spread(side_by_side(gate_rows))
    output_spread = spread(output_sum)
    output_spread.further()
    block_arriving = send_rows(block_partial)
    output_spread.over()
    gate_spread.further()
    input_spread = spread(input_sum)
    (output_total,) = clock.run(widen_pieces, *output_spread.finish())
    input_spread.further()
    gate_spread.over()
    input_spread.over()
    (block_out,) = clock(total_of([hidden, block_own] + clock(*block_arriving)).astype(bf16))
    (input_total,) = clock.run(widen_pieces, *input_spread.finish())
    for line in (core, first, second):
        small = total_of(
            [small] + clock(*[line.shift(small, step) for step in range(1, line.size)])
        )
    small = total_of(clock(*place_sends(small)))
    (gate_total,) = clock.run(widen_pieces, *gate_spread.finish())
    down_total = clock(down_spread)[0].astype(f32)

    small = small + clock.token[0, 0]
    small_totals, at = [], 0
    for part in small_parts:
        size = part.shape[0] // shards
        small_totals.append(small[at : at + size])
        at += size
    return (
        block_out,
        tokens_gradient,
        small_totals[0],
        input_total,
        small_totals[2],
        small_totals[3],
        output_total,
        small_totals[1],
        gate_total,
        up_total,
        down_total,
    )


def solution(mesh):
    placed = (
        P(("rep", "shard"), None),
        P("rep", None),
        P("shard"),
        P("shard", None),
        P("shard"),
        P("shard", None),
        P("shard"),
        P("shard", None),
        P("shard", None),
        P("shard", None),
        P(("rep", "shard"), None),
    )
    return jax.shard_map(
        on_device,
        mesh=mesh,
        in_specs=placed,
        out_specs=(
            P(("rep", "shard"), None),
            P(("rep", "shard"), None),
            P("shard"),
            P("shard", None),
            P("shard"),
            P("shard"),
            P("shard", None),
            P("shard"),
            P("shard", None),
            P("shard", None),
            P("shard", None),
        ),
        check_vma=False,
    )
```

```python
import math

import jax
import jax.numpy as jnp
from jax import lax
from jax.experimental import pallas as pl
from jax.experimental.pallas import tpu as pltpu
from jax.sharding import PartitionSpec as P

QH = 12
KVH = 2
HD = 128
SEQS = 3


EPSILON = 1e-06
LOG_THETA = math.log(1000000.0)
MASKED = -1e30
VMEM_LIMIT = 56 * 1024 * 1024
TILE = 512
COST = pl.CostEstimate(flops=1, bytes_accessed=1, transcendentals=0)


def rope_tables(places, head_width):
    half_width = head_width // 2
    frequency = jnp.exp(jnp.arange(half_width, dtype=jnp.float32) * (-2.0 * LOG_THETA / head_width))
    angles = places.astype(jnp.float32)[:, None] * frequency[None, :]
    angles = jnp.concatenate([angles, angles], axis=-1)
    return (jnp.cos(angles), jnp.sin(angles))


def positions(segments):
    labels = jnp.arange(SEQS, dtype=jnp.int32)
    starts = jnp.sum((segments[None, :] < labels[:, None]).astype(jnp.int32), axis=1)
    own_start = jnp.sum(jnp.where(segments[:, None] == labels[None, :], starts[None, :], 0), axis=1)
    return jnp.arange(segments.shape[0], dtype=jnp.int32) - own_start


def rotate(field_rows, cosine_table, sine_table):
    half_width = field_rows.shape[-1] // 2
    turned = jnp.concatenate([-field_rows[..., half_width:], field_rows[..., :half_width]], axis=-1)
    return field_rows * cosine_table[:, None, :] + turned * sine_table[:, None, :]


def transposed_times(left_side, right_side):
    return lax.dot_general(
        left_side, right_side, (((0,), (0,)), ((), ())), preferred_element_type=jnp.float32
    )


def times_transposed(left_side, right_side):
    return lax.dot_general(
        left_side, right_side, (((1,), (1,)), ((), ())), preferred_element_type=jnp.float32
    )


def norm_back(normed_gradient, unit_rows, inverse_rms, gain_row):
    scaled = normed_gradient * gain_row
    return inverse_rms * (scaled - unit_rows * jnp.mean(scaled * unit_rows, axis=-1, keepdims=True))


class Line:
    def __init__(self, name, size, place, pairs, crossed=False):
        self.name, self.size, self.place, self.pairs = name, size, place, pairs
        self.crossed = crossed

    def shift(self, value, step):
        return lax.ppermute(value, self.name, self.pairs(step % self.size))

    def behind(self, step):
        return lax.rem(self.place + (self.size - step % self.size), self.size)

    def ahead(self, step):
        return lax.rem(self.place + step % self.size, self.size) if step else self.place


def make_lines(reps, shards):
    inner = 2 if reps % 4 == 0 else 1
    outer = reps // (2 * inner)
    square = inner == outer

    def split(index):
        core, b, a = index % 2, (index // 2) % inner, index // (2 * inner)
        return core, b, a

    def join(core, b, a):
        return (a * inner + b) * 2 + core

    def first_pairs(step):
        pairs = []
        for index in range(reps):
            core, b, a = split(index)
            if square and core == 0:
                pairs.append((index, join(core, (b + step) % inner, a)))
            else:
                pairs.append((index, join(core, b, (a + step) % outer)))
        return pairs

    def second_pairs(step):
        pairs = []
        for index in range(reps):
            core, b, a = split(index)
            if square and core == 0:
                pairs.append((index, join(core, b, (a + step) % outer)))
            else:
                pairs.append((index, join(core, (b + step) % inner, a)))
        return pairs

    def core_pairs(step):
        pairs = []
        for index in range(reps):
            core, b, a = split(index)
            pairs.append((index, join((core + step) % 2, b, a)))
        return pairs

    def shard_pairs(step):
        return [(index, (index + step) % shards) for index in range(shards)]

    core, b, a = split(lax.axis_index("rep"))
    first, second = (jnp.where(core == 0, b, a), jnp.where(core == 0, a, b)) if square else (a, b)
    return (
        Line("shard", shards, lax.axis_index("shard"), shard_pairs),
        Line("rep", 2, core, core_pairs, square),
        Line("rep", outer, first, first_pairs),
        Line("rep", inner, second, second_pairs),
    )


def rep_places(reps):
    inner = 2 if reps % 4 == 0 else 1
    outer = reps // (2 * inner)
    places = []
    for index in range(reps):
        core, b, a = index % 2, (index // 2) % inner, index // (2 * inner)
        one, two = (b, a) if inner == outer and core == 0 else (a, b)
        places.append((core * outer + one) * inner + two)
    return places


def pick(array, index, axis):
    return lax.dynamic_index_in_dim(array, index, axis, keepdims=False)


def put(array, piece, index, axis):
    return lax.dynamic_update_index_in_dim(array, piece, index, axis)


def in_place_order(pieces, line):
    ordered = []
    for place in range(line.size):
        chosen = pieces[0]
        for step in range(1, line.size):
            chosen = jnp.where(line.behind(step) == place, pieces[step], chosen)
        ordered.append(chosen)
    return ordered


def tie(*arrays):
    return lax.optimization_barrier(arrays)


def gather_line(value, line):
    return [value] + [line.shift(value, step) for step in range(1, line.size)]


class Clock:
    def __init__(self):
        self.token = jnp.zeros((8, 128), jnp.float32)

    def __call__(self, *arrays):
        self.token, *arrays = tie(self.token, *arrays)
        return arrays

    def run(self, step, *arrays):
        return self(*step(*self(*arrays)))


def total_of(terms):
    total = terms[0].astype(jnp.float32)
    for term in terms[1:]:
        total = total + term.astype(jnp.float32)
    return total


class Halving:
    def __init__(self, clock, sent, own, core, first, second):
        self.clock, self.first, self.second = clock, first, second
        self.terms = [own]
        self.moving = [core.shift(sent, 1)]

    def along(self, line):
        self.terms = self.terms + self.clock(*self.moving)
        blocks = [
            total_of([pick(term, line.ahead(step), 1) for term in self.terms]).astype(jnp.bfloat16)
            for step in range(1, line.size)
        ]
        self.moving = [
            line.shift(block, step) for step, block in enumerate(self.clock(*blocks), 1)
        ]
        self.terms = [pick(term, line.place, 1) for term in self.terms]

    def along_first(self):
        self.along(self.first)

    def along_second(self):
        self.along(self.second)

    def finish(self):
        self.terms = self.terms + self.clock(*self.moving)
        return self.clock(total_of(self.terms).astype(jnp.bfloat16))[0]


class Spread:
    def __init__(self, clock, piece, core, first, second):
        self.clock, self.lines = clock, (core, first, second)
        self.across = {(0, two): second.shift(piece, two) for two in range(1, second.size)}
        self.along = {(one, 0): first.shift(piece, one) for one in range(1, first.size)}
        self.here = {(0, 0): piece}

    def waits(self):
        if hasattr(self, "there"):
            return [self.there]
        if hasattr(self, "beyond"):
            return list(self.beyond.values())
        return list(self.across.values()) + list(self.along.values())

    def further(self, *values):
        values = values or self.clock(*self.waits())
        self.here.update(zip(list(self.across) + list(self.along), values))
        self.beyond = {
            (one, two): self.lines[1].shift(self.here[0, two], one)
            for one in range(1, self.lines[1].size)
            for two in range(1, self.lines[2].size)
        }

    def over(self, *values):
        values = values or self.clock(*self.waits())
        self.here.update(zip(self.beyond, values))
        (stacked,) = self.clock(jnp.stack(list(self.here.values())))
        self.there = self.lines[0].shift(stacked, 1)

    def finish(self, *values):
        core, first, second = self.lines
        (others,) = values or self.clock(*self.waits())
        placed = [(core.place, first.behind(one), second.behind(two)) for one, two in self.here]
        far, near = (second, first) if core.crossed else (first, second)
        placed += [(core.behind(1), far.behind(one), near.behind(two)) for one, two in self.here]
        places = [(c * first.size + f) * second.size + s for c, f, s in placed]
        return [jnp.stack(places).astype(jnp.int32), others] + list(self.here.values())


def piece_of(r, sources):
    return sources[r] if r < len(sources) - 1 else sources[-1].at[r - len(sources) + 1]


def place_blocks(order, places, others, *pieces):
    reps = 2 * len(pieces)
    groups, shards = pieces[0].shape[:2]
    block = pieces[0].shape[2:]

    def body(order_ref, places_ref, *refs):
        sources, rest = refs[: len(pieces) + 1], refs[len(pieces) + 1 :]
        move_blocks(
            lambda g, k, r: piece_of(r, sources).at[g, k],
            lambda r: places_ref[r],
            order_ref,
            rest[:groups],
            *rest[groups:],
        )

    return blocks_call(body, 2, len(pieces) + 1, groups, shards, reps, block)(
        order, places, *pieces, others
    )


def place_gathered(order, gathered):
    reps, shards, groups = gathered.shape[:3]

    def body(order_ref, source, *rest):
        move_blocks(
            lambda g, k, r: source.at[r, k, g], lambda r: r, order_ref, rest[:groups], *rest[groups:]
        )

    return blocks_call(body, 1, 1, groups, shards, reps, gathered.shape[3:])(order, gathered)


def move_blocks(source_of, place_of, order_ref, outs, held, in_sems, out_sems):
    groups, shards, reps = in_sems.shape
    slabs = [(g, k) for g in range(groups) for k in range(shards)]

    def load(g, k, r):
        return pltpu.make_async_copy(
            source_of(g, k, r), held.at[g, k, place_of(r)], in_sems.at[g, k, r]
        )

    def store(g, k):
        return pltpu.make_async_copy(held.at[g, k], outs[g].at[order_ref[k]], out_sems.at[g, k])

    for g, k in slabs:
        for r in range(reps):
            load(g, k, r).start()
    for g, k in slabs:
        for r in range(reps):
            load(g, k, r).wait()
        store(g, k).start()
    for g, k in slabs:
        store(g, k).wait()


def blocks_call(body, scalars, sources, groups, shards, reps, block):
    whole = (shards, reps) + block
    return pl.pallas_call(
        body,
        out_shape=[jax.ShapeDtypeStruct(whole, jnp.bfloat16)] * groups,
        in_specs=[pl.BlockSpec(memory_space=pltpu.SMEM)] * scalars
        + [pl.BlockSpec(memory_space=pl.ANY)] * sources,
        out_specs=[pl.BlockSpec(memory_space=pl.ANY)] * groups,
        scratch_shapes=[
            pltpu.VMEM((groups,) + whole, jnp.bfloat16),
            pltpu.SemaphoreType.DMA((groups, shards, reps)),
            pltpu.SemaphoreType.DMA((groups, shards)),
        ],
        compiler_params=pltpu.CompilerParams(vmem_limit_bytes=VMEM_LIMIT),
        cost_estimate=COST,
        name="place_blocks",
    )


def widen_pieces(places, others, *pieces):
    reps = 2 * len(pieces)
    rows, columns = pieces[0].shape
    strip = next(size for size in (16, 8, rows) if rows % size == 0)

    def body(places_ref, *refs):
        sources = refs[: len(pieces) + 1]
        out_ref, narrow, wide, in_sems, out_sems = refs[len(pieces) + 1 :]
        loads = [
            pltpu.make_async_copy(piece_of(r, sources), narrow.at[r], in_sems.at[r])
            for r in range(reps)
        ]
        stores = [
            pltpu.make_async_copy(wide.at[r], out_ref.at[places_ref[r]], out_sems.at[r])
            for r in range(reps)
        ]
        for load in loads:
            load.start()
        for r in range(reps):
            loads[r].wait()

            def convert(at, carry):
                cut = pl.ds(pl.multiple_of(at * strip, strip), strip)
                wide[r, cut, :] = narrow[r, cut, :].astype(jnp.float32)
                return carry

            lax.fori_loop(0, rows // strip, convert, 0)
            stores[r].start()
        for store in stores:
            store.wait()

    result = pl.pallas_call(
        body,
        out_shape=jax.ShapeDtypeStruct((reps, rows, columns), jnp.float32),
        in_specs=[pl.BlockSpec(memory_space=pltpu.SMEM)]
        + [pl.BlockSpec(memory_space=pl.ANY)] * (len(pieces) + 1),
        out_specs=pl.BlockSpec(memory_space=pl.ANY),
        scratch_shapes=[
            pltpu.VMEM((reps, rows, columns), jnp.bfloat16),
            pltpu.VMEM((reps, rows, columns), jnp.float32),
            pltpu.SemaphoreType.DMA((reps,)),
            pltpu.SemaphoreType.DMA((reps,)),
        ],
        compiler_params=pltpu.CompilerParams(vmem_limit_bytes=VMEM_LIMIT),
        cost_estimate=COST,
        name="widen_pieces",
    )(places, *pieces, others)
    return (result.reshape(reps * rows, columns),)


def resident(shape):
    return pl.BlockSpec(shape, lambda i: (0, 0), pipeline_mode=pl.Buffered(1))


def feed_forward(rows, cotangents, gate_matrix, up_matrix, down_matrix):
    count, width = rows.shape
    units = gate_matrix.shape[1]
    steps = pl.cdiv(units, TILE)
    slabs = next(size for size in range(min(steps, width // 128), 0, -1) if width % (128 * size) == 0)
    slab = width // slabs

    def body(
        rows_ref,
        cotangents_ref,
        gate_ref,
        up_ref,
        down_ref,
        inner_ref,
        d_gate_ref,
        d_up_ref,
        turned_rows_ref,
        turned_inner_ref,
    ):
        gate = jnp.dot(rows_ref[...], gate_ref[...], preferred_element_type=jnp.float32)
        up = jnp.dot(rows_ref[...], up_ref[...], preferred_element_type=jnp.float32)
        sigmoid = jax.nn.sigmoid(gate)
        silu = gate * sigmoid
        inner = (silu * up).astype(jnp.bfloat16)
        inner_ref[...] = inner
        turned_inner_ref[...] = inner.T
        d_inner = times_transposed(cotangents_ref[...], down_ref[...])
        d_up_ref[...] = (d_inner * silu).astype(jnp.bfloat16)
        d_gate_ref[...] = (d_inner * up * sigmoid * (1.0 + gate * (1.0 - sigmoid))).astype(
            jnp.bfloat16
        )
        for step in range(slabs):

            @pl.when(pl.program_id(0) == step)
            def turn():
                turned_rows_ref[...] = rows_ref[:, step * slab : (step + 1) * slab].T

    columns = pl.BlockSpec((width, TILE), lambda i: (0, i))
    results = pl.BlockSpec((count, TILE), lambda i: (0, i))
    return pl.pallas_call(
        body,
        grid=(steps,),
        out_shape=[jax.ShapeDtypeStruct((count, units), jnp.bfloat16)] * 3
        + [
            jax.ShapeDtypeStruct((width, count), jnp.bfloat16),
            jax.ShapeDtypeStruct((units, count), jnp.bfloat16),
        ],
        in_specs=[
            resident((count, width)),
            resident((count, width)),
            columns,
            columns,
            pl.BlockSpec((TILE, width), lambda i: (i, 0)),
        ],
        out_specs=[results] * 3
        + [
            pl.BlockSpec((slab, count), lambda i: (jnp.minimum(i, slabs - 1), 0)),
            pl.BlockSpec((TILE, count), lambda i: (i, 0)),
        ],
        compiler_params=pltpu.CompilerParams(vmem_limit_bytes=VMEM_LIMIT),
        cost_estimate=COST,
        name="feed_forward",
    )(rows, cotangents, gate_matrix, up_matrix, down_matrix)


def split_gradient(left, right, groups, core_place):
    rows, count = left.shape
    columns = right.shape[1]
    half = rows // (2 * groups)

    def body(core_ref, left_ref, right_ref, other_ref, own_ref):
        core = core_ref[0]
        for out_ref, which in ((other_ref, 1 - core), (own_ref, core)):
            halves = [
                left_ref[pl.ds(pl.multiple_of((2 * group + which) * half, 16), half), :]
                for group in range(groups)
            ]
            product = jnp.dot(
                jnp.concatenate(halves, axis=0), right_ref[...], preferred_element_type=jnp.float32
            )
            for group in range(groups):
                out_ref[group] = product[group * half : (group + 1) * half].astype(jnp.bfloat16)

    return pl.pallas_call(
        body,
        grid=(pl.cdiv(columns, TILE),),
        out_shape=[jax.ShapeDtypeStruct((groups, half, columns), jnp.bfloat16)] * 2,
        in_specs=[
            pl.BlockSpec(memory_space=pltpu.SMEM),
            resident((rows, count)),
            pl.BlockSpec((count, TILE), lambda i: (0, i)),
        ],
        out_specs=[pl.BlockSpec((groups, half, TILE), lambda i: (0, 0, i))] * 2,
        compiler_params=pltpu.CompilerParams(vmem_limit_bytes=VMEM_LIMIT),
        cost_estimate=COST,
        name="split_gradient",
    )(core_place.reshape(1).astype(jnp.int32), left, right)


def ordered_gradient(left, right, shards, order):
    reps = len(order)
    rows, count = left.shape
    columns = right.shape[1]
    part = rows // (shards * reps)

    def body(left_ref, right_ref, out_ref):
        product = jnp.dot(left_ref[...], right_ref[...], preferred_element_type=jnp.float32)
        for z in range(shards):
            for r in range(reps):
                at = (z * reps + order[r]) * part
                out_ref[r, z] = product[at : at + part].astype(jnp.bfloat16)

    return pl.pallas_call(
        body,
        grid=(pl.cdiv(columns, TILE),),
        out_shape=[jax.ShapeDtypeStruct((reps, shards, part, columns), jnp.bfloat16)],
        in_specs=[
            resident((rows, count)),
            pl.BlockSpec((count, TILE), lambda i: (0, i)),
        ],
        out_specs=[pl.BlockSpec((reps, shards, part, TILE), lambda i: (0, 0, 0, i))],
        compiler_params=pltpu.CompilerParams(vmem_limit_bytes=VMEM_LIMIT),
        cost_estimate=COST,
        name="ordered_gradient",
    )(left, right)


def rows_product(lefts, rights, turned, blocks):
    count, depth = lefts[0].shape
    columns = rights[0].shape[0 if turned else 1]
    pairs, part = len(lefts), count // blocks

    def body(*refs):
        total = None
        for left_ref, right_ref in zip(refs[:pairs], refs[pairs : 2 * pairs]):
            if turned:
                product = times_transposed(left_ref[...], right_ref[...])
            else:
                product = jnp.dot(
                    left_ref[...], right_ref[...], preferred_element_type=jnp.float32
                )
            total = product if total is None else total + product
        for block in range(blocks):
            refs[2 * pairs + block][...] = total[block * part : (block + 1) * part].astype(
                jnp.bfloat16
            )

    right_spec = (
        pl.BlockSpec((TILE, depth), lambda i: (i, 0))
        if turned
        else pl.BlockSpec((depth, TILE), lambda i: (0, i))
    )
    return pl.pallas_call(
        body,
        grid=(pl.cdiv(columns, TILE),),
        out_shape=[jax.ShapeDtypeStruct((part, columns), jnp.bfloat16)] * blocks,
        in_specs=[resident((count, depth))] * pairs + [right_spec] * pairs,
        out_specs=[pl.BlockSpec((part, TILE), lambda i: (0, i))] * blocks,
        compiler_params=pltpu.CompilerParams(vmem_limit_bytes=VMEM_LIMIT),
        cost_estimate=COST,
        name="rows_product",
    )(*lefts, *rights)


def kept_bias(row_segments, row_index, key_segments, key_index):
    kept = (row_segments == key_segments) & (key_index <= row_index)
    return jnp.where(kept, 0.0, MASKED)


def in_vmem(count):
    return [pl.BlockSpec(memory_space=pltpu.VMEM)] * count


def attention_forward(projected, cosine, signed_sine, pairs, rows, keys):
    count = projected.shape[0]
    per_group = QH // KVH
    scale = 1.0 / math.sqrt(HD)
    shape = (KVH, per_group * count, HD)

    def body(projected_ref, cosine_ref, sine_ref, pairs_ref, rows_ref, keys_ref, queries_ref, out_ref):
        bias = kept_bias(rows_ref[:, 0:1], rows_ref[:, 1:2], keys_ref[0:1, :], keys_ref[1:2, :])
        for k in range(KVH):
            for h in range(per_group):
                at = (k * per_group + h) * HD
                field = projected_ref[:, at : at + HD]
                queries_ref[k, h * count : (h + 1) * count, :] = (
                    field * cosine_ref[...] + pltpu.roll(field, HD // 2, 1) * sine_ref[...]
                ).astype(jnp.bfloat16)
            keys_here = pairs_ref[:, k * HD : (k + 1) * HD]
            values_here = pairs_ref[:, (KVH + k) * HD : (KVH + k + 1) * HD]
            scores = times_transposed(queries_ref[k], keys_here) * scale + bias
            powers = jnp.exp(scores - jnp.max(scores, axis=1, keepdims=True))
            shares = powers * (1.0 / jnp.sum(powers, axis=1, keepdims=True))
            result = jnp.dot(
                shares.astype(jnp.bfloat16), values_here, preferred_element_type=jnp.float32
            ).astype(jnp.bfloat16)
            for h in range(per_group):
                at = (k * per_group + h) * HD
                out_ref[:, at : at + HD] = result[h * count : (h + 1) * count]

    return pl.pallas_call(
        body,
        out_shape=[
            jax.ShapeDtypeStruct(shape, jnp.bfloat16),
            jax.ShapeDtypeStruct((count, QH * HD), jnp.bfloat16),
        ],
        in_specs=in_vmem(6),
        out_specs=in_vmem(2),
        compiler_params=pltpu.CompilerParams(vmem_limit_bytes=VMEM_LIMIT),
        cost_estimate=COST,
        name="attention_forward",
    )(projected, cosine, signed_sine, pairs, rows, keys)


def attention_backward(queries, gradient, pairs, cosine, signed_sine, rows, keys, blocks):
    count = gradient.shape[0]
    per_group = QH // KVH
    scale = 1.0 / math.sqrt(HD)
    group_rows = pairs.shape[0]
    part = group_rows // blocks

    def body(queries_ref, gradient_ref, pairs_ref, cosine_ref, sine_ref, rows_ref, keys_ref, d_ref, *outs):
        block_refs, stacked = outs[:blocks], outs[blocks]
        bias = kept_bias(rows_ref[0:1, :], rows_ref[1:2, :], keys_ref[:, 0:1], keys_ref[:, 1:2])
        for k in range(KVH):
            for h in range(per_group):
                at = (k * per_group + h) * HD
                stacked[h * count : (h + 1) * count, :] = gradient_ref[:, at : at + HD]
            keys_here = pairs_ref[:, k * HD : (k + 1) * HD]
            values_here = pairs_ref[:, (KVH + k) * HD : (KVH + k + 1) * HD]
            scores = times_transposed(keys_here, queries_ref[k]) * scale + bias
            powers = jnp.exp(scores - jnp.max(scores, axis=0, keepdims=True))
            shares = powers * (1.0 / jnp.sum(powers, axis=0, keepdims=True))
            d_shares = times_transposed(values_here, stacked[...])
            dots = jnp.sum(shares * d_shares, axis=0, keepdims=True)
            d_scores = (shares * (d_shares - dots)).astype(jnp.bfloat16)
            d_keys = jnp.dot(d_scores, queries_ref[k], preferred_element_type=jnp.float32) * scale
            d_values = jnp.dot(
                shares.astype(jnp.bfloat16), stacked[...], preferred_element_type=jnp.float32
            )
            for block in range(blocks):
                cut = slice(block * part, (block + 1) * part)
                block_refs[block][:, k * HD : (k + 1) * HD] = d_keys[cut].astype(jnp.bfloat16)
                block_refs[block][:, (KVH + k) * HD : (KVH + k + 1) * HD] = d_values[cut].astype(
                    jnp.bfloat16
                )
            d_queries = transposed_times(d_scores, keys_here) * scale
            for h in range(per_group):
                at = (k * per_group + h) * HD
                field = d_queries[h * count : (h + 1) * count]
                d_ref[:, at : at + HD] = (
                    field * cosine_ref[...] - pltpu.roll(field, HD // 2, 1) * sine_ref[...]
                ).astype(jnp.bfloat16)

    return pl.pallas_call(
        body,
        out_shape=[jax.ShapeDtypeStruct((count, QH * HD), jnp.bfloat16)]
        + [jax.ShapeDtypeStruct((part, 2 * KVH * HD), jnp.bfloat16)] * blocks,
        in_specs=in_vmem(7),
        out_specs=in_vmem(1 + blocks),
        scratch_shapes=[pltpu.VMEM((per_group * count, HD), jnp.bfloat16)],
        compiler_params=pltpu.CompilerParams(vmem_limit_bytes=VMEM_LIMIT),
        cost_estimate=COST,
        name="attention_backward",
    )(queries, gradient, pairs, cosine, signed_sine, rows, keys)


def join_projected(d_queries, pair_terms, cosine, signed_sine):
    count, query_width = d_queries.shape
    pair_width = KVH * HD
    terms = len(pair_terms)

    def body(d_queries_ref, cosine_ref, sine_ref, *refs):
        term_refs, out_ref, sum_ref = refs[:terms], refs[terms], refs[terms + 1]
        out_ref[:, :query_width] = d_queries_ref[...]
        for at in range(0, 2 * pair_width, HD):
            field = total_of([term[:, at : at + HD] for term in term_refs])
            if at < pair_width:
                field = field * cosine_ref[...] - pltpu.roll(field, HD // 2, 1) * sine_ref[...]
            out_ref[:, query_width + at : query_width + at + HD] = field.astype(jnp.bfloat16)
        sum_ref[...] = jnp.sum(out_ref[...].astype(jnp.float32), axis=0, keepdims=True)

    return pl.pallas_call(
        body,
        out_shape=[
            jax.ShapeDtypeStruct((count, query_width + 2 * pair_width), jnp.bfloat16),
            jax.ShapeDtypeStruct((1, query_width + 2 * pair_width), jnp.float32),
        ],
        in_specs=in_vmem(3 + terms),
        out_specs=in_vmem(2),
        cost_estimate=COST,
        name="join_projected",
    )(d_queries, cosine, signed_sine, *pair_terms)


def on_device(
    tokens,
    segment_ids,
    first_gain,
    input_weight,
    input_bias,
    output_weight,
    second_gain,
    gate_weight,
    up_weight,
    down_weight,
    output_cotangent,
):
    bf16, f32 = jnp.bfloat16, jnp.float32
    shards, reps = lax.axis_size("shard"), lax.axis_size("rep")
    shard, core, first, second = make_lines(reps, shards)
    rep_place = (core.place * first.size + first.place) * second.size + second.place
    own_rows, width = tokens.shape
    segments = segment_ids[0]
    per_group = QH // KVH
    query_width = QH * HD
    pair_width = KVH * HD
    first_row = shard.place * own_rows
    part_rows = input_weight.shape[0] // reps
    hidden_units = gate_weight.shape[1]
    block_units = hidden_units // shards
    clock = Clock()
    z_order = jnp.stack([shard.behind(step) for step in range(shards)]).astype(jnp.int32)

    def weight_piece(weight, place):
        return pick(weight.reshape(reps, part_rows, weight.shape[1]), place, 0)

    def column_piece(weight, place):
        return weight_piece(weight, place).reshape(part_rows, shards, block_units).transpose(1, 0, 2)

    def spread(piece):
        return Spread(clock, piece, core, first, second)

    def send_rows(rows):
        return [shard.shift(row, shards - step) for step, row in enumerate(rows, 1)]

    def sends_of(blocks):
        return [pick(blocks, shard.ahead(step), 0) for step in range(shards)]

    def shift_blocks(blocks):
        return [blocks[0]] + [shard.shift(block, step) for step, block in enumerate(blocks[1:], 1)]

    def together(*groups):
        flat = clock(*[array for group in groups for array in group])
        parts, at = [], 0
        for group in groups:
            parts.append(flat[at : at + len(group)])
            at += len(group)
        return parts

    rep_index = lax.axis_index("rep")
    shard_vectors = jnp.concatenate([first_gain, second_gain, input_bias])
    vector_row = jnp.pad(shard_vectors, (0, input_weight.shape[1] - shard_vectors.shape[0]))
    input_moving = gather_line(
        jnp.concatenate([weight_piece(input_weight, rep_place), vector_row[None]], axis=0), shard
    )
    output_piece = weight_piece(output_weight, rep_index)
    gate_blocks = sends_of(column_piece(gate_weight, rep_index))
    up_blocks = sends_of(column_piece(up_weight, rep_place))
    input_rows, gate_blocks, up_blocks, (output_piece,) = together(
        input_moving, gate_blocks, up_blocks, [output_piece]
    )
    input_spread = spread(jnp.stack([rows[:part_rows] for rows in input_rows])[None])
    output_matrix = lax.all_gather(output_piece, ("shard", "rep"), axis=0, tiled=True)
    gate_moving = shift_blocks(gate_blocks)
    vector_rows = jnp.stack(in_place_order([rows[part_rows] for rows in input_rows], shard))
    own_gain = first_gain.shape[0]
    gain_one = vector_rows[:, :own_gain].reshape(width).astype(f32)
    gain_two = vector_rows[:, own_gain : 2 * own_gain].reshape(width).astype(f32)
    shift_row = (
        vector_rows[:, 2 * own_gain : shard_vectors.shape[0]].reshape(-1).astype(f32)
    )

    places = positions(segments)
    cosine_table, sine_table = rope_tables(
        lax.dynamic_slice_in_dim(places, first_row, own_rows), HD
    )
    signed_sine = jnp.concatenate(
        [-sine_table[:, : HD // 2], sine_table[:, HD // 2 :]], axis=1
    )
    own_segments = lax.dynamic_slice_in_dim(segments, first_row, own_rows)
    row_index = jnp.arange(own_rows, dtype=jnp.int32)
    key_index = jnp.concatenate([shard.behind(step) * own_rows + row_index for step in range(shards)])
    key_segments = jnp.concatenate(
        [
            lax.dynamic_slice_in_dim(segments, shard.behind(step) * own_rows, own_rows)
            for step in range(shards)
        ]
    )
    key_marks = jnp.stack([key_segments, key_index])
    row_marks = jnp.tile(jnp.stack([own_segments, first_row + row_index]), (1, per_group))
    wide_tokens = tokens.astype(f32)
    inverse_one = lax.rsqrt(jnp.mean(wide_tokens * wide_tokens, axis=-1, keepdims=True) + EPSILON)
    unit_one = wide_tokens * inverse_one
    normed_one = (unit_one * gain_one).astype(bf16)
    (
        normed_one,
        cosine_table,
        sine_table,
        signed_sine,
        key_marks,
        row_marks,
    ) = clock(normed_one, cosine_table, sine_table, signed_sine, key_marks, row_marks)

    far = list(range(2, shards - 1))
    cotangent_arrived = [output_cotangent, shard.shift(output_cotangent, 1)] + [None] * (shards - 2)
    input_spread.further()
    input_arrived, gate_rows, (cotangent_arrived[1],) = together(
        input_spread.waits(), gate_moving, cotangent_arrived[1:2]
    )
    input_spread.over(*input_arrived)
    gate_gathered = lax.all_gather(jnp.stack(gate_rows)[None, :, None], "rep", axis=0, tiled=True)
    up_moving = shift_blocks(up_blocks)
    (input_matrix,) = clock.run(place_blocks, z_order, *input_spread.finish())
    input_matrix = input_matrix.reshape(width, -1)
    projected = jnp.dot(normed_one, input_matrix, preferred_element_type=f32) + shift_row
    key_part = rotate(
        projected[:, query_width : query_width + pair_width].reshape(own_rows, KVH, HD),
        cosine_table,
        sine_table,
    )
    (own_pairs,) = clock(
        jnp.concatenate(
            [key_part.reshape(own_rows, pair_width), projected[:, query_width + pair_width :]],
            axis=1,
        ).astype(bf16)
    )
    up_rows = clock(*up_moving)
    pair_moving = gather_line(own_pairs, shard)
    up_spread = spread(jnp.stack(up_rows)[None])
    pair_rows, up_arrived = together(pair_moving, up_spread.waits())
    pairs = jnp.concatenate(pair_rows, axis=0)
    up_spread.further(*up_arrived)
    for step in far:
        cotangent_arrived[step] = shard.shift(output_cotangent, step)
    queries, attention_low = clock.run(
        attention_forward, projected, cosine_table, signed_sine, pairs, row_marks.T, key_marks
    )
    output_matrix, attention_low = clock(output_matrix, attention_low)
    hidden = wide_tokens + jnp.dot(attention_low, output_matrix, preferred_element_type=f32)
    inverse_two = lax.rsqrt(jnp.mean(hidden * hidden, axis=-1, keepdims=True) + EPSILON)
    unit_two = hidden * inverse_two
    (normed_two,) = clock((unit_two * gain_two).astype(bf16))
    normed_moving = gather_line(normed_two, shard)
    up_spread.over()
    up_arrived = clock(*up_spread.waits())
    if shards > 2:
        cotangent_arrived[-1] = shard.shift(output_cotangent, shards - 1)
    (up_matrix,) = clock.run(place_blocks, z_order, *up_spread.finish(*up_arrived))
    up_matrix = up_matrix.reshape(width, block_units)
    (gate_matrix,) = clock.run(place_gathered, z_order, gate_gathered)
    gate_matrix = gate_matrix.reshape(width, block_units)
    normed_arrived, cotangent_arrived = together(normed_moving, cotangent_arrived)
    cotangents = jnp.concatenate(cotangent_arrived, axis=0)
    group_normed = jnp.concatenate(normed_arrived, axis=0)

    inner_act, d_gate, d_up, turned_normed, turned_inner = clock.run(
        feed_forward, group_normed, cotangents, gate_matrix, up_matrix, down_weight
    )

    def start_halving(left, right, groups):
        sent, own = clock.run(
            lambda left, right: split_gradient(left, right, groups, core.place), left, right
        )
        shape = (groups, first.size, second.size, -1, right.shape[1])
        return Halving(clock, sent.reshape(shape), own.reshape(shape), core, first, second)

    def side_by_side(rows):
        return clock(jnp.concatenate(in_place_order(rows, shard), axis=1))[0]

    def sum_over_rep(blocks):
        return lax.psum_scatter(blocks, "rep", scatter_dimension=0, tiled=True)

    def row_sum(arrived):
        return clock(total_of(arrived).astype(bf16))[0]

    (down_blocks,) = clock.run(
        lambda left, right: ordered_gradient(left, right, 1, list(range(reps))),
        turned_inner,
        cotangents,
    )
    down_piece = sum_over_rep(down_blocks.reshape(block_units, width))
    normed_own, *normed_partial = clock.run(
        lambda *operands: rows_product(operands[:2], operands[2:], True, shards),
        d_gate,
        d_up,
        gate_matrix,
        up_matrix,
    )
    normed_arriving = send_rows(normed_partial)
    up = start_halving(turned_normed, d_up, shards)
    (gate_blocks,) = clock.run(
        lambda left, right: ordered_gradient(left, right, shards, rep_places(reps)),
        turned_normed,
        d_gate,
    )
    gate_piece = sum_over_rep(gate_blocks.reshape(width, block_units))
    up.along_first()
    block_own, *block_partial = clock.run(
        lambda left, right: rows_product((left,), (right,), False, shards), inner_act, down_weight
    )
    block_arrived = [None] * len(block_partial)

    def move_block(at):
        block_arrived[at] = shard.shift(block_partial[at], shards - 1 - at)

    up.along_second()

    normed_two_gradient = total_of([normed_own] + clock(*normed_arriving))
    gain_two_gradient = jnp.sum(normed_two_gradient * unit_two, axis=0)
    hidden_gradient = output_cotangent.astype(f32) + norm_back(
        normed_two_gradient, unit_two, inverse_two, gain_two
    )
    (branch_gradient,) = clock(hidden_gradient.astype(bf16))
    (attention_gradient,) = clock(times_transposed(branch_gradient, output_matrix).astype(bf16))
    d_queries, pair_own, *pair_partial = clock.run(
        lambda *operands: attention_backward(*operands, shards),
        queries,
        attention_gradient,
        pairs,
        cosine_table,
        signed_sine,
        row_marks,
        key_marks.T,
    )
    pair_arriving = send_rows(pair_partial)
    output = start_halving(clock(attention_low.T)[0], branch_gradient, shards)
    up_blocks = up.finish()
    output.along_first()
    (down_piece,) = clock(down_piece)
    down_gathered = lax.all_gather(down_piece, "rep", axis=0, tiled=True)
    pair_terms = [pair_own] + clock(*pair_arriving)
    projected_gradient, bias_sum = clock.run(
        lambda *operands: join_projected(operands[0], operands[3:], *operands[1:3]),
        d_queries,
        cosine_table,
        signed_sine,
        *pair_terms,
    )
    projected = start_halving(clock(normed_one.T)[0], projected_gradient, shards)
    up_moving = shift_blocks(clock(*sends_of(up_blocks)))
    output.along_second()
    projected.along_first()
    up_rows = clock(*up_moving)
    up_spread = spread(side_by_side(up_rows))
    move_block(0)
    output_blocks = output.finish()
    projected_gradient, hidden_gradient = clock(projected_gradient, hidden_gradient)
    normed_one_gradient = times_transposed(projected_gradient, input_matrix)
    gain_one_gradient = jnp.sum(normed_one_gradient * unit_one, axis=0)
    (tokens_gradient,) = clock(
        (
            hidden_gradient + norm_back(normed_one_gradient, unit_one, inverse_one, gain_one)
        ).astype(bf16)
    )
    bias_gradient = bias_sum[0]
    bias_split = query_width + pair_width
    small_parts = (
        gain_one_gradient,
        gain_two_gradient,
        bias_gradient[:bias_split],
        bias_gradient[bias_split:],
    )
    (small,) = clock(
        jnp.concatenate([part.reshape(shards, -1) for part in small_parts], axis=1)
    )
    projected.along_second()
    up_arrived, block_arrived[:1] = together(up_spread.waits(), block_arrived[:1])
    up_spread.further(*up_arrived)
    output_moving = shift_blocks(clock(*sends_of(output_blocks)))
    input_blocks = clock(*sends_of(projected.finish()))
    output_sum = row_sum(clock(*output_moving))
    input_moving = shift_blocks(input_blocks)
    up_spread.over()
    input_sum = row_sum(clock(*input_moving))
    input_spread = spread(input_sum)
    up_arrived = clock(*up_spread.waits())
    (gate_piece,) = clock(gate_piece)
    gate_moving = shift_blocks(
        clock(*sends_of(gate_piece.reshape(shards, part_rows, block_units)))
    )
    (up_total,) = clock.run(widen_pieces, *up_spread.finish(*up_arrived))
    input_spread.further()
    for at in range(1, len(block_partial) - 1):
        move_block(at)
    input_spread.over()
    gate_spread = spread(side_by_side(clock(*gate_moving)))
    output_spread = spread(output_sum)
    (input_total,) = clock.run(widen_pieces, *input_spread.finish())
    block_arrived[1:-1] = clock(*block_arrived[1:-1])
    output_spread.further()
    gate_spread.further()
    move_block(len(block_partial) - 1)
    output_spread.over()
    for line in (core, first, second):
        small = total_of(
            [small] + clock(*[line.shift(small, step) for step in range(1, line.size)])
        )
    small_moving = shift_blocks(clock(*sends_of(small)))
    gate_spread.over()
    small = total_of(clock(*small_moving))
    (output_total,) = clock.run(widen_pieces, *output_spread.finish())
    down_total = clock(clock(down_gathered)[0].astype(f32))[0]
    (block_out,) = clock(total_of([hidden, block_own] + clock(*block_arrived)).astype(bf16))
    (gate_total,) = clock.run(widen_pieces, *gate_spread.finish())

    small = small + clock.token[0, 0]
    small_totals, at = [], 0
    for part in small_parts:
        size = part.shape[0] // shards
        small_totals.append(small[at : at + size])
        at += size
    return (
        block_out,
        tokens_gradient,
        small_totals[0],
        input_total,
        small_totals[2],
        small_totals[3],
        output_total,
        small_totals[1],
        gate_total,
        up_total,
        down_total,
    )


def solution(mesh):
    placed = (
        P(("rep", "shard"), None),
        P("rep", None),
        P("shard"),
        P("shard", None),
        P("shard"),
        P("shard", None),
        P("shard"),
        P("shard", None),
        P("shard", None),
        P("shard", None),
        P(("rep", "shard"), None),
    )
    return jax.shard_map(
        on_device,
        mesh=mesh,
        in_specs=placed,
        out_specs=(
            P(("rep", "shard"), None),
            P(("rep", "shard"), None),
            P("shard"),
            P("shard", None),
            P("shard"),
            P("shard"),
            P("shard", None),
            P("shard"),
            P("shard", None),
            P("shard", None),
            P("shard", None),
        ),
        check_vma=False,
    )
```

```python
import math

import jax
import jax.numpy as jnp
from jax import lax
from jax.experimental import pallas as pl
from jax.experimental.pallas import tpu as pltpu
from jax.sharding import PartitionSpec as P

QH = 12
KVH = 2
HD = 128
SEQS = 3


EPSILON = 1e-06
LOG_THETA = math.log(1000000.0)
MASKED = -1e30
VMEM_LIMIT = 56 * 1024 * 1024
TILE = 512
COST = pl.CostEstimate(flops=1, bytes_accessed=1, transcendentals=0)


def rope_tables(places, head_width):
    half_width = head_width // 2
    frequency = jnp.exp(jnp.arange(half_width, dtype=jnp.float32) * (-2.0 * LOG_THETA / head_width))
    angles = places.astype(jnp.float32)[:, None] * frequency[None, :]
    angles = jnp.concatenate([angles, angles], axis=-1)
    return (jnp.cos(angles), jnp.sin(angles))


def positions(segments):
    labels = jnp.arange(SEQS, dtype=jnp.int32)
    starts = jnp.sum((segments[None, :] < labels[:, None]).astype(jnp.int32), axis=1)
    own_start = jnp.sum(jnp.where(segments[:, None] == labels[None, :], starts[None, :], 0), axis=1)
    return jnp.arange(segments.shape[0], dtype=jnp.int32) - own_start


def rotate(field_rows, cosine_table, sine_table):
    half_width = field_rows.shape[-1] // 2
    turned = jnp.concatenate([-field_rows[..., half_width:], field_rows[..., :half_width]], axis=-1)
    return field_rows * cosine_table[:, None, :] + turned * sine_table[:, None, :]


def transposed_times(left_side, right_side):
    return lax.dot_general(
        left_side, right_side, (((0,), (0,)), ((), ())), preferred_element_type=jnp.float32
    )


def times_transposed(left_side, right_side):
    return lax.dot_general(
        left_side, right_side, (((1,), (1,)), ((), ())), preferred_element_type=jnp.float32
    )


def norm_back(normed_gradient, unit_rows, inverse_rms, gain_row):
    scaled = normed_gradient * gain_row
    return inverse_rms * (scaled - unit_rows * jnp.mean(scaled * unit_rows, axis=-1, keepdims=True))


class Line:
    def __init__(self, name, size, place, pairs, crossed=False):
        self.name, self.size, self.place, self.pairs = name, size, place, pairs
        self.crossed = crossed

    def shift(self, value, step):
        return lax.ppermute(value, self.name, self.pairs(step % self.size))

    def behind(self, step):
        return lax.rem(self.place + (self.size - step % self.size), self.size)

    def ahead(self, step):
        return lax.rem(self.place + step % self.size, self.size) if step else self.place


def make_lines(reps, shards):
    inner = 2 if reps % 4 == 0 else 1
    outer = reps // (2 * inner)
    square = inner == outer

    def split(index):
        core, b, a = index % 2, (index // 2) % inner, index // (2 * inner)
        return core, b, a

    def join(core, b, a):
        return (a * inner + b) * 2 + core

    def first_pairs(step):
        pairs = []
        for index in range(reps):
            core, b, a = split(index)
            if square and core == 0:
                pairs.append((index, join(core, (b + step) % inner, a)))
            else:
                pairs.append((index, join(core, b, (a + step) % outer)))
        return pairs

    def second_pairs(step):
        pairs = []
        for index in range(reps):
            core, b, a = split(index)
            if square and core == 0:
                pairs.append((index, join(core, b, (a + step) % outer)))
            else:
                pairs.append((index, join(core, (b + step) % inner, a)))
        return pairs

    def core_pairs(step):
        pairs = []
        for index in range(reps):
            core, b, a = split(index)
            pairs.append((index, join((core + step) % 2, b, a)))
        return pairs

    def shard_pairs(step):
        return [(index, (index + step) % shards) for index in range(shards)]

    core, b, a = split(lax.axis_index("rep"))
    first, second = (jnp.where(core == 0, b, a), jnp.where(core == 0, a, b)) if square else (a, b)
    return (
        Line("shard", shards, lax.axis_index("shard"), shard_pairs),
        Line("rep", 2, core, core_pairs, square),
        Line("rep", outer, first, first_pairs),
        Line("rep", inner, second, second_pairs),
    )


def rep_places(reps):
    inner = 2 if reps % 4 == 0 else 1
    outer = reps // (2 * inner)
    places = []
    for index in range(reps):
        core, b, a = index % 2, (index // 2) % inner, index // (2 * inner)
        one, two = (b, a) if inner == outer and core == 0 else (a, b)
        places.append((core * outer + one) * inner + two)
    return places


def pick(array, index, axis):
    return lax.dynamic_index_in_dim(array, index, axis, keepdims=False)


def put(array, piece, index, axis):
    return lax.dynamic_update_index_in_dim(array, piece, index, axis)


def in_place_order(pieces, line):
    ordered = []
    for place in range(line.size):
        chosen = pieces[0]
        for step in range(1, line.size):
            chosen = jnp.where(line.behind(step) == place, pieces[step], chosen)
        ordered.append(chosen)
    return ordered


def tie(*arrays):
    return lax.optimization_barrier(arrays)


def gather_line(value, line):
    return [value] + [line.shift(value, step) for step in range(1, line.size)]


class Clock:
    def __init__(self):
        self.token = jnp.zeros((8, 128), jnp.float32)
        self.open = 0

    def __call__(self, *arrays):
        self.token, *arrays = tie(self.token, *arrays)
        return arrays

    def run(self, step, *arrays):
        return self(*step(*self(*arrays)))

    def send(self, line, values, steps):
        self.open += len(values)
        return [line.shift(value, step) for value, step in zip(self(*values), steps)]

    def wait(self, *groups):
        flat = self(*[array for group in groups for array in group])
        self.open -= len(flat)
        parts, at = [], 0
        for group in groups:
            parts.append(flat[at : at + len(group)])
            at += len(group)
        return parts


def total_of(terms):
    total = terms[0].astype(jnp.float32)
    for term in terms[1:]:
        total = total + term.astype(jnp.float32)
    return total


class Halving:
    def __init__(self, clock, sent, own, core, first, second):
        self.clock, self.first, self.second = clock, first, second
        self.terms = [own]
        self.moving = clock.send(core, [sent], [1])

    def along(self, line):
        (arrived,) = self.clock.wait(self.moving)
        self.terms = self.terms + arrived
        steps = range(1, line.size)
        blocks = [
            total_of([pick(term, line.ahead(step), 1) for term in self.terms]).astype(jnp.bfloat16)
            for step in steps
        ]
        self.moving = self.clock.send(line, blocks, steps)
        self.terms = [pick(term, line.place, 1) for term in self.terms]

    def along_first(self):
        self.along(self.first)

    def along_second(self):
        self.along(self.second)

    def finish(self):
        (arrived,) = self.clock.wait(self.moving)
        return self.clock(total_of(self.terms + arrived).astype(jnp.bfloat16))[0]


class Spread:
    def __init__(self, clock, piece, core, first, second):
        self.clock, self.lines = clock, (core, first, second)
        self.pieces = [piece]
        self.moving = clock.send(second, [piece], range(1, 2)) if second.size == 2 else []

    def further(self):
        core, first, second = self.lines
        if self.moving:
            (arrived,) = self.clock.wait(self.moving)
            self.pieces = self.pieces + arrived
        steps = range(1, first.size)
        self.moving = self.clock.send(first, [jnp.stack(self.pieces)] * len(steps), steps)

    def over(self):
        core, first, second = self.lines
        (arrived,) = self.clock.wait(self.moving)
        rows = [jnp.stack(self.pieces)] + arrived
        self.pieces = jnp.concatenate(rows, axis=0)
        self.moving = self.clock.send(core, [self.pieces], [1])

    def finish(self):
        core, first, second = self.lines
        ((others,),) = self.clock.wait(self.moving)
        offsets = [(one, two) for one in range(first.size) for two in range(second.size)]
        placed = [(core.place, first.behind(one), second.behind(two)) for one, two in offsets]
        far, near = (second, first) if core.crossed else (first, second)
        placed += [(core.behind(1), far.behind(one), near.behind(two)) for one, two in offsets]
        places = [(c * first.size + f) * second.size + s for c, f, s in placed]
        return [jnp.stack(places).astype(jnp.int32), self.pieces, others]


def place_blocks(order, places, pieces, others):
    half, groups, shards = pieces.shape[:3]

    def body(order_ref, places_ref, pieces_ref, others_ref, *rest):
        def source_of(g, k, r):
            return (pieces_ref if r < half else others_ref).at[r % half, g, k]

        move_blocks(source_of, lambda r: places_ref[r], order_ref, rest[:groups], *rest[groups:])

    return blocks_call(body, 2, 2, groups, shards, 2 * half, pieces.shape[3:])(
        order, places, pieces, others
    )


def place_gathered(order, gathered):
    reps, shards, groups = gathered.shape[:3]

    def body(order_ref, source, *rest):
        move_blocks(
            lambda g, k, r: source.at[r, k, g], lambda r: r, order_ref, rest[:groups], *rest[groups:]
        )

    return blocks_call(body, 1, 1, groups, shards, reps, gathered.shape[3:])(order, gathered)


def move_blocks(source_of, place_of, order_ref, outs, held, in_sems, out_sems):
    groups, shards, reps = in_sems.shape
    slabs = [(g, k) for g in range(groups) for k in range(shards)]

    def load(g, k, r):
        return pltpu.make_async_copy(
            source_of(g, k, r), held.at[g, k, place_of(r)], in_sems.at[g, k, r]
        )

    def store(g, k):
        return pltpu.make_async_copy(held.at[g, k], outs[g].at[order_ref[k]], out_sems.at[g, k])

    for g, k in slabs:
        for r in range(reps):
            load(g, k, r).start()
    for g, k in slabs:
        for r in range(reps):
            load(g, k, r).wait()
        store(g, k).start()
    for g, k in slabs:
        store(g, k).wait()


def blocks_call(body, scalars, sources, groups, shards, reps, block):
    whole = (shards, reps) + block
    return pl.pallas_call(
        body,
        out_shape=[jax.ShapeDtypeStruct(whole, jnp.bfloat16)] * groups,
        in_specs=[pl.BlockSpec(memory_space=pltpu.SMEM)] * scalars
        + [pl.BlockSpec(memory_space=pl.ANY)] * sources,
        out_specs=[pl.BlockSpec(memory_space=pl.ANY)] * groups,
        scratch_shapes=[
            pltpu.VMEM((groups,) + whole, jnp.bfloat16),
            pltpu.SemaphoreType.DMA((groups, shards, reps)),
            pltpu.SemaphoreType.DMA((groups, shards)),
        ],
        compiler_params=pltpu.CompilerParams(vmem_limit_bytes=VMEM_LIMIT),
        cost_estimate=COST,
        name="place_blocks",
    )


def widen_pieces(places, pieces, others):
    half, rows, columns = pieces.shape
    reps = 2 * half
    strip = next(size for size in (16, 8, rows) if rows % size == 0)

    def body(places_ref, pieces_ref, others_ref, out_ref, narrow, wide, in_sems, out_sems):
        loads = [
            pltpu.make_async_copy(
                (pieces_ref if r < half else others_ref).at[r % half], narrow.at[r], in_sems.at[r]
            )
            for r in range(reps)
        ]
        stores = [
            pltpu.make_async_copy(wide.at[r], out_ref.at[places_ref[r]], out_sems.at[r])
            for r in range(reps)
        ]
        for load in loads:
            load.start()
        for r in range(reps):
            loads[r].wait()

            def convert(at, carry):
                cut = pl.ds(pl.multiple_of(at * strip, strip), strip)
                wide[r, cut, :] = narrow[r, cut, :].astype(jnp.float32)
                return carry

            lax.fori_loop(0, rows // strip, convert, 0)
            stores[r].start()
        for store in stores:
            store.wait()

    result = pl.pallas_call(
        body,
        out_shape=jax.ShapeDtypeStruct((reps, rows, columns), jnp.float32),
        in_specs=[pl.BlockSpec(memory_space=pltpu.SMEM)]
        + [pl.BlockSpec(memory_space=pl.ANY)] * 2,
        out_specs=pl.BlockSpec(memory_space=pl.ANY),
        scratch_shapes=[
            pltpu.VMEM((reps, rows, columns), jnp.bfloat16),
            pltpu.VMEM((reps, rows, columns), jnp.float32),
            pltpu.SemaphoreType.DMA((reps,)),
            pltpu.SemaphoreType.DMA((reps,)),
        ],
        compiler_params=pltpu.CompilerParams(vmem_limit_bytes=VMEM_LIMIT),
        cost_estimate=COST,
        name="widen_pieces",
    )(places, pieces, others)
    return (result.reshape(reps * rows, columns),)


def resident(shape):
    return pl.BlockSpec(shape, lambda i: (0, 0), pipeline_mode=pl.Buffered(1))


def feed_forward(rows, cotangents, gate_matrix, up_matrix, down_matrix):
    count, width = rows.shape
    units = gate_matrix.shape[1]
    steps = pl.cdiv(units, TILE)
    slabs = next(size for size in range(min(steps, width // 128), 0, -1) if width % (128 * size) == 0)
    slab = width // slabs

    def body(
        rows_ref,
        cotangents_ref,
        gate_ref,
        up_ref,
        down_ref,
        inner_ref,
        d_gate_ref,
        d_up_ref,
        turned_rows_ref,
        turned_inner_ref,
    ):
        gate = jnp.dot(rows_ref[...], gate_ref[...], preferred_element_type=jnp.float32)
        up = jnp.dot(rows_ref[...], up_ref[...], preferred_element_type=jnp.float32)
        sigmoid = jax.nn.sigmoid(gate)
        silu = gate * sigmoid
        inner = (silu * up).astype(jnp.bfloat16)
        inner_ref[...] = inner
        turned_inner_ref[...] = inner.T
        d_inner = times_transposed(cotangents_ref[...], down_ref[...])
        d_up_ref[...] = (d_inner * silu).astype(jnp.bfloat16)
        d_gate_ref[...] = (d_inner * up * sigmoid * (1.0 + gate * (1.0 - sigmoid))).astype(
            jnp.bfloat16
        )
        for step in range(slabs):

            @pl.when(pl.program_id(0) == step)
            def turn():
                turned_rows_ref[...] = rows_ref[:, step * slab : (step + 1) * slab].T

    columns = pl.BlockSpec((width, TILE), lambda i: (0, i))
    results = pl.BlockSpec((count, TILE), lambda i: (0, i))
    return pl.pallas_call(
        body,
        grid=(steps,),
        out_shape=[jax.ShapeDtypeStruct((count, units), jnp.bfloat16)] * 3
        + [
            jax.ShapeDtypeStruct((width, count), jnp.bfloat16),
            jax.ShapeDtypeStruct((units, count), jnp.bfloat16),
        ],
        in_specs=[
            resident((count, width)),
            resident((count, width)),
            columns,
            columns,
            pl.BlockSpec((TILE, width), lambda i: (i, 0)),
        ],
        out_specs=[results] * 3
        + [
            pl.BlockSpec((slab, count), lambda i: (jnp.minimum(i, slabs - 1), 0)),
            pl.BlockSpec((TILE, count), lambda i: (i, 0)),
        ],
        compiler_params=pltpu.CompilerParams(vmem_limit_bytes=VMEM_LIMIT),
        cost_estimate=COST,
        name="feed_forward",
    )(rows, cotangents, gate_matrix, up_matrix, down_matrix)


def split_gradient(left, right, groups, core_place, turned):
    rows, count = left.shape if turned else left.shape[::-1]
    columns = right.shape[1]
    half = rows // (2 * groups)

    def body(core_ref, left_ref, right_ref, other_ref, own_ref, *scratch):
        if turned:
            rows_ref = left_ref
        else:
            (rows_ref,) = scratch

            @pl.when(pl.program_id(0) == 0)
            def turn():
                rows_ref[...] = left_ref[...].T

        core = core_ref[0]
        for out_ref, which in ((other_ref, 1 - core), (own_ref, core)):
            halves = [
                rows_ref[pl.ds(pl.multiple_of((2 * group + which) * half, 16), half), :]
                for group in range(groups)
            ]
            product = jnp.dot(
                jnp.concatenate(halves, axis=0), right_ref[...], preferred_element_type=jnp.float32
            )
            for group in range(groups):
                out_ref[group] = product[group * half : (group + 1) * half].astype(jnp.bfloat16)

    return pl.pallas_call(
        body,
        grid=(pl.cdiv(columns, TILE),),
        out_shape=[jax.ShapeDtypeStruct((groups, half, columns), jnp.bfloat16)] * 2,
        in_specs=[
            pl.BlockSpec(memory_space=pltpu.SMEM),
            resident(left.shape),
            pl.BlockSpec((count, TILE), lambda i: (0, i)),
        ],
        out_specs=[pl.BlockSpec((groups, half, TILE), lambda i: (0, 0, i))] * 2,
        scratch_shapes=[] if turned else [pltpu.VMEM((rows, count), jnp.bfloat16)],
        compiler_params=pltpu.CompilerParams(vmem_limit_bytes=VMEM_LIMIT),
        cost_estimate=COST,
        name="split_gradient",
    )(core_place.reshape(1).astype(jnp.int32), left, right)


def ordered_gradient(left, right, shards, order):
    reps = len(order)
    rows, count = left.shape
    columns = right.shape[1]
    part = rows // (shards * reps)

    def body(left_ref, right_ref, out_ref):
        product = jnp.dot(left_ref[...], right_ref[...], preferred_element_type=jnp.float32)
        for z in range(shards):
            for r in range(reps):
                at = (z * reps + order[r]) * part
                out_ref[r, z] = product[at : at + part].astype(jnp.bfloat16)

    return pl.pallas_call(
        body,
        grid=(pl.cdiv(columns, TILE),),
        out_shape=[jax.ShapeDtypeStruct((reps, shards, part, columns), jnp.bfloat16)],
        in_specs=[
            resident((rows, count)),
            pl.BlockSpec((count, TILE), lambda i: (0, i)),
        ],
        out_specs=[pl.BlockSpec((reps, shards, part, TILE), lambda i: (0, 0, 0, i))],
        compiler_params=pltpu.CompilerParams(vmem_limit_bytes=VMEM_LIMIT),
        cost_estimate=COST,
        name="ordered_gradient",
    )(left, right)


def rows_product(lefts, rights, turned, blocks):
    count, depth = lefts[0].shape
    columns = rights[0].shape[0 if turned else 1]
    pairs, part = len(lefts), count // blocks

    def body(*refs):
        total = None
        for left_ref, right_ref in zip(refs[:pairs], refs[pairs : 2 * pairs]):
            if turned:
                product = times_transposed(left_ref[...], right_ref[...])
            else:
                product = jnp.dot(
                    left_ref[...], right_ref[...], preferred_element_type=jnp.float32
                )
            total = product if total is None else total + product
        for block in range(blocks):
            refs[2 * pairs + block][...] = total[block * part : (block + 1) * part].astype(
                jnp.bfloat16
            )

    right_spec = (
        pl.BlockSpec((TILE, depth), lambda i: (i, 0))
        if turned
        else pl.BlockSpec((depth, TILE), lambda i: (0, i))
    )
    return pl.pallas_call(
        body,
        grid=(pl.cdiv(columns, TILE),),
        out_shape=[jax.ShapeDtypeStruct((part, columns), jnp.bfloat16)] * blocks,
        in_specs=[resident((count, depth))] * pairs + [right_spec] * pairs,
        out_specs=[pl.BlockSpec((part, TILE), lambda i: (0, i))] * blocks,
        compiler_params=pltpu.CompilerParams(vmem_limit_bytes=VMEM_LIMIT),
        cost_estimate=COST,
        name="rows_product",
    )(*lefts, *rights)


def kept_bias(row_segments, row_index, key_segments, key_index):
    kept = (row_segments == key_segments) & (key_index <= row_index)
    return jnp.where(kept, 0.0, MASKED)


def in_vmem(count):
    return [pl.BlockSpec(memory_space=pltpu.VMEM)] * count


def attention_forward(projected, cosine, signed_sine, pairs, rows, keys):
    count = projected.shape[0]
    per_group = QH // KVH
    scale = 1.0 / math.sqrt(HD)
    shape = (KVH, per_group * count, HD)

    def body(projected_ref, cosine_ref, sine_ref, pairs_ref, rows_ref, keys_ref, queries_ref, out_ref):
        bias = kept_bias(rows_ref[:, 0:1], rows_ref[:, 1:2], keys_ref[0:1, :], keys_ref[1:2, :])
        for k in range(KVH):
            for h in range(per_group):
                at = (k * per_group + h) * HD
                field = projected_ref[:, at : at + HD]
                queries_ref[k, h * count : (h + 1) * count, :] = (
                    field * cosine_ref[...] + pltpu.roll(field, HD // 2, 1) * sine_ref[...]
                ).astype(jnp.bfloat16)
            keys_here = pairs_ref[:, k * HD : (k + 1) * HD]
            values_here = pairs_ref[:, (KVH + k) * HD : (KVH + k + 1) * HD]
            scores = times_transposed(queries_ref[k], keys_here) * scale + bias
            powers = jnp.exp(scores - jnp.max(scores, axis=1, keepdims=True))
            shares = powers * (1.0 / jnp.sum(powers, axis=1, keepdims=True))
            result = jnp.dot(
                shares.astype(jnp.bfloat16), values_here, preferred_element_type=jnp.float32
            ).astype(jnp.bfloat16)
            for h in range(per_group):
                at = (k * per_group + h) * HD
                out_ref[:, at : at + HD] = result[h * count : (h + 1) * count]

    return pl.pallas_call(
        body,
        out_shape=[
            jax.ShapeDtypeStruct(shape, jnp.bfloat16),
            jax.ShapeDtypeStruct((count, QH * HD), jnp.bfloat16),
        ],
        in_specs=in_vmem(6),
        out_specs=in_vmem(2),
        compiler_params=pltpu.CompilerParams(vmem_limit_bytes=VMEM_LIMIT),
        cost_estimate=COST,
        name="attention_forward",
    )(projected, cosine, signed_sine, pairs, rows, keys)


def attention_backward(queries, gradient, pairs, cosine, signed_sine, rows, keys, blocks):
    count = gradient.shape[0]
    per_group = QH // KVH
    scale = 1.0 / math.sqrt(HD)
    group_rows = pairs.shape[0]
    part = group_rows // blocks

    def body(queries_ref, gradient_ref, pairs_ref, cosine_ref, sine_ref, rows_ref, keys_ref, d_ref, *outs):
        block_refs, stacked = outs[:blocks], outs[blocks]
        bias = kept_bias(rows_ref[0:1, :], rows_ref[1:2, :], keys_ref[:, 0:1], keys_ref[:, 1:2])
        for k in range(KVH):
            for h in range(per_group):
                at = (k * per_group + h) * HD
                stacked[h * count : (h + 1) * count, :] = gradient_ref[:, at : at + HD]
            keys_here = pairs_ref[:, k * HD : (k + 1) * HD]
            values_here = pairs_ref[:, (KVH + k) * HD : (KVH + k + 1) * HD]
            scores = times_transposed(keys_here, queries_ref[k]) * scale + bias
            powers = jnp.exp(scores - jnp.max(scores, axis=0, keepdims=True))
            shares = powers * (1.0 / jnp.sum(powers, axis=0, keepdims=True))
            d_shares = times_transposed(values_here, stacked[...])
            dots = jnp.sum(shares * d_shares, axis=0, keepdims=True)
            d_scores = (shares * (d_shares - dots)).astype(jnp.bfloat16)
            d_keys = jnp.dot(d_scores, queries_ref[k], preferred_element_type=jnp.float32) * scale
            d_values = jnp.dot(
                shares.astype(jnp.bfloat16), stacked[...], preferred_element_type=jnp.float32
            )
            for block in range(blocks):
                cut = slice(block * part, (block + 1) * part)
                block_refs[block][:, k * HD : (k + 1) * HD] = d_keys[cut].astype(jnp.bfloat16)
                block_refs[block][:, (KVH + k) * HD : (KVH + k + 1) * HD] = d_values[cut].astype(
                    jnp.bfloat16
                )
            d_queries = transposed_times(d_scores, keys_here) * scale
            for h in range(per_group):
                at = (k * per_group + h) * HD
                field = d_queries[h * count : (h + 1) * count]
                d_ref[:, at : at + HD] = (
                    field * cosine_ref[...] - pltpu.roll(field, HD // 2, 1) * sine_ref[...]
                ).astype(jnp.bfloat16)

    return pl.pallas_call(
        body,
        out_shape=[jax.ShapeDtypeStruct((count, QH * HD), jnp.bfloat16)]
        + [jax.ShapeDtypeStruct((part, 2 * KVH * HD), jnp.bfloat16)] * blocks,
        in_specs=in_vmem(7),
        out_specs=in_vmem(1 + blocks),
        scratch_shapes=[pltpu.VMEM((per_group * count, HD), jnp.bfloat16)],
        compiler_params=pltpu.CompilerParams(vmem_limit_bytes=VMEM_LIMIT),
        cost_estimate=COST,
        name="attention_backward",
    )(queries, gradient, pairs, cosine, signed_sine, rows, keys)


def join_projected(d_queries, pair_terms, cosine, signed_sine):
    count, query_width = d_queries.shape
    pair_width = KVH * HD
    terms = len(pair_terms)

    def body(d_queries_ref, cosine_ref, sine_ref, *refs):
        term_refs, out_ref, sum_ref = refs[:terms], refs[terms], refs[terms + 1]
        out_ref[:, :query_width] = d_queries_ref[...]
        for at in range(0, 2 * pair_width, HD):
            field = total_of([term[:, at : at + HD] for term in term_refs])
            if at < pair_width:
                field = field * cosine_ref[...] - pltpu.roll(field, HD // 2, 1) * sine_ref[...]
            out_ref[:, query_width + at : query_width + at + HD] = field.astype(jnp.bfloat16)
        sum_ref[...] = jnp.sum(out_ref[...].astype(jnp.float32), axis=0, keepdims=True)

    return pl.pallas_call(
        body,
        out_shape=[
            jax.ShapeDtypeStruct((count, query_width + 2 * pair_width), jnp.bfloat16),
            jax.ShapeDtypeStruct((1, query_width + 2 * pair_width), jnp.float32),
        ],
        in_specs=in_vmem(3 + terms),
        out_specs=in_vmem(2),
        cost_estimate=COST,
        name="join_projected",
    )(d_queries, cosine, signed_sine, *pair_terms)


def on_device(
    tokens,
    segment_ids,
    first_gain,
    input_weight,
    input_bias,
    output_weight,
    second_gain,
    gate_weight,
    up_weight,
    down_weight,
    output_cotangent,
):
    bf16, f32 = jnp.bfloat16, jnp.float32
    shards, reps = lax.axis_size("shard"), lax.axis_size("rep")
    shard, core, first, second = make_lines(reps, shards)
    rep_place = (core.place * first.size + first.place) * second.size + second.place
    own_rows, width = tokens.shape
    segments = segment_ids[0]
    per_group = QH // KVH
    query_width = QH * HD
    pair_width = KVH * HD
    first_row = shard.place * own_rows
    part_rows = input_weight.shape[0] // reps
    hidden_units = gate_weight.shape[1]
    block_units = hidden_units // shards
    clock = Clock()
    z_order = jnp.stack([shard.behind(step) for step in range(shards)]).astype(jnp.int32)

    def weight_piece(weight, place):
        return pick(weight.reshape(reps, part_rows, weight.shape[1]), place, 0)

    def column_piece(weight, place):
        return weight_piece(weight, place).reshape(part_rows, shards, block_units).transpose(1, 0, 2)

    def spread(piece):
        return Spread(clock, piece, core, first, second)

    def blocks_of(blocks):
        return [pick(blocks, shard.ahead(step), 0) for step in range(shards)]

    steps = range(1, shards)

    def send_blocks(blocks):
        return clock.send(shard, blocks[1:], steps)

    def send_around(value):
        return clock.send(shard, [value] * len(steps), steps)

    def send_back(rows):
        return clock.send(shard, rows, [shards - step for step in steps])

    rep_index = lax.axis_index("rep")
    shard_vectors = jnp.concatenate([first_gain, second_gain, input_bias])
    vector_row = jnp.pad(shard_vectors, (0, input_weight.shape[1] - shard_vectors.shape[0]))
    own_input = jnp.concatenate([weight_piece(input_weight, rep_place), vector_row[None]], axis=0)
    input_moving = send_around(own_input)
    output_piece, *gate_blocks = clock(
        weight_piece(output_weight, rep_index), *blocks_of(column_piece(gate_weight, rep_index))
    )
    up_blocks = clock(*blocks_of(column_piece(up_weight, rep_place)))
    (input_rows,) = clock.wait(input_moving)
    input_rows = [own_input] + input_rows
    input_spread = spread(jnp.stack([rows[:part_rows] for rows in input_rows])[None])
    output_matrix = lax.all_gather(clock(output_piece)[0], ("shard", "rep"), axis=0, tiled=True)
    gate_moving = send_blocks(gate_blocks)

    vector_rows = jnp.stack(in_place_order([rows[part_rows] for rows in input_rows], shard))
    own_gain = first_gain.shape[0]
    gain_one = vector_rows[:, :own_gain].reshape(width).astype(f32)
    gain_two = vector_rows[:, own_gain : 2 * own_gain].reshape(width).astype(f32)
    shift_row = (
        vector_rows[:, 2 * own_gain : shard_vectors.shape[0]].reshape(-1).astype(f32)
    )
    places = positions(segments)
    cosine_table, sine_table = rope_tables(
        lax.dynamic_slice_in_dim(places, first_row, own_rows), HD
    )
    signed_sine = jnp.concatenate(
        [-sine_table[:, : HD // 2], sine_table[:, HD // 2 :]], axis=1
    )
    own_segments = lax.dynamic_slice_in_dim(segments, first_row, own_rows)
    row_index = jnp.arange(own_rows, dtype=jnp.int32)
    key_index = jnp.concatenate([shard.behind(step) * own_rows + row_index for step in range(shards)])
    key_segments = jnp.concatenate(
        [
            lax.dynamic_slice_in_dim(segments, shard.behind(step) * own_rows, own_rows)
            for step in range(shards)
        ]
    )
    key_marks = jnp.stack([key_segments, key_index])
    row_marks = jnp.tile(jnp.stack([own_segments, first_row + row_index]), (1, per_group))
    wide_tokens = tokens.astype(f32)
    inverse_one = lax.rsqrt(jnp.mean(wide_tokens * wide_tokens, axis=-1, keepdims=True) + EPSILON)
    unit_one = wide_tokens * inverse_one
    normed_one = (unit_one * gain_one).astype(bf16)
    (
        normed_one,
        cosine_table,
        sine_table,
        signed_sine,
        key_marks,
        row_marks,
    ) = clock(normed_one, cosine_table, sine_table, signed_sine, key_marks, row_marks)

    input_spread.further()
    (gate_rows,) = clock.wait(gate_moving)
    gate_gathered = lax.all_gather(
        clock(jnp.stack(gate_blocks[:1] + gate_rows))[0][None, :, None], "rep", axis=0, tiled=True
    )
    up_moving = send_blocks(up_blocks)
    input_spread.over()
    (input_matrix,) = clock.run(place_blocks, z_order, *input_spread.finish())
    input_matrix = input_matrix.reshape(width, -1)
    projected = jnp.dot(normed_one, input_matrix, preferred_element_type=f32) + shift_row
    key_part = rotate(
        projected[:, query_width : query_width + pair_width].reshape(own_rows, KVH, HD),
        cosine_table,
        sine_table,
    )
    (own_pairs,) = clock(
        jnp.concatenate(
            [key_part.reshape(own_rows, pair_width), projected[:, query_width + pair_width :]],
            axis=1,
        ).astype(bf16)
    )
    (up_rows,) = clock.wait(up_moving)
    pair_moving = send_around(own_pairs)
    up_spread = spread(jnp.stack(up_blocks[:1] + up_rows)[None])
    (pair_rows,) = clock.wait(pair_moving)
    pairs = jnp.concatenate([own_pairs] + pair_rows, axis=0)
    far = list(range(2, shards - 1))
    near = sorted({1, shards - 1})
    far_moving = clock.send(shard, [output_cotangent] * len(far), far)
    up_spread.further()
    queries, attention_low = clock.run(
        attention_forward, projected, cosine_table, signed_sine, pairs, row_marks.T, key_marks
    )
    output_matrix, attention_low = clock(output_matrix, attention_low)
    hidden = wide_tokens + jnp.dot(attention_low, output_matrix, preferred_element_type=f32)
    inverse_two = lax.rsqrt(jnp.mean(hidden * hidden, axis=-1, keepdims=True) + EPSILON)
    unit_two = hidden * inverse_two
    (normed_two,) = clock((unit_two * gain_two).astype(bf16))
    normed_moving = send_around(normed_two)
    up_spread.over()
    (far_arrived,) = clock.wait(far_moving)
    near_moving = clock.send(shard, [output_cotangent] * (len(near) - 1), near[1:])
    (up_matrix,) = clock.run(place_blocks, z_order, *up_spread.finish())
    near_moving = clock.send(shard, [output_cotangent], near[:1]) + near_moving
    up_matrix = up_matrix.reshape(width, block_units)
    (gate_matrix,) = clock.run(place_gathered, z_order, gate_gathered)
    gate_matrix = gate_matrix.reshape(width, block_units)
    normed_arrived, near_arrived = clock.wait(normed_moving, near_moving)
    group_normed = jnp.concatenate([normed_two] + normed_arrived, axis=0)
    cotangent_arrived = dict(zip(near + far, near_arrived + far_arrived))
    cotangents = jnp.concatenate(
        [output_cotangent] + [cotangent_arrived[step] for step in steps], axis=0
    )

    inner_act, d_gate, d_up, turned_normed, turned_inner = clock.run(
        feed_forward, group_normed, cotangents, gate_matrix, up_matrix, down_weight
    )

    def start_halving(left, right, groups, turned):
        sent, own = clock.run(
            lambda left, right: split_gradient(left, right, groups, core.place, turned),
            left,
            right,
        )
        shape = (groups, first.size, second.size, -1, right.shape[1])
        return Halving(clock, sent.reshape(shape), own.reshape(shape), core, first, second)

    def side_by_side(rows):
        return clock(jnp.concatenate(in_place_order(rows, shard), axis=1))[0]

    def sum_over_rep(blocks):
        return lax.psum_scatter(blocks, "rep", scatter_dimension=0, tiled=True)

    (down_blocks,) = clock.run(
        lambda left, right: ordered_gradient(left, right, 1, list(range(reps))),
        turned_inner,
        cotangents,
    )
    down_piece = sum_over_rep(down_blocks.reshape(block_units, width))
    normed_own, *normed_partial = clock.run(
        lambda *operands: rows_product(operands[:2], operands[2:], True, shards),
        d_gate,
        d_up,
        gate_matrix,
        up_matrix,
    )
    normed_moving = send_back(normed_partial)
    up = start_halving(turned_normed, d_up, shards, True)
    (gate_blocks,) = clock.run(
        lambda left, right: ordered_gradient(left, right, shards, rep_places(reps)),
        turned_normed,
        d_gate,
    )
    gate_piece = sum_over_rep(gate_blocks.reshape(width, block_units))
    up.along_first()
    block_own, *block_partial = clock.run(
        lambda left, right: rows_product((left,), (right,), False, shards), inner_act, down_weight
    )

    def send_block(at):
        return clock.send(shard, [block_partial[at]], [shards - 1 - at])

    up.along_second()
    (normed_arrived,) = clock.wait(normed_moving)
    normed_two_gradient = total_of([normed_own] + normed_arrived)
    gain_two_gradient = jnp.sum(normed_two_gradient * unit_two, axis=0)
    hidden_gradient = output_cotangent.astype(f32) + norm_back(
        normed_two_gradient, unit_two, inverse_two, gain_two
    )
    (branch_gradient,) = clock(hidden_gradient.astype(bf16))
    (attention_gradient,) = clock(times_transposed(branch_gradient, output_matrix).astype(bf16))
    d_queries, pair_own, *pair_partial = clock.run(
        lambda *operands: attention_backward(*operands, shards),
        queries,
        attention_gradient,
        pairs,
        cosine_table,
        signed_sine,
        row_marks,
        key_marks.T,
    )
    pair_moving = send_back(pair_partial)
    output = start_halving(attention_low, branch_gradient, shards, False)
    up_blocks = clock(*blocks_of(up.finish()))
    output.along_first()
    (down_piece,) = clock(down_piece)
    down_gathered = lax.all_gather(down_piece, "rep", axis=0, tiled=True)
    (pair_arrived,) = clock.wait(pair_moving)
    up_moving = send_blocks(up_blocks)
    projected_gradient, bias_sum = clock.run(
        lambda *operands: join_projected(operands[0], operands[3:], *operands[1:3]),
        d_queries,
        cosine_table,
        signed_sine,
        pair_own,
        *pair_arrived,
    )
    projected = start_halving(normed_one, projected_gradient, shards, False)
    output.along_second()
    projected.along_first()
    (up_rows,) = clock.wait(up_moving)
    up_spread = spread(side_by_side(up_blocks[:1] + up_rows))
    output_blocks = clock(*blocks_of(output.finish()))
    output_moving = send_blocks(output_blocks)
    projected_gradient, hidden_gradient = clock(projected_gradient, hidden_gradient)
    normed_one_gradient = times_transposed(projected_gradient, input_matrix)
    gain_one_gradient = jnp.sum(normed_one_gradient * unit_one, axis=0)
    (tokens_gradient,) = clock(
        (
            hidden_gradient + norm_back(normed_one_gradient, unit_one, inverse_one, gain_one)
        ).astype(bf16)
    )
    bias_gradient = bias_sum[0]
    bias_split = query_width + pair_width
    small_parts = (
        gain_one_gradient,
        gain_two_gradient,
        bias_gradient[:bias_split],
        bias_gradient[bias_split:],
    )
    (small,) = clock(
        jnp.concatenate([part.reshape(shards, -1) for part in small_parts], axis=1)
    )
    projected.along_second()
    up_spread.further()
    (output_rows,) = clock.wait(output_moving)
    output_spread = spread(clock(total_of(output_blocks[:1] + output_rows).astype(bf16))[0])
    block_first = send_block(0)
    small_moving = clock.send(core, [small], [1])
    input_blocks = clock(*blocks_of(projected.finish()))
    output_spread.further()
    block_first, small_arrived = clock.wait(block_first, small_moving)
    small = total_of([small] + small_arrived)
    (gate_piece,) = clock(gate_piece)
    gate_blocks = clock(*blocks_of(gate_piece.reshape(shards, part_rows, block_units)))
    gate_moving = send_blocks(gate_blocks)
    output_spread.over()
    (output_total,) = clock.run(widen_pieces, *output_spread.finish())
    up_spread.over()
    small_moving = clock.send(first, [small] * (first.size - 1), range(1, first.size))
    (gate_rows,) = clock.wait(gate_moving)
    gate_spread = spread(side_by_side(gate_blocks[:1] + gate_rows))
    (small_arrived,) = clock.wait(small_moving)
    small = total_of([small] + small_arrived)
    input_moving = send_blocks(input_blocks)
    (up_total,) = clock.run(widen_pieces, *up_spread.finish())
    gate_spread.further()
    (input_rows,) = clock.wait(input_moving)
    input_spread = spread(clock(total_of(input_blocks[:1] + input_rows).astype(bf16))[0])
    block_moving = []
    for at in range(1, len(block_partial) - 1):
        block_moving += send_block(at)
    small_moving = clock.send(second, [small] * (second.size - 1), range(1, second.size))
    input_spread.further()
    gate_spread.over()
    (small_arrived,) = clock.wait(small_moving)
    small = total_of([small] + small_arrived)
    input_spread.over()
    block_last = send_block(len(block_partial) - 1) if len(block_partial) > 1 else []
    (gate_total,) = clock.run(widen_pieces, *gate_spread.finish())
    (input_total,) = clock.run(widen_pieces, *input_spread.finish())
    small_blocks = clock(*blocks_of(small))
    small_moving = send_blocks(small_blocks)
    (down_gathered,) = clock(down_gathered)
    (down_total,) = clock(down_gathered.astype(f32))
    small_arrived, block_arrived, block_last = clock.wait(small_moving, block_moving, block_last)
    small = total_of(small_blocks[:1] + small_arrived)
    (block_out,) = clock(
        total_of([hidden, block_own] + block_first + block_arrived + block_last).astype(bf16)
    )

    small = small + clock.token[0, 0]
    small_totals, at = [], 0
    for part in small_parts:
        size = part.shape[0] // shards
        small_totals.append(small[at : at + size])
        at += size
    return (
        block_out,
        tokens_gradient,
        small_totals[0],
        input_total,
        small_totals[2],
        small_totals[3],
        output_total,
        small_totals[1],
        gate_total,
        up_total,
        down_total,
    )


def solution(mesh):
    placed = (
        P(("rep", "shard"), None),
        P("rep", None),
        P("shard"),
        P("shard", None),
        P("shard"),
        P("shard", None),
        P("shard"),
        P("shard", None),
        P("shard", None),
        P("shard", None),
        P(("rep", "shard"), None),
    )
    return jax.shard_map(
        on_device,
        mesh=mesh,
        in_specs=placed,
        out_specs=(
            P(("rep", "shard"), None),
            P(("rep", "shard"), None),
            P("shard"),
            P("shard", None),
            P("shard"),
            P("shard"),
            P("shard", None),
            P("shard"),
            P("shard", None),
            P("shard", None),
            P("shard", None),
        ),
        check_vma=False,
    )
```

```python
import math

import jax
import jax.numpy as jnp
from jax import lax
from jax.experimental import pallas as pl
from jax.experimental.pallas import tpu as pltpu
from jax.sharding import PartitionSpec as P

QH = 12
KVH = 2
HD = 128
SEQS = 3


EPSILON = 1e-06
LOG_THETA = math.log(1000000.0)
MASKED = -1e30
VMEM_LIMIT = 56 * 1024 * 1024
TILE = 512
COST = pl.CostEstimate(flops=1, bytes_accessed=1, transcendentals=0)


def rope_tables(places, head_width):
    half_width = head_width // 2
    frequency = jnp.exp(jnp.arange(half_width, dtype=jnp.float32) * (-2.0 * LOG_THETA / head_width))
    angles = places.astype(jnp.float32)[:, None] * frequency[None, :]
    angles = jnp.concatenate([angles, angles], axis=-1)
    return (jnp.cos(angles), jnp.sin(angles))


def positions(segments):
    labels = jnp.arange(SEQS, dtype=jnp.int32)
    starts = jnp.sum((segments[None, :] < labels[:, None]).astype(jnp.int32), axis=1)
    own_start = jnp.sum(jnp.where(segments[:, None] == labels[None, :], starts[None, :], 0), axis=1)
    return jnp.arange(segments.shape[0], dtype=jnp.int32) - own_start


def rotate(field_rows, cosine_table, sine_table):
    half_width = field_rows.shape[-1] // 2
    turned = jnp.concatenate([-field_rows[..., half_width:], field_rows[..., :half_width]], axis=-1)
    return field_rows * cosine_table[:, None, :] + turned * sine_table[:, None, :]


def transposed_times(left_side, right_side):
    return lax.dot_general(
        left_side, right_side, (((0,), (0,)), ((), ())), preferred_element_type=jnp.float32
    )


def times_transposed(left_side, right_side):
    return lax.dot_general(
        left_side, right_side, (((1,), (1,)), ((), ())), preferred_element_type=jnp.float32
    )


def norm_back(normed_gradient, unit_rows, inverse_rms, gain_row):
    scaled = normed_gradient * gain_row
    return inverse_rms * (scaled - unit_rows * jnp.mean(scaled * unit_rows, axis=-1, keepdims=True))


class Line:
    def __init__(self, name, size, place, pairs, crossed=False):
        self.name, self.size, self.place, self.pairs = name, size, place, pairs
        self.crossed = crossed

    def shift(self, value, step):
        return lax.ppermute(value, self.name, self.pairs(step % self.size))

    def pass_on(self, value, up):
        places = range(self.size - 1)
        pairs = [(at, at + 1) if up else (at + 1, at) for at in places]
        return lax.ppermute(value, self.name, pairs)

    def behind(self, step):
        return lax.rem(self.place + (self.size - step % self.size), self.size)

    def ahead(self, step):
        return lax.rem(self.place + step % self.size, self.size) if step else self.place


def make_lines(reps, shards):
    inner = 2 if reps % 4 == 0 else 1
    outer = reps // (2 * inner)
    square = inner == outer

    def split(index):
        core, b, a = index % 2, (index // 2) % inner, index // (2 * inner)
        return core, b, a

    def join(core, b, a):
        return (a * inner + b) * 2 + core

    def first_pairs(step):
        pairs = []
        for index in range(reps):
            core, b, a = split(index)
            if square and core == 0:
                pairs.append((index, join(core, (b + step) % inner, a)))
            else:
                pairs.append((index, join(core, b, (a + step) % outer)))
        return pairs

    def second_pairs(step):
        pairs = []
        for index in range(reps):
            core, b, a = split(index)
            if square and core == 0:
                pairs.append((index, join(core, b, (a + step) % outer)))
            else:
                pairs.append((index, join(core, (b + step) % inner, a)))
        return pairs

    def core_pairs(step):
        pairs = []
        for index in range(reps):
            core, b, a = split(index)
            pairs.append((index, join((core + step) % 2, b, a)))
        return pairs

    def shard_pairs(step):
        return [(index, (index + step) % shards) for index in range(shards)]

    core, b, a = split(lax.axis_index("rep"))
    first, second = (jnp.where(core == 0, b, a), jnp.where(core == 0, a, b)) if square else (a, b)
    return (
        Line("shard", shards, lax.axis_index("shard"), shard_pairs),
        Line("rep", 2, core, core_pairs, square),
        Line("rep", outer, first, first_pairs),
        Line("rep", inner, second, second_pairs),
    )


def rep_places(reps):
    inner = 2 if reps % 4 == 0 else 1
    outer = reps // (2 * inner)
    places = []
    for index in range(reps):
        core, b, a = index % 2, (index // 2) % inner, index // (2 * inner)
        one, two = (b, a) if inner == outer and core == 0 else (a, b)
        places.append((core * outer + one) * inner + two)
    return places


def pick(array, index, axis):
    return lax.dynamic_index_in_dim(array, index, axis, keepdims=False)


def put(array, piece, index, axis):
    return lax.dynamic_update_index_in_dim(array, piece, index, axis)


def in_place_order(pieces, line):
    ordered = []
    for place in range(line.size):
        chosen = pieces[0]
        for step in range(1, line.size):
            chosen = jnp.where(line.behind(step) == place, pieces[step], chosen)
        ordered.append(chosen)
    return ordered


def tie(*arrays):
    return lax.optimization_barrier(arrays)


def gather_line(value, line):
    return [value] + [line.shift(value, step) for step in range(1, line.size)]


class Clock:
    def __init__(self):
        self.token = jnp.zeros((8, 128), jnp.float32)
        self.open = 0

    def __call__(self, *arrays):
        self.token, *arrays = tie(self.token, *arrays)
        return arrays

    def run(self, step, *arrays):
        return self(*step(*self(*arrays)))

    def send(self, line, values, steps):
        self.open += len(values)
        return [line.shift(value, step) for value, step in zip(self(*values), steps)]

    def pass_on(self, line, lower, upper):
        self.open += 2
        lower, upper = self(lower, upper)
        return [line.pass_on(lower, True), line.pass_on(upper, False)]

    def wait(self, *groups):
        flat = self(*[array for group in groups for array in group])
        self.open -= len(flat)
        parts, at = [], 0
        for group in groups:
            parts.append(flat[at : at + len(group)])
            at += len(group)
        return parts


def total_of(terms):
    total = terms[0].astype(jnp.float32)
    for term in terms[1:]:
        total = total + term.astype(jnp.float32)
    return total


class Halving:
    def __init__(self, clock, sent, own, core, first, second):
        self.clock, self.first, self.second = clock, first, second
        self.terms = [own]
        self.moving = clock.send(core, [sent], [1])

    def along(self, line, arrived):
        self.terms = self.terms + arrived
        steps = range(1, line.size)
        blocks = [
            total_of([pick(term, line.ahead(step), 0) for term in self.terms]).astype(jnp.bfloat16)
            for step in steps
        ]
        self.moving = self.clock.send(line, blocks, steps)
        self.terms = [pick(term, line.place, 0) for term in self.terms]

    def along_first(self, arrived):
        self.along(self.first, arrived)

    def along_second(self, arrived):
        self.along(self.second, arrived)

    def finish(self, arrived):
        return self.clock(total_of(self.terms + arrived).astype(jnp.bfloat16))[0]


class Spread:
    def __init__(self, clock, piece, core, first, second):
        self.clock, self.lines = clock, (core, first, second)
        self.pieces = [piece]
        steps = range(1, second.size)
        self.moving = clock.send(second, [piece] * len(steps), steps)

    def along(self, arrived):
        core, first, second = self.lines
        self.pieces = self.pieces + arrived
        steps = range(1, first.size)
        self.moving = self.clock.send(first, [jnp.stack(self.pieces)] * len(steps), steps)

    def over(self, arrived):
        core, first, second = self.lines
        rows = [jnp.stack(self.pieces)] + arrived
        self.pieces = jnp.concatenate(rows, axis=0)
        self.moving = self.clock.send(core, [self.pieces], [1])

    def finish(self, arrived):
        core, first, second = self.lines
        (others,) = arrived
        offsets = [(one, two) for one in range(first.size) for two in range(second.size)]
        placed = [(core.place, first.behind(one), second.behind(two)) for one, two in offsets]
        far, near = (second, first) if core.crossed else (first, second)
        placed += [(core.behind(1), far.behind(one), near.behind(two)) for one, two in offsets]
        places = [(c * first.size + f) * second.size + s for c, f, s in placed]
        return [jnp.stack(places).astype(jnp.int32), self.pieces, others]


def place_blocks(order, places, pieces, others):
    half, groups, shards = pieces.shape[:3]

    def body(order_ref, places_ref, pieces_ref, others_ref, *rest):
        def source_of(g, k, r):
            return (pieces_ref if r < half else others_ref).at[r % half, g, k]

        move_blocks(source_of, lambda r: places_ref[r], order_ref, rest[:groups], *rest[groups:])

    return blocks_call(body, 2, 2, groups, shards, 2 * half, pieces.shape[3:])(
        order, places, pieces, others
    )


def place_gathered(order, gathered):
    reps, shards, groups = gathered.shape[:3]

    def body(order_ref, source, *rest):
        move_blocks(
            lambda g, k, r: source.at[r, k, g], lambda r: r, order_ref, rest[:groups], *rest[groups:]
        )

    return blocks_call(body, 1, 1, groups, shards, reps, gathered.shape[3:])(order, gathered)


def move_blocks(source_of, place_of, order_ref, outs, held, in_sems, out_sems):
    groups, shards, reps = in_sems.shape
    slabs = [(g, k) for g in range(groups) for k in range(shards)]

    def load(g, k, r):
        return pltpu.make_async_copy(
            source_of(g, k, r), held.at[g, k, place_of(r)], in_sems.at[g, k, r]
        )

    def store(g, k):
        return pltpu.make_async_copy(held.at[g, k], outs[g].at[order_ref[k]], out_sems.at[g, k])

    for g, k in slabs:
        for r in range(reps):
            load(g, k, r).start()
    for g, k in slabs:
        for r in range(reps):
            load(g, k, r).wait()
        store(g, k).start()
    for g, k in slabs:
        store(g, k).wait()


def blocks_call(body, scalars, sources, groups, shards, reps, block):
    whole = (shards, reps) + block
    return pl.pallas_call(
        body,
        out_shape=[jax.ShapeDtypeStruct(whole, jnp.bfloat16)] * groups,
        in_specs=[pl.BlockSpec(memory_space=pltpu.SMEM)] * scalars
        + [pl.BlockSpec(memory_space=pl.ANY)] * sources,
        out_specs=[pl.BlockSpec(memory_space=pl.ANY)] * groups,
        scratch_shapes=[
            pltpu.VMEM((groups,) + whole, jnp.bfloat16),
            pltpu.SemaphoreType.DMA((groups, shards, reps)),
            pltpu.SemaphoreType.DMA((groups, shards)),
        ],
        compiler_params=pltpu.CompilerParams(vmem_limit_bytes=VMEM_LIMIT),
        cost_estimate=COST,
        name="place_blocks",
    )


def widen_pieces(places, pieces, others):
    half, rows, columns = pieces.shape
    reps = 2 * half
    strip = next(size for size in (16, 8, rows) if rows % size == 0)

    def body(places_ref, pieces_ref, others_ref, out_ref, narrow, wide, in_sems, out_sems):
        loads = [
            pltpu.make_async_copy(
                (pieces_ref if r < half else others_ref).at[r % half], narrow.at[r], in_sems.at[r]
            )
            for r in range(reps)
        ]
        stores = [
            pltpu.make_async_copy(wide.at[r], out_ref.at[places_ref[r]], out_sems.at[r])
            for r in range(reps)
        ]
        for load in loads:
            load.start()
        for r in range(reps):
            loads[r].wait()

            def convert(at, carry):
                cut = pl.ds(pl.multiple_of(at * strip, strip), strip)
                wide[r, cut, :] = narrow[r, cut, :].astype(jnp.float32)
                return carry

            lax.fori_loop(0, rows // strip, convert, 0)
            stores[r].start()
        for store in stores:
            store.wait()

    result = pl.pallas_call(
        body,
        out_shape=jax.ShapeDtypeStruct((reps, rows, columns), jnp.float32),
        in_specs=[pl.BlockSpec(memory_space=pltpu.SMEM)]
        + [pl.BlockSpec(memory_space=pl.ANY)] * 2,
        out_specs=pl.BlockSpec(memory_space=pl.ANY),
        scratch_shapes=[
            pltpu.VMEM((reps, rows, columns), jnp.bfloat16),
            pltpu.VMEM((reps, rows, columns), jnp.float32),
            pltpu.SemaphoreType.DMA((reps,)),
            pltpu.SemaphoreType.DMA((reps,)),
        ],
        compiler_params=pltpu.CompilerParams(vmem_limit_bytes=VMEM_LIMIT),
        cost_estimate=COST,
        name="widen_pieces",
    )(places, pieces, others)
    return (result.reshape(reps * rows, columns),)


def resident(shape):
    return pl.BlockSpec(shape, lambda i: (0, 0), pipeline_mode=pl.Buffered(1))


def feed_forward(rows, cotangents, gate_matrix, up_matrix, down_matrix):
    count, width = rows.shape
    units = gate_matrix.shape[1]
    steps = pl.cdiv(units, TILE)
    slabs = next(size for size in range(min(steps, width // 128), 0, -1) if width % (128 * size) == 0)
    slab = width // slabs

    def body(
        rows_ref,
        cotangents_ref,
        gate_ref,
        up_ref,
        down_ref,
        inner_ref,
        d_gate_ref,
        d_up_ref,
        turned_rows_ref,
        turned_inner_ref,
    ):
        gate = jnp.dot(rows_ref[...], gate_ref[...], preferred_element_type=jnp.float32)
        up = jnp.dot(rows_ref[...], up_ref[...], preferred_element_type=jnp.float32)
        sigmoid = jax.nn.sigmoid(gate)
        silu = gate * sigmoid
        inner = (silu * up).astype(jnp.bfloat16)
        inner_ref[...] = inner
        turned_inner_ref[...] = inner.T
        d_inner = times_transposed(cotangents_ref[...], down_ref[...])
        d_up_ref[...] = (d_inner * silu).astype(jnp.bfloat16)
        d_gate_ref[...] = (d_inner * up * sigmoid * (1.0 + gate * (1.0 - sigmoid))).astype(
            jnp.bfloat16
        )
        for step in range(slabs):

            @pl.when(pl.program_id(0) == step)
            def turn():
                turned_rows_ref[...] = rows_ref[:, step * slab : (step + 1) * slab].T

    columns = pl.BlockSpec((width, TILE), lambda i: (0, i))
    results = pl.BlockSpec((count, TILE), lambda i: (0, i))
    return pl.pallas_call(
        body,
        grid=(steps,),
        out_shape=[jax.ShapeDtypeStruct((count, units), jnp.bfloat16)] * 3
        + [
            jax.ShapeDtypeStruct((width, count), jnp.bfloat16),
            jax.ShapeDtypeStruct((units, count), jnp.bfloat16),
        ],
        in_specs=[
            resident((count, width)),
            resident((count, width)),
            columns,
            columns,
            pl.BlockSpec((TILE, width), lambda i: (i, 0)),
        ],
        out_specs=[results] * 3
        + [
            pl.BlockSpec((slab, count), lambda i: (jnp.minimum(i, slabs - 1), 0)),
            pl.BlockSpec((TILE, count), lambda i: (i, 0)),
        ],
        compiler_params=pltpu.CompilerParams(vmem_limit_bytes=VMEM_LIMIT),
        cost_estimate=COST,
        name="feed_forward",
    )(rows, cotangents, gate_matrix, up_matrix, down_matrix)


def split_gradient(left, right, groups, places, core_place, turned):
    rows, count = left.shape if turned else left.shape[::-1]
    columns = right.shape[1]
    half = rows // (2 * groups)
    part = half // places

    def body(core_ref, left_ref, right_ref, other_ref, own_ref, *scratch):
        if turned:
            rows_ref = left_ref
        else:
            (rows_ref,) = scratch

            @pl.when(pl.program_id(0) == 0)
            def turn():
                rows_ref[...] = left_ref[...].T

        core = core_ref[0]
        for out_ref, which in ((other_ref, 1 - core), (own_ref, core)):
            halves = [
                rows_ref[pl.ds(pl.multiple_of((2 * group + which) * half, 16), half), :]
                for group in range(groups)
            ]
            product = jnp.dot(
                jnp.concatenate(halves, axis=0), right_ref[...], preferred_element_type=jnp.float32
            )
            for group in range(groups):
                for place in range(places):
                    at = group * half + place * part
                    out_ref[place, group] = product[at : at + part].astype(jnp.bfloat16)

    return pl.pallas_call(
        body,
        grid=(pl.cdiv(columns, TILE),),
        out_shape=[jax.ShapeDtypeStruct((places, groups, part, columns), jnp.bfloat16)] * 2,
        in_specs=[
            pl.BlockSpec(memory_space=pltpu.SMEM),
            resident(left.shape),
            pl.BlockSpec((count, TILE), lambda i: (0, i)),
        ],
        out_specs=[pl.BlockSpec((places, groups, part, TILE), lambda i: (0, 0, 0, i))] * 2,
        scratch_shapes=[] if turned else [pltpu.VMEM((rows, count), jnp.bfloat16)],
        compiler_params=pltpu.CompilerParams(vmem_limit_bytes=VMEM_LIMIT),
        cost_estimate=COST,
        name="split_gradient",
    )(core_place.reshape(1).astype(jnp.int32), left, right)


def ordered_gradient(left, right, shards, order):
    reps = len(order)
    rows, count = left.shape
    columns = right.shape[1]
    part = rows // (shards * reps)

    def body(left_ref, right_ref, out_ref):
        product = jnp.dot(left_ref[...], right_ref[...], preferred_element_type=jnp.float32)
        for z in range(shards):
            for r in range(reps):
                at = (z * reps + order[r]) * part
                out_ref[r, z] = product[at : at + part].astype(jnp.bfloat16)

    return pl.pallas_call(
        body,
        grid=(pl.cdiv(columns, TILE),),
        out_shape=[jax.ShapeDtypeStruct((reps, shards, part, columns), jnp.bfloat16)],
        in_specs=[
            resident((rows, count)),
            pl.BlockSpec((count, TILE), lambda i: (0, i)),
        ],
        out_specs=[pl.BlockSpec((reps, shards, part, TILE), lambda i: (0, 0, 0, i))],
        compiler_params=pltpu.CompilerParams(vmem_limit_bytes=VMEM_LIMIT),
        cost_estimate=COST,
        name="ordered_gradient",
    )(left, right)


def rows_product(lefts, rights, turned, blocks):
    count, depth = lefts[0].shape
    columns = rights[0].shape[0 if turned else 1]
    pairs, part = len(lefts), count // blocks

    def body(*refs):
        total = None
        for left_ref, right_ref in zip(refs[:pairs], refs[pairs : 2 * pairs]):
            if turned:
                product = times_transposed(left_ref[...], right_ref[...])
            else:
                product = jnp.dot(
                    left_ref[...], right_ref[...], preferred_element_type=jnp.float32
                )
            total = product if total is None else total + product
        for block in range(blocks):
            refs[2 * pairs + block][...] = total[block * part : (block + 1) * part].astype(
                jnp.bfloat16
            )

    right_spec = (
        pl.BlockSpec((TILE, depth), lambda i: (i, 0))
        if turned
        else pl.BlockSpec((depth, TILE), lambda i: (0, i))
    )
    return pl.pallas_call(
        body,
        grid=(pl.cdiv(columns, TILE),),
        out_shape=[jax.ShapeDtypeStruct((part, columns), jnp.bfloat16)] * blocks,
        in_specs=[resident((count, depth))] * pairs + [right_spec] * pairs,
        out_specs=[pl.BlockSpec((part, TILE), lambda i: (0, i))] * blocks,
        compiler_params=pltpu.CompilerParams(vmem_limit_bytes=VMEM_LIMIT),
        cost_estimate=COST,
        name="rows_product",
    )(*lefts, *rights)


def kept_bias(row_segments, row_index, key_segments, key_index):
    kept = (row_segments == key_segments) & (key_index <= row_index)
    return jnp.where(kept, 0.0, MASKED)


def in_vmem(count):
    return [pl.BlockSpec(memory_space=pltpu.VMEM)] * count


def attention_forward(projected, cosine, signed_sine, pairs, rows, keys):
    count = projected.shape[0]
    per_group = QH // KVH
    scale = 1.0 / math.sqrt(HD)
    shape = (KVH, per_group * count, HD)

    def body(projected_ref, cosine_ref, sine_ref, pairs_ref, rows_ref, keys_ref, queries_ref, out_ref):
        bias = kept_bias(rows_ref[:, 0:1], rows_ref[:, 1:2], keys_ref[0:1, :], keys_ref[1:2, :])
        for k in range(KVH):
            for h in range(per_group):
                at = (k * per_group + h) * HD
                field = projected_ref[:, at : at + HD]
                queries_ref[k, h * count : (h + 1) * count, :] = (
                    field * cosine_ref[...] + pltpu.roll(field, HD // 2, 1) * sine_ref[...]
                ).astype(jnp.bfloat16)
            keys_here = pairs_ref[:, k * HD : (k + 1) * HD]
            values_here = pairs_ref[:, (KVH + k) * HD : (KVH + k + 1) * HD]
            scores = times_transposed(queries_ref[k], keys_here) * scale + bias
            powers = jnp.exp(scores - jnp.max(scores, axis=1, keepdims=True))
            shares = powers * (1.0 / jnp.sum(powers, axis=1, keepdims=True))
            result = jnp.dot(
                shares.astype(jnp.bfloat16), values_here, preferred_element_type=jnp.float32
            ).astype(jnp.bfloat16)
            for h in range(per_group):
                at = (k * per_group + h) * HD
                out_ref[:, at : at + HD] = result[h * count : (h + 1) * count]

    return pl.pallas_call(
        body,
        out_shape=[
            jax.ShapeDtypeStruct(shape, jnp.bfloat16),
            jax.ShapeDtypeStruct((count, QH * HD), jnp.bfloat16),
        ],
        in_specs=in_vmem(6),
        out_specs=in_vmem(2),
        compiler_params=pltpu.CompilerParams(vmem_limit_bytes=VMEM_LIMIT),
        cost_estimate=COST,
        name="attention_forward",
    )(projected, cosine, signed_sine, pairs, rows, keys)


def attention_backward(queries, gradient, pairs, cosine, signed_sine, rows, keys, blocks):
    count = gradient.shape[0]
    per_group = QH // KVH
    scale = 1.0 / math.sqrt(HD)
    group_rows = pairs.shape[0]
    part = group_rows // blocks

    def body(queries_ref, gradient_ref, pairs_ref, cosine_ref, sine_ref, rows_ref, keys_ref, d_ref, *outs):
        block_refs, stacked = outs[:blocks], outs[blocks]
        bias = kept_bias(rows_ref[0:1, :], rows_ref[1:2, :], keys_ref[:, 0:1], keys_ref[:, 1:2])
        for k in range(KVH):
            for h in range(per_group):
                at = (k * per_group + h) * HD
                stacked[h * count : (h + 1) * count, :] = gradient_ref[:, at : at + HD]
            keys_here = pairs_ref[:, k * HD : (k + 1) * HD]
            values_here = pairs_ref[:, (KVH + k) * HD : (KVH + k + 1) * HD]
            scores = times_transposed(keys_here, queries_ref[k]) * scale + bias
            powers = jnp.exp(scores - jnp.max(scores, axis=0, keepdims=True))
            shares = powers * (1.0 / jnp.sum(powers, axis=0, keepdims=True))
            d_shares = times_transposed(values_here, stacked[...])
            dots = jnp.sum(shares * d_shares, axis=0, keepdims=True)
            d_scores = (shares * (d_shares - dots)).astype(jnp.bfloat16)
            d_keys = jnp.dot(d_scores, queries_ref[k], preferred_element_type=jnp.float32) * scale
            d_values = jnp.dot(
                shares.astype(jnp.bfloat16), stacked[...], preferred_element_type=jnp.float32
            )
            for block in range(blocks):
                cut = slice(block * part, (block + 1) * part)
                block_refs[block][:, k * HD : (k + 1) * HD] = d_keys[cut].astype(jnp.bfloat16)
                block_refs[block][:, (KVH + k) * HD : (KVH + k + 1) * HD] = d_values[cut].astype(
                    jnp.bfloat16
                )
            d_queries = transposed_times(d_scores, keys_here) * scale
            for h in range(per_group):
                at = (k * per_group + h) * HD
                field = d_queries[h * count : (h + 1) * count]
                d_ref[:, at : at + HD] = (
                    field * cosine_ref[...] - pltpu.roll(field, HD // 2, 1) * sine_ref[...]
                ).astype(jnp.bfloat16)

    return pl.pallas_call(
        body,
        out_shape=[jax.ShapeDtypeStruct((count, QH * HD), jnp.bfloat16)]
        + [jax.ShapeDtypeStruct((part, 2 * KVH * HD), jnp.bfloat16)] * blocks,
        in_specs=in_vmem(7),
        out_specs=in_vmem(1 + blocks),
        scratch_shapes=[pltpu.VMEM((per_group * count, HD), jnp.bfloat16)],
        compiler_params=pltpu.CompilerParams(vmem_limit_bytes=VMEM_LIMIT),
        cost_estimate=COST,
        name="attention_backward",
    )(queries, gradient, pairs, cosine, signed_sine, rows, keys)


def join_projected(d_queries, pair_terms, cosine, signed_sine):
    count, query_width = d_queries.shape
    pair_width = KVH * HD
    terms = len(pair_terms)

    def body(d_queries_ref, cosine_ref, sine_ref, *refs):
        term_refs, out_ref, sum_ref = refs[:terms], refs[terms], refs[terms + 1]
        out_ref[:, :query_width] = d_queries_ref[...]
        for at in range(0, 2 * pair_width, HD):
            field = total_of([term[:, at : at + HD] for term in term_refs])
            if at < pair_width:
                field = field * cosine_ref[...] - pltpu.roll(field, HD // 2, 1) * sine_ref[...]
            out_ref[:, query_width + at : query_width + at + HD] = field.astype(jnp.bfloat16)
        sum_ref[...] = jnp.sum(out_ref[...].astype(jnp.float32), axis=0, keepdims=True)

    return pl.pallas_call(
        body,
        out_shape=[
            jax.ShapeDtypeStruct((count, query_width + 2 * pair_width), jnp.bfloat16),
            jax.ShapeDtypeStruct((1, query_width + 2 * pair_width), jnp.float32),
        ],
        in_specs=in_vmem(3 + terms),
        out_specs=in_vmem(2),
        cost_estimate=COST,
        name="join_projected",
    )(d_queries, cosine, signed_sine, *pair_terms)


def on_device(
    tokens,
    segment_ids,
    first_gain,
    input_weight,
    input_bias,
    output_weight,
    second_gain,
    gate_weight,
    up_weight,
    down_weight,
    output_cotangent,
):
    bf16, f32 = jnp.bfloat16, jnp.float32
    shards, reps = lax.axis_size("shard"), lax.axis_size("rep")
    shard, core, first, second = make_lines(reps, shards)
    rep_place = (core.place * first.size + first.place) * second.size + second.place
    own_rows, width = tokens.shape
    segments = segment_ids[0]
    per_group = QH // KVH
    query_width = QH * HD
    pair_width = KVH * HD
    first_row = shard.place * own_rows
    part_rows = input_weight.shape[0] // reps
    hidden_units = gate_weight.shape[1]
    block_units = hidden_units // shards
    clock = Clock()
    z_order = jnp.stack([shard.behind(step) for step in range(shards)]).astype(jnp.int32)

    def weight_piece(weight, place):
        return pick(weight.reshape(reps, part_rows, weight.shape[1]), place, 0)

    def column_piece(weight, place):
        return weight_piece(weight, place).reshape(part_rows, shards, block_units).transpose(1, 0, 2)

    def spread(piece):
        return Spread(clock, piece, core, first, second)

    def blocks_of(blocks):
        return [pick(blocks, shard.ahead(step), 0) for step in range(shards)]

    steps = range(1, shards)

    def send_blocks(blocks):
        return clock.send(shard, blocks[1:], steps)

    def send_around(value):
        return clock.send(shard, [value] * len(steps), steps)

    def send_back(rows):
        return clock.send(shard, rows, [shards - step for step in steps])

    rep_index = lax.axis_index("rep")
    input_matrix = lax.all_gather(
        weight_piece(input_weight, rep_index), ("shard", "rep"), axis=0, tiled=True
    )
    shard_vectors = jnp.concatenate([first_gain, second_gain, input_bias])
    vector_row = jnp.pad(shard_vectors, (0, output_weight.shape[1] - shard_vectors.shape[0]))
    own_output = jnp.concatenate(
        [weight_piece(output_weight, rep_place), vector_row[None]], axis=0
    )
    output_moving = send_around(own_output)
    gate_blocks = clock(*blocks_of(column_piece(gate_weight, rep_index)))
    up_blocks = clock(*blocks_of(column_piece(up_weight, rep_place)))
    (output_rows,) = clock.wait(output_moving)
    output_rows = [own_output] + output_rows

    output_spread = spread(jnp.stack([rows[:part_rows] for rows in output_rows])[None])
    gate_moving = send_blocks(gate_blocks)
    vector_rows = jnp.stack(in_place_order([rows[part_rows] for rows in output_rows], shard))
    own_gain = first_gain.shape[0]
    gain_one = vector_rows[:, :own_gain].reshape(width).astype(f32)
    gain_two = vector_rows[:, own_gain : 2 * own_gain].reshape(width).astype(f32)
    shift_row = (
        vector_rows[:, 2 * own_gain : shard_vectors.shape[0]].reshape(-1).astype(f32)
    )
    places = positions(segments)
    cosine_table, sine_table = rope_tables(
        lax.dynamic_slice_in_dim(places, first_row, own_rows), HD
    )
    signed_sine = jnp.concatenate(
        [-sine_table[:, : HD // 2], sine_table[:, HD // 2 :]], axis=1
    )
    own_segments = lax.dynamic_slice_in_dim(segments, first_row, own_rows)
    row_index = jnp.arange(own_rows, dtype=jnp.int32)
    key_index = jnp.concatenate([shard.behind(step) * own_rows + row_index for step in range(shards)])
    key_segments = jnp.concatenate(
        [
            lax.dynamic_slice_in_dim(segments, shard.behind(step) * own_rows, own_rows)
            for step in range(shards)
        ]
    )
    key_marks = jnp.stack([key_segments, key_index])
    row_marks = jnp.tile(jnp.stack([own_segments, first_row + row_index]), (1, per_group))
    wide_tokens = tokens.astype(f32)
    inverse_one = lax.rsqrt(jnp.mean(wide_tokens * wide_tokens, axis=-1, keepdims=True) + EPSILON)
    unit_one = wide_tokens * inverse_one
    normed_one = (unit_one * gain_one).astype(bf16)
    (
        normed_one,
        cosine_table,
        sine_table,
        signed_sine,
        key_marks,
        row_marks,
    ) = clock(normed_one, cosine_table, sine_table, signed_sine, key_marks, row_marks)
    output_arrived, gate_rows = clock.wait(output_spread.moving, gate_moving)

    output_spread.along(output_arrived)
    gate_gathered = lax.all_gather(
        clock(jnp.stack(gate_blocks[:1] + gate_rows))[0][None, :, None], "rep", axis=0, tiled=True
    )
    up_moving = send_blocks(up_blocks)
    output_arrived, up_rows = clock.wait(output_spread.moving, up_moving)

    output_spread.over(output_arrived)
    up_spread = spread(jnp.stack(up_blocks[:1] + up_rows)[None])
    passed = [[output_cotangent] * 2]
    passing = clock.pass_on(shard, *passed[-1])
    output_arrived, up_arrived, arrived = clock.wait(
        output_spread.moving, up_spread.moving, passing
    )
    passed.append(arrived)
    (output_matrix,) = clock.run(place_blocks, z_order, *output_spread.finish(output_arrived))
    output_matrix = output_matrix.reshape(width, width)

    input_matrix, normed_one = clock(input_matrix, normed_one)
    projected = jnp.dot(normed_one, input_matrix, preferred_element_type=f32) + shift_row
    key_part = rotate(
        projected[:, query_width : query_width + pair_width].reshape(own_rows, KVH, HD),
        cosine_table,
        sine_table,
    )
    (own_pairs,) = clock(
        jnp.concatenate(
            [key_part.reshape(own_rows, pair_width), projected[:, query_width + pair_width :]],
            axis=1,
        ).astype(bf16)
    )
    pair_moving = send_around(own_pairs)
    up_spread.along(up_arrived)
    pair_rows, up_arrived = clock.wait(pair_moving, up_spread.moving)

    pairs = jnp.concatenate([own_pairs] + pair_rows, axis=0)
    up_spread.over(up_arrived)
    passing = clock.pass_on(shard, *passed[-1]) if shards > 2 else []
    queries, attention_low = clock.run(
        attention_forward, projected, cosine_table, signed_sine, pairs, row_marks.T, key_marks
    )
    hidden = wide_tokens + jnp.dot(attention_low, output_matrix, preferred_element_type=f32)
    inverse_two = lax.rsqrt(jnp.mean(hidden * hidden, axis=-1, keepdims=True) + EPSILON)
    unit_two = hidden * inverse_two
    (normed_two,) = clock((unit_two * gain_two).astype(bf16))
    up_arrived, arrived = clock.wait(up_spread.moving, passing)
    passed.append(arrived)

    normed_moving = send_around(normed_two)
    passing = clock.pass_on(shard, *passed[-1]) if shards > 3 else []
    (up_matrix,) = clock.run(place_blocks, z_order, *up_spread.finish(up_arrived))
    up_matrix = up_matrix.reshape(width, block_units)
    (gate_matrix,) = clock.run(place_gathered, z_order, gate_gathered)
    gate_matrix = gate_matrix.reshape(width, block_units)
    normed_arrived, arrived = clock.wait(normed_moving, passing)
    passed.append(arrived)
    while len(passed) < shards:
        (arrived,) = clock.wait(clock.pass_on(shard, *passed[-1]))
        passed.append(arrived)
    group_normed = jnp.concatenate([normed_two] + normed_arrived, axis=0)
    cotangents = jnp.concatenate(
        [output_cotangent]
        + [
            jnp.where(shard.place >= step, passed[step][0], passed[shards - step][1])
            for step in steps
        ],
        axis=0,
    )

    inner_act, d_gate, d_up, turned_normed, turned_inner = clock.run(
        feed_forward, group_normed, cotangents, gate_matrix, up_matrix, down_weight
    )

    def start_halving(left, right, groups, turned):
        count = first.size * second.size
        sent, own = clock.run(
            lambda left, right: split_gradient(left, right, groups, count, core.place, turned),
            left,
            right,
        )
        shape = (first.size, second.size) + own.shape[1:]
        return Halving(clock, sent.reshape(shape), own.reshape(shape), core, first, second)

    def side_by_side(rows):
        return clock(jnp.concatenate(in_place_order(rows, shard), axis=1))[0]

    def sum_over_rep(blocks):
        return lax.psum_scatter(blocks, "rep", scatter_dimension=0, tiled=True)

    def row_sum(own, arrived):
        return clock(total_of(own + arrived).astype(bf16))[0]

    def send_some(rows, chosen):
        return clock.send(shard, [rows[k] for k in chosen], [shards - 1 - k for k in chosen])

    edges = sorted({0, shards - 2})
    inside = list(range(1, shards - 2))

    (down_blocks,) = clock.run(
        lambda left, right: ordered_gradient(left, right, 1, list(range(reps))),
        turned_inner,
        cotangents,
    )
    down_piece = sum_over_rep(down_blocks.reshape(block_units, width))
    normed_own, *normed_partial = clock.run(
        lambda *operands: rows_product(operands[:2], operands[2:], True, shards),
        d_gate,
        d_up,
        gate_matrix,
        up_matrix,
    )

    normed_moving = send_some(normed_partial, edges)
    up = start_halving(turned_normed, d_up, shards, True)
    (gate_blocks,) = clock.run(
        lambda left, right: ordered_gradient(left, right, shards, rep_places(reps)),
        turned_normed,
        d_gate,
    )
    gate_piece = sum_over_rep(gate_blocks.reshape(width, block_units))
    normed_arrived, up_arrived = clock.wait(normed_moving, up.moving)

    up.along_first(up_arrived)
    normed_moving = send_some(normed_partial, inside)
    block_own, *block_partial = clock.run(
        lambda left, right: rows_product((left,), (right,), False, shards), inner_act, down_weight
    )
    more_arrived, up_arrived = clock.wait(normed_moving, up.moving)

    up.along_second(up_arrived)
    normed_two_gradient = total_of([normed_own] + normed_arrived + more_arrived)
    gain_two_gradient = jnp.sum(normed_two_gradient * unit_two, axis=0)
    hidden_gradient = output_cotangent.astype(f32) + norm_back(
        normed_two_gradient, unit_two, inverse_two, gain_two
    )
    (branch_gradient,) = clock(hidden_gradient.astype(bf16))
    (attention_gradient,) = clock(times_transposed(branch_gradient, output_matrix).astype(bf16))
    d_queries, pair_own, *pair_partial = clock.run(
        lambda *operands: attention_backward(*operands, shards),
        queries,
        attention_gradient,
        pairs,
        cosine_table,
        signed_sine,
        row_marks,
        key_marks.T,
    )
    (up_arrived,) = clock.wait(up.moving)

    pair_moving = send_back(pair_partial)
    output = start_halving(attention_low, branch_gradient, shards, False)
    up_blocks = clock(*blocks_of(up.finish(up_arrived)))
    pair_arrived, output_arrived = clock.wait(pair_moving, output.moving)

    output.along_first(output_arrived)
    block_moving = send_some(block_partial, edges[:1])
    (down_piece,) = clock(down_piece)
    down_gathered = lax.all_gather(down_piece, "rep", axis=0, tiled=True)
    projected_gradient, bias_sum = clock.run(
        lambda *operands: join_projected(operands[0], operands[3:], *operands[1:3]),
        d_queries,
        cosine_table,
        signed_sine,
        pair_own,
        *pair_arrived,
    )
    projected = start_halving(normed_one, projected_gradient, shards, False)
    output_arrived, block_arrived, projected_arrived = clock.wait(
        output.moving, block_moving, projected.moving
    )

    projected.along_first(projected_arrived)
    output.along_second(output_arrived)
    up_moving = send_blocks(up_blocks)
    projected_gradient, hidden_gradient = clock(projected_gradient, hidden_gradient)
    normed_one_gradient = times_transposed(projected_gradient, input_matrix)
    gain_one_gradient = jnp.sum(normed_one_gradient * unit_one, axis=0)
    (tokens_gradient,) = clock(
        (
            hidden_gradient + norm_back(normed_one_gradient, unit_one, inverse_one, gain_one)
        ).astype(bf16)
    )
    bias_gradient = bias_sum[0]
    bias_split = query_width + pair_width
    small_parts = (
        gain_one_gradient,
        gain_two_gradient,
        bias_gradient[:bias_split],
        bias_gradient[bias_split:],
    )
    (small,) = clock(
        jnp.concatenate([part.reshape(shards, -1) for part in small_parts], axis=1)
    )
    projected_arrived, output_arrived, up_rows = clock.wait(
        projected.moving, output.moving, up_moving
    )

    projected.along_second(projected_arrived)
    output_blocks = clock(*blocks_of(output.finish(output_arrived)))
    output_moving = send_blocks(output_blocks)
    up_spread = spread(side_by_side(up_blocks[:1] + up_rows))
    projected_arrived, output_rows, up_arrived = clock.wait(
        projected.moving, output_moving, up_spread.moving
    )

    up_spread.along(up_arrived)
    input_blocks = clock(*blocks_of(projected.finish(projected_arrived)))
    input_moving = send_blocks(input_blocks)
    output_spread = spread(row_sum(output_blocks[:1], output_rows))
    up_arrived, input_rows, output_arrived = clock.wait(
        up_spread.moving, input_moving, output_spread.moving
    )

    (gate_piece,) = clock(gate_piece)
    gate_blocks = clock(*blocks_of(gate_piece.reshape(shards, part_rows, block_units)))
    gate_moving = send_blocks(gate_blocks)
    output_spread.along(output_arrived)
    input_spread = spread(row_sum(input_blocks[:1], input_rows))
    gate_rows, output_arrived, input_arrived = clock.wait(
        gate_moving, output_spread.moving, input_spread.moving
    )

    gate_spread = spread(side_by_side(gate_blocks[:1] + gate_rows))
    input_spread.along(input_arrived)
    output_spread.over(output_arrived)
    up_spread.over(up_arrived)
    block_moving = send_some(block_partial, edges[1:])
    gate_arrived, input_arrived, output_arrived, up_arrived, more_arrived = clock.wait(
        gate_spread.moving, input_spread.moving, output_spread.moving, up_spread.moving, block_moving
    )
    block_arrived = block_arrived + more_arrived

    gate_spread.along(gate_arrived)
    input_spread.over(input_arrived)
    block_moving = send_some(block_partial, inside)
    small_moving = clock.send(core, [small], [1])
    (up_total,) = clock.run(widen_pieces, *up_spread.finish(up_arrived))
    (output_total,) = clock.run(widen_pieces, *output_spread.finish(output_arrived))
    gate_arrived, input_arrived, more_arrived, small_arrived = clock.wait(
        gate_spread.moving, input_spread.moving, block_moving, small_moving
    )
    block_arrived = block_arrived + more_arrived
    small = total_of([small] + small_arrived)

    gate_spread.over(gate_arrived)
    small_moving = clock.send(first, [small] * (first.size - 1), range(1, first.size))
    (input_total,) = clock.run(widen_pieces, *input_spread.finish(input_arrived))
    down_gathered, hidden, block_own = clock(down_gathered, hidden, block_own)
    (down_total,) = clock(down_gathered.astype(f32))
    gate_arrived, small_arrived = clock.wait(gate_spread.moving, small_moving)
    small = total_of([small] + small_arrived)

    small_moving = clock.send(second, [small] * (second.size - 1), range(1, second.size))
    (gate_total,) = clock.run(widen_pieces, *gate_spread.finish(gate_arrived))
    (small_arrived,) = clock.wait(small_moving)
    small_blocks = clock(*blocks_of(total_of([small] + small_arrived)))
    small_moving = send_blocks(small_blocks)
    (block_out,) = clock(total_of([hidden, block_own] + block_arrived).astype(bf16))
    (small_arrived,) = clock.wait(small_moving)
    small = total_of(small_blocks[:1] + small_arrived)

    small = small + clock.token[0, 0]
    small_totals, at = [], 0
    for part in small_parts:
        size = part.shape[0] // shards
        small_totals.append(small[at : at + size])
        at += size
    return (
        block_out,
        tokens_gradient,
        small_totals[0],
        input_total,
        small_totals[2],
        small_totals[3],
        output_total,
        small_totals[1],
        gate_total,
        up_total,
        down_total,
    )


def solution(mesh):
    placed = (
        P(("rep", "shard"), None),
        P("rep", None),
        P("shard"),
        P("shard", None),
        P("shard"),
        P("shard", None),
        P("shard"),
        P("shard", None),
        P("shard", None),
        P("shard", None),
        P(("rep", "shard"), None),
    )
    return jax.shard_map(
        on_device,
        mesh=mesh,
        in_specs=placed,
        out_specs=(
            P(("rep", "shard"), None),
            P(("rep", "shard"), None),
            P("shard"),
            P("shard", None),
            P("shard"),
            P("shard"),
            P("shard", None),
            P("shard"),
            P("shard", None),
            P("shard", None),
            P("shard", None),
        ),
        check_vma=False,
    )
```

```python
import math

import jax
import jax.numpy as jnp
from jax import lax
from jax.experimental import pallas as pl
from jax.experimental.pallas import tpu as pltpu
from jax.sharding import PartitionSpec as P

QH = 12
KVH = 2
HD = 128
SEQS = 3


EPSILON = 1e-06
LOG_THETA = math.log(1000000.0)
MASKED = -1e30
VMEM_LIMIT = 56 * 1024 * 1024
TILE = 512
COST = pl.CostEstimate(flops=1, bytes_accessed=1, transcendentals=0)


def rope_tables(places, head_width):
    half_width = head_width // 2
    frequency = jnp.exp(jnp.arange(half_width, dtype=jnp.float32) * (-2.0 * LOG_THETA / head_width))
    angles = places.astype(jnp.float32)[:, None] * frequency[None, :]
    angles = jnp.concatenate([angles, angles], axis=-1)
    return (jnp.cos(angles), jnp.sin(angles))


def positions(segments):
    labels = jnp.arange(SEQS, dtype=jnp.int32)
    starts = jnp.sum((segments[None, :] < labels[:, None]).astype(jnp.int32), axis=1)
    own_start = jnp.sum(jnp.where(segments[:, None] == labels[None, :], starts[None, :], 0), axis=1)
    return jnp.arange(segments.shape[0], dtype=jnp.int32) - own_start


def rotate(field_rows, cosine_table, sine_table):
    half_width = field_rows.shape[-1] // 2
    turned = jnp.concatenate([-field_rows[..., half_width:], field_rows[..., :half_width]], axis=-1)
    return field_rows * cosine_table[:, None, :] + turned * sine_table[:, None, :]


def transposed_times(left_side, right_side):
    return lax.dot_general(
        left_side, right_side, (((0,), (0,)), ((), ())), preferred_element_type=jnp.float32
    )


def times_transposed(left_side, right_side):
    return lax.dot_general(
        left_side, right_side, (((1,), (1,)), ((), ())), preferred_element_type=jnp.float32
    )


def norm_back(normed_gradient, unit_rows, inverse_rms, gain_row):
    scaled = normed_gradient * gain_row
    return inverse_rms * (scaled - unit_rows * jnp.mean(scaled * unit_rows, axis=-1, keepdims=True))


class Line:
    def __init__(self, name, size, place, pairs, crossed=False):
        self.name, self.size, self.place, self.pairs = name, size, place, pairs
        self.crossed = crossed

    def shift(self, value, step):
        return lax.ppermute(value, self.name, self.pairs(step % self.size))

    def pass_on(self, value, up):
        places = range(self.size - 1)
        pairs = [(at, at + 1) if up else (at + 1, at) for at in places]
        return lax.ppermute(value, self.name, pairs)

    def behind(self, step):
        return lax.rem(self.place + (self.size - step % self.size), self.size)

    def ahead(self, step):
        return lax.rem(self.place + step % self.size, self.size) if step else self.place


def make_lines(reps, shards):
    inner = 2 if reps % 4 == 0 else 1
    outer = reps // (2 * inner)
    square = inner == outer

    def split(index):
        core, b, a = index % 2, (index // 2) % inner, index // (2 * inner)
        return core, b, a

    def join(core, b, a):
        return (a * inner + b) * 2 + core

    def first_pairs(step):
        pairs = []
        for index in range(reps):
            core, b, a = split(index)
            if square and core == 0:
                pairs.append((index, join(core, (b + step) % inner, a)))
            else:
                pairs.append((index, join(core, b, (a + step) % outer)))
        return pairs

    def second_pairs(step):
        pairs = []
        for index in range(reps):
            core, b, a = split(index)
            if square and core == 0:
                pairs.append((index, join(core, b, (a + step) % outer)))
            else:
                pairs.append((index, join(core, (b + step) % inner, a)))
        return pairs

    def core_pairs(step):
        pairs = []
        for index in range(reps):
            core, b, a = split(index)
            pairs.append((index, join((core + step) % 2, b, a)))
        return pairs

    def shard_pairs(step):
        return [(index, (index + step) % shards) for index in range(shards)]

    core, b, a = split(lax.axis_index("rep"))
    first, second = (jnp.where(core == 0, b, a), jnp.where(core == 0, a, b)) if square else (a, b)
    return (
        Line("shard", shards, lax.axis_index("shard"), shard_pairs),
        Line("rep", 2, core, core_pairs, square),
        Line("rep", outer, first, first_pairs),
        Line("rep", inner, second, second_pairs),
    )


def rep_places(reps):
    inner = 2 if reps % 4 == 0 else 1
    outer = reps // (2 * inner)
    places = []
    for index in range(reps):
        core, b, a = index % 2, (index // 2) % inner, index // (2 * inner)
        one, two = (b, a) if inner == outer and core == 0 else (a, b)
        places.append((core * outer + one) * inner + two)
    return places


def pick(array, index, axis):
    return lax.dynamic_index_in_dim(array, index, axis, keepdims=False)


def put(array, piece, index, axis):
    return lax.dynamic_update_index_in_dim(array, piece, index, axis)


def in_place_order(pieces, line):
    ordered = []
    for place in range(line.size):
        chosen = pieces[0]
        for step in range(1, line.size):
            chosen = jnp.where(line.behind(step) == place, pieces[step], chosen)
        ordered.append(chosen)
    return ordered


def tie(*arrays):
    return lax.optimization_barrier(arrays)


def gather_line(value, line):
    return [value] + [line.shift(value, step) for step in range(1, line.size)]


class Clock:
    def __init__(self):
        self.token = jnp.zeros((8, 128), jnp.float32)
        self.open = 0

    def __call__(self, *arrays):
        self.token, *arrays = tie(self.token, *arrays)
        return arrays

    def run(self, step, *arrays):
        return self(*step(*self(*arrays)))

    def send(self, line, values, steps):
        self.open += len(values)
        return [line.shift(value, step) for value, step in zip(self(*values), steps)]

    def pass_on(self, line, lower, upper):
        self.open += 2
        lower, upper = self(lower, upper)
        return [line.pass_on(lower, True), line.pass_on(upper, False)]

    def wait(self, *groups):
        flat = self(*[array for group in groups for array in group])
        self.open -= len(flat)
        parts, at = [], 0
        for group in groups:
            parts.append(flat[at : at + len(group)])
            at += len(group)
        return parts


def total_of(terms):
    total = terms[0].astype(jnp.float32)
    for term in terms[1:]:
        total = total + term.astype(jnp.float32)
    return total


class Halving:
    def __init__(self, clock, sent, own, core, first, second):
        self.clock, self.first, self.second = clock, first, second
        self.terms = [own]
        self.moving = clock.send(core, [sent], [1])

    def along(self, line, arrived):
        self.terms = self.terms + arrived
        steps = range(1, line.size)
        blocks = [
            total_of([pick(term, line.ahead(step), 0) for term in self.terms]).astype(jnp.bfloat16)
            for step in steps
        ]
        self.moving = self.clock.send(line, blocks, steps)
        self.terms = [pick(term, line.place, 0) for term in self.terms]

    def along_first(self, arrived):
        self.along(self.first, arrived)

    def along_second(self, arrived):
        self.along(self.second, arrived)

    def finish(self, arrived):
        return self.clock(total_of(self.terms + arrived).astype(jnp.bfloat16))[0]


class Spread:
    def __init__(self, clock, piece, core, first, second):
        self.clock, self.lines = clock, (core, first, second)
        self.pieces = [piece]
        steps = range(1, second.size)
        self.moving = clock.send(second, [piece] * len(steps), steps)

    def along(self, arrived):
        core, first, second = self.lines
        self.pieces = self.pieces + arrived
        steps = range(1, first.size)
        self.moving = self.clock.send(first, [jnp.stack(self.pieces)] * len(steps), steps)

    def over(self, arrived):
        core, first, second = self.lines
        rows = [jnp.stack(self.pieces)] + arrived
        self.pieces = jnp.concatenate(rows, axis=0)
        self.moving = self.clock.send(core, [self.pieces], [1])

    def finish(self, arrived):
        core, first, second = self.lines
        (others,) = arrived
        offsets = [(one, two) for one in range(first.size) for two in range(second.size)]
        placed = [(core.place, first.behind(one), second.behind(two)) for one, two in offsets]
        far, near = (second, first) if core.crossed else (first, second)
        placed += [(core.behind(1), far.behind(one), near.behind(two)) for one, two in offsets]
        places = [(c * first.size + f) * second.size + s for c, f, s in placed]
        return [jnp.stack(places).astype(jnp.int32), self.pieces, others]


def column_blocks(place, shard_place, *weights):
    count = len(weights)
    rows, columns = weights[0].shape[1:]
    shards = lax.axis_size("shard")
    block = columns // shards

    def body(places_ref, *refs):
        sources, outs = refs[:count], refs[count : 2 * count]
        held, cut, in_sems, out_sems = refs[2 * count :]
        loads = [
            pltpu.make_async_copy(sources[at].at[places_ref[0]], held.at[at], in_sems.at[at])
            for at in range(count)
        ]

        def store(at, z):
            ahead = lax.rem(z + shards - places_ref[1], shards)
            return pltpu.make_async_copy(cut.at[at, z], outs[at].at[ahead], out_sems.at[at, z])

        for load in loads:
            load.start()
        for at in range(count):
            loads[at].wait()
            for z in range(shards):
                cut[at, z] = held[at, :, z * block : (z + 1) * block]
                store(at, z).start()
        for at in range(count):
            for z in range(shards):
                store(at, z).wait()

    return pl.pallas_call(
        body,
        out_shape=[jax.ShapeDtypeStruct((shards, rows, block), jnp.bfloat16)] * count,
        in_specs=[pl.BlockSpec(memory_space=pltpu.SMEM)]
        + [pl.BlockSpec(memory_space=pl.ANY)] * count,
        out_specs=[pl.BlockSpec(memory_space=pl.ANY)] * count,
        scratch_shapes=[
            pltpu.VMEM((count, rows, columns), jnp.bfloat16),
            pltpu.VMEM((count, shards, rows, block), jnp.bfloat16),
            pltpu.SemaphoreType.DMA((count,)),
            pltpu.SemaphoreType.DMA((count, shards)),
        ],
        compiler_params=pltpu.CompilerParams(vmem_limit_bytes=VMEM_LIMIT),
        cost_estimate=COST,
        name="column_blocks",
    )(jnp.stack([place, shard_place]).astype(jnp.int32), *weights)


def place_blocks(order, places, pieces, others):
    half, groups, shards = pieces.shape[:3]

    def body(order_ref, places_ref, pieces_ref, others_ref, *rest):
        def source_of(g, k, r):
            return (pieces_ref if r < half else others_ref).at[r % half, g, k]

        move_blocks(source_of, lambda r: places_ref[r], order_ref, rest[:groups], *rest[groups:])

    return blocks_call(body, 2, 2, groups, shards, 2 * half, pieces.shape[3:])(
        order, places, pieces, others
    )


def place_gathered(order, gathered):
    reps, shards, groups = gathered.shape[:3]

    def body(order_ref, source, *rest):
        move_blocks(
            lambda g, k, r: source.at[r, k, g], lambda r: r, order_ref, rest[:groups], *rest[groups:]
        )

    return blocks_call(body, 1, 1, groups, shards, reps, gathered.shape[3:])(order, gathered)


def move_blocks(source_of, place_of, order_ref, outs, held, in_sems, out_sems):
    groups, shards, reps = in_sems.shape
    slabs = [(g, k) for g in range(groups) for k in range(shards)]

    def load(g, k, r):
        return pltpu.make_async_copy(
            source_of(g, k, r), held.at[g, k, place_of(r)], in_sems.at[g, k, r]
        )

    def store(g, k):
        return pltpu.make_async_copy(held.at[g, k], outs[g].at[order_ref[k]], out_sems.at[g, k])

    for g, k in slabs:
        for r in range(reps):
            load(g, k, r).start()
    for g, k in slabs:
        for r in range(reps):
            load(g, k, r).wait()
        store(g, k).start()
    for g, k in slabs:
        store(g, k).wait()


def blocks_call(body, scalars, sources, groups, shards, reps, block):
    whole = (shards, reps) + block
    return pl.pallas_call(
        body,
        out_shape=[jax.ShapeDtypeStruct(whole, jnp.bfloat16)] * groups,
        in_specs=[pl.BlockSpec(memory_space=pltpu.SMEM)] * scalars
        + [pl.BlockSpec(memory_space=pl.ANY)] * sources,
        out_specs=[pl.BlockSpec(memory_space=pl.ANY)] * groups,
        scratch_shapes=[
            pltpu.VMEM((groups,) + whole, jnp.bfloat16),
            pltpu.SemaphoreType.DMA((groups, shards, reps)),
            pltpu.SemaphoreType.DMA((groups, shards)),
        ],
        compiler_params=pltpu.CompilerParams(vmem_limit_bytes=VMEM_LIMIT),
        cost_estimate=COST,
        name="place_blocks",
    )


def widen_pieces(places, pieces, others):
    half, rows, columns = pieces.shape
    reps = 2 * half
    strip = next(size for size in (16, 8, rows) if rows % size == 0)

    def body(places_ref, pieces_ref, others_ref, out_ref, narrow, wide, in_sems, out_sems):
        loads = [
            pltpu.make_async_copy(
                (pieces_ref if r < half else others_ref).at[r % half], narrow.at[r], in_sems.at[r]
            )
            for r in range(reps)
        ]
        stores = [
            pltpu.make_async_copy(wide.at[r], out_ref.at[places_ref[r]], out_sems.at[r])
            for r in range(reps)
        ]
        for load in loads:
            load.start()
        for r in range(reps):
            loads[r].wait()

            def convert(at, carry):
                cut = pl.ds(pl.multiple_of(at * strip, strip), strip)
                wide[r, cut, :] = narrow[r, cut, :].astype(jnp.float32)
                return carry

            lax.fori_loop(0, rows // strip, convert, 0)
            stores[r].start()
        for store in stores:
            store.wait()

    result = pl.pallas_call(
        body,
        out_shape=jax.ShapeDtypeStruct((reps, rows, columns), jnp.float32),
        in_specs=[pl.BlockSpec(memory_space=pltpu.SMEM)]
        + [pl.BlockSpec(memory_space=pl.ANY)] * 2,
        out_specs=pl.BlockSpec(memory_space=pl.ANY),
        scratch_shapes=[
            pltpu.VMEM((reps, rows, columns), jnp.bfloat16),
            pltpu.VMEM((reps, rows, columns), jnp.float32),
            pltpu.SemaphoreType.DMA((reps,)),
            pltpu.SemaphoreType.DMA((reps,)),
        ],
        compiler_params=pltpu.CompilerParams(vmem_limit_bytes=VMEM_LIMIT),
        cost_estimate=COST,
        name="widen_pieces",
    )(places, pieces, others)
    return (result.reshape(reps * rows, columns),)


def resident(shape):
    return pl.BlockSpec(shape, lambda i: (0, 0), pipeline_mode=pl.Buffered(1))


def feed_forward(rows, cotangents, gate_matrix, up_matrix, down_matrix):
    count, width = rows.shape
    units = gate_matrix.shape[1]
    steps = pl.cdiv(units, TILE)
    slabs = next(size for size in range(min(steps, width // 128), 0, -1) if width % (128 * size) == 0)
    slab = width // slabs

    def body(
        rows_ref,
        cotangents_ref,
        gate_ref,
        up_ref,
        down_ref,
        inner_ref,
        d_gate_ref,
        d_up_ref,
        turned_rows_ref,
        turned_inner_ref,
    ):
        gate = jnp.dot(rows_ref[...], gate_ref[...], preferred_element_type=jnp.float32)
        up = jnp.dot(rows_ref[...], up_ref[...], preferred_element_type=jnp.float32)
        sigmoid = jax.nn.sigmoid(gate)
        silu = gate * sigmoid
        inner = (silu * up).astype(jnp.bfloat16)
        inner_ref[...] = inner
        turned_inner_ref[...] = inner.T
        d_inner = times_transposed(cotangents_ref[...], down_ref[...])
        d_up_ref[...] = (d_inner * silu).astype(jnp.bfloat16)
        d_gate_ref[...] = (d_inner * up * sigmoid * (1.0 + gate * (1.0 - sigmoid))).astype(
            jnp.bfloat16
        )
        for step in range(slabs):

            @pl.when(pl.program_id(0) == step)
            def turn():
                turned_rows_ref[...] = rows_ref[:, step * slab : (step + 1) * slab].T

    columns = pl.BlockSpec((width, TILE), lambda i: (0, i))
    results = pl.BlockSpec((count, TILE), lambda i: (0, i))
    return pl.pallas_call(
        body,
        grid=(steps,),
        out_shape=[jax.ShapeDtypeStruct((count, units), jnp.bfloat16)] * 3
        + [
            jax.ShapeDtypeStruct((width, count), jnp.bfloat16),
            jax.ShapeDtypeStruct((units, count), jnp.bfloat16),
        ],
        in_specs=[
            resident((count, width)),
            resident((count, width)),
            columns,
            columns,
            pl.BlockSpec((TILE, width), lambda i: (i, 0)),
        ],
        out_specs=[results] * 3
        + [
            pl.BlockSpec((slab, count), lambda i: (jnp.minimum(i, slabs - 1), 0)),
            pl.BlockSpec((TILE, count), lambda i: (i, 0)),
        ],
        compiler_params=pltpu.CompilerParams(vmem_limit_bytes=VMEM_LIMIT),
        cost_estimate=COST,
        name="feed_forward",
    )(rows, cotangents, gate_matrix, up_matrix, down_matrix)


def split_gradient(left, right, groups, places, core_place, turned):
    rows, count = left.shape if turned else left.shape[::-1]
    columns = right.shape[1]
    half = rows // (2 * groups)
    part = half // places

    def body(core_ref, left_ref, right_ref, other_ref, own_ref, *scratch):
        if turned:
            rows_ref = left_ref
        else:
            (rows_ref,) = scratch

            @pl.when(pl.program_id(0) == 0)
            def turn():
                rows_ref[...] = left_ref[...].T

        core = core_ref[0]
        for out_ref, which in ((other_ref, 1 - core), (own_ref, core)):
            halves = [
                rows_ref[pl.ds(pl.multiple_of((2 * group + which) * half, 16), half), :]
                for group in range(groups)
            ]
            product = jnp.dot(
                jnp.concatenate(halves, axis=0), right_ref[...], preferred_element_type=jnp.float32
            )
            for group in range(groups):
                for place in range(places):
                    at = group * half + place * part
                    out_ref[place, group] = product[at : at + part].astype(jnp.bfloat16)

    return pl.pallas_call(
        body,
        grid=(pl.cdiv(columns, TILE),),
        out_shape=[jax.ShapeDtypeStruct((places, groups, part, columns), jnp.bfloat16)] * 2,
        in_specs=[
            pl.BlockSpec(memory_space=pltpu.SMEM),
            resident(left.shape),
            pl.BlockSpec((count, TILE), lambda i: (0, i)),
        ],
        out_specs=[pl.BlockSpec((places, groups, part, TILE), lambda i: (0, 0, 0, i))] * 2,
        scratch_shapes=[] if turned else [pltpu.VMEM((rows, count), jnp.bfloat16)],
        compiler_params=pltpu.CompilerParams(vmem_limit_bytes=VMEM_LIMIT),
        cost_estimate=COST,
        name="split_gradient",
    )(core_place.reshape(1).astype(jnp.int32), left, right)


def ordered_gradient(left, right, shards, order):
    reps = len(order)
    rows, count = left.shape
    columns = right.shape[1]
    part = rows // (shards * reps)

    def body(left_ref, right_ref, out_ref):
        product = jnp.dot(left_ref[...], right_ref[...], preferred_element_type=jnp.float32)
        for z in range(shards):
            for r in range(reps):
                at = (z * reps + order[r]) * part
                out_ref[r, z] = product[at : at + part].astype(jnp.bfloat16)

    return pl.pallas_call(
        body,
        grid=(pl.cdiv(columns, TILE),),
        out_shape=[jax.ShapeDtypeStruct((reps, shards, part, columns), jnp.bfloat16)],
        in_specs=[
            resident((rows, count)),
            pl.BlockSpec((count, TILE), lambda i: (0, i)),
        ],
        out_specs=[pl.BlockSpec((reps, shards, part, TILE), lambda i: (0, 0, 0, i))],
        compiler_params=pltpu.CompilerParams(vmem_limit_bytes=VMEM_LIMIT),
        cost_estimate=COST,
        name="ordered_gradient",
    )(left, right)


def rows_product(lefts, rights, turned, blocks):
    count, depth = lefts[0].shape
    columns = rights[0].shape[0 if turned else 1]
    pairs, part = len(lefts), count // blocks

    def body(*refs):
        total = None
        for left_ref, right_ref in zip(refs[:pairs], refs[pairs : 2 * pairs]):
            if turned:
                product = times_transposed(left_ref[...], right_ref[...])
            else:
                product = jnp.dot(
                    left_ref[...], right_ref[...], preferred_element_type=jnp.float32
                )
            total = product if total is None else total + product
        for block in range(blocks):
            refs[2 * pairs + block][...] = total[block * part : (block + 1) * part].astype(
                jnp.bfloat16
            )

    right_spec = (
        pl.BlockSpec((TILE, depth), lambda i: (i, 0))
        if turned
        else pl.BlockSpec((depth, TILE), lambda i: (0, i))
    )
    return pl.pallas_call(
        body,
        grid=(pl.cdiv(columns, TILE),),
        out_shape=[jax.ShapeDtypeStruct((part, columns), jnp.bfloat16)] * blocks,
        in_specs=[resident((count, depth))] * pairs + [right_spec] * pairs,
        out_specs=[pl.BlockSpec((part, TILE), lambda i: (0, i))] * blocks,
        compiler_params=pltpu.CompilerParams(vmem_limit_bytes=VMEM_LIMIT),
        cost_estimate=COST,
        name="rows_product",
    )(*lefts, *rights)


def kept_bias(row_segments, row_index, key_segments, key_index):
    kept = (row_segments == key_segments) & (key_index <= row_index)
    return jnp.where(kept, 0.0, MASKED)


def in_vmem(count):
    return [pl.BlockSpec(memory_space=pltpu.VMEM)] * count


def attention_forward(projected, cosine, signed_sine, pairs, rows, keys):
    count = projected.shape[0]
    per_group = QH // KVH
    scale = 1.0 / math.sqrt(HD)
    shape = (KVH, per_group * count, HD)

    def body(projected_ref, cosine_ref, sine_ref, pairs_ref, rows_ref, keys_ref, queries_ref, out_ref):
        bias = kept_bias(rows_ref[:, 0:1], rows_ref[:, 1:2], keys_ref[0:1, :], keys_ref[1:2, :])
        for k in range(KVH):
            for h in range(per_group):
                at = (k * per_group + h) * HD
                field = projected_ref[:, at : at + HD]
                queries_ref[k, h * count : (h + 1) * count, :] = (
                    field * cosine_ref[...] + pltpu.roll(field, HD // 2, 1) * sine_ref[...]
                ).astype(jnp.bfloat16)
            keys_here = pairs_ref[:, k * HD : (k + 1) * HD]
            values_here = pairs_ref[:, (KVH + k) * HD : (KVH + k + 1) * HD]
            scores = times_transposed(queries_ref[k], keys_here) * scale + bias
            powers = jnp.exp(scores - jnp.max(scores, axis=1, keepdims=True))
            shares = powers * (1.0 / jnp.sum(powers, axis=1, keepdims=True))
            result = jnp.dot(
                shares.astype(jnp.bfloat16), values_here, preferred_element_type=jnp.float32
            ).astype(jnp.bfloat16)
            for h in range(per_group):
                at = (k * per_group + h) * HD
                out_ref[:, at : at + HD] = result[h * count : (h + 1) * count]

    return pl.pallas_call(
        body,
        out_shape=[
            jax.ShapeDtypeStruct(shape, jnp.bfloat16),
            jax.ShapeDtypeStruct((count, QH * HD), jnp.bfloat16),
        ],
        in_specs=in_vmem(6),
        out_specs=in_vmem(2),
        compiler_params=pltpu.CompilerParams(vmem_limit_bytes=VMEM_LIMIT),
        cost_estimate=COST,
        name="attention_forward",
    )(projected, cosine, signed_sine, pairs, rows, keys)


def attention_backward(queries, gradient, pairs, cosine, signed_sine, rows, keys, blocks):
    count = gradient.shape[0]
    per_group = QH // KVH
    scale = 1.0 / math.sqrt(HD)
    group_rows = pairs.shape[0]
    part = group_rows // blocks

    def body(queries_ref, gradient_ref, pairs_ref, cosine_ref, sine_ref, rows_ref, keys_ref, d_ref, *outs):
        block_refs, stacked = outs[:blocks], outs[blocks]
        bias = kept_bias(rows_ref[0:1, :], rows_ref[1:2, :], keys_ref[:, 0:1], keys_ref[:, 1:2])
        for k in range(KVH):
            for h in range(per_group):
                at = (k * per_group + h) * HD
                stacked[h * count : (h + 1) * count, :] = gradient_ref[:, at : at + HD]
            keys_here = pairs_ref[:, k * HD : (k + 1) * HD]
            values_here = pairs_ref[:, (KVH + k) * HD : (KVH + k + 1) * HD]
            scores = times_transposed(keys_here, queries_ref[k]) * scale + bias
            powers = jnp.exp(scores - jnp.max(scores, axis=0, keepdims=True))
            shares = powers * (1.0 / jnp.sum(powers, axis=0, keepdims=True))
            d_shares = times_transposed(values_here, stacked[...])
            dots = jnp.sum(shares * d_shares, axis=0, keepdims=True)
            d_scores = (shares * (d_shares - dots)).astype(jnp.bfloat16)
            d_keys = jnp.dot(d_scores, queries_ref[k], preferred_element_type=jnp.float32) * scale
            d_values = jnp.dot(
                shares.astype(jnp.bfloat16), stacked[...], preferred_element_type=jnp.float32
            )
            for block in range(blocks):
                cut = slice(block * part, (block + 1) * part)
                block_refs[block][:, k * HD : (k + 1) * HD] = d_keys[cut].astype(jnp.bfloat16)
                block_refs[block][:, (KVH + k) * HD : (KVH + k + 1) * HD] = d_values[cut].astype(
                    jnp.bfloat16
                )
            d_queries = transposed_times(d_scores, keys_here) * scale
            for h in range(per_group):
                at = (k * per_group + h) * HD
                field = d_queries[h * count : (h + 1) * count]
                d_ref[:, at : at + HD] = (
                    field * cosine_ref[...] - pltpu.roll(field, HD // 2, 1) * sine_ref[...]
                ).astype(jnp.bfloat16)

    return pl.pallas_call(
        body,
        out_shape=[jax.ShapeDtypeStruct((count, QH * HD), jnp.bfloat16)]
        + [jax.ShapeDtypeStruct((part, 2 * KVH * HD), jnp.bfloat16)] * blocks,
        in_specs=in_vmem(7),
        out_specs=in_vmem(1 + blocks),
        scratch_shapes=[pltpu.VMEM((per_group * count, HD), jnp.bfloat16)],
        compiler_params=pltpu.CompilerParams(vmem_limit_bytes=VMEM_LIMIT),
        cost_estimate=COST,
        name="attention_backward",
    )(queries, gradient, pairs, cosine, signed_sine, rows, keys)


def join_projected(d_queries, pair_terms, cosine, signed_sine):
    count, query_width = d_queries.shape
    pair_width = KVH * HD
    terms = len(pair_terms)

    def body(d_queries_ref, cosine_ref, sine_ref, *refs):
        term_refs, out_ref, sum_ref = refs[:terms], refs[terms], refs[terms + 1]
        out_ref[:, :query_width] = d_queries_ref[...]
        for at in range(0, 2 * pair_width, HD):
            field = total_of([term[:, at : at + HD] for term in term_refs])
            if at < pair_width:
                field = field * cosine_ref[...] - pltpu.roll(field, HD // 2, 1) * sine_ref[...]
            out_ref[:, query_width + at : query_width + at + HD] = field.astype(jnp.bfloat16)
        sum_ref[...] = jnp.sum(out_ref[...].astype(jnp.float32), axis=0, keepdims=True)

    return pl.pallas_call(
        body,
        out_shape=[
            jax.ShapeDtypeStruct((count, query_width + 2 * pair_width), jnp.bfloat16),
            jax.ShapeDtypeStruct((1, query_width + 2 * pair_width), jnp.float32),
        ],
        in_specs=in_vmem(3 + terms),
        out_specs=in_vmem(2),
        cost_estimate=COST,
        name="join_projected",
    )(d_queries, cosine, signed_sine, *pair_terms)


def on_device(
    tokens,
    segment_ids,
    first_gain,
    input_weight,
    input_bias,
    output_weight,
    second_gain,
    gate_weight,
    up_weight,
    down_weight,
    output_cotangent,
):
    bf16, f32 = jnp.bfloat16, jnp.float32
    shards, reps = lax.axis_size("shard"), lax.axis_size("rep")
    shard, core, first, second = make_lines(reps, shards)
    rep_place = (core.place * first.size + first.place) * second.size + second.place
    own_rows, width = tokens.shape
    segments = segment_ids[0]
    per_group = QH // KVH
    query_width = QH * HD
    pair_width = KVH * HD
    first_row = shard.place * own_rows
    part_rows = input_weight.shape[0] // reps
    hidden_units = gate_weight.shape[1]
    block_units = hidden_units // shards
    clock = Clock()
    z_order = jnp.stack([shard.behind(step) for step in range(shards)]).astype(jnp.int32)

    def weight_piece(weight, place):
        return pick(weight.reshape(reps, part_rows, weight.shape[1]), place, 0)

    def spread(piece):
        return Spread(clock, piece, core, first, second)

    def blocks_of(blocks):
        return [pick(blocks, shard.ahead(step), 0) for step in range(shards)]

    steps = range(1, shards)

    def send_blocks(blocks):
        return clock.send(shard, blocks[1:], steps)

    def send_around(value):
        return clock.send(shard, [value] * len(steps), steps)

    def send_back(rows):
        return clock.send(shard, rows, [shards - step for step in steps])

    rep_index = lax.axis_index("rep")
    input_matrix = lax.all_gather(
        weight_piece(input_weight, rep_index), ("shard", "rep"), axis=0, tiled=True
    )
    shard_vectors = jnp.concatenate([first_gain, second_gain, input_bias])
    vector_row = jnp.pad(shard_vectors, (0, output_weight.shape[1] - shard_vectors.shape[0]))
    own_output = jnp.concatenate(
        [weight_piece(output_weight, rep_place), vector_row[None]], axis=0
    )
    output_moving = send_around(own_output)
    gate_blocks, up_blocks = clock.run(
        lambda *weights: column_blocks(rep_index, shard.place, *weights),
        gate_weight.reshape(reps, part_rows, hidden_units),
        up_weight.reshape(reps, part_rows, hidden_units),
    )
    (output_rows,) = clock.wait(output_moving)
    output_rows = [own_output] + output_rows

    output_spread = spread(jnp.stack([rows[:part_rows] for rows in output_rows])[None])
    gate_moving = send_blocks(gate_blocks)
    vector_rows = jnp.stack(in_place_order([rows[part_rows] for rows in output_rows], shard))
    own_gain = first_gain.shape[0]
    gain_one = vector_rows[:, :own_gain].reshape(width).astype(f32)
    gain_two = vector_rows[:, own_gain : 2 * own_gain].reshape(width).astype(f32)
    shift_row = (
        vector_rows[:, 2 * own_gain : shard_vectors.shape[0]].reshape(-1).astype(f32)
    )
    places = positions(segments)
    cosine_table, sine_table = rope_tables(
        lax.dynamic_slice_in_dim(places, first_row, own_rows), HD
    )
    signed_sine = jnp.concatenate(
        [-sine_table[:, : HD // 2], sine_table[:, HD // 2 :]], axis=1
    )
    own_segments = lax.dynamic_slice_in_dim(segments, first_row, own_rows)
    row_index = jnp.arange(own_rows, dtype=jnp.int32)
    key_index = jnp.concatenate([shard.behind(step) * own_rows + row_index for step in range(shards)])
    key_segments = jnp.concatenate(
        [
            lax.dynamic_slice_in_dim(segments, shard.behind(step) * own_rows, own_rows)
            for step in range(shards)
        ]
    )
    key_marks = jnp.stack([key_segments, key_index])
    row_marks = jnp.tile(jnp.stack([own_segments, first_row + row_index]), (1, per_group))
    wide_tokens = tokens.astype(f32)
    inverse_one = lax.rsqrt(jnp.mean(wide_tokens * wide_tokens, axis=-1, keepdims=True) + EPSILON)
    unit_one = wide_tokens * inverse_one
    normed_one = (unit_one * gain_one).astype(bf16)
    (
        normed_one,
        cosine_table,
        sine_table,
        signed_sine,
        key_marks,
        row_marks,
    ) = clock(normed_one, cosine_table, sine_table, signed_sine, key_marks, row_marks)
    output_arrived, gate_rows = clock.wait(output_spread.moving, gate_moving)

    output_spread.along(output_arrived)
    up_moving = send_blocks(up_blocks)
    output_arrived, up_rows = clock.wait(output_spread.moving, up_moving)

    gate_up = jnp.stack(
        [jnp.stack([gate_blocks[0]] + gate_rows), jnp.stack([up_blocks[0]] + up_rows)], axis=1
    )
    gate_up = lax.all_gather(clock(gate_up)[0][None], "rep", axis=0, tiled=True)
    passed = [[output_cotangent] * 2]
    output_spread.over(output_arrived)
    passing = clock.pass_on(shard, *passed[-1])
    output_arrived, arrived = clock.wait(output_spread.moving, passing)
    passed.append(arrived)

    passing = clock.pass_on(shard, *passed[-1]) if shards > 2 else []
    (output_matrix,) = clock.run(place_blocks, z_order, *output_spread.finish(output_arrived))
    output_matrix = output_matrix.reshape(width, width)
    input_matrix, normed_one = clock(input_matrix, normed_one)
    projected = jnp.dot(normed_one, input_matrix, preferred_element_type=f32) + shift_row
    key_part = rotate(
        projected[:, query_width : query_width + pair_width].reshape(own_rows, KVH, HD),
        cosine_table,
        sine_table,
    )
    (own_pairs,) = clock(
        jnp.concatenate(
            [key_part.reshape(own_rows, pair_width), projected[:, query_width + pair_width :]],
            axis=1,
        ).astype(bf16)
    )
    (arrived,) = clock.wait(passing)
    passed.append(arrived)

    (pair_rows,) = clock.wait(send_around(own_pairs))
    pairs = jnp.concatenate([own_pairs] + pair_rows, axis=0)

    passing = clock.pass_on(shard, *passed[-1]) if shards > 3 else []
    queries, attention_low = clock.run(
        attention_forward, projected, cosine_table, signed_sine, pairs, row_marks.T, key_marks
    )
    hidden = wide_tokens + jnp.dot(attention_low, output_matrix, preferred_element_type=f32)
    inverse_two = lax.rsqrt(jnp.mean(hidden * hidden, axis=-1, keepdims=True) + EPSILON)
    unit_two = hidden * inverse_two
    (normed_two,) = clock((unit_two * gain_two).astype(bf16))
    (arrived,) = clock.wait(passing)
    passed.append(arrived)

    normed_moving = send_around(normed_two)
    gate_matrix, up_matrix = clock.run(place_gathered, z_order, gate_up)
    gate_matrix = gate_matrix.reshape(width, block_units)
    up_matrix = up_matrix.reshape(width, block_units)
    (normed_arrived,) = clock.wait(normed_moving)
    while len(passed) < shards:
        (arrived,) = clock.wait(clock.pass_on(shard, *passed[-1]))
        passed.append(arrived)
    group_normed = jnp.concatenate([normed_two] + normed_arrived, axis=0)
    cotangents = jnp.concatenate(
        [output_cotangent]
        + [
            jnp.where(shard.place >= step, passed[step][0], passed[shards - step][1])
            for step in steps
        ],
        axis=0,
    )

    inner_act, d_gate, d_up, turned_normed, turned_inner = clock.run(
        feed_forward, group_normed, cotangents, gate_matrix, up_matrix, down_weight
    )

    def split_halves(left, right, groups, turned):
        count = first.size * second.size
        halves = clock.run(
            lambda left, right: split_gradient(left, right, groups, count, core.place, turned),
            left,
            right,
        )
        return [half.reshape((first.size, second.size) + half.shape[1:]) for half in halves]

    def side_by_side(rows):
        return clock(jnp.concatenate(in_place_order(rows, shard), axis=1))[0]

    def sum_over_rep(blocks):
        return lax.psum_scatter(blocks, "rep", scatter_dimension=0, tiled=True)

    def row_sum(own, arrived):
        return clock(total_of(own + arrived).astype(bf16))[0]

    def send_some(rows, chosen):
        return clock.send(shard, [rows[k] for k in chosen], [shards - 1 - k for k in chosen])

    edges = sorted({0, shards - 2})
    inside = list(range(1, shards - 2))

    normed_own, *normed_partial = clock.run(
        lambda *operands: rows_product(operands[:2], operands[2:], True, shards),
        d_gate,
        d_up,
        gate_matrix,
        up_matrix,
    )

    normed_moving = send_some(normed_partial, edges)
    (down_blocks,) = clock.run(
        lambda left, right: ordered_gradient(left, right, 1, list(range(reps))),
        turned_inner,
        cotangents,
    )
    down_piece = sum_over_rep(down_blocks.reshape(block_units, width))
    up_halves = split_halves(turned_normed, d_up, shards, True)
    (normed_arrived,) = clock.wait(normed_moving)

    normed_moving = send_some(normed_partial, inside)
    up = Halving(clock, *up_halves, core, first, second)
    (gate_blocks,) = clock.run(
        lambda left, right: ordered_gradient(left, right, shards, rep_places(reps)),
        turned_normed,
        d_gate,
    )
    gate_piece = sum_over_rep(gate_blocks.reshape(width, block_units))
    block_own, *block_partial = clock.run(
        lambda left, right: rows_product((left,), (right,), False, shards), inner_act, down_weight
    )
    more_arrived, up_arrived = clock.wait(normed_moving, up.moving)

    up.along_first(up_arrived)
    block_moving = send_some(block_partial, inside)
    normed_two_gradient = total_of([normed_own] + normed_arrived + more_arrived)
    gain_two_gradient = jnp.sum(normed_two_gradient * unit_two, axis=0)
    hidden_gradient = output_cotangent.astype(f32) + norm_back(
        normed_two_gradient, unit_two, inverse_two, gain_two
    )
    (branch_gradient,) = clock(hidden_gradient.astype(bf16))
    (attention_gradient,) = clock(times_transposed(branch_gradient, output_matrix).astype(bf16))
    d_queries, pair_own, *pair_partial = clock.run(
        lambda *operands: attention_backward(*operands, shards),
        queries,
        attention_gradient,
        pairs,
        cosine_table,
        signed_sine,
        row_marks,
        key_marks.T,
    )
    output_halves = split_halves(attention_low, branch_gradient, shards, False)
    up_arrived, block_arrived = clock.wait(up.moving, block_moving)

    pair_moving = send_back(pair_partial)
    output = Halving(clock, *output_halves, core, first, second)
    pair_arrived, output_arrived = clock.wait(pair_moving, output.moving)

    up.along_second(up_arrived)
    output.along_first(output_arrived)
    block_moving = send_some(block_partial, edges[:1])
    projected_gradient, bias_sum = clock.run(
        lambda *operands: join_projected(operands[0], operands[3:], *operands[1:3]),
        d_queries,
        cosine_table,
        signed_sine,
        pair_own,
        *pair_arrived,
    )
    projected_halves = split_halves(normed_one, projected_gradient, shards, False)
    up_arrived, output_arrived, more_arrived = clock.wait(up.moving, output.moving, block_moving)
    block_arrived = block_arrived + more_arrived

    projected = Halving(clock, *projected_halves, core, first, second)
    output.along_second(output_arrived)
    block_moving = send_some(block_partial, edges[1:])
    (down_piece,) = clock(down_piece)
    down_gathered = lax.all_gather(down_piece, "rep", axis=0, tiled=True)
    up_blocks = clock(*blocks_of(up.finish(up_arrived)))
    projected_gradient, hidden_gradient = clock(projected_gradient, hidden_gradient)
    normed_one_gradient = times_transposed(projected_gradient, input_matrix)
    gain_one_gradient = jnp.sum(normed_one_gradient * unit_one, axis=0)
    (tokens_gradient,) = clock(
        (
            hidden_gradient + norm_back(normed_one_gradient, unit_one, inverse_one, gain_one)
        ).astype(bf16)
    )
    projected_arrived, output_arrived, more_arrived = clock.wait(
        projected.moving, output.moving, block_moving
    )
    block_arrived = block_arrived + more_arrived

    projected.along_first(projected_arrived)
    up_moving = send_blocks(up_blocks)
    output_blocks = clock(*blocks_of(output.finish(output_arrived)))
    (block_out,) = clock(total_of([hidden, block_own] + block_arrived).astype(bf16))
    bias_gradient = bias_sum[0]
    bias_split = query_width + pair_width
    small_parts = (
        gain_one_gradient,
        gain_two_gradient,
        bias_gradient[:bias_split],
        bias_gradient[bias_split:],
    )
    (small,) = clock(
        jnp.concatenate([part.reshape(shards, -1) for part in small_parts], axis=1)
    )
    projected_arrived, up_rows = clock.wait(projected.moving, up_moving)

    projected.along_second(projected_arrived)
    output_moving = send_blocks(output_blocks)
    up_spread = spread(side_by_side(up_blocks[:1] + up_rows))
    projected_arrived, output_rows, up_arrived = clock.wait(
        projected.moving, output_moving, up_spread.moving
    )

    (gate_piece,) = clock(gate_piece)
    gate_blocks = clock(*blocks_of(gate_piece.reshape(shards, part_rows, block_units)))
    gate_moving = send_blocks(gate_blocks)
    up_spread.along(up_arrived)
    output_spread = spread(row_sum(output_blocks[:1], output_rows))
    input_blocks = clock(*blocks_of(projected.finish(projected_arrived)))
    gate_rows, up_arrived, output_arrived = clock.wait(
        gate_moving, up_spread.moving, output_spread.moving
    )

    input_moving = send_blocks(input_blocks)
    gate_spread = spread(side_by_side(gate_blocks[:1] + gate_rows))
    output_spread.along(output_arrived)
    input_rows, gate_arrived, output_arrived = clock.wait(
        input_moving, gate_spread.moving, output_spread.moving
    )

    gate_spread.along(gate_arrived)
    input_spread = spread(row_sum(input_blocks[:1], input_rows))
    up_spread.over(up_arrived)
    output_spread.over(output_arrived)
    small_moving = clock.send(core, [small], [1])
    gate_arrived, input_arrived, up_arrived, output_arrived, small_arrived = clock.wait(
        gate_spread.moving, input_spread.moving, up_spread.moving, output_spread.moving, small_moving
    )
    small = total_of([small] + small_arrived)

    input_spread.along(input_arrived)
    gate_spread.over(gate_arrived)
    small_moving = clock.send(first, [small] * (first.size - 1), range(1, first.size))
    (up_total,) = clock.run(widen_pieces, *up_spread.finish(up_arrived))
    (output_total,) = clock.run(widen_pieces, *output_spread.finish(output_arrived))
    input_arrived, gate_arrived, small_arrived = clock.wait(
        input_spread.moving, gate_spread.moving, small_moving
    )
    small = total_of([small] + small_arrived)

    input_spread.over(input_arrived)
    small_moving = clock.send(second, [small] * (second.size - 1), range(1, second.size))
    (gate_total,) = clock.run(widen_pieces, *gate_spread.finish(gate_arrived))
    input_arrived, small_arrived = clock.wait(input_spread.moving, small_moving)
    small_blocks = clock(*blocks_of(total_of([small] + small_arrived)))

    small_moving = send_blocks(small_blocks)
    (input_total,) = clock.run(widen_pieces, *input_spread.finish(input_arrived))
    (down_gathered,) = clock(down_gathered)
    (down_total,) = clock(down_gathered.astype(f32))
    (small_arrived,) = clock.wait(small_moving)
    small = total_of(small_blocks[:1] + small_arrived)

    small = small + clock.token[0, 0]
    small_totals, at = [], 0
    for part in small_parts:
        size = part.shape[0] // shards
        small_totals.append(small[at : at + size])
        at += size
    return (
        block_out,
        tokens_gradient,
        small_totals[0],
        input_total,
        small_totals[2],
        small_totals[3],
        output_total,
        small_totals[1],
        gate_total,
        up_total,
        down_total,
    )


def solution(mesh):
    placed = (
        P(("rep", "shard"), None),
        P("rep", None),
        P("shard"),
        P("shard", None),
        P("shard"),
        P("shard", None),
        P("shard"),
        P("shard", None),
        P("shard", None),
        P("shard", None),
        P(("rep", "shard"), None),
    )
    return jax.shard_map(
        on_device,
        mesh=mesh,
        in_specs=placed,
        out_specs=(
            P(("rep", "shard"), None),
            P(("rep", "shard"), None),
            P("shard"),
            P("shard", None),
            P("shard"),
            P("shard"),
            P("shard", None),
            P("shard"),
            P("shard", None),
            P("shard", None),
            P("shard", None),
        ),
        check_vma=False,
    )
```

```python
import math

import jax
import jax.numpy as jnp
from jax import lax
from jax.experimental import pallas as pl
from jax.experimental.pallas import tpu as pltpu
from jax.sharding import PartitionSpec as P

QH = 12
KVH = 2
HD = 128
SEQS = 3


EPSILON = 1e-06
LOG_THETA = math.log(1000000.0)
MASKED = -1e30
VMEM_LIMIT = 56 * 1024 * 1024
TILE = 512
COST = pl.CostEstimate(flops=1, bytes_accessed=1, transcendentals=0)


def rope_tables(places, head_width):
    half_width = head_width // 2
    frequency = jnp.exp(jnp.arange(half_width, dtype=jnp.float32) * (-2.0 * LOG_THETA / head_width))
    angles = places.astype(jnp.float32)[:, None] * frequency[None, :]
    angles = jnp.concatenate([angles, angles], axis=-1)
    return (jnp.cos(angles), jnp.sin(angles))


def positions(segments):
    labels = jnp.arange(SEQS, dtype=jnp.int32)
    starts = jnp.sum((segments[None, :] < labels[:, None]).astype(jnp.int32), axis=1)
    own_start = jnp.sum(jnp.where(segments[:, None] == labels[None, :], starts[None, :], 0), axis=1)
    return jnp.arange(segments.shape[0], dtype=jnp.int32) - own_start


def rotate(field_rows, cosine_table, sine_table):
    half_width = field_rows.shape[-1] // 2
    turned = jnp.concatenate([-field_rows[..., half_width:], field_rows[..., :half_width]], axis=-1)
    return field_rows * cosine_table[:, None, :] + turned * sine_table[:, None, :]


def transposed_times(left_side, right_side):
    return lax.dot_general(
        left_side, right_side, (((0,), (0,)), ((), ())), preferred_element_type=jnp.float32
    )


def times_transposed(left_side, right_side):
    return lax.dot_general(
        left_side, right_side, (((1,), (1,)), ((), ())), preferred_element_type=jnp.float32
    )


def norm_back(normed_gradient, unit_rows, inverse_rms, gain_row):
    scaled = normed_gradient * gain_row
    return inverse_rms * (scaled - unit_rows * jnp.mean(scaled * unit_rows, axis=-1, keepdims=True))


class Line:
    def __init__(self, name, size, place, pairs, crossed=False):
        self.name, self.size, self.place, self.pairs = name, size, place, pairs
        self.crossed = crossed

    def shift(self, value, step):
        return lax.ppermute(value, self.name, self.pairs(step % self.size))

    def pass_on(self, value, up):
        places = range(self.size - 1)
        pairs = [(at, at + 1) if up else (at + 1, at) for at in places]
        return lax.ppermute(value, self.name, pairs)

    def behind(self, step):
        return lax.rem(self.place + (self.size - step % self.size), self.size)

    def ahead(self, step):
        return lax.rem(self.place + step % self.size, self.size) if step else self.place


def make_lines(reps, shards):
    inner = 2 if reps % 4 == 0 else 1
    outer = reps // (2 * inner)
    square = inner == outer

    def split(index):
        core, b, a = index % 2, (index // 2) % inner, index // (2 * inner)
        return core, b, a

    def join(core, b, a):
        return (a * inner + b) * 2 + core

    def first_pairs(step):
        pairs = []
        for index in range(reps):
            core, b, a = split(index)
            if square and core == 0:
                pairs.append((index, join(core, (b + step) % inner, a)))
            else:
                pairs.append((index, join(core, b, (a + step) % outer)))
        return pairs

    def second_pairs(step):
        pairs = []
        for index in range(reps):
            core, b, a = split(index)
            if square and core == 0:
                pairs.append((index, join(core, b, (a + step) % outer)))
            else:
                pairs.append((index, join(core, (b + step) % inner, a)))
        return pairs

    def core_pairs(step):
        pairs = []
        for index in range(reps):
            core, b, a = split(index)
            pairs.append((index, join((core + step) % 2, b, a)))
        return pairs

    def shard_pairs(step):
        return [(index, (index + step) % shards) for index in range(shards)]

    core, b, a = split(lax.axis_index("rep"))
    first, second = (jnp.where(core == 0, b, a), jnp.where(core == 0, a, b)) if square else (a, b)
    return (
        Line("shard", shards, lax.axis_index("shard"), shard_pairs),
        Line("rep", 2, core, core_pairs, square),
        Line("rep", outer, first, first_pairs),
        Line("rep", inner, second, second_pairs),
    )


def rep_places(reps):
    inner = 2 if reps % 4 == 0 else 1
    outer = reps // (2 * inner)
    places = []
    for index in range(reps):
        core, b, a = index % 2, (index // 2) % inner, index // (2 * inner)
        one, two = (b, a) if inner == outer and core == 0 else (a, b)
        places.append((core * outer + one) * inner + two)
    return places


def pick(array, index, axis):
    return lax.dynamic_index_in_dim(array, index, axis, keepdims=False)


def put(array, piece, index, axis):
    return lax.dynamic_update_index_in_dim(array, piece, index, axis)


def in_place_order(pieces, line):
    ordered = []
    for place in range(line.size):
        chosen = pieces[0]
        for step in range(1, line.size):
            chosen = jnp.where(line.behind(step) == place, pieces[step], chosen)
        ordered.append(chosen)
    return ordered


def tie(*arrays):
    return lax.optimization_barrier(arrays)


def gather_line(value, line):
    return [value] + [line.shift(value, step) for step in range(1, line.size)]


class Clock:
    def __init__(self):
        self.token = jnp.zeros((8, 128), jnp.float32)
        self.open = 0

    def __call__(self, *arrays):
        self.token, *arrays = tie(self.token, *arrays)
        return arrays

    def run(self, step, *arrays):
        return self(*step(*self(*arrays)))

    def send(self, line, values, steps):
        self.open += len(values)
        return [line.shift(value, step) for value, step in zip(self(*values), steps)]

    def pass_on(self, line, lower, upper):
        self.open += 2
        lower, upper = self(lower, upper)
        return [line.pass_on(lower, True), line.pass_on(upper, False)]

    def wait(self, *groups):
        flat = self(*[array for group in groups for array in group])
        self.open -= len(flat)
        parts, at = [], 0
        for group in groups:
            parts.append(flat[at : at + len(group)])
            at += len(group)
        return parts


def total_of(terms):
    total = terms[0].astype(jnp.float32)
    for term in terms[1:]:
        total = total + term.astype(jnp.float32)
    return total


class Halving:
    def __init__(self, clock, sent, own, core, first, second):
        self.clock, self.first, self.second = clock, first, second
        self.terms = [own]
        self.moving = clock.send(core, [sent], [1])

    def along(self, line, arrived):
        self.terms = self.terms + arrived
        steps = range(1, line.size)
        blocks = [
            total_of([pick(term, line.ahead(step), 0) for term in self.terms]).astype(jnp.bfloat16)
            for step in steps
        ]
        self.moving = self.clock.send(line, blocks, steps)
        self.terms = [pick(term, line.place, 0) for term in self.terms]

    def along_first(self, arrived):
        self.along(self.first, arrived)

    def along_second(self, arrived):
        self.along(self.second, arrived)

    def finish(self, arrived):
        return self.clock(total_of(self.terms + arrived).astype(jnp.bfloat16))[0]


class Spread:
    def __init__(self, clock, piece, core, first, second):
        self.clock, self.lines = clock, (core, first, second)
        self.pieces = [piece]
        steps = range(1, second.size)
        self.moving = clock.send(second, [piece] * len(steps), steps)

    def along(self, arrived):
        core, first, second = self.lines
        self.pieces = self.pieces + arrived
        steps = range(1, first.size)
        self.moving = self.clock.send(first, [jnp.stack(self.pieces)] * len(steps), steps)

    def over(self, arrived):
        core, first, second = self.lines
        rows = [jnp.stack(self.pieces)] + arrived
        self.pieces = jnp.concatenate(rows, axis=0)
        self.moving = self.clock.send(core, [self.pieces], [1])

    def finish(self, arrived):
        core, first, second = self.lines
        (others,) = arrived
        offsets = [(one, two) for one in range(first.size) for two in range(second.size)]
        placed = [(core.place, first.behind(one), second.behind(two)) for one, two in offsets]
        far, near = (second, first) if core.crossed else (first, second)
        placed += [(core.behind(1), far.behind(one), near.behind(two)) for one, two in offsets]
        places = [(c * first.size + f) * second.size + s for c, f, s in placed]
        return [jnp.stack(places).astype(jnp.int32), self.pieces, others]


def column_blocks(place, shard_place, *weights):
    count = len(weights)
    rows, columns = weights[0].shape[1:]
    shards = lax.axis_size("shard")
    block = columns // shards

    def body(places_ref, *refs):
        sources, outs = refs[:count], refs[count : 2 * count]
        held, cut, in_sems, out_sems = refs[2 * count :]
        loads = [
            pltpu.make_async_copy(sources[at].at[places_ref[0]], held.at[at], in_sems.at[at])
            for at in range(count)
        ]

        def store(at, z):
            ahead = lax.rem(z + shards - places_ref[1], shards)
            return pltpu.make_async_copy(cut.at[at, z], outs[at].at[ahead], out_sems.at[at, z])

        for load in loads:
            load.start()
        for at in range(count):
            loads[at].wait()
            for z in range(shards):
                cut[at, z] = held[at, :, z * block : (z + 1) * block]
                store(at, z).start()
        for at in range(count):
            for z in range(shards):
                store(at, z).wait()

    return pl.pallas_call(
        body,
        out_shape=[jax.ShapeDtypeStruct((shards, rows, block), jnp.bfloat16)] * count,
        in_specs=[pl.BlockSpec(memory_space=pltpu.SMEM)]
        + [pl.BlockSpec(memory_space=pl.ANY)] * count,
        out_specs=[pl.BlockSpec(memory_space=pl.ANY)] * count,
        scratch_shapes=[
            pltpu.VMEM((count, rows, columns), jnp.bfloat16),
            pltpu.VMEM((count, shards, rows, block), jnp.bfloat16),
            pltpu.SemaphoreType.DMA((count,)),
            pltpu.SemaphoreType.DMA((count, shards)),
        ],
        compiler_params=pltpu.CompilerParams(vmem_limit_bytes=VMEM_LIMIT),
        cost_estimate=COST,
        name="column_blocks",
    )(jnp.stack([place, shard_place]).astype(jnp.int32), *weights)


def place_blocks(order, places, pieces, others):
    half, groups, shards = pieces.shape[:3]

    def body(order_ref, places_ref, pieces_ref, others_ref, *rest):
        def source_of(g, k, r):
            return (pieces_ref if r < half else others_ref).at[r % half, g, k]

        move_blocks(source_of, lambda r: places_ref[r], order_ref, rest[:groups], *rest[groups:])

    return blocks_call(body, 2, 2, groups, shards, 2 * half, pieces.shape[3:])(
        order, places, pieces, others
    )


def place_gathered(order, gathered, groups):
    shards = lax.axis_size("shard")
    reps = gathered.shape[0] // (shards * groups)

    def body(order_ref, source, *rest):
        move_blocks(
            lambda g, k, r: source.at[(r * shards + k) * groups + g],
            lambda r: r,
            order_ref,
            rest[:groups],
            *rest[groups:],
        )

    return blocks_call(body, 1, 1, groups, shards, reps, gathered.shape[1:])(order, gathered)


def move_blocks(source_of, place_of, order_ref, outs, held, in_sems, out_sems):
    groups, shards, reps = in_sems.shape
    slabs = [(g, k) for g in range(groups) for k in range(shards)]

    def load(g, k, r):
        return pltpu.make_async_copy(
            source_of(g, k, r), held.at[g, k, place_of(r)], in_sems.at[g, k, r]
        )

    def store(g, k):
        return pltpu.make_async_copy(held.at[g, k], outs[g].at[order_ref[k]], out_sems.at[g, k])

    for g, k in slabs:
        for r in range(reps):
            load(g, k, r).start()
    for g, k in slabs:
        for r in range(reps):
            load(g, k, r).wait()
        store(g, k).start()
    for g, k in slabs:
        store(g, k).wait()


def blocks_call(body, scalars, sources, groups, shards, reps, block):
    whole = (shards, reps) + block
    return pl.pallas_call(
        body,
        out_shape=[jax.ShapeDtypeStruct(whole, jnp.bfloat16)] * groups,
        in_specs=[pl.BlockSpec(memory_space=pltpu.SMEM)] * scalars
        + [pl.BlockSpec(memory_space=pl.ANY)] * sources,
        out_specs=[pl.BlockSpec(memory_space=pl.ANY)] * groups,
        scratch_shapes=[
            pltpu.VMEM((groups,) + whole, jnp.bfloat16),
            pltpu.SemaphoreType.DMA((groups, shards, reps)),
            pltpu.SemaphoreType.DMA((groups, shards)),
        ],
        compiler_params=pltpu.CompilerParams(vmem_limit_bytes=VMEM_LIMIT),
        cost_estimate=COST,
        name="place_blocks",
    )


def widen_pieces(places, pieces, others):
    half, rows, columns = pieces.shape
    reps = 2 * half
    strip = next(size for size in (16, 8, rows) if rows % size == 0)

    def body(places_ref, pieces_ref, others_ref, out_ref, narrow, wide, in_sems, out_sems):
        loads = [
            pltpu.make_async_copy(
                (pieces_ref if r < half else others_ref).at[r % half], narrow.at[r], in_sems.at[r]
            )
            for r in range(reps)
        ]
        stores = [
            pltpu.make_async_copy(wide.at[r], out_ref.at[places_ref[r]], out_sems.at[r])
            for r in range(reps)
        ]
        for load in loads:
            load.start()
        for r in range(reps):
            loads[r].wait()

            def convert(at, carry):
                cut = pl.ds(pl.multiple_of(at * strip, strip), strip)
                wide[r, cut, :] = narrow[r, cut, :].astype(jnp.float32)
                return carry

            lax.fori_loop(0, rows // strip, convert, 0)
            stores[r].start()
        for store in stores:
            store.wait()

    result = pl.pallas_call(
        body,
        out_shape=jax.ShapeDtypeStruct((reps, rows, columns), jnp.float32),
        in_specs=[pl.BlockSpec(memory_space=pltpu.SMEM)]
        + [pl.BlockSpec(memory_space=pl.ANY)] * 2,
        out_specs=pl.BlockSpec(memory_space=pl.ANY),
        scratch_shapes=[
            pltpu.VMEM((reps, rows, columns), jnp.bfloat16),
            pltpu.VMEM((reps, rows, columns), jnp.float32),
            pltpu.SemaphoreType.DMA((reps,)),
            pltpu.SemaphoreType.DMA((reps,)),
        ],
        compiler_params=pltpu.CompilerParams(vmem_limit_bytes=VMEM_LIMIT),
        cost_estimate=COST,
        name="widen_pieces",
    )(places, pieces, others)
    return (result.reshape(reps * rows, columns),)


def resident(shape):
    return pl.BlockSpec(shape, lambda i: (0, 0), pipeline_mode=pl.Buffered(1))


def feed_forward(rows, cotangents, gate_matrix, up_matrix, down_matrix):
    count, width = rows.shape
    units = gate_matrix.shape[1]
    steps = pl.cdiv(units, TILE)
    slabs = next(size for size in range(min(steps, width // 128), 0, -1) if width % (128 * size) == 0)
    slab = width // slabs

    def body(
        rows_ref,
        cotangents_ref,
        gate_ref,
        up_ref,
        down_ref,
        inner_ref,
        d_gate_ref,
        d_up_ref,
        turned_rows_ref,
        turned_inner_ref,
    ):
        gate = jnp.dot(rows_ref[...], gate_ref[...], preferred_element_type=jnp.float32)
        up = jnp.dot(rows_ref[...], up_ref[...], preferred_element_type=jnp.float32)
        sigmoid = jax.nn.sigmoid(gate)
        silu = gate * sigmoid
        inner = (silu * up).astype(jnp.bfloat16)
        inner_ref[...] = inner
        turned_inner_ref[...] = inner.T
        d_inner = times_transposed(cotangents_ref[...], down_ref[...])
        d_up_ref[...] = (d_inner * silu).astype(jnp.bfloat16)
        d_gate_ref[...] = (d_inner * up * sigmoid * (1.0 + gate * (1.0 - sigmoid))).astype(
            jnp.bfloat16
        )
        for step in range(slabs):

            @pl.when(pl.program_id(0) == step)
            def turn():
                turned_rows_ref[...] = rows_ref[:, step * slab : (step + 1) * slab].T

    columns = pl.BlockSpec((width, TILE), lambda i: (0, i))
    results = pl.BlockSpec((count, TILE), lambda i: (0, i))
    return pl.pallas_call(
        body,
        grid=(steps,),
        out_shape=[jax.ShapeDtypeStruct((count, units), jnp.bfloat16)] * 3
        + [
            jax.ShapeDtypeStruct((width, count), jnp.bfloat16),
            jax.ShapeDtypeStruct((units, count), jnp.bfloat16),
        ],
        in_specs=[
            resident((count, width)),
            resident((count, width)),
            columns,
            columns,
            pl.BlockSpec((TILE, width), lambda i: (i, 0)),
        ],
        out_specs=[results] * 3
        + [
            pl.BlockSpec((slab, count), lambda i: (jnp.minimum(i, slabs - 1), 0)),
            pl.BlockSpec((TILE, count), lambda i: (i, 0)),
        ],
        compiler_params=pltpu.CompilerParams(vmem_limit_bytes=VMEM_LIMIT),
        cost_estimate=COST,
        name="feed_forward",
    )(rows, cotangents, gate_matrix, up_matrix, down_matrix)


def split_gradient(left, right, groups, places, core_place, turned):
    rows, count = left.shape if turned else left.shape[::-1]
    columns = right.shape[1]
    half = rows // (2 * groups)
    part = half // places

    def body(core_ref, left_ref, right_ref, other_ref, own_ref, *scratch):
        if turned:
            rows_ref = left_ref
        else:
            (rows_ref,) = scratch

            @pl.when(pl.program_id(0) == 0)
            def turn():
                rows_ref[...] = left_ref[...].T

        core = core_ref[0]
        for out_ref, which in ((other_ref, 1 - core), (own_ref, core)):
            halves = [
                rows_ref[pl.ds(pl.multiple_of((2 * group + which) * half, 16), half), :]
                for group in range(groups)
            ]
            product = jnp.dot(
                jnp.concatenate(halves, axis=0), right_ref[...], preferred_element_type=jnp.float32
            )
            for group in range(groups):
                for place in range(places):
                    at = group * half + place * part
                    out_ref[place, group] = product[at : at + part].astype(jnp.bfloat16)

    return pl.pallas_call(
        body,
        grid=(pl.cdiv(columns, TILE),),
        out_shape=[jax.ShapeDtypeStruct((places, groups, part, columns), jnp.bfloat16)] * 2,
        in_specs=[
            pl.BlockSpec(memory_space=pltpu.SMEM),
            resident(left.shape),
            pl.BlockSpec((count, TILE), lambda i: (0, i)),
        ],
        out_specs=[pl.BlockSpec((places, groups, part, TILE), lambda i: (0, 0, 0, i))] * 2,
        scratch_shapes=[] if turned else [pltpu.VMEM((rows, count), jnp.bfloat16)],
        compiler_params=pltpu.CompilerParams(vmem_limit_bytes=VMEM_LIMIT),
        cost_estimate=COST,
        name="split_gradient",
    )(core_place.reshape(1).astype(jnp.int32), left, right)


def ordered_gradient(left, right, shards, order):
    reps = len(order)
    rows, count = left.shape
    columns = right.shape[1]
    part = rows // (shards * reps)

    def body(left_ref, right_ref, out_ref):
        product = jnp.dot(left_ref[...], right_ref[...], preferred_element_type=jnp.float32)
        for z in range(shards):
            for r in range(reps):
                at = (z * reps + order[r]) * part
                out_ref[r, z] = product[at : at + part].astype(jnp.bfloat16)

    return pl.pallas_call(
        body,
        grid=(pl.cdiv(columns, TILE),),
        out_shape=[jax.ShapeDtypeStruct((reps, shards, part, columns), jnp.bfloat16)],
        in_specs=[
            resident((rows, count)),
            pl.BlockSpec((count, TILE), lambda i: (0, i)),
        ],
        out_specs=[pl.BlockSpec((reps, shards, part, TILE), lambda i: (0, 0, 0, i))],
        compiler_params=pltpu.CompilerParams(vmem_limit_bytes=VMEM_LIMIT),
        cost_estimate=COST,
        name="ordered_gradient",
    )(left, right)


def rows_product(lefts, rights, turned, blocks):
    count, depth = lefts[0].shape
    columns = rights[0].shape[0 if turned else 1]
    pairs, part = len(lefts), count // blocks

    def body(*refs):
        total = None
        for left_ref, right_ref in zip(refs[:pairs], refs[pairs : 2 * pairs]):
            if turned:
                product = times_transposed(left_ref[...], right_ref[...])
            else:
                product = jnp.dot(
                    left_ref[...], right_ref[...], preferred_element_type=jnp.float32
                )
            total = product if total is None else total + product
        for block in range(blocks):
            refs[2 * pairs + block][...] = total[block * part : (block + 1) * part].astype(
                jnp.bfloat16
            )

    right_spec = (
        pl.BlockSpec((TILE, depth), lambda i: (i, 0))
        if turned
        else pl.BlockSpec((depth, TILE), lambda i: (0, i))
    )
    return pl.pallas_call(
        body,
        grid=(pl.cdiv(columns, TILE),),
        out_shape=[jax.ShapeDtypeStruct((part, columns), jnp.bfloat16)] * blocks,
        in_specs=[resident((count, depth))] * pairs + [right_spec] * pairs,
        out_specs=[pl.BlockSpec((part, TILE), lambda i: (0, i))] * blocks,
        compiler_params=pltpu.CompilerParams(vmem_limit_bytes=VMEM_LIMIT),
        cost_estimate=COST,
        name="rows_product",
    )(*lefts, *rights)


def kept_bias(row_segments, row_index, key_segments, key_index):
    kept = (row_segments == key_segments) & (key_index <= row_index)
    return jnp.where(kept, 0.0, MASKED)


def in_vmem(count):
    return [pl.BlockSpec(memory_space=pltpu.VMEM)] * count


def attention_forward(projected, cosine, signed_sine, pairs, rows, keys):
    count = projected.shape[0]
    per_group = QH // KVH
    scale = 1.0 / math.sqrt(HD)
    shape = (KVH, per_group * count, HD)

    def body(projected_ref, cosine_ref, sine_ref, pairs_ref, rows_ref, keys_ref, queries_ref, out_ref):
        bias = kept_bias(rows_ref[:, 0:1], rows_ref[:, 1:2], keys_ref[0:1, :], keys_ref[1:2, :])
        for k in range(KVH):
            for h in range(per_group):
                at = (k * per_group + h) * HD
                field = projected_ref[:, at : at + HD]
                queries_ref[k, h * count : (h + 1) * count, :] = (
                    field * cosine_ref[...] + pltpu.roll(field, HD // 2, 1) * sine_ref[...]
                ).astype(jnp.bfloat16)
            keys_here = pairs_ref[:, k * HD : (k + 1) * HD]
            values_here = pairs_ref[:, (KVH + k) * HD : (KVH + k + 1) * HD]
            scores = times_transposed(queries_ref[k], keys_here) * scale + bias
            powers = jnp.exp(scores - jnp.max(scores, axis=1, keepdims=True))
            shares = powers * (1.0 / jnp.sum(powers, axis=1, keepdims=True))
            result = jnp.dot(
                shares.astype(jnp.bfloat16), values_here, preferred_element_type=jnp.float32
            ).astype(jnp.bfloat16)
            for h in range(per_group):
                at = (k * per_group + h) * HD
                out_ref[:, at : at + HD] = result[h * count : (h + 1) * count]

    return pl.pallas_call(
        body,
        out_shape=[
            jax.ShapeDtypeStruct(shape, jnp.bfloat16),
            jax.ShapeDtypeStruct((count, QH * HD), jnp.bfloat16),
        ],
        in_specs=in_vmem(6),
        out_specs=in_vmem(2),
        compiler_params=pltpu.CompilerParams(vmem_limit_bytes=VMEM_LIMIT),
        cost_estimate=COST,
        name="attention_forward",
    )(projected, cosine, signed_sine, pairs, rows, keys)


def attention_backward(queries, gradient, pairs, cosine, signed_sine, rows, keys, blocks):
    count = gradient.shape[0]
    per_group = QH // KVH
    scale = 1.0 / math.sqrt(HD)
    group_rows = pairs.shape[0]
    part = group_rows // blocks

    def body(queries_ref, gradient_ref, pairs_ref, cosine_ref, sine_ref, rows_ref, keys_ref, d_ref, *outs):
        block_refs, stacked = outs[:blocks], outs[blocks]
        bias = kept_bias(rows_ref[0:1, :], rows_ref[1:2, :], keys_ref[:, 0:1], keys_ref[:, 1:2])
        for k in range(KVH):
            for h in range(per_group):
                at = (k * per_group + h) * HD
                stacked[h * count : (h + 1) * count, :] = gradient_ref[:, at : at + HD]
            keys_here = pairs_ref[:, k * HD : (k + 1) * HD]
            values_here = pairs_ref[:, (KVH + k) * HD : (KVH + k + 1) * HD]
            scores = times_transposed(keys_here, queries_ref[k]) * scale + bias
            powers = jnp.exp(scores - jnp.max(scores, axis=0, keepdims=True))
            shares = powers * (1.0 / jnp.sum(powers, axis=0, keepdims=True))
            d_shares = times_transposed(values_here, stacked[...])
            dots = jnp.sum(shares * d_shares, axis=0, keepdims=True)
            d_scores = (shares * (d_shares - dots)).astype(jnp.bfloat16)
            d_keys = jnp.dot(d_scores, queries_ref[k], preferred_element_type=jnp.float32) * scale
            d_values = jnp.dot(
                shares.astype(jnp.bfloat16), stacked[...], preferred_element_type=jnp.float32
            )
            for block in range(blocks):
                cut = slice(block * part, (block + 1) * part)
                block_refs[block][:, k * HD : (k + 1) * HD] = d_keys[cut].astype(jnp.bfloat16)
                block_refs[block][:, (KVH + k) * HD : (KVH + k + 1) * HD] = d_values[cut].astype(
                    jnp.bfloat16
                )
            d_queries = transposed_times(d_scores, keys_here) * scale
            for h in range(per_group):
                at = (k * per_group + h) * HD
                field = d_queries[h * count : (h + 1) * count]
                d_ref[:, at : at + HD] = (
                    field * cosine_ref[...] - pltpu.roll(field, HD // 2, 1) * sine_ref[...]
                ).astype(jnp.bfloat16)

    return pl.pallas_call(
        body,
        out_shape=[jax.ShapeDtypeStruct((count, QH * HD), jnp.bfloat16)]
        + [jax.ShapeDtypeStruct((part, 2 * KVH * HD), jnp.bfloat16)] * blocks,
        in_specs=in_vmem(7),
        out_specs=in_vmem(1 + blocks),
        scratch_shapes=[pltpu.VMEM((per_group * count, HD), jnp.bfloat16)],
        compiler_params=pltpu.CompilerParams(vmem_limit_bytes=VMEM_LIMIT),
        cost_estimate=COST,
        name="attention_backward",
    )(queries, gradient, pairs, cosine, signed_sine, rows, keys)


def join_projected(d_queries, pair_terms, cosine, signed_sine):
    count, query_width = d_queries.shape
    pair_width = KVH * HD
    terms = len(pair_terms)

    def body(d_queries_ref, cosine_ref, sine_ref, *refs):
        term_refs, out_ref, sum_ref = refs[:terms], refs[terms], refs[terms + 1]
        out_ref[:, :query_width] = d_queries_ref[...]
        for at in range(0, 2 * pair_width, HD):
            field = total_of([term[:, at : at + HD] for term in term_refs])
            if at < pair_width:
                field = field * cosine_ref[...] - pltpu.roll(field, HD // 2, 1) * sine_ref[...]
            out_ref[:, query_width + at : query_width + at + HD] = field.astype(jnp.bfloat16)
        sum_ref[...] = jnp.sum(out_ref[...].astype(jnp.float32), axis=0, keepdims=True)

    return pl.pallas_call(
        body,
        out_shape=[
            jax.ShapeDtypeStruct((count, query_width + 2 * pair_width), jnp.bfloat16),
            jax.ShapeDtypeStruct((1, query_width + 2 * pair_width), jnp.float32),
        ],
        in_specs=in_vmem(3 + terms),
        out_specs=in_vmem(2),
        cost_estimate=COST,
        name="join_projected",
    )(d_queries, cosine, signed_sine, *pair_terms)


def on_device(
    tokens,
    segment_ids,
    first_gain,
    input_weight,
    input_bias,
    output_weight,
    second_gain,
    gate_weight,
    up_weight,
    down_weight,
    output_cotangent,
):
    bf16, f32 = jnp.bfloat16, jnp.float32
    shards, reps = lax.axis_size("shard"), lax.axis_size("rep")
    shard, core, first, second = make_lines(reps, shards)
    rep_place = (core.place * first.size + first.place) * second.size + second.place
    own_rows, width = tokens.shape
    segments = segment_ids[0]
    per_group = QH // KVH
    query_width = QH * HD
    pair_width = KVH * HD
    first_row = shard.place * own_rows
    part_rows = input_weight.shape[0] // reps
    hidden_units = gate_weight.shape[1]
    block_units = hidden_units // shards
    clock = Clock()
    z_order = jnp.stack([shard.behind(step) for step in range(shards)]).astype(jnp.int32)

    def weight_piece(weight, place):
        return pick(weight.reshape(reps, part_rows, weight.shape[1]), place, 0)

    def spread(piece):
        return Spread(clock, piece, core, first, second)

    def blocks_of(blocks):
        return [pick(blocks, shard.ahead(step), 0) for step in range(shards)]

    steps = range(1, shards)

    def send_blocks(blocks):
        return clock.send(shard, blocks[1:], steps)

    def send_around(value):
        return clock.send(shard, [value] * len(steps), steps)

    def send_back(rows):
        return clock.send(shard, rows, [shards - step for step in steps])

    rep_index = lax.axis_index("rep")
    input_matrix = lax.all_gather(
        weight_piece(input_weight, rep_index), ("shard", "rep"), axis=0, tiled=True
    )
    shard_vectors = jnp.concatenate([first_gain, second_gain, input_bias])
    vector_row = jnp.pad(shard_vectors, (0, output_weight.shape[1] - shard_vectors.shape[0]))
    own_output = jnp.concatenate(
        [weight_piece(output_weight, rep_place), vector_row[None]], axis=0
    )
    output_moving = send_around(own_output)
    gate_blocks, up_blocks = clock.run(
        lambda *weights: column_blocks(rep_index, shard.place, *weights),
        gate_weight.reshape(reps, part_rows, hidden_units),
        up_weight.reshape(reps, part_rows, hidden_units),
    )
    (output_rows,) = clock.wait(output_moving)
    output_rows = [own_output] + output_rows

    output_spread = spread(jnp.stack([rows[:part_rows] for rows in output_rows])[None])
    gate_moving = send_blocks(gate_blocks)
    vector_rows = jnp.stack(in_place_order([rows[part_rows] for rows in output_rows], shard))
    own_gain = first_gain.shape[0]
    gain_one = vector_rows[:, :own_gain].reshape(width).astype(f32)
    gain_two = vector_rows[:, own_gain : 2 * own_gain].reshape(width).astype(f32)
    shift_row = (
        vector_rows[:, 2 * own_gain : shard_vectors.shape[0]].reshape(-1).astype(f32)
    )
    places = positions(segments)
    cosine_table, sine_table = rope_tables(
        lax.dynamic_slice_in_dim(places, first_row, own_rows), HD
    )
    signed_sine = jnp.concatenate(
        [-sine_table[:, : HD // 2], sine_table[:, HD // 2 :]], axis=1
    )
    own_segments = lax.dynamic_slice_in_dim(segments, first_row, own_rows)
    row_index = jnp.arange(own_rows, dtype=jnp.int32)
    key_index = jnp.concatenate([shard.behind(step) * own_rows + row_index for step in range(shards)])
    key_segments = jnp.concatenate(
        [
            lax.dynamic_slice_in_dim(segments, shard.behind(step) * own_rows, own_rows)
            for step in range(shards)
        ]
    )
    key_marks = jnp.stack([key_segments, key_index])
    row_marks = jnp.tile(jnp.stack([own_segments, first_row + row_index]), (1, per_group))
    wide_tokens = tokens.astype(f32)
    inverse_one = lax.rsqrt(jnp.mean(wide_tokens * wide_tokens, axis=-1, keepdims=True) + EPSILON)
    unit_one = wide_tokens * inverse_one
    normed_one = (unit_one * gain_one).astype(bf16)
    (
        normed_one,
        cosine_table,
        sine_table,
        signed_sine,
        key_marks,
        row_marks,
    ) = clock(normed_one, cosine_table, sine_table, signed_sine, key_marks, row_marks)
    output_arrived, gate_rows = clock.wait(output_spread.moving, gate_moving)

    output_spread.along(output_arrived)
    up_moving = send_blocks(up_blocks)
    output_arrived, up_rows = clock.wait(output_spread.moving, up_moving)

    gate_up = jnp.stack(
        [row for pair in zip([gate_blocks[0]] + gate_rows, [up_blocks[0]] + up_rows) for row in pair]
    )
    gate_up = lax.all_gather(clock(gate_up)[0], "rep", axis=0, tiled=True)
    passed = [[output_cotangent] * 2]
    passing = clock.pass_on(shard, *passed[-1])
    output_spread.over(output_arrived)
    input_matrix, normed_one = clock(input_matrix, normed_one)
    projected = jnp.dot(normed_one, input_matrix, preferred_element_type=f32) + shift_row
    key_part = rotate(
        projected[:, query_width : query_width + pair_width].reshape(own_rows, KVH, HD),
        cosine_table,
        sine_table,
    )
    (own_pairs,) = clock(
        jnp.concatenate(
            [key_part.reshape(own_rows, pair_width), projected[:, query_width + pair_width :]],
            axis=1,
        ).astype(bf16)
    )
    arrived, output_arrived = clock.wait(passing, output_spread.moving)
    passed.append(arrived)

    pair_moving = send_around(own_pairs)
    passing = clock.pass_on(shard, *passed[-1]) if shards > 2 else []
    pair_rows, arrived = clock.wait(pair_moving, passing)
    passed.append(arrived)
    pairs = jnp.concatenate([own_pairs] + pair_rows, axis=0)

    passing = clock.pass_on(shard, *passed[-1]) if shards > 3 else []
    (output_matrix,) = clock.run(place_blocks, z_order, *output_spread.finish(output_arrived))
    output_matrix = output_matrix.reshape(width, width)
    queries, attention_low = clock.run(
        attention_forward, projected, cosine_table, signed_sine, pairs, row_marks.T, key_marks
    )
    hidden = wide_tokens + jnp.dot(attention_low, output_matrix, preferred_element_type=f32)
    inverse_two = lax.rsqrt(jnp.mean(hidden * hidden, axis=-1, keepdims=True) + EPSILON)
    unit_two = hidden * inverse_two
    (normed_two,) = clock((unit_two * gain_two).astype(bf16))
    (arrived,) = clock.wait(passing)
    passed.append(arrived)

    normed_moving = send_around(normed_two)
    gate_matrix, up_matrix = clock.run(
        lambda order, gathered: place_gathered(order, gathered, 2), z_order, gate_up
    )
    gate_matrix = gate_matrix.reshape(width, block_units)
    up_matrix = up_matrix.reshape(width, block_units)
    (normed_arrived,) = clock.wait(normed_moving)
    while len(passed) < shards:
        (arrived,) = clock.wait(clock.pass_on(shard, *passed[-1]))
        passed.append(arrived)
    group_normed = jnp.concatenate([normed_two] + normed_arrived, axis=0)
    cotangents = jnp.concatenate(
        [output_cotangent]
        + [
            jnp.where(shard.place >= step, passed[step][0], passed[shards - step][1])
            for step in steps
        ],
        axis=0,
    )

    inner_act, d_gate, d_up, turned_normed, turned_inner = clock.run(
        feed_forward, group_normed, cotangents, gate_matrix, up_matrix, down_weight
    )

    def split_halves(left, right, groups, turned):
        count = first.size * second.size
        halves = clock.run(
            lambda left, right: split_gradient(left, right, groups, count, core.place, turned),
            left,
            right,
        )
        return [half.reshape((first.size, second.size) + half.shape[1:]) for half in halves]

    def side_by_side(rows):
        return clock(jnp.concatenate(in_place_order(rows, shard), axis=1))[0]

    def sum_over_rep(blocks):
        return lax.psum_scatter(blocks, "rep", scatter_dimension=0, tiled=True)

    def row_sum(own, arrived):
        return clock(total_of(own + arrived).astype(bf16))[0]

    def send_some(rows, chosen):
        return clock.send(shard, [rows[k] for k in chosen], [shards - 1 - k for k in chosen])

    edges = sorted({0, shards - 2})
    inside = list(range(1, shards - 2))

    up_halves = split_halves(turned_normed, d_up, shards, True)

    up = Halving(clock, *up_halves, core, first, second)
    normed_own, *normed_partial = clock.run(
        lambda *operands: rows_product(operands[:2], operands[2:], True, shards),
        d_gate,
        d_up,
        gate_matrix,
        up_matrix,
    )
    (up_arrived,) = clock.wait(up.moving)

    up.along_first(up_arrived)
    normed_moving = send_some(normed_partial, edges)
    (gate_blocks,) = clock.run(
        lambda left, right: ordered_gradient(left, right, shards, rep_places(reps)),
        turned_normed,
        d_gate,
    )
    gate_piece = sum_over_rep(gate_blocks.reshape(width, block_units))
    (down_blocks,) = clock.run(
        lambda left, right: ordered_gradient(left, right, 1, list(range(reps))),
        turned_inner,
        cotangents,
    )
    up_arrived, normed_arrived = clock.wait(up.moving, normed_moving)

    up.along_second(up_arrived)
    normed_moving = send_some(normed_partial, inside)
    block_own, *block_partial = clock.run(
        lambda left, right: rows_product((left,), (right,), False, shards), inner_act, down_weight
    )
    up_arrived, more_arrived = clock.wait(up.moving, normed_moving)

    up_blocks = clock(*blocks_of(up.finish(up_arrived)))
    up_moving = send_blocks(up_blocks)
    normed_two_gradient = total_of([normed_own] + normed_arrived + more_arrived)
    gain_two_gradient = jnp.sum(normed_two_gradient * unit_two, axis=0)
    hidden_gradient = output_cotangent.astype(f32) + norm_back(
        normed_two_gradient, unit_two, inverse_two, gain_two
    )
    (branch_gradient,) = clock(hidden_gradient.astype(bf16))
    (attention_gradient,) = clock(times_transposed(branch_gradient, output_matrix).astype(bf16))
    d_queries, pair_own, *pair_partial = clock.run(
        lambda *operands: attention_backward(*operands, shards),
        queries,
        attention_gradient,
        pairs,
        cosine_table,
        signed_sine,
        row_marks,
        key_marks.T,
    )
    output_halves = split_halves(attention_low, branch_gradient, shards, False)
    (up_rows,) = clock.wait(up_moving)

    pair_moving = send_back(pair_partial)
    output = Halving(clock, *output_halves, core, first, second)
    up_piece = side_by_side(up_blocks[:1] + up_rows)
    pair_arrived, output_arrived = clock.wait(pair_moving, output.moving)

    up_spread = spread(up_piece)
    output.along_first(output_arrived)
    block_moving = send_some(block_partial, inside)
    projected_gradient, bias_sum = clock.run(
        lambda *operands: join_projected(operands[0], operands[3:], *operands[1:3]),
        d_queries,
        cosine_table,
        signed_sine,
        pair_own,
        *pair_arrived,
    )
    projected_halves = split_halves(normed_one, projected_gradient, shards, False)
    up_arrived, output_arrived, block_arrived = clock.wait(
        up_spread.moving, output.moving, block_moving
    )

    projected = Halving(clock, *projected_halves, core, first, second)
    output.along_second(output_arrived)
    up_spread.along(up_arrived)
    block_moving = send_some(block_partial, edges)
    (gate_piece,) = clock(gate_piece)
    down_piece = sum_over_rep(clock(down_blocks)[0].reshape(block_units, width))
    projected_gradient, hidden_gradient = clock(projected_gradient, hidden_gradient)
    normed_one_gradient = times_transposed(projected_gradient, input_matrix)
    gain_one_gradient = jnp.sum(normed_one_gradient * unit_one, axis=0)
    (tokens_gradient,) = clock(
        (
            hidden_gradient + norm_back(normed_one_gradient, unit_one, inverse_one, gain_one)
        ).astype(bf16)
    )
    projected_arrived, output_arrived, more_arrived = clock.wait(
        projected.moving, output.moving, block_moving
    )
    block_arrived = block_arrived + more_arrived

    projected.along_first(projected_arrived)
    gate_blocks = clock(*blocks_of(gate_piece.reshape(shards, part_rows, block_units)))
    gate_moving = send_blocks(gate_blocks)
    output_blocks = clock(*blocks_of(output.finish(output_arrived)))
    (block_out,) = clock(total_of([hidden, block_own] + block_arrived).astype(bf16))
    bias_gradient = bias_sum[0]
    bias_split = query_width + pair_width
    small_parts = (
        gain_one_gradient,
        gain_two_gradient,
        bias_gradient[:bias_split],
        bias_gradient[bias_split:],
    )
    (small,) = clock(
        jnp.concatenate([part.reshape(shards, -1) for part in small_parts], axis=1)
    )
    projected_arrived, up_arrived, gate_rows = clock.wait(
        projected.moving, up_spread.moving, gate_moving
    )

    projected.along_second(projected_arrived)
    gate_spread = spread(side_by_side(gate_blocks[:1] + gate_rows))
    output_moving = send_blocks(output_blocks)
    projected_arrived, gate_arrived, output_rows = clock.wait(
        projected.moving, gate_spread.moving, output_moving
    )

    input_blocks = clock(*blocks_of(projected.finish(projected_arrived)))
    input_moving = send_blocks(input_blocks)
    gate_spread.along(gate_arrived)
    output_spread = spread(row_sum(output_blocks[:1], output_rows))
    input_rows, gate_arrived, output_arrived = clock.wait(
        input_moving, gate_spread.moving, output_spread.moving
    )

    input_spread = spread(row_sum(input_blocks[:1], input_rows))
    output_spread.along(output_arrived)
    up_spread.over(up_arrived)
    gate_spread.over(gate_arrived)
    small_moving = clock.send(core, [small], [1])
    (down_piece,) = clock(down_piece)
    down_gathered = lax.all_gather(down_piece, "rep", axis=0, tiled=True)
    input_arrived, output_arrived, up_arrived, gate_arrived, small_arrived = clock.wait(
        input_spread.moving, output_spread.moving, up_spread.moving, gate_spread.moving, small_moving
    )
    small = total_of([small] + small_arrived)

    input_spread.along(input_arrived)
    output_spread.over(output_arrived)
    small_moving = clock.send(first, [small] * (first.size - 1), range(1, first.size))
    (up_total,) = clock.run(widen_pieces, *up_spread.finish(up_arrived))
    input_arrived, output_arrived, small_arrived = clock.wait(
        input_spread.moving, output_spread.moving, small_moving
    )
    small = total_of([small] + small_arrived)

    input_spread.over(input_arrived)
    small_moving = clock.send(second, [small] * (second.size - 1), range(1, second.size))
    (gate_total,) = clock.run(widen_pieces, *gate_spread.finish(gate_arrived))
    input_arrived, small_arrived = clock.wait(input_spread.moving, small_moving)
    small_blocks = clock(*blocks_of(total_of([small] + small_arrived)))

    small_moving = send_blocks(small_blocks)
    (output_total,) = clock.run(widen_pieces, *output_spread.finish(output_arrived))
    (input_total,) = clock.run(widen_pieces, *input_spread.finish(input_arrived))
    (small_arrived,) = clock.wait(small_moving)
    small = total_of(small_blocks[:1] + small_arrived)
    (down_gathered,) = clock(down_gathered)
    (down_total,) = clock(down_gathered.astype(f32))

    small = small + clock.token[0, 0]
    small_totals, at = [], 0
    for part in small_parts:
        size = part.shape[0] // shards
        small_totals.append(small[at : at + size])
        at += size
    return (
        block_out,
        tokens_gradient,
        small_totals[0],
        input_total,
        small_totals[2],
        small_totals[3],
        output_total,
        small_totals[1],
        gate_total,
        up_total,
        down_total,
    )


def solution(mesh):
    placed = (
        P(("rep", "shard"), None),
        P("rep", None),
        P("shard"),
        P("shard", None),
        P("shard"),
        P("shard", None),
        P("shard"),
        P("shard", None),
        P("shard", None),
        P("shard", None),
        P(("rep", "shard"), None),
    )
    return jax.shard_map(
        on_device,
        mesh=mesh,
        in_specs=placed,
        out_specs=(
            P(("rep", "shard"), None),
            P(("rep", "shard"), None),
            P("shard"),
            P("shard", None),
            P("shard"),
            P("shard"),
            P("shard", None),
            P("shard"),
            P("shard", None),
            P("shard", None),
            P("shard", None),
        ),
        check_vma=False,
    )
```

```python
import math

import jax
import jax.numpy as jnp
from jax import lax
from jax.experimental import pallas as pl
from jax.experimental.pallas import tpu as pltpu
from jax.sharding import PartitionSpec as P

QH = 12
KVH = 2
HD = 128
SEQS = 3


EPSILON = 1e-06
LOG_THETA = math.log(1000000.0)
MASKED = -1e30
VMEM_LIMIT = 56 * 1024 * 1024
TILE = 512
COST = pl.CostEstimate(flops=1, bytes_accessed=1, transcendentals=0)


def rope_tables(places, head_width):
    half_width = head_width // 2
    frequency = jnp.exp(jnp.arange(half_width, dtype=jnp.float32) * (-2.0 * LOG_THETA / head_width))
    angles = places.astype(jnp.float32)[:, None] * frequency[None, :]
    angles = jnp.concatenate([angles, angles], axis=-1)
    return (jnp.cos(angles), jnp.sin(angles))


def positions(segments):
    labels = jnp.arange(SEQS, dtype=jnp.int32)
    starts = jnp.sum((segments[None, :] < labels[:, None]).astype(jnp.int32), axis=1)
    own_start = jnp.sum(jnp.where(segments[:, None] == labels[None, :], starts[None, :], 0), axis=1)
    return jnp.arange(segments.shape[0], dtype=jnp.int32) - own_start


def rotate(field_rows, cosine_table, sine_table):
    half_width = field_rows.shape[-1] // 2
    turned = jnp.concatenate([-field_rows[..., half_width:], field_rows[..., :half_width]], axis=-1)
    return field_rows * cosine_table[:, None, :] + turned * sine_table[:, None, :]


def transposed_times(left_side, right_side):
    return lax.dot_general(
        left_side, right_side, (((0,), (0,)), ((), ())), preferred_element_type=jnp.float32
    )


def times_transposed(left_side, right_side):
    return lax.dot_general(
        left_side, right_side, (((1,), (1,)), ((), ())), preferred_element_type=jnp.float32
    )


def norm_back(normed_gradient, unit_rows, inverse_rms, gain_row):
    scaled = normed_gradient * gain_row
    return inverse_rms * (scaled - unit_rows * jnp.mean(scaled * unit_rows, axis=-1, keepdims=True))


class Line:
    def __init__(self, name, size, place, pairs, crossed=False):
        self.name, self.size, self.place, self.pairs = name, size, place, pairs
        self.crossed = crossed

    def shift(self, value, step):
        return lax.ppermute(value, self.name, self.pairs(step % self.size))

    def pass_on(self, value, up):
        places = range(self.size - 1)
        pairs = [(at, at + 1) if up else (at + 1, at) for at in places]
        return lax.ppermute(value, self.name, pairs)

    def behind(self, step):
        return lax.rem(self.place + (self.size - step % self.size), self.size)

    def ahead(self, step):
        return lax.rem(self.place + step % self.size, self.size) if step else self.place


def make_lines(reps, shards):
    inner = 2 if reps % 4 == 0 else 1
    outer = reps // (2 * inner)
    square = inner == outer

    def split(index):
        core, b, a = index % 2, (index // 2) % inner, index // (2 * inner)
        return core, b, a

    def join(core, b, a):
        return (a * inner + b) * 2 + core

    def first_pairs(step):
        pairs = []
        for index in range(reps):
            core, b, a = split(index)
            if square and core == 0:
                pairs.append((index, join(core, (b + step) % inner, a)))
            else:
                pairs.append((index, join(core, b, (a + step) % outer)))
        return pairs

    def second_pairs(step):
        pairs = []
        for index in range(reps):
            core, b, a = split(index)
            if square and core == 0:
                pairs.append((index, join(core, b, (a + step) % outer)))
            else:
                pairs.append((index, join(core, (b + step) % inner, a)))
        return pairs

    def core_pairs(step):
        pairs = []
        for index in range(reps):
            core, b, a = split(index)
            pairs.append((index, join((core + step) % 2, b, a)))
        return pairs

    def shard_pairs(step):
        return [(index, (index + step) % shards) for index in range(shards)]

    core, b, a = split(lax.axis_index("rep"))
    first, second = (jnp.where(core == 0, b, a), jnp.where(core == 0, a, b)) if square else (a, b)
    return (
        Line("shard", shards, lax.axis_index("shard"), shard_pairs),
        Line("rep", 2, core, core_pairs, square),
        Line("rep", outer, first, first_pairs),
        Line("rep", inner, second, second_pairs),
    )


def rep_places(reps):
    inner = 2 if reps % 4 == 0 else 1
    outer = reps // (2 * inner)
    places = []
    for index in range(reps):
        core, b, a = index % 2, (index // 2) % inner, index // (2 * inner)
        one, two = (b, a) if inner == outer and core == 0 else (a, b)
        places.append((core * outer + one) * inner + two)
    return places


def pick(array, index, axis):
    return lax.dynamic_index_in_dim(array, index, axis, keepdims=False)


def put(array, piece, index, axis):
    return lax.dynamic_update_index_in_dim(array, piece, index, axis)


def in_place_order(pieces, line):
    ordered = []
    for place in range(line.size):
        chosen = pieces[0]
        for step in range(1, line.size):
            chosen = jnp.where(line.behind(step) == place, pieces[step], chosen)
        ordered.append(chosen)
    return ordered


def tie(*arrays):
    return lax.optimization_barrier(arrays)


def gather_line(value, line):
    return [value] + [line.shift(value, step) for step in range(1, line.size)]


class Clock:
    def __init__(self):
        self.token = jnp.zeros((8, 128), jnp.float32)
        self.open = 0

    def __call__(self, *arrays):
        self.token, *arrays = tie(self.token, *arrays)
        return arrays

    def run(self, step, *arrays):
        return self(*step(*self(*arrays)))

    def send(self, line, values, steps):
        self.open += len(values)
        return [line.shift(value, step) for value, step in zip(self(*values), steps)]

    def pass_on(self, line, lower, upper):
        self.open += 2
        lower, upper = self(lower, upper)
        return [line.pass_on(lower, True), line.pass_on(upper, False)]

    def wait(self, *groups):
        flat = self(*[array for group in groups for array in group])
        self.open -= len(flat)
        parts, at = [], 0
        for group in groups:
            parts.append(flat[at : at + len(group)])
            at += len(group)
        return parts


def total_of(terms):
    total = terms[0].astype(jnp.float32)
    for term in terms[1:]:
        total = total + term.astype(jnp.float32)
    return total


class Halving:
    def __init__(self, clock, sent, own, core, first, second):
        self.clock, self.first, self.second = clock, first, second
        self.terms = [own]
        self.moving = clock.send(core, [sent], [1])

    def along(self, line, arrived):
        self.terms = self.terms + arrived
        steps = range(1, line.size)
        blocks = [
            total_of([pick(term, line.ahead(step), 0) for term in self.terms]).astype(jnp.bfloat16)
            for step in steps
        ]
        self.moving = self.clock.send(line, blocks, steps)
        self.terms = [pick(term, line.place, 0) for term in self.terms]

    def along_first(self, arrived):
        self.along(self.first, arrived)

    def along_second(self, arrived):
        self.along(self.second, arrived)

    def finish(self, arrived):
        return self.clock(total_of(self.terms + arrived).astype(jnp.bfloat16))[0]


class Spread:
    def __init__(self, clock, piece, core, first, second):
        self.clock, self.lines = clock, (core, first, second)
        self.pieces = [piece]
        steps = range(1, second.size)
        self.moving = clock.send(second, [piece] * len(steps), steps)

    def along(self, arrived):
        core, first, second = self.lines
        self.pieces = self.pieces + arrived
        steps = range(1, first.size)
        self.moving = self.clock.send(first, [jnp.stack(self.pieces)] * len(steps), steps)

    def over(self, arrived):
        core, first, second = self.lines
        rows = [jnp.stack(self.pieces)] + arrived
        self.pieces = jnp.concatenate(rows, axis=0)
        self.moving = self.clock.send(core, [self.pieces], [1])

    def finish(self, arrived):
        core, first, second = self.lines
        (others,) = arrived
        offsets = [(one, two) for one in range(first.size) for two in range(second.size)]
        placed = [(core.place, first.behind(one), second.behind(two)) for one, two in offsets]
        far, near = (second, first) if core.crossed else (first, second)
        placed += [(core.behind(1), far.behind(one), near.behind(two)) for one, two in offsets]
        places = [(c * first.size + f) * second.size + s for c, f, s in placed]
        return [jnp.stack(places).astype(jnp.int32), self.pieces, others]


def column_blocks(place, shard_place, *weights):
    count = len(weights)
    rows, columns = weights[0].shape[1:]
    shards = lax.axis_size("shard")
    block = columns // shards

    def body(places_ref, *refs):
        sources, outs = refs[:count], refs[count : 2 * count]
        held, cut, in_sems, out_sems = refs[2 * count :]
        loads = [
            pltpu.make_async_copy(sources[at].at[places_ref[0]], held.at[at], in_sems.at[at])
            for at in range(count)
        ]

        def store(at, z):
            ahead = lax.rem(z + shards - places_ref[1], shards)
            return pltpu.make_async_copy(cut.at[at, z], outs[at].at[ahead], out_sems.at[at, z])

        for load in loads:
            load.start()
        for at in range(count):
            loads[at].wait()
            for z in range(shards):
                cut[at, z] = held[at, :, z * block : (z + 1) * block]
                store(at, z).start()
        for at in range(count):
            for z in range(shards):
                store(at, z).wait()

    return pl.pallas_call(
        body,
        out_shape=[jax.ShapeDtypeStruct((shards, rows, block), jnp.bfloat16)] * count,
        in_specs=[pl.BlockSpec(memory_space=pltpu.SMEM)]
        + [pl.BlockSpec(memory_space=pl.ANY)] * count,
        out_specs=[pl.BlockSpec(memory_space=pl.ANY)] * count,
        scratch_shapes=[
            pltpu.VMEM((count, rows, columns), jnp.bfloat16),
            pltpu.VMEM((count, shards, rows, block), jnp.bfloat16),
            pltpu.SemaphoreType.DMA((count,)),
            pltpu.SemaphoreType.DMA((count, shards)),
        ],
        compiler_params=pltpu.CompilerParams(vmem_limit_bytes=VMEM_LIMIT),
        cost_estimate=COST,
        name="column_blocks",
    )(jnp.stack([place, shard_place]).astype(jnp.int32), *weights)


def place_blocks(order, places, pieces, others):
    half, groups, shards = pieces.shape[:3]

    def body(order_ref, places_ref, pieces_ref, others_ref, *rest):
        def source_of(g, k, r):
            return (pieces_ref if r < half else others_ref).at[r % half, g, k]

        move_blocks(source_of, lambda r: places_ref[r], order_ref, rest[:groups], *rest[groups:])

    return blocks_call(body, 2, 2, groups, shards, 2 * half, pieces.shape[3:])(
        order, places, pieces, others
    )


def place_gathered(order, gathered, groups):
    shards = lax.axis_size("shard")
    reps = gathered.shape[0] // (shards * groups)

    def body(order_ref, source, *rest):
        move_blocks(
            lambda g, k, r: source.at[(r * shards + k) * groups + g],
            lambda r: r,
            order_ref,
            rest[:groups],
            *rest[groups:],
        )

    return blocks_call(body, 1, 1, groups, shards, reps, gathered.shape[1:])(order, gathered)


def move_blocks(source_of, place_of, order_ref, outs, held, in_sems, out_sems):
    groups, shards, reps = in_sems.shape
    slabs = [(g, k) for g in range(groups) for k in range(shards)]

    def load(g, k, r):
        return pltpu.make_async_copy(
            source_of(g, k, r), held.at[g, k, place_of(r)], in_sems.at[g, k, r]
        )

    def store(g, k):
        return pltpu.make_async_copy(held.at[g, k], outs[g].at[order_ref[k]], out_sems.at[g, k])

    for g, k in slabs:
        for r in range(reps):
            load(g, k, r).start()
    for g, k in slabs:
        for r in range(reps):
            load(g, k, r).wait()
        store(g, k).start()
    for g, k in slabs:
        store(g, k).wait()


def blocks_call(body, scalars, sources, groups, shards, reps, block):
    whole = (shards, reps) + block
    return pl.pallas_call(
        body,
        out_shape=[jax.ShapeDtypeStruct(whole, jnp.bfloat16)] * groups,
        in_specs=[pl.BlockSpec(memory_space=pltpu.SMEM)] * scalars
        + [pl.BlockSpec(memory_space=pl.ANY)] * sources,
        out_specs=[pl.BlockSpec(memory_space=pl.ANY)] * groups,
        scratch_shapes=[
            pltpu.VMEM((groups,) + whole, jnp.bfloat16),
            pltpu.SemaphoreType.DMA((groups, shards, reps)),
            pltpu.SemaphoreType.DMA((groups, shards)),
        ],
        compiler_params=pltpu.CompilerParams(vmem_limit_bytes=VMEM_LIMIT),
        cost_estimate=COST,
        name="place_blocks",
    )


def widen_pieces(places, pieces, others):
    half, rows, columns = pieces.shape
    reps = 2 * half
    strip = next(size for size in (16, 8, rows) if rows % size == 0)

    def body(places_ref, pieces_ref, others_ref, out_ref, narrow, wide, in_sems, out_sems):
        loads = [
            pltpu.make_async_copy(
                (pieces_ref if r < half else others_ref).at[r % half], narrow.at[r], in_sems.at[r]
            )
            for r in range(reps)
        ]
        stores = [
            pltpu.make_async_copy(wide.at[r], out_ref.at[places_ref[r]], out_sems.at[r])
            for r in range(reps)
        ]
        for load in loads:
            load.start()
        for r in range(reps):
            loads[r].wait()

            def convert(at, carry):
                cut = pl.ds(pl.multiple_of(at * strip, strip), strip)
                wide[r, cut, :] = narrow[r, cut, :].astype(jnp.float32)
                return carry

            lax.fori_loop(0, rows // strip, convert, 0)
            stores[r].start()
        for store in stores:
            store.wait()

    result = pl.pallas_call(
        body,
        out_shape=jax.ShapeDtypeStruct((reps, rows, columns), jnp.float32),
        in_specs=[pl.BlockSpec(memory_space=pltpu.SMEM)]
        + [pl.BlockSpec(memory_space=pl.ANY)] * 2,
        out_specs=pl.BlockSpec(memory_space=pl.ANY),
        scratch_shapes=[
            pltpu.VMEM((reps, rows, columns), jnp.bfloat16),
            pltpu.VMEM((reps, rows, columns), jnp.float32),
            pltpu.SemaphoreType.DMA((reps,)),
            pltpu.SemaphoreType.DMA((reps,)),
        ],
        compiler_params=pltpu.CompilerParams(vmem_limit_bytes=VMEM_LIMIT),
        cost_estimate=COST,
        name="widen_pieces",
    )(places, pieces, others)
    return (result.reshape(reps * rows, columns),)


def resident(shape):
    return pl.BlockSpec(shape, lambda i: (0, 0), pipeline_mode=pl.Buffered(1))


def feed_forward(rows, cotangents, gate_matrix, up_matrix, down_matrix):
    count, width = rows.shape
    units = gate_matrix.shape[1]
    steps = pl.cdiv(units, TILE)
    slabs = next(size for size in range(min(steps, width // 128), 0, -1) if width % (128 * size) == 0)
    slab = width // slabs

    def body(
        rows_ref,
        cotangents_ref,
        gate_ref,
        up_ref,
        down_ref,
        inner_ref,
        d_gate_ref,
        d_up_ref,
        turned_rows_ref,
        turned_inner_ref,
    ):
        gate = jnp.dot(rows_ref[...], gate_ref[...], preferred_element_type=jnp.float32)
        up = jnp.dot(rows_ref[...], up_ref[...], preferred_element_type=jnp.float32)
        sigmoid = jax.nn.sigmoid(gate)
        silu = gate * sigmoid
        inner = (silu * up).astype(jnp.bfloat16)
        inner_ref[...] = inner
        turned_inner_ref[...] = inner.T
        d_inner = times_transposed(cotangents_ref[...], down_ref[...])
        d_up_ref[...] = (d_inner * silu).astype(jnp.bfloat16)
        d_gate_ref[...] = (d_inner * up * sigmoid * (1.0 + gate * (1.0 - sigmoid))).astype(
            jnp.bfloat16
        )
        for step in range(slabs):

            @pl.when(pl.program_id(0) == step)
            def turn():
                turned_rows_ref[...] = rows_ref[:, step * slab : (step + 1) * slab].T

    columns = pl.BlockSpec((width, TILE), lambda i: (0, i))
    results = pl.BlockSpec((count, TILE), lambda i: (0, i))
    return pl.pallas_call(
        body,
        grid=(steps,),
        out_shape=[jax.ShapeDtypeStruct((count, units), jnp.bfloat16)] * 3
        + [
            jax.ShapeDtypeStruct((width, count), jnp.bfloat16),
            jax.ShapeDtypeStruct((units, count), jnp.bfloat16),
        ],
        in_specs=[
            resident((count, width)),
            resident((count, width)),
            columns,
            columns,
            pl.BlockSpec((TILE, width), lambda i: (i, 0)),
        ],
        out_specs=[results] * 3
        + [
            pl.BlockSpec((slab, count), lambda i: (jnp.minimum(i, slabs - 1), 0)),
            pl.BlockSpec((TILE, count), lambda i: (i, 0)),
        ],
        compiler_params=pltpu.CompilerParams(vmem_limit_bytes=VMEM_LIMIT),
        cost_estimate=COST,
        name="feed_forward",
    )(rows, cotangents, gate_matrix, up_matrix, down_matrix)


def split_gradient(left, right, groups, places, core_place, turned):
    rows, count = left.shape if turned else left.shape[::-1]
    columns = right.shape[1]
    half = rows // (2 * groups)
    part = half // places

    def body(core_ref, left_ref, right_ref, other_ref, own_ref, *scratch):
        if turned:
            rows_ref = left_ref
        else:
            (rows_ref,) = scratch

            @pl.when(pl.program_id(0) == 0)
            def turn():
                rows_ref[...] = left_ref[...].T

        core = core_ref[0]
        for out_ref, which in ((other_ref, 1 - core), (own_ref, core)):
            halves = [
                rows_ref[pl.ds(pl.multiple_of((2 * group + which) * half, 16), half), :]
                for group in range(groups)
            ]
            product = jnp.dot(
                jnp.concatenate(halves, axis=0), right_ref[...], preferred_element_type=jnp.float32
            )
            for group in range(groups):
                for place in range(places):
                    at = group * half + place * part
                    out_ref[place, group] = product[at : at + part].astype(jnp.bfloat16)

    return pl.pallas_call(
        body,
        grid=(pl.cdiv(columns, TILE),),
        out_shape=[jax.ShapeDtypeStruct((places, groups, part, columns), jnp.bfloat16)] * 2,
        in_specs=[
            pl.BlockSpec(memory_space=pltpu.SMEM),
            resident(left.shape),
            pl.BlockSpec((count, TILE), lambda i: (0, i)),
        ],
        out_specs=[pl.BlockSpec((places, groups, part, TILE), lambda i: (0, 0, 0, i))] * 2,
        scratch_shapes=[] if turned else [pltpu.VMEM((rows, count), jnp.bfloat16)],
        compiler_params=pltpu.CompilerParams(vmem_limit_bytes=VMEM_LIMIT),
        cost_estimate=COST,
        name="split_gradient",
    )(core_place.reshape(1).astype(jnp.int32), left, right)


def ordered_gradient(left, right, shards, order):
    reps = len(order)
    rows, count = left.shape
    columns = right.shape[1]
    part = rows // (shards * reps)

    def body(left_ref, right_ref, out_ref):
        product = jnp.dot(left_ref[...], right_ref[...], preferred_element_type=jnp.float32)
        for z in range(shards):
            for r in range(reps):
                at = (z * reps + order[r]) * part
                out_ref[r, z] = product[at : at + part].astype(jnp.bfloat16)

    return pl.pallas_call(
        body,
        grid=(pl.cdiv(columns, TILE),),
        out_shape=[jax.ShapeDtypeStruct((reps, shards, part, columns), jnp.bfloat16)],
        in_specs=[
            resident((rows, count)),
            pl.BlockSpec((count, TILE), lambda i: (0, i)),
        ],
        out_specs=[pl.BlockSpec((reps, shards, part, TILE), lambda i: (0, 0, 0, i))],
        compiler_params=pltpu.CompilerParams(vmem_limit_bytes=VMEM_LIMIT),
        cost_estimate=COST,
        name="ordered_gradient",
    )(left, right)


def rows_product(lefts, rights, turned, blocks):
    count, depth = lefts[0].shape
    columns = rights[0].shape[0 if turned else 1]
    pairs, part = len(lefts), count // blocks

    def body(*refs):
        total = None
        for left_ref, right_ref in zip(refs[:pairs], refs[pairs : 2 * pairs]):
            if turned:
                product = times_transposed(left_ref[...], right_ref[...])
            else:
                product = jnp.dot(
                    left_ref[...], right_ref[...], preferred_element_type=jnp.float32
                )
            total = product if total is None else total + product
        for block in range(blocks):
            refs[2 * pairs + block][...] = total[block * part : (block + 1) * part].astype(
                jnp.bfloat16
            )

    right_spec = (
        pl.BlockSpec((TILE, depth), lambda i: (i, 0))
        if turned
        else pl.BlockSpec((depth, TILE), lambda i: (0, i))
    )
    return pl.pallas_call(
        body,
        grid=(pl.cdiv(columns, TILE),),
        out_shape=[jax.ShapeDtypeStruct((part, columns), jnp.bfloat16)] * blocks,
        in_specs=[resident((count, depth))] * pairs + [right_spec] * pairs,
        out_specs=[pl.BlockSpec((part, TILE), lambda i: (0, i))] * blocks,
        compiler_params=pltpu.CompilerParams(vmem_limit_bytes=VMEM_LIMIT),
        cost_estimate=COST,
        name="rows_product",
    )(*lefts, *rights)


def kept_bias(row_segments, row_index, key_segments, key_index):
    kept = (row_segments == key_segments) & (key_index <= row_index)
    return jnp.where(kept, 0.0, MASKED)


def in_vmem(count):
    return [pl.BlockSpec(memory_space=pltpu.VMEM)] * count


def attention_forward(projected, cosine, signed_sine, pairs, rows, keys):
    count = projected.shape[0]
    per_group = QH // KVH
    scale = 1.0 / math.sqrt(HD)
    shape = (KVH, per_group * count, HD)

    def body(projected_ref, cosine_ref, sine_ref, pairs_ref, rows_ref, keys_ref, queries_ref, out_ref):
        bias = kept_bias(rows_ref[:, 0:1], rows_ref[:, 1:2], keys_ref[0:1, :], keys_ref[1:2, :])
        for k in range(KVH):
            for h in range(per_group):
                at = (k * per_group + h) * HD
                field = projected_ref[:, at : at + HD]
                queries_ref[k, h * count : (h + 1) * count, :] = (
                    field * cosine_ref[...] + pltpu.roll(field, HD // 2, 1) * sine_ref[...]
                ).astype(jnp.bfloat16)
            keys_here = pairs_ref[:, k * HD : (k + 1) * HD]
            values_here = pairs_ref[:, (KVH + k) * HD : (KVH + k + 1) * HD]
            scores = times_transposed(queries_ref[k], keys_here) * scale + bias
            powers = jnp.exp(scores - jnp.max(scores, axis=1, keepdims=True))
            shares = powers * (1.0 / jnp.sum(powers, axis=1, keepdims=True))
            result = jnp.dot(
                shares.astype(jnp.bfloat16), values_here, preferred_element_type=jnp.float32
            ).astype(jnp.bfloat16)
            for h in range(per_group):
                at = (k * per_group + h) * HD
                out_ref[:, at : at + HD] = result[h * count : (h + 1) * count]

    return pl.pallas_call(
        body,
        out_shape=[
            jax.ShapeDtypeStruct(shape, jnp.bfloat16),
            jax.ShapeDtypeStruct((count, QH * HD), jnp.bfloat16),
        ],
        in_specs=in_vmem(6),
        out_specs=in_vmem(2),
        compiler_params=pltpu.CompilerParams(vmem_limit_bytes=VMEM_LIMIT),
        cost_estimate=COST,
        name="attention_forward",
    )(projected, cosine, signed_sine, pairs, rows, keys)


def attention_backward(queries, gradient, pairs, cosine, signed_sine, rows, keys, blocks):
    count = gradient.shape[0]
    per_group = QH // KVH
    scale = 1.0 / math.sqrt(HD)
    group_rows = pairs.shape[0]
    part = group_rows // blocks

    def body(queries_ref, gradient_ref, pairs_ref, cosine_ref, sine_ref, rows_ref, keys_ref, d_ref, *outs):
        block_refs, stacked = outs[:blocks], outs[blocks]
        bias = kept_bias(rows_ref[0:1, :], rows_ref[1:2, :], keys_ref[:, 0:1], keys_ref[:, 1:2])
        for k in range(KVH):
            for h in range(per_group):
                at = (k * per_group + h) * HD
                stacked[h * count : (h + 1) * count, :] = gradient_ref[:, at : at + HD]
            keys_here = pairs_ref[:, k * HD : (k + 1) * HD]
            values_here = pairs_ref[:, (KVH + k) * HD : (KVH + k + 1) * HD]
            scores = times_transposed(keys_here, queries_ref[k]) * scale + bias
            powers = jnp.exp(scores - jnp.max(scores, axis=0, keepdims=True))
            shares = powers * (1.0 / jnp.sum(powers, axis=0, keepdims=True))
            d_shares = times_transposed(values_here, stacked[...])
            dots = jnp.sum(shares * d_shares, axis=0, keepdims=True)
            d_scores = (shares * (d_shares - dots)).astype(jnp.bfloat16)
            d_keys = jnp.dot(d_scores, queries_ref[k], preferred_element_type=jnp.float32) * scale
            d_values = jnp.dot(
                shares.astype(jnp.bfloat16), stacked[...], preferred_element_type=jnp.float32
            )
            for block in range(blocks):
                cut = slice(block * part, (block + 1) * part)
                block_refs[block][:, k * HD : (k + 1) * HD] = d_keys[cut].astype(jnp.bfloat16)
                block_refs[block][:, (KVH + k) * HD : (KVH + k + 1) * HD] = d_values[cut].astype(
                    jnp.bfloat16
                )
            d_queries = transposed_times(d_scores, keys_here) * scale
            for h in range(per_group):
                at = (k * per_group + h) * HD
                field = d_queries[h * count : (h + 1) * count]
                d_ref[:, at : at + HD] = (
                    field * cosine_ref[...] - pltpu.roll(field, HD // 2, 1) * sine_ref[...]
                ).astype(jnp.bfloat16)

    return pl.pallas_call(
        body,
        out_shape=[jax.ShapeDtypeStruct((count, QH * HD), jnp.bfloat16)]
        + [jax.ShapeDtypeStruct((part, 2 * KVH * HD), jnp.bfloat16)] * blocks,
        in_specs=in_vmem(7),
        out_specs=in_vmem(1 + blocks),
        scratch_shapes=[pltpu.VMEM((per_group * count, HD), jnp.bfloat16)],
        compiler_params=pltpu.CompilerParams(vmem_limit_bytes=VMEM_LIMIT),
        cost_estimate=COST,
        name="attention_backward",
    )(queries, gradient, pairs, cosine, signed_sine, rows, keys)


def join_projected(d_queries, pair_terms, cosine, signed_sine):
    count, query_width = d_queries.shape
    pair_width = KVH * HD
    terms = len(pair_terms)

    def body(d_queries_ref, cosine_ref, sine_ref, *refs):
        term_refs, out_ref, sum_ref = refs[:terms], refs[terms], refs[terms + 1]
        out_ref[:, :query_width] = d_queries_ref[...]
        for at in range(0, 2 * pair_width, HD):
            field = total_of([term[:, at : at + HD] for term in term_refs])
            if at < pair_width:
                field = field * cosine_ref[...] - pltpu.roll(field, HD // 2, 1) * sine_ref[...]
            out_ref[:, query_width + at : query_width + at + HD] = field.astype(jnp.bfloat16)
        sum_ref[...] = jnp.sum(out_ref[...].astype(jnp.float32), axis=0, keepdims=True)

    return pl.pallas_call(
        body,
        out_shape=[
            jax.ShapeDtypeStruct((count, query_width + 2 * pair_width), jnp.bfloat16),
            jax.ShapeDtypeStruct((1, query_width + 2 * pair_width), jnp.float32),
        ],
        in_specs=in_vmem(3 + terms),
        out_specs=in_vmem(2),
        cost_estimate=COST,
        name="join_projected",
    )(d_queries, cosine, signed_sine, *pair_terms)


def on_device(
    tokens,
    segment_ids,
    first_gain,
    input_weight,
    input_bias,
    output_weight,
    second_gain,
    gate_weight,
    up_weight,
    down_weight,
    output_cotangent,
):
    bf16, f32 = jnp.bfloat16, jnp.float32
    shards, reps = lax.axis_size("shard"), lax.axis_size("rep")
    shard, core, first, second = make_lines(reps, shards)
    rep_place = (core.place * first.size + first.place) * second.size + second.place
    own_rows, width = tokens.shape
    segments = segment_ids[0]
    per_group = QH // KVH
    query_width = QH * HD
    pair_width = KVH * HD
    first_row = shard.place * own_rows
    part_rows = input_weight.shape[0] // reps
    hidden_units = gate_weight.shape[1]
    block_units = hidden_units // shards
    clock = Clock()
    z_order = jnp.stack([shard.behind(step) for step in range(shards)]).astype(jnp.int32)

    def weight_piece(weight, place):
        return pick(weight.reshape(reps, part_rows, weight.shape[1]), place, 0)

    def spread(piece):
        return Spread(clock, piece, core, first, second)

    def blocks_of(blocks):
        return [pick(blocks, shard.ahead(step), 0) for step in range(shards)]

    steps = range(1, shards)

    def send_blocks(blocks):
        return clock.send(shard, blocks[1:], steps)

    def send_around(value):
        return clock.send(shard, [value] * len(steps), steps)

    def send_back(rows):
        return clock.send(shard, rows, [shards - step for step in steps])

    rep_index = lax.axis_index("rep")
    shard_vectors = jnp.concatenate([first_gain, second_gain, input_bias])
    vector_row = jnp.pad(shard_vectors, (0, input_weight.shape[1] - shard_vectors.shape[0]))
    own_input = jnp.concatenate([weight_piece(input_weight, rep_place), vector_row[None]], axis=0)
    input_moving = send_around(own_input)
    gate_blocks, up_blocks = clock.run(
        lambda *weights: column_blocks(rep_index, shard.place, *weights),
        gate_weight.reshape(reps, part_rows, hidden_units),
        up_weight.reshape(reps, part_rows, hidden_units),
    )
    (output_piece,) = clock(weight_piece(output_weight, rep_index))
    (input_rows,) = clock.wait(input_moving)
    input_rows = [own_input] + input_rows

    input_spread = spread(jnp.stack([rows[:part_rows] for rows in input_rows])[None])
    passed = [[output_cotangent] * 2]
    passing = clock.pass_on(shard, *passed[-1])
    output_matrix = lax.all_gather(clock(output_piece)[0], ("shard", "rep"), axis=0, tiled=True)
    vector_rows = jnp.stack(in_place_order([rows[part_rows] for rows in input_rows], shard))
    own_gain = first_gain.shape[0]
    gain_one = vector_rows[:, :own_gain].reshape(width).astype(f32)
    gain_two = vector_rows[:, own_gain : 2 * own_gain].reshape(width).astype(f32)
    shift_row = (
        vector_rows[:, 2 * own_gain : shard_vectors.shape[0]].reshape(-1).astype(f32)
    )
    places = positions(segments)
    cosine_table, sine_table = rope_tables(
        lax.dynamic_slice_in_dim(places, first_row, own_rows), HD
    )
    signed_sine = jnp.concatenate(
        [-sine_table[:, : HD // 2], sine_table[:, HD // 2 :]], axis=1
    )
    own_segments = lax.dynamic_slice_in_dim(segments, first_row, own_rows)
    row_index = jnp.arange(own_rows, dtype=jnp.int32)
    key_index = jnp.concatenate([shard.behind(step) * own_rows + row_index for step in range(shards)])
    key_segments = jnp.concatenate(
        [
            lax.dynamic_slice_in_dim(segments, shard.behind(step) * own_rows, own_rows)
            for step in range(shards)
        ]
    )
    key_marks = jnp.stack([key_segments, key_index])
    row_marks = jnp.tile(jnp.stack([own_segments, first_row + row_index]), (1, per_group))
    wide_tokens = tokens.astype(f32)
    inverse_one = lax.rsqrt(jnp.mean(wide_tokens * wide_tokens, axis=-1, keepdims=True) + EPSILON)
    unit_one = wide_tokens * inverse_one
    normed_one = (unit_one * gain_one).astype(bf16)
    (
        normed_one,
        cosine_table,
        sine_table,
        signed_sine,
        key_marks,
        row_marks,
    ) = clock(normed_one, cosine_table, sine_table, signed_sine, key_marks, row_marks)
    input_arrived, arrived = clock.wait(input_spread.moving, passing)
    passed.append(arrived)

    input_spread.along(input_arrived)
    gate_moving = send_blocks(gate_blocks)
    input_arrived, gate_rows = clock.wait(input_spread.moving, gate_moving)

    input_spread.over(input_arrived)
    up_moving = send_blocks(up_blocks)
    input_arrived, up_rows = clock.wait(input_spread.moving, up_moving)

    (input_matrix,) = clock.run(place_blocks, z_order, *input_spread.finish(input_arrived))
    input_matrix = input_matrix.reshape(width, -1)
    gate_up = jnp.stack(
        [row for pair in zip([gate_blocks[0]] + gate_rows, [up_blocks[0]] + up_rows) for row in pair]
    )
    projected = jnp.dot(normed_one, input_matrix, preferred_element_type=f32) + shift_row
    key_part = rotate(
        projected[:, query_width : query_width + pair_width].reshape(own_rows, KVH, HD),
        cosine_table,
        sine_table,
    )
    (own_pairs,) = clock(
        jnp.concatenate(
            [key_part.reshape(own_rows, pair_width), projected[:, query_width + pair_width :]],
            axis=1,
        ).astype(bf16)
    )
    pair_moving = send_around(own_pairs)
    passing = clock.pass_on(shard, *passed[-1]) if shards > 2 else []
    gate_up = lax.all_gather(clock(gate_up)[0], "rep", axis=0, tiled=True)
    pair_rows, arrived = clock.wait(pair_moving, passing)
    passed.append(arrived)
    pairs = jnp.concatenate([own_pairs] + pair_rows, axis=0)

    passing = clock.pass_on(shard, *passed[-1]) if shards > 3 else []
    queries, attention_low = clock.run(
        attention_forward, projected, cosine_table, signed_sine, pairs, row_marks.T, key_marks
    )
    output_matrix, attention_low = clock(output_matrix, attention_low)
    hidden = wide_tokens + jnp.dot(attention_low, output_matrix, preferred_element_type=f32)
    inverse_two = lax.rsqrt(jnp.mean(hidden * hidden, axis=-1, keepdims=True) + EPSILON)
    unit_two = hidden * inverse_two
    (normed_two,) = clock((unit_two * gain_two).astype(bf16))
    (arrived,) = clock.wait(passing)
    passed.append(arrived)

    normed_moving = send_around(normed_two)
    gate_matrix, up_matrix = clock.run(
        lambda order, gathered: place_gathered(order, gathered, 2), z_order, gate_up
    )
    gate_matrix = gate_matrix.reshape(width, block_units)
    up_matrix = up_matrix.reshape(width, block_units)
    (normed_arrived,) = clock.wait(normed_moving)
    while len(passed) < shards:
        (arrived,) = clock.wait(clock.pass_on(shard, *passed[-1]))
        passed.append(arrived)
    group_normed = jnp.concatenate([normed_two] + normed_arrived, axis=0)
    cotangents = jnp.concatenate(
        [output_cotangent]
        + [
            jnp.where(shard.place >= step, passed[step][0], passed[shards - step][1])
            for step in steps
        ],
        axis=0,
    )

    inner_act, d_gate, d_up, turned_normed, turned_inner = clock.run(
        feed_forward, group_normed, cotangents, gate_matrix, up_matrix, down_weight
    )

    def split_halves(left, right, groups, turned):
        count = first.size * second.size
        halves = clock.run(
            lambda left, right: split_gradient(left, right, groups, count, core.place, turned),
            left,
            right,
        )
        return [half.reshape((first.size, second.size) + half.shape[1:]) for half in halves]

    def side_by_side(rows):
        return clock(jnp.concatenate(list(rows), axis=1))[0]

    def sum_over_rep(blocks):
        return lax.psum_scatter(blocks, "rep", scatter_dimension=0, tiled=True)

    def row_sum(rows):
        return clock(total_of(list(rows)).astype(bf16))[0]

    def send_some(rows, chosen):
        return clock.send(shard, [rows[k] for k in chosen], [shards - 1 - k for k in chosen])

    edges = sorted({0, shards - 2})
    inside = list(range(1, shards - 2))

    def exchange(blocks):
        return clock(lax.all_to_all(blocks, "shard", 0, 0, tiled=True))[0]

    normed_own, *normed_partial = clock.run(
        lambda *operands: rows_product(operands[:2], operands[2:], True, shards),
        d_gate,
        d_up,
        gate_matrix,
        up_matrix,
    )
    up_halves = split_halves(turned_normed, d_up, shards, True)

    up = Halving(clock, *up_halves, core, first, second)
    normed_moving = send_some(normed_partial, edges)
    (gate_blocks,) = clock.run(
        lambda left, right: ordered_gradient(left, right, shards, rep_places(reps)),
        turned_normed,
        d_gate,
    )
    up_arrived, normed_arrived = clock.wait(up.moving, normed_moving)
    gate_piece = sum_over_rep(clock(gate_blocks)[0].reshape(width, block_units))

    up.along_first(up_arrived)
    normed_moving = send_some(normed_partial, inside)
    (down_blocks,) = clock.run(
        lambda left, right: ordered_gradient(left, right, 1, list(range(reps))),
        turned_inner,
        cotangents,
    )
    up_arrived, more_arrived = clock.wait(up.moving, normed_moving)

    up.along_second(up_arrived)
    normed_two_gradient = total_of([normed_own] + normed_arrived + more_arrived)
    gain_two_gradient = jnp.sum(normed_two_gradient * unit_two, axis=0)
    hidden_gradient = output_cotangent.astype(f32) + norm_back(
        normed_two_gradient, unit_two, inverse_two, gain_two
    )
    (branch_gradient,) = clock(hidden_gradient.astype(bf16))
    (attention_gradient,) = clock(times_transposed(branch_gradient, output_matrix).astype(bf16))
    d_queries, pair_own, *pair_partial = clock.run(
        lambda *operands: attention_backward(*operands, shards),
        queries,
        attention_gradient,
        pairs,
        cosine_table,
        signed_sine,
        row_marks,
        key_marks.T,
    )
    output_halves = split_halves(attention_low, branch_gradient, shards, False)
    (up_arrived,) = clock.wait(up.moving)

    pair_moving = send_back(pair_partial)
    output = Halving(clock, *output_halves, core, first, second)
    up_blocks = clock(*blocks_of(up.finish(up_arrived)))
    pair_arrived, output_arrived = clock.wait(pair_moving, output.moving)

    output.along_first(output_arrived)
    up_moving = send_blocks(up_blocks)
    projected_gradient, bias_sum = clock.run(
        lambda *operands: join_projected(operands[0], operands[3:], *operands[1:3]),
        d_queries,
        cosine_table,
        signed_sine,
        pair_own,
        *pair_arrived,
    )
    projected_halves = split_halves(normed_one, projected_gradient, shards, False)
    output_arrived, up_rows = clock.wait(output.moving, up_moving)

    projected = Halving(clock, *projected_halves, core, first, second)
    output.along_second(output_arrived)
    up_spread = spread(side_by_side(in_place_order(up_blocks[:1] + up_rows, shard)))
    (gate_piece,) = clock(gate_piece)
    down_piece = sum_over_rep(clock(down_blocks)[0].reshape(block_units, width))
    block_own, *block_partial = clock.run(
        lambda left, right: rows_product((left,), (right,), False, shards), inner_act, down_weight
    )
    projected_gradient, hidden_gradient = clock(projected_gradient, hidden_gradient)
    normed_one_gradient = times_transposed(projected_gradient, input_matrix)
    gain_one_gradient = jnp.sum(normed_one_gradient * unit_one, axis=0)
    (tokens_gradient,) = clock(
        (
            hidden_gradient + norm_back(normed_one_gradient, unit_one, inverse_one, gain_one)
        ).astype(bf16)
    )
    projected_arrived, output_arrived, up_arrived = clock.wait(
        projected.moving, output.moving, up_spread.moving
    )

    projected.along_first(projected_arrived)
    up_spread.along(up_arrived)
    block_moving = send_some(block_partial, edges[:1])
    output_sum = output.finish(output_arrived)
    gate_sum = exchange(gate_piece.reshape(shards, part_rows, block_units))
    bias_gradient = bias_sum[0]
    bias_split = query_width + pair_width
    small_parts = (
        gain_one_gradient,
        gain_two_gradient,
        bias_gradient[:bias_split],
        bias_gradient[bias_split:],
    )
    (small,) = clock(
        jnp.concatenate([part.reshape(shards, -1) for part in small_parts], axis=1)
    )
    projected_arrived, up_arrived, block_arrived = clock.wait(
        projected.moving, up_spread.moving, block_moving
    )

    projected.along_second(projected_arrived)
    gate_spread = spread(side_by_side(gate_sum))
    up_spread.over(up_arrived)
    block_moving = send_some(block_partial, edges[1:])
    output_sum = row_sum(exchange(output_sum))
    projected_arrived, gate_arrived, up_arrived, more_arrived = clock.wait(
        projected.moving, gate_spread.moving, up_spread.moving, block_moving
    )
    block_arrived = block_arrived + more_arrived

    input_sum = projected.finish(projected_arrived)
    gate_spread.along(gate_arrived)
    output_spread = spread(output_sum)
    small_moving = clock.send(core, [small], [1])
    input_sum = row_sum(exchange(input_sum))
    gate_arrived, output_arrived, small_arrived = clock.wait(
        gate_spread.moving, output_spread.moving, small_moving
    )
    small = total_of([small] + small_arrived)

    input_spread = spread(input_sum)
    output_spread.along(output_arrived)
    gate_spread.over(gate_arrived)
    small_moving = clock.send(first, [small] * (first.size - 1), range(1, first.size))
    (down_piece,) = clock(down_piece)
    down_gathered = lax.all_gather(down_piece, "rep", axis=0, tiled=True)
    (up_total,) = clock.run(widen_pieces, *up_spread.finish(up_arrived))
    input_arrived, output_arrived, gate_arrived, small_arrived = clock.wait(
        input_spread.moving, output_spread.moving, gate_spread.moving, small_moving
    )
    small = total_of([small] + small_arrived)

    input_spread.along(input_arrived)
    output_spread.over(output_arrived)
    small_moving = clock.send(second, [small] * (second.size - 1), range(1, second.size))
    block_moving = send_some(block_partial, inside)
    (gate_total,) = clock.run(widen_pieces, *gate_spread.finish(gate_arrived))
    input_arrived, output_arrived, small_arrived, more_arrived = clock.wait(
        input_spread.moving, output_spread.moving, small_moving, block_moving
    )
    small = total_of([small] + small_arrived)
    block_arrived = block_arrived + more_arrived

    input_spread.over(input_arrived)
    small_blocks = clock(*blocks_of(small))
    small_moving = send_blocks(small_blocks)
    (output_total,) = clock.run(widen_pieces, *output_spread.finish(output_arrived))
    input_arrived, small_arrived = clock.wait(input_spread.moving, small_moving)
    small = total_of(small_blocks[:1] + small_arrived)
    (block_out,) = clock(total_of([hidden, block_own] + block_arrived).astype(bf16))
    (down_gathered,) = clock(down_gathered)
    (down_total,) = clock(down_gathered.astype(f32))
    (input_total,) = clock.run(widen_pieces, *input_spread.finish(input_arrived))

    small = small + clock.token[0, 0]
    small_totals, at = [], 0
    for part in small_parts:
        size = part.shape[0] // shards
        small_totals.append(small[at : at + size])
        at += size
    return (
        block_out,
        tokens_gradient,
        small_totals[0],
        input_total,
        small_totals[2],
        small_totals[3],
        output_total,
        small_totals[1],
        gate_total,
        up_total,
        down_total,
    )


def solution(mesh):
    placed = (
        P(("rep", "shard"), None),
        P("rep", None),
        P("shard"),
        P("shard", None),
        P("shard"),
        P("shard", None),
        P("shard"),
        P("shard", None),
        P("shard", None),
        P("shard", None),
        P(("rep", "shard"), None),
    )
    return jax.shard_map(
        on_device,
        mesh=mesh,
        in_specs=placed,
        out_specs=(
            P(("rep", "shard"), None),
            P(("rep", "shard"), None),
            P("shard"),
            P("shard", None),
            P("shard"),
            P("shard"),
            P("shard", None),
            P("shard"),
            P("shard", None),
            P("shard", None),
            P("shard", None),
        ),
        check_vma=False,
    )
```

```python
import math

import jax
import jax.numpy as jnp
from jax import lax
from jax.experimental import pallas as pl
from jax.experimental.pallas import tpu as pltpu
from jax.sharding import PartitionSpec as P

QH = 12
KVH = 2
HD = 128
SEQS = 3


EPSILON = 1e-06
LOG_THETA = math.log(1000000.0)
MASKED = -1e30
VMEM_LIMIT = 56 * 1024 * 1024
TILE = 512
COST = pl.CostEstimate(flops=1, bytes_accessed=1, transcendentals=0)


def rope_tables(places, head_width):
    half_width = head_width // 2
    frequency = jnp.exp(jnp.arange(half_width, dtype=jnp.float32) * (-2.0 * LOG_THETA / head_width))
    angles = places.astype(jnp.float32)[:, None] * frequency[None, :]
    angles = jnp.concatenate([angles, angles], axis=-1)
    return (jnp.cos(angles), jnp.sin(angles))


def positions(segments):
    labels = jnp.arange(SEQS, dtype=jnp.int32)
    starts = jnp.sum((segments[None, :] < labels[:, None]).astype(jnp.int32), axis=1)
    own_start = jnp.sum(jnp.where(segments[:, None] == labels[None, :], starts[None, :], 0), axis=1)
    return jnp.arange(segments.shape[0], dtype=jnp.int32) - own_start


def rotate(field_rows, cosine_table, sine_table):
    half_width = field_rows.shape[-1] // 2
    turned = jnp.concatenate([-field_rows[..., half_width:], field_rows[..., :half_width]], axis=-1)
    return field_rows * cosine_table[:, None, :] + turned * sine_table[:, None, :]


def transposed_times(left_side, right_side):
    return lax.dot_general(
        left_side, right_side, (((0,), (0,)), ((), ())), preferred_element_type=jnp.float32
    )


def times_transposed(left_side, right_side):
    return lax.dot_general(
        left_side, right_side, (((1,), (1,)), ((), ())), preferred_element_type=jnp.float32
    )


def norm_back(normed_gradient, unit_rows, inverse_rms, gain_row):
    scaled = normed_gradient * gain_row
    return inverse_rms * (scaled - unit_rows * jnp.mean(scaled * unit_rows, axis=-1, keepdims=True))


class Line:
    def __init__(self, name, size, place, pairs, crossed=False):
        self.name, self.size, self.place, self.pairs = name, size, place, pairs
        self.crossed = crossed

    def shift(self, value, step):
        return lax.ppermute(value, self.name, self.pairs(step % self.size))

    def pass_on(self, value, up):
        places = range(self.size - 1)
        pairs = [(at, at + 1) if up else (at + 1, at) for at in places]
        return lax.ppermute(value, self.name, pairs)

    def behind(self, step):
        return lax.rem(self.place + (self.size - step % self.size), self.size)

    def ahead(self, step):
        return lax.rem(self.place + step % self.size, self.size) if step else self.place


def make_lines(reps, shards):
    inner = 2 if reps % 4 == 0 else 1
    outer = reps // (2 * inner)
    square = inner == outer

    def split(index):
        core, b, a = index % 2, (index // 2) % inner, index // (2 * inner)
        return core, b, a

    def join(core, b, a):
        return (a * inner + b) * 2 + core

    def first_pairs(step):
        pairs = []
        for index in range(reps):
            core, b, a = split(index)
            if square and core == 0:
                pairs.append((index, join(core, (b + step) % inner, a)))
            else:
                pairs.append((index, join(core, b, (a + step) % outer)))
        return pairs

    def second_pairs(step):
        pairs = []
        for index in range(reps):
            core, b, a = split(index)
            if square and core == 0:
                pairs.append((index, join(core, b, (a + step) % outer)))
            else:
                pairs.append((index, join(core, (b + step) % inner, a)))
        return pairs

    def core_pairs(step):
        pairs = []
        for index in range(reps):
            core, b, a = split(index)
            pairs.append((index, join((core + step) % 2, b, a)))
        return pairs

    def shard_pairs(step):
        return [(index, (index + step) % shards) for index in range(shards)]

    core, b, a = split(lax.axis_index("rep"))
    first, second = (jnp.where(core == 0, b, a), jnp.where(core == 0, a, b)) if square else (a, b)
    return (
        Line("shard", shards, lax.axis_index("shard"), shard_pairs),
        Line("rep", 2, core, core_pairs, square),
        Line("rep", outer, first, first_pairs),
        Line("rep", inner, second, second_pairs),
    )


def rep_places(reps):
    inner = 2 if reps % 4 == 0 else 1
    outer = reps // (2 * inner)
    places = []
    for index in range(reps):
        core, b, a = index % 2, (index // 2) % inner, index // (2 * inner)
        one, two = (b, a) if inner == outer and core == 0 else (a, b)
        places.append((core * outer + one) * inner + two)
    return places


def pick(array, index, axis):
    return lax.dynamic_index_in_dim(array, index, axis, keepdims=False)


def put(array, piece, index, axis):
    return lax.dynamic_update_index_in_dim(array, piece, index, axis)


def in_place_order(pieces, line):
    ordered = []
    for place in range(line.size):
        chosen = pieces[0]
        for step in range(1, line.size):
            chosen = jnp.where(line.behind(step) == place, pieces[step], chosen)
        ordered.append(chosen)
    return ordered


def tie(*arrays):
    return lax.optimization_barrier(arrays)


def gather_line(value, line):
    return [value] + [line.shift(value, step) for step in range(1, line.size)]


class Clock:
    def __init__(self):
        self.token = jnp.zeros((8, 128), jnp.float32)
        self.open = 0

    def __call__(self, *arrays):
        self.token, *arrays = tie(self.token, *arrays)
        return arrays

    def run(self, step, *arrays):
        return self(*step(*self(*arrays)))

    def send(self, line, values, steps):
        self.open += len(values)
        return [line.shift(value, step) for value, step in zip(self(*values), steps)]

    def pass_on(self, line, lower, upper):
        self.open += 2
        lower, upper = self(lower, upper)
        return [line.pass_on(lower, True), line.pass_on(upper, False)]

    def wait(self, *groups):
        flat = self(*[array for group in groups for array in group])
        self.open -= len(flat)
        parts, at = [], 0
        for group in groups:
            parts.append(flat[at : at + len(group)])
            at += len(group)
        return parts


def total_of(terms):
    total = terms[0].astype(jnp.float32)
    for term in terms[1:]:
        total = total + term.astype(jnp.float32)
    return total


class Halving:
    def __init__(self, clock, sent, own, core, first, second):
        self.clock, self.first, self.second = clock, first, second
        self.terms = [own]
        self.moving = clock.send(core, [sent], [1])

    def along(self, line, arrived):
        self.terms = self.terms + arrived
        steps = range(1, line.size)
        blocks = [
            total_of([pick(term, line.ahead(step), 0) for term in self.terms]).astype(jnp.bfloat16)
            for step in steps
        ]
        self.moving = self.clock.send(line, blocks, steps)
        self.terms = [pick(term, line.place, 0) for term in self.terms]

    def along_first(self, arrived):
        self.along(self.first, arrived)

    def along_second(self, arrived):
        self.along(self.second, arrived)

    def finish(self, arrived):
        return self.clock(total_of(self.terms + arrived).astype(jnp.bfloat16))[0]


class Spread:
    def __init__(self, clock, piece, core, first, second):
        self.clock, self.lines = clock, (core, first, second)
        self.pieces = [piece]
        steps = range(1, second.size)
        self.moving = clock.send(second, [piece] * len(steps), steps)

    def along(self, arrived):
        core, first, second = self.lines
        self.pieces = self.pieces + arrived
        steps = range(1, first.size)
        self.moving = self.clock.send(first, [jnp.stack(self.pieces)] * len(steps), steps)

    def over(self, arrived):
        core, first, second = self.lines
        rows = [jnp.stack(self.pieces)] + arrived
        self.pieces = jnp.concatenate(rows, axis=0)
        self.moving = self.clock.send(core, [self.pieces], [1])

    def finish(self, arrived):
        core, first, second = self.lines
        (others,) = arrived
        offsets = [(one, two) for one in range(first.size) for two in range(second.size)]
        placed = [(core.place, first.behind(one), second.behind(two)) for one, two in offsets]
        far, near = (second, first) if core.crossed else (first, second)
        placed += [(core.behind(1), far.behind(one), near.behind(two)) for one, two in offsets]
        places = [(c * first.size + f) * second.size + s for c, f, s in placed]
        return [jnp.stack(places).astype(jnp.int32), self.pieces, others]


def column_blocks(place, shard_place, *weights):
    count = len(weights)
    rows, columns = weights[0].shape[1:]
    shards = lax.axis_size("shard")
    block = columns // shards

    def body(places_ref, *refs):
        sources, outs = refs[:count], refs[count : 2 * count]
        held, cut, in_sems, out_sems = refs[2 * count :]
        loads = [
            pltpu.make_async_copy(sources[at].at[places_ref[0]], held.at[at], in_sems.at[at])
            for at in range(count)
        ]

        def store(at, z):
            ahead = lax.rem(z + shards - places_ref[1], shards)
            return pltpu.make_async_copy(cut.at[at, z], outs[at].at[ahead], out_sems.at[at, z])

        for load in loads:
            load.start()
        for at in range(count):
            loads[at].wait()
            for z in range(shards):
                cut[at, z] = held[at, :, z * block : (z + 1) * block]
                store(at, z).start()
        for at in range(count):
            for z in range(shards):
                store(at, z).wait()

    return pl.pallas_call(
        body,
        out_shape=[jax.ShapeDtypeStruct((shards, rows, block), jnp.bfloat16)] * count,
        in_specs=[pl.BlockSpec(memory_space=pltpu.SMEM)]
        + [pl.BlockSpec(memory_space=pl.ANY)] * count,
        out_specs=[pl.BlockSpec(memory_space=pl.ANY)] * count,
        scratch_shapes=[
            pltpu.VMEM((count, rows, columns), jnp.bfloat16),
            pltpu.VMEM((count, shards, rows, block), jnp.bfloat16),
            pltpu.SemaphoreType.DMA((count,)),
            pltpu.SemaphoreType.DMA((count, shards)),
        ],
        compiler_params=pltpu.CompilerParams(vmem_limit_bytes=VMEM_LIMIT),
        cost_estimate=COST,
        name="column_blocks",
    )(jnp.stack([place, shard_place]).astype(jnp.int32), *weights)


def place_blocks(order, places, pieces, others):
    half, groups, shards = pieces.shape[:3]

    def body(order_ref, places_ref, pieces_ref, others_ref, *rest):
        def source_of(g, k, r):
            return (pieces_ref if r < half else others_ref).at[r % half, g, k]

        move_blocks(source_of, lambda r: places_ref[r], order_ref, rest[:groups], *rest[groups:])

    return blocks_call(body, 2, 2, groups, shards, 2 * half, pieces.shape[3:])(
        order, places, pieces, others
    )


def place_gathered(order, gathered, groups):
    shards = lax.axis_size("shard")
    reps = gathered.shape[0] // (shards * groups)

    def body(order_ref, source, *rest):
        move_blocks(
            lambda g, k, r: source.at[(r * shards + k) * groups + g],
            lambda r: r,
            order_ref,
            rest[:groups],
            *rest[groups:],
        )

    return blocks_call(body, 1, 1, groups, shards, reps, gathered.shape[1:])(order, gathered)


def move_blocks(source_of, place_of, order_ref, outs, held, in_sems, out_sems):
    groups, shards, reps = in_sems.shape
    slabs = [(g, k) for g in range(groups) for k in range(shards)]

    def load(g, k, r):
        return pltpu.make_async_copy(
            source_of(g, k, r), held.at[g, k, place_of(r)], in_sems.at[g, k, r]
        )

    def store(g, k):
        return pltpu.make_async_copy(held.at[g, k], outs[g].at[order_ref[k]], out_sems.at[g, k])

    for g, k in slabs:
        for r in range(reps):
            load(g, k, r).start()
    for g, k in slabs:
        for r in range(reps):
            load(g, k, r).wait()
        store(g, k).start()
    for g, k in slabs:
        store(g, k).wait()


def blocks_call(body, scalars, sources, groups, shards, reps, block):
    whole = (shards, reps) + block
    return pl.pallas_call(
        body,
        out_shape=[jax.ShapeDtypeStruct(whole, jnp.bfloat16)] * groups,
        in_specs=[pl.BlockSpec(memory_space=pltpu.SMEM)] * scalars
        + [pl.BlockSpec(memory_space=pl.ANY)] * sources,
        out_specs=[pl.BlockSpec(memory_space=pl.ANY)] * groups,
        scratch_shapes=[
            pltpu.VMEM((groups,) + whole, jnp.bfloat16),
            pltpu.SemaphoreType.DMA((groups, shards, reps)),
            pltpu.SemaphoreType.DMA((groups, shards)),
        ],
        compiler_params=pltpu.CompilerParams(vmem_limit_bytes=VMEM_LIMIT),
        cost_estimate=COST,
        name="place_blocks",
    )


def widen_pieces(places, pieces, others):
    half, rows, columns = pieces.shape
    reps = 2 * half
    strip = next(size for size in (16, 8, rows) if rows % size == 0)

    def body(places_ref, pieces_ref, others_ref, out_ref, narrow, wide, in_sems, out_sems):
        loads = [
            pltpu.make_async_copy(
                (pieces_ref if r < half else others_ref).at[r % half], narrow.at[r], in_sems.at[r]
            )
            for r in range(reps)
        ]
        stores = [
            pltpu.make_async_copy(wide.at[r], out_ref.at[places_ref[r]], out_sems.at[r])
            for r in range(reps)
        ]
        for load in loads:
            load.start()
        for r in range(reps):
            loads[r].wait()

            def convert(at, carry):
                cut = pl.ds(pl.multiple_of(at * strip, strip), strip)
                wide[r, cut, :] = narrow[r, cut, :].astype(jnp.float32)
                return carry

            lax.fori_loop(0, rows // strip, convert, 0)
            stores[r].start()
        for store in stores:
            store.wait()

    result = pl.pallas_call(
        body,
        out_shape=jax.ShapeDtypeStruct((reps, rows, columns), jnp.float32),
        in_specs=[pl.BlockSpec(memory_space=pltpu.SMEM)]
        + [pl.BlockSpec(memory_space=pl.ANY)] * 2,
        out_specs=pl.BlockSpec(memory_space=pl.ANY),
        scratch_shapes=[
            pltpu.VMEM((reps, rows, columns), jnp.bfloat16),
            pltpu.VMEM((reps, rows, columns), jnp.float32),
            pltpu.SemaphoreType.DMA((reps,)),
            pltpu.SemaphoreType.DMA((reps,)),
        ],
        compiler_params=pltpu.CompilerParams(vmem_limit_bytes=VMEM_LIMIT),
        cost_estimate=COST,
        name="widen_pieces",
    )(places, pieces, others)
    return (result.reshape(reps * rows, columns),)


def resident(shape):
    return pl.BlockSpec(shape, lambda i: (0, 0), pipeline_mode=pl.Buffered(1))


def feed_forward(rows, cotangents, gate_matrix, up_matrix, down_matrix):
    count, width = rows.shape
    units = gate_matrix.shape[1]
    steps = pl.cdiv(units, TILE)
    slabs = next(size for size in range(min(steps, width // 128), 0, -1) if width % (128 * size) == 0)
    slab = width // slabs

    def body(
        rows_ref,
        cotangents_ref,
        gate_ref,
        up_ref,
        down_ref,
        inner_ref,
        d_gate_ref,
        d_up_ref,
        turned_rows_ref,
        turned_inner_ref,
    ):
        gate = jnp.dot(rows_ref[...], gate_ref[...], preferred_element_type=jnp.float32)
        up = jnp.dot(rows_ref[...], up_ref[...], preferred_element_type=jnp.float32)
        sigmoid = jax.nn.sigmoid(gate)
        silu = gate * sigmoid
        inner = (silu * up).astype(jnp.bfloat16)
        inner_ref[...] = inner
        turned_inner_ref[...] = inner.T
        d_inner = times_transposed(cotangents_ref[...], down_ref[...])
        d_up_ref[...] = (d_inner * silu).astype(jnp.bfloat16)
        d_gate_ref[...] = (d_inner * up * sigmoid * (1.0 + gate * (1.0 - sigmoid))).astype(
            jnp.bfloat16
        )
        for step in range(slabs):

            @pl.when(pl.program_id(0) == step)
            def turn():
                turned_rows_ref[...] = rows_ref[:, step * slab : (step + 1) * slab].T

    columns = pl.BlockSpec((width, TILE), lambda i: (0, i))
    results = pl.BlockSpec((count, TILE), lambda i: (0, i))
    return pl.pallas_call(
        body,
        grid=(steps,),
        out_shape=[jax.ShapeDtypeStruct((count, units), jnp.bfloat16)] * 3
        + [
            jax.ShapeDtypeStruct((width, count), jnp.bfloat16),
            jax.ShapeDtypeStruct((units, count), jnp.bfloat16),
        ],
        in_specs=[
            resident((count, width)),
            resident((count, width)),
            columns,
            columns,
            pl.BlockSpec((TILE, width), lambda i: (i, 0)),
        ],
        out_specs=[results] * 3
        + [
            pl.BlockSpec((slab, count), lambda i: (jnp.minimum(i, slabs - 1), 0)),
            pl.BlockSpec((TILE, count), lambda i: (i, 0)),
        ],
        compiler_params=pltpu.CompilerParams(vmem_limit_bytes=VMEM_LIMIT),
        cost_estimate=COST,
        name="feed_forward",
    )(rows, cotangents, gate_matrix, up_matrix, down_matrix)


def split_gradient(left, right, groups, places, core_place, turned):
    rows, count = left.shape if turned else left.shape[::-1]
    columns = right.shape[1]
    half = rows // (2 * groups)
    part = half // places

    def body(core_ref, left_ref, right_ref, other_ref, own_ref, *scratch):
        if turned:
            rows_ref = left_ref
        else:
            (rows_ref,) = scratch

            @pl.when(pl.program_id(0) == 0)
            def turn():
                rows_ref[...] = left_ref[...].T

        core = core_ref[0]
        for out_ref, which in ((other_ref, 1 - core), (own_ref, core)):
            halves = [
                rows_ref[pl.ds(pl.multiple_of((2 * group + which) * half, 16), half), :]
                for group in range(groups)
            ]
            product = jnp.dot(
                jnp.concatenate(halves, axis=0), right_ref[...], preferred_element_type=jnp.float32
            )
            for group in range(groups):
                for place in range(places):
                    at = group * half + place * part
                    out_ref[place, group] = product[at : at + part].astype(jnp.bfloat16)

    return pl.pallas_call(
        body,
        grid=(pl.cdiv(columns, TILE),),
        out_shape=[jax.ShapeDtypeStruct((places, groups, part, columns), jnp.bfloat16)] * 2,
        in_specs=[
            pl.BlockSpec(memory_space=pltpu.SMEM),
            resident(left.shape),
            pl.BlockSpec((count, TILE), lambda i: (0, i)),
        ],
        out_specs=[pl.BlockSpec((places, groups, part, TILE), lambda i: (0, 0, 0, i))] * 2,
        scratch_shapes=[] if turned else [pltpu.VMEM((rows, count), jnp.bfloat16)],
        compiler_params=pltpu.CompilerParams(vmem_limit_bytes=VMEM_LIMIT),
        cost_estimate=COST,
        name="split_gradient",
    )(core_place.reshape(1).astype(jnp.int32), left, right)


def ordered_gradient(left, right, shards, order):
    reps = len(order)
    rows, count = left.shape
    columns = right.shape[1]
    part = rows // (shards * reps)

    def body(left_ref, right_ref, out_ref):
        product = jnp.dot(left_ref[...], right_ref[...], preferred_element_type=jnp.float32)
        for z in range(shards):
            for r in range(reps):
                at = (z * reps + order[r]) * part
                out_ref[r, z] = product[at : at + part].astype(jnp.bfloat16)

    return pl.pallas_call(
        body,
        grid=(pl.cdiv(columns, TILE),),
        out_shape=[jax.ShapeDtypeStruct((reps, shards, part, columns), jnp.bfloat16)],
        in_specs=[
            resident((rows, count)),
            pl.BlockSpec((count, TILE), lambda i: (0, i)),
        ],
        out_specs=[pl.BlockSpec((reps, shards, part, TILE), lambda i: (0, 0, 0, i))],
        compiler_params=pltpu.CompilerParams(vmem_limit_bytes=VMEM_LIMIT),
        cost_estimate=COST,
        name="ordered_gradient",
    )(left, right)


def rows_product(lefts, rights, turned, blocks):
    count, depth = lefts[0].shape
    columns = rights[0].shape[0 if turned else 1]
    pairs, part = len(lefts), count // blocks

    def body(*refs):
        total = None
        for left_ref, right_ref in zip(refs[:pairs], refs[pairs : 2 * pairs]):
            if turned:
                product = times_transposed(left_ref[...], right_ref[...])
            else:
                product = jnp.dot(
                    left_ref[...], right_ref[...], preferred_element_type=jnp.float32
                )
            total = product if total is None else total + product
        for block in range(blocks):
            refs[2 * pairs + block][...] = total[block * part : (block + 1) * part].astype(
                jnp.bfloat16
            )

    right_spec = (
        pl.BlockSpec((TILE, depth), lambda i: (i, 0))
        if turned
        else pl.BlockSpec((depth, TILE), lambda i: (0, i))
    )
    return pl.pallas_call(
        body,
        grid=(pl.cdiv(columns, TILE),),
        out_shape=[jax.ShapeDtypeStruct((part, columns), jnp.bfloat16)] * blocks,
        in_specs=[resident((count, depth))] * pairs + [right_spec] * pairs,
        out_specs=[pl.BlockSpec((part, TILE), lambda i: (0, i))] * blocks,
        compiler_params=pltpu.CompilerParams(vmem_limit_bytes=VMEM_LIMIT),
        cost_estimate=COST,
        name="rows_product",
    )(*lefts, *rights)


def kept_bias(row_segments, row_index, key_segments, key_index):
    kept = (row_segments == key_segments) & (key_index <= row_index)
    return jnp.where(kept, 0.0, MASKED)


def in_vmem(count):
    return [pl.BlockSpec(memory_space=pltpu.VMEM)] * count


def attention_forward(projected, cosine, signed_sine, pairs, rows, keys):
    count = projected.shape[0]
    per_group = QH // KVH
    scale = 1.0 / math.sqrt(HD)
    shape = (KVH, per_group * count, HD)

    def body(projected_ref, cosine_ref, sine_ref, pairs_ref, rows_ref, keys_ref, queries_ref, out_ref):
        bias = kept_bias(rows_ref[:, 0:1], rows_ref[:, 1:2], keys_ref[0:1, :], keys_ref[1:2, :])
        for k in range(KVH):
            for h in range(per_group):
                at = (k * per_group + h) * HD
                field = projected_ref[:, at : at + HD]
                queries_ref[k, h * count : (h + 1) * count, :] = (
                    field * cosine_ref[...] + pltpu.roll(field, HD // 2, 1) * sine_ref[...]
                ).astype(jnp.bfloat16)
            keys_here = pairs_ref[:, k * HD : (k + 1) * HD]
            values_here = pairs_ref[:, (KVH + k) * HD : (KVH + k + 1) * HD]
            scores = times_transposed(queries_ref[k], keys_here) * scale + bias
            powers = jnp.exp(scores - jnp.max(scores, axis=1, keepdims=True))
            shares = powers * (1.0 / jnp.sum(powers, axis=1, keepdims=True))
            result = jnp.dot(
                shares.astype(jnp.bfloat16), values_here, preferred_element_type=jnp.float32
            ).astype(jnp.bfloat16)
            for h in range(per_group):
                at = (k * per_group + h) * HD
                out_ref[:, at : at + HD] = result[h * count : (h + 1) * count]

    return pl.pallas_call(
        body,
        out_shape=[
            jax.ShapeDtypeStruct(shape, jnp.bfloat16),
            jax.ShapeDtypeStruct((count, QH * HD), jnp.bfloat16),
        ],
        in_specs=in_vmem(6),
        out_specs=in_vmem(2),
        compiler_params=pltpu.CompilerParams(vmem_limit_bytes=VMEM_LIMIT),
        cost_estimate=COST,
        name="attention_forward",
    )(projected, cosine, signed_sine, pairs, rows, keys)


def attention_backward(queries, gradient, pairs, cosine, signed_sine, rows, keys, blocks):
    count = gradient.shape[0]
    per_group = QH // KVH
    scale = 1.0 / math.sqrt(HD)
    group_rows = pairs.shape[0]
    part = group_rows // blocks

    def body(queries_ref, gradient_ref, pairs_ref, cosine_ref, sine_ref, rows_ref, keys_ref, d_ref, *outs):
        block_refs, stacked = outs[:blocks], outs[blocks]
        bias = kept_bias(rows_ref[0:1, :], rows_ref[1:2, :], keys_ref[:, 0:1], keys_ref[:, 1:2])
        for k in range(KVH):
            for h in range(per_group):
                at = (k * per_group + h) * HD
                stacked[h * count : (h + 1) * count, :] = gradient_ref[:, at : at + HD]
            keys_here = pairs_ref[:, k * HD : (k + 1) * HD]
            values_here = pairs_ref[:, (KVH + k) * HD : (KVH + k + 1) * HD]
            scores = times_transposed(keys_here, queries_ref[k]) * scale + bias
            powers = jnp.exp(scores - jnp.max(scores, axis=0, keepdims=True))
            shares = powers * (1.0 / jnp.sum(powers, axis=0, keepdims=True))
            d_shares = times_transposed(values_here, stacked[...])
            dots = jnp.sum(shares * d_shares, axis=0, keepdims=True)
            d_scores = (shares * (d_shares - dots)).astype(jnp.bfloat16)
            d_keys = jnp.dot(d_scores, queries_ref[k], preferred_element_type=jnp.float32) * scale
            d_values = jnp.dot(
                shares.astype(jnp.bfloat16), stacked[...], preferred_element_type=jnp.float32
            )
            for block in range(blocks):
                cut = slice(block * part, (block + 1) * part)
                block_refs[block][:, k * HD : (k + 1) * HD] = d_keys[cut].astype(jnp.bfloat16)
                block_refs[block][:, (KVH + k) * HD : (KVH + k + 1) * HD] = d_values[cut].astype(
                    jnp.bfloat16
                )
            d_queries = transposed_times(d_scores, keys_here) * scale
            for h in range(per_group):
                at = (k * per_group + h) * HD
                field = d_queries[h * count : (h + 1) * count]
                d_ref[:, at : at + HD] = (
                    field * cosine_ref[...] - pltpu.roll(field, HD // 2, 1) * sine_ref[...]
                ).astype(jnp.bfloat16)

    return pl.pallas_call(
        body,
        out_shape=[jax.ShapeDtypeStruct((count, QH * HD), jnp.bfloat16)]
        + [jax.ShapeDtypeStruct((part, 2 * KVH * HD), jnp.bfloat16)] * blocks,
        in_specs=in_vmem(7),
        out_specs=in_vmem(1 + blocks),
        scratch_shapes=[pltpu.VMEM((per_group * count, HD), jnp.bfloat16)],
        compiler_params=pltpu.CompilerParams(vmem_limit_bytes=VMEM_LIMIT),
        cost_estimate=COST,
        name="attention_backward",
    )(queries, gradient, pairs, cosine, signed_sine, rows, keys)


def join_projected(d_queries, pair_terms, cosine, signed_sine):
    count, query_width = d_queries.shape
    pair_width = KVH * HD
    terms = len(pair_terms)

    def body(d_queries_ref, cosine_ref, sine_ref, *refs):
        term_refs, out_ref, sum_ref = refs[:terms], refs[terms], refs[terms + 1]
        out_ref[:, :query_width] = d_queries_ref[...]
        for at in range(0, 2 * pair_width, HD):
            field = total_of([term[:, at : at + HD] for term in term_refs])
            if at < pair_width:
                field = field * cosine_ref[...] - pltpu.roll(field, HD // 2, 1) * sine_ref[...]
            out_ref[:, query_width + at : query_width + at + HD] = field.astype(jnp.bfloat16)
        sum_ref[...] = jnp.sum(out_ref[...].astype(jnp.float32), axis=0, keepdims=True)

    return pl.pallas_call(
        body,
        out_shape=[
            jax.ShapeDtypeStruct((count, query_width + 2 * pair_width), jnp.bfloat16),
            jax.ShapeDtypeStruct((1, query_width + 2 * pair_width), jnp.float32),
        ],
        in_specs=in_vmem(3 + terms),
        out_specs=in_vmem(2),
        cost_estimate=COST,
        name="join_projected",
    )(d_queries, cosine, signed_sine, *pair_terms)


def on_device(
    tokens,
    segment_ids,
    first_gain,
    input_weight,
    input_bias,
    output_weight,
    second_gain,
    gate_weight,
    up_weight,
    down_weight,
    output_cotangent,
):
    bf16, f32 = jnp.bfloat16, jnp.float32
    shards, reps = lax.axis_size("shard"), lax.axis_size("rep")
    shard, core, first, second = make_lines(reps, shards)
    rep_place = (core.place * first.size + first.place) * second.size + second.place
    own_rows, width = tokens.shape
    segments = segment_ids[0]
    per_group = QH // KVH
    query_width = QH * HD
    pair_width = KVH * HD
    first_row = shard.place * own_rows
    part_rows = input_weight.shape[0] // reps
    hidden_units = gate_weight.shape[1]
    block_units = hidden_units // shards
    clock = Clock()
    z_order = jnp.stack([shard.behind(step) for step in range(shards)]).astype(jnp.int32)

    def weight_piece(weight, place):
        return pick(weight.reshape(reps, part_rows, weight.shape[1]), place, 0)

    def spread(piece):
        return Spread(clock, piece, core, first, second)

    def blocks_of(blocks):
        return [pick(blocks, shard.ahead(step), 0) for step in range(shards)]

    steps = range(1, shards)

    def send_blocks(blocks):
        return clock.send(shard, blocks[1:], steps)

    def send_around(value):
        return clock.send(shard, [value] * len(steps), steps)

    def send_back(rows):
        return clock.send(shard, rows, [shards - step for step in steps])

    rep_index = lax.axis_index("rep")
    input_matrix = lax.all_gather(
        weight_piece(input_weight, rep_index), ("shard", "rep"), axis=0, tiled=True
    )
    shard_vectors = jnp.concatenate([first_gain, second_gain, input_bias])
    vector_row = jnp.pad(shard_vectors, (0, output_weight.shape[1] - shard_vectors.shape[0]))
    own_output = jnp.concatenate(
        [weight_piece(output_weight, rep_place), vector_row[None]], axis=0
    )
    output_moving = send_around(own_output)
    gate_blocks, up_blocks = clock.run(
        lambda *weights: column_blocks(rep_index, shard.place, *weights),
        gate_weight.reshape(reps, part_rows, hidden_units),
        up_weight.reshape(reps, part_rows, hidden_units),
    )
    (output_rows,) = clock.wait(output_moving)
    output_rows = [own_output] + output_rows

    output_spread = spread(jnp.stack([rows[:part_rows] for rows in output_rows])[None])
    gate_moving = send_blocks(gate_blocks)
    vector_rows = jnp.stack(in_place_order([rows[part_rows] for rows in output_rows], shard))
    own_gain = first_gain.shape[0]
    gain_one = vector_rows[:, :own_gain].reshape(width).astype(f32)
    gain_two = vector_rows[:, own_gain : 2 * own_gain].reshape(width).astype(f32)
    shift_row = (
        vector_rows[:, 2 * own_gain : shard_vectors.shape[0]].reshape(-1).astype(f32)
    )
    places = positions(segments)
    cosine_table, sine_table = rope_tables(
        lax.dynamic_slice_in_dim(places, first_row, own_rows), HD
    )
    signed_sine = jnp.concatenate(
        [-sine_table[:, : HD // 2], sine_table[:, HD // 2 :]], axis=1
    )
    own_segments = lax.dynamic_slice_in_dim(segments, first_row, own_rows)
    row_index = jnp.arange(own_rows, dtype=jnp.int32)
    key_index = jnp.concatenate([shard.behind(step) * own_rows + row_index for step in range(shards)])
    key_segments = jnp.concatenate(
        [
            lax.dynamic_slice_in_dim(segments, shard.behind(step) * own_rows, own_rows)
            for step in range(shards)
        ]
    )
    key_marks = jnp.stack([key_segments, key_index])
    row_marks = jnp.tile(jnp.stack([own_segments, first_row + row_index]), (1, per_group))
    wide_tokens = tokens.astype(f32)
    inverse_one = lax.rsqrt(jnp.mean(wide_tokens * wide_tokens, axis=-1, keepdims=True) + EPSILON)
    unit_one = wide_tokens * inverse_one
    normed_one = (unit_one * gain_one).astype(bf16)
    (
        normed_one,
        cosine_table,
        sine_table,
        signed_sine,
        key_marks,
        row_marks,
    ) = clock(normed_one, cosine_table, sine_table, signed_sine, key_marks, row_marks)
    output_arrived, gate_rows = clock.wait(output_spread.moving, gate_moving)

    output_spread.along(output_arrived)
    up_moving = send_blocks(up_blocks)
    output_arrived, up_rows = clock.wait(output_spread.moving, up_moving)

    gate_up = jnp.stack(
        [row for pair in zip([gate_blocks[0]] + gate_rows, [up_blocks[0]] + up_rows) for row in pair]
    )
    gate_up = lax.all_gather(clock(gate_up)[0], "rep", axis=0, tiled=True)
    passed = [[output_cotangent] * 2]
    passing = clock.pass_on(shard, *passed[-1])
    output_spread.over(output_arrived)
    input_matrix, normed_one = clock(input_matrix, normed_one)
    projected = jnp.dot(normed_one, input_matrix, preferred_element_type=f32) + shift_row
    key_part = rotate(
        projected[:, query_width : query_width + pair_width].reshape(own_rows, KVH, HD),
        cosine_table,
        sine_table,
    )
    (own_pairs,) = clock(
        jnp.concatenate(
            [key_part.reshape(own_rows, pair_width), projected[:, query_width + pair_width :]],
            axis=1,
        ).astype(bf16)
    )
    arrived, output_arrived = clock.wait(passing, output_spread.moving)
    passed.append(arrived)

    pair_moving = send_around(own_pairs)
    passing = clock.pass_on(shard, *passed[-1]) if shards > 2 else []
    pair_rows, arrived = clock.wait(pair_moving, passing)
    passed.append(arrived)
    pairs = jnp.concatenate([own_pairs] + pair_rows, axis=0)

    passing = clock.pass_on(shard, *passed[-1]) if shards > 3 else []
    (output_matrix,) = clock.run(place_blocks, z_order, *output_spread.finish(output_arrived))
    output_matrix = output_matrix.reshape(width, width)
    queries, attention_low = clock.run(
        attention_forward, projected, cosine_table, signed_sine, pairs, row_marks.T, key_marks
    )
    hidden = wide_tokens + jnp.dot(attention_low, output_matrix, preferred_element_type=f32)
    inverse_two = lax.rsqrt(jnp.mean(hidden * hidden, axis=-1, keepdims=True) + EPSILON)
    unit_two = hidden * inverse_two
    (normed_two,) = clock((unit_two * gain_two).astype(bf16))
    (arrived,) = clock.wait(passing)
    passed.append(arrived)

    normed_moving = send_around(normed_two)
    gate_matrix, up_matrix = clock.run(
        lambda order, gathered: place_gathered(order, gathered, 2), z_order, gate_up
    )
    gate_matrix = gate_matrix.reshape(width, block_units)
    up_matrix = up_matrix.reshape(width, block_units)
    (normed_arrived,) = clock.wait(normed_moving)
    while len(passed) < shards:
        (arrived,) = clock.wait(clock.pass_on(shard, *passed[-1]))
        passed.append(arrived)
    group_normed = jnp.concatenate([normed_two] + normed_arrived, axis=0)
    cotangents = jnp.concatenate(
        [output_cotangent]
        + [
            jnp.where(shard.place >= step, passed[step][0], passed[shards - step][1])
            for step in steps
        ],
        axis=0,
    )

    inner_act, d_gate, d_up, turned_normed, turned_inner = clock.run(
        feed_forward, group_normed, cotangents, gate_matrix, up_matrix, down_weight
    )

    def split_halves(left, right, groups, turned):
        count = first.size * second.size
        halves = clock.run(
            lambda left, right: split_gradient(left, right, groups, count, core.place, turned),
            left,
            right,
        )
        return [half.reshape((first.size, second.size) + half.shape[1:]) for half in halves]

    def side_by_side(rows):
        return clock(jnp.concatenate(list(rows), axis=1))[0]

    def sum_over_rep(blocks):
        return lax.psum_scatter(blocks, "rep", scatter_dimension=0, tiled=True)

    def row_sum(rows):
        return clock(total_of(list(rows)).astype(bf16))[0]

    def send_some(rows, chosen):
        return clock.send(shard, [rows[k] for k in chosen], [shards - 1 - k for k in chosen])

    edges = sorted({0, shards - 2})
    inside = list(range(1, shards - 2))

    def exchange(blocks):
        return lax.all_to_all(clock(blocks)[0], "shard", 0, 0, tiled=True)

    normed_own, *normed_partial = clock.run(
        lambda *operands: rows_product(operands[:2], operands[2:], True, shards),
        d_gate,
        d_up,
        gate_matrix,
        up_matrix,
    )
    up_halves = split_halves(turned_normed, d_up, shards, True)

    up = Halving(clock, *up_halves, core, first, second)
    normed_moving = send_some(normed_partial, edges)
    (gate_blocks,) = clock.run(
        lambda left, right: ordered_gradient(left, right, shards, rep_places(reps)),
        turned_normed,
        d_gate,
    )
    up_arrived, normed_arrived = clock.wait(up.moving, normed_moving)
    gate_piece = sum_over_rep(clock(gate_blocks)[0].reshape(width, block_units))

    up.along_first(up_arrived)
    normed_moving = send_some(normed_partial, inside)
    (down_blocks,) = clock.run(
        lambda left, right: ordered_gradient(left, right, 1, list(range(reps))),
        turned_inner,
        cotangents,
    )
    up_arrived, more_arrived = clock.wait(up.moving, normed_moving)

    up.along_second(up_arrived)
    normed_two_gradient = total_of([normed_own] + normed_arrived + more_arrived)
    gain_two_gradient = jnp.sum(normed_two_gradient * unit_two, axis=0)
    hidden_gradient = output_cotangent.astype(f32) + norm_back(
        normed_two_gradient, unit_two, inverse_two, gain_two
    )
    (branch_gradient,) = clock(hidden_gradient.astype(bf16))
    (attention_gradient,) = clock(times_transposed(branch_gradient, output_matrix).astype(bf16))
    d_queries, pair_own, *pair_partial = clock.run(
        lambda *operands: attention_backward(*operands, shards),
        queries,
        attention_gradient,
        pairs,
        cosine_table,
        signed_sine,
        row_marks,
        key_marks.T,
    )
    output_halves = split_halves(attention_low, branch_gradient, shards, False)
    (up_arrived,) = clock.wait(up.moving)

    pair_moving = send_back(pair_partial)
    output = Halving(clock, *output_halves, core, first, second)
    up_sum = exchange(up.finish(up_arrived))
    block_own, *block_partial = clock.run(
        lambda left, right: rows_product((left,), (right,), False, shards), inner_act, down_weight
    )
    pair_arrived, output_arrived = clock.wait(pair_moving, output.moving)

    (gate_piece,) = clock(gate_piece)
    down_piece = sum_over_rep(clock(down_blocks)[0].reshape(block_units, width))
    projected_gradient, bias_sum = clock.run(
        lambda *operands: join_projected(operands[0], operands[3:], *operands[1:3]),
        d_queries,
        cosine_table,
        signed_sine,
        pair_own,
        *pair_arrived,
    )
    projected_halves = split_halves(normed_one, projected_gradient, shards, False)
    (up_sum,) = clock(up_sum)
    gate_sum = exchange(gate_piece.reshape(shards, part_rows, block_units))

    projected = Halving(clock, *projected_halves, core, first, second)
    output.along_first(output_arrived)
    up_spread = spread(side_by_side(up_sum))
    projected_gradient, hidden_gradient = clock(projected_gradient, hidden_gradient)
    normed_one_gradient = times_transposed(projected_gradient, input_matrix)
    gain_one_gradient = jnp.sum(normed_one_gradient * unit_one, axis=0)
    (tokens_gradient,) = clock(
        (
            hidden_gradient + norm_back(normed_one_gradient, unit_one, inverse_one, gain_one)
        ).astype(bf16)
    )
    projected_arrived, output_arrived, up_arrived = clock.wait(
        projected.moving, output.moving, up_spread.moving
    )

    projected.along_first(projected_arrived)
    output.along_second(output_arrived)
    gate_spread = spread(side_by_side(clock(gate_sum)[0]))
    bias_gradient = bias_sum[0]
    bias_split = query_width + pair_width
    small_parts = (
        gain_one_gradient,
        gain_two_gradient,
        bias_gradient[:bias_split],
        bias_gradient[bias_split:],
    )
    (small,) = clock(
        jnp.concatenate([part.reshape(shards, -1) for part in small_parts], axis=1)
    )
    projected_arrived, output_arrived, gate_arrived = clock.wait(
        projected.moving, output.moving, gate_spread.moving
    )

    projected.along_second(projected_arrived)
    up_spread.along(up_arrived)
    output_sum = exchange(output.finish(output_arrived))
    block_moving = send_some(block_partial, edges[:1])
    projected_arrived, up_arrived, block_arrived = clock.wait(
        projected.moving, up_spread.moving, block_moving
    )

    (output_sum,) = clock(output_sum)
    input_sum = exchange(projected.finish(projected_arrived))
    gate_spread.along(gate_arrived)
    output_spread = spread(row_sum(output_sum))
    up_spread.over(up_arrived)
    small_moving = clock.send(core, [small], [1])
    gate_arrived, output_arrived, up_arrived, small_arrived = clock.wait(
        gate_spread.moving, output_spread.moving, up_spread.moving, small_moving
    )
    small = total_of([small] + small_arrived)

    (input_sum,) = clock(input_sum)
    (down_piece,) = clock(down_piece)
    down_gathered = lax.all_gather(down_piece, "rep", axis=0, tiled=True)
    input_spread = spread(row_sum(input_sum))
    output_spread.along(output_arrived)
    gate_spread.over(gate_arrived)
    small_moving = clock.send(first, [small] * (first.size - 1), range(1, first.size))
    (up_total,) = clock.run(widen_pieces, *up_spread.finish(up_arrived))
    input_arrived, output_arrived, gate_arrived, small_arrived = clock.wait(
        input_spread.moving, output_spread.moving, gate_spread.moving, small_moving
    )
    small = total_of([small] + small_arrived)

    input_spread.along(input_arrived)
    output_spread.over(output_arrived)
    small_moving = clock.send(second, [small] * (second.size - 1), range(1, second.size))
    block_moving = send_some(block_partial, edges[1:])
    (gate_total,) = clock.run(widen_pieces, *gate_spread.finish(gate_arrived))
    input_arrived, output_arrived, small_arrived, more_arrived = clock.wait(
        input_spread.moving, output_spread.moving, small_moving, block_moving
    )
    small = total_of([small] + small_arrived)
    block_arrived = block_arrived + more_arrived

    input_spread.over(input_arrived)
    small_sum = exchange(small)
    block_moving = send_some(block_partial, inside)
    (output_total,) = clock.run(widen_pieces, *output_spread.finish(output_arrived))
    (down_gathered,) = clock(down_gathered)
    (down_total,) = clock(down_gathered.astype(f32))
    input_arrived, more_arrived = clock.wait(input_spread.moving, block_moving)
    block_arrived = block_arrived + more_arrived
    (block_out,) = clock(total_of([hidden, block_own] + block_arrived).astype(bf16))
    (input_total,) = clock.run(widen_pieces, *input_spread.finish(input_arrived))
    small = total_of(list(clock(small_sum)[0]))

    small = small + clock.token[0, 0]
    small_totals, at = [], 0
    for part in small_parts:
        size = part.shape[0] // shards
        small_totals.append(small[at : at + size])
        at += size
    return (
        block_out,
        tokens_gradient,
        small_totals[0],
        input_total,
        small_totals[2],
        small_totals[3],
        output_total,
        small_totals[1],
        gate_total,
        up_total,
        down_total,
    )


def solution(mesh):
    placed = (
        P(("rep", "shard"), None),
        P("rep", None),
        P("shard"),
        P("shard", None),
        P("shard"),
        P("shard", None),
        P("shard"),
        P("shard", None),
        P("shard", None),
        P("shard", None),
        P(("rep", "shard"), None),
    )
    return jax.shard_map(
        on_device,
        mesh=mesh,
        in_specs=placed,
        out_specs=(
            P(("rep", "shard"), None),
            P(("rep", "shard"), None),
            P("shard"),
            P("shard", None),
            P("shard"),
            P("shard"),
            P("shard", None),
            P("shard"),
            P("shard", None),
            P("shard", None),
            P("shard", None),
        ),
        check_vma=False,
    )
```

```python
import math

import jax
import jax.numpy as jnp
from jax import lax
from jax.experimental import pallas as pl
from jax.experimental.pallas import tpu as pltpu
from jax.sharding import PartitionSpec as P

QH = 12
KVH = 2
HD = 128
SEQS = 3


EPSILON = 1e-06
LOG_THETA = math.log(1000000.0)
MASKED = -1e30
VMEM_LIMIT = 56 * 1024 * 1024
TILE = 512
COST = pl.CostEstimate(flops=1, bytes_accessed=1, transcendentals=0)


def rope_tables(places, head_width):
    half_width = head_width // 2
    frequency = jnp.exp(jnp.arange(half_width, dtype=jnp.float32) * (-2.0 * LOG_THETA / head_width))
    angles = places.astype(jnp.float32)[:, None] * frequency[None, :]
    angles = jnp.concatenate([angles, angles], axis=-1)
    return (jnp.cos(angles), jnp.sin(angles))


def positions(segments):
    labels = jnp.arange(SEQS, dtype=jnp.int32)
    starts = jnp.sum((segments[None, :] < labels[:, None]).astype(jnp.int32), axis=1)
    own_start = jnp.sum(jnp.where(segments[:, None] == labels[None, :], starts[None, :], 0), axis=1)
    return jnp.arange(segments.shape[0], dtype=jnp.int32) - own_start


def rotate(field_rows, cosine_table, sine_table):
    half_width = field_rows.shape[-1] // 2
    turned = jnp.concatenate([-field_rows[..., half_width:], field_rows[..., :half_width]], axis=-1)
    return field_rows * cosine_table[:, None, :] + turned * sine_table[:, None, :]


def transposed_times(left_side, right_side):
    return lax.dot_general(
        left_side, right_side, (((0,), (0,)), ((), ())), preferred_element_type=jnp.float32
    )


def times_transposed(left_side, right_side):
    return lax.dot_general(
        left_side, right_side, (((1,), (1,)), ((), ())), preferred_element_type=jnp.float32
    )


def norm_back(normed_gradient, unit_rows, inverse_rms, gain_row):
    scaled = normed_gradient * gain_row
    return inverse_rms * (scaled - unit_rows * jnp.mean(scaled * unit_rows, axis=-1, keepdims=True))


class Line:
    def __init__(self, name, size, place, pairs, crossed=False):
        self.name, self.size, self.place, self.pairs = name, size, place, pairs
        self.crossed = crossed

    def shift(self, value, step):
        return lax.ppermute(value, self.name, self.pairs(step % self.size))

    def pass_on(self, value, up):
        places = range(self.size - 1)
        pairs = [(at, at + 1) if up else (at + 1, at) for at in places]
        return lax.ppermute(value, self.name, pairs)

    def behind(self, step):
        return lax.rem(self.place + (self.size - step % self.size), self.size)

    def ahead(self, step):
        return lax.rem(self.place + step % self.size, self.size) if step else self.place


def make_lines(reps, shards):
    inner = 2 if reps % 4 == 0 else 1
    outer = reps // (2 * inner)
    square = inner == outer

    def split(index):
        core, b, a = index % 2, (index // 2) % inner, index // (2 * inner)
        return core, b, a

    def join(core, b, a):
        return (a * inner + b) * 2 + core

    def first_pairs(step):
        pairs = []
        for index in range(reps):
            core, b, a = split(index)
            if square and core == 0:
                pairs.append((index, join(core, (b + step) % inner, a)))
            else:
                pairs.append((index, join(core, b, (a + step) % outer)))
        return pairs

    def second_pairs(step):
        pairs = []
        for index in range(reps):
            core, b, a = split(index)
            if square and core == 0:
                pairs.append((index, join(core, b, (a + step) % outer)))
            else:
                pairs.append((index, join(core, (b + step) % inner, a)))
        return pairs

    def core_pairs(step):
        pairs = []
        for index in range(reps):
            core, b, a = split(index)
            pairs.append((index, join((core + step) % 2, b, a)))
        return pairs

    def shard_pairs(step):
        return [(index, (index + step) % shards) for index in range(shards)]

    core, b, a = split(lax.axis_index("rep"))
    first, second = (jnp.where(core == 0, b, a), jnp.where(core == 0, a, b)) if square else (a, b)
    return (
        Line("shard", shards, lax.axis_index("shard"), shard_pairs),
        Line("rep", 2, core, core_pairs, square),
        Line("rep", outer, first, first_pairs),
        Line("rep", inner, second, second_pairs),
    )


def rep_places(reps):
    inner = 2 if reps % 4 == 0 else 1
    outer = reps // (2 * inner)
    places = []
    for index in range(reps):
        core, b, a = index % 2, (index // 2) % inner, index // (2 * inner)
        one, two = (b, a) if inner == outer and core == 0 else (a, b)
        places.append((core * outer + one) * inner + two)
    return places


def pick(array, index, axis):
    return lax.dynamic_index_in_dim(array, index, axis, keepdims=False)


def put(array, piece, index, axis):
    return lax.dynamic_update_index_in_dim(array, piece, index, axis)


def in_place_order(pieces, line):
    ordered = []
    for place in range(line.size):
        chosen = pieces[0]
        for step in range(1, line.size):
            chosen = jnp.where(line.behind(step) == place, pieces[step], chosen)
        ordered.append(chosen)
    return ordered


def tie(*arrays):
    return lax.optimization_barrier(arrays)


def gather_line(value, line):
    return [value] + [line.shift(value, step) for step in range(1, line.size)]


class Clock:
    def __init__(self):
        self.token = jnp.zeros((8, 128), jnp.float32)
        self.open = 0

    def __call__(self, *arrays):
        self.token, *arrays = tie(self.token, *arrays)
        return arrays

    def run(self, step, *arrays):
        return self(*step(*self(*arrays)))

    def send(self, line, values, steps):
        self.open += len(values)
        return [line.shift(value, step) for value, step in zip(self(*values), steps)]

    def pass_on(self, line, lower, upper):
        self.open += 2
        lower, upper = self(lower, upper)
        return [line.pass_on(lower, True), line.pass_on(upper, False)]

    def wait(self, *groups):
        flat = self(*[array for group in groups for array in group])
        self.open -= len(flat)
        parts, at = [], 0
        for group in groups:
            parts.append(flat[at : at + len(group)])
            at += len(group)
        return parts


def total_of(terms):
    total = terms[0].astype(jnp.float32)
    for term in terms[1:]:
        total = total + term.astype(jnp.float32)
    return total


class Halving:
    def __init__(self, clock, sent, own, core, first, second):
        self.clock, self.first, self.second = clock, first, second
        self.terms = [own]
        self.moving = clock.send(core, [sent], [1])

    def along(self, line, arrived):
        self.terms = self.terms + arrived
        steps = range(1, line.size)
        blocks = [
            total_of([pick(term, line.ahead(step), 0) for term in self.terms]).astype(jnp.bfloat16)
            for step in steps
        ]
        self.moving = self.clock.send(line, blocks, steps)
        self.terms = [pick(term, line.place, 0) for term in self.terms]

    def along_first(self, arrived):
        self.along(self.first, arrived)

    def along_second(self, arrived):
        self.along(self.second, arrived)

    def finish(self, arrived):
        return self.clock(total_of(self.terms + arrived).astype(jnp.bfloat16))[0]


class Spread:
    def __init__(self, clock, piece, core, first, second):
        self.clock, self.lines = clock, (core, first, second)
        self.pieces = [piece]
        steps = range(1, second.size)
        self.moving = clock.send(second, [piece] * len(steps), steps)

    def along(self, arrived):
        core, first, second = self.lines
        self.pieces = self.pieces + arrived
        steps = range(1, first.size)
        self.moving = self.clock.send(first, [jnp.stack(self.pieces)] * len(steps), steps)

    def over(self, arrived):
        core, first, second = self.lines
        rows = [jnp.stack(self.pieces)] + arrived
        self.pieces = jnp.concatenate(rows, axis=0)
        self.moving = self.clock.send(core, [self.pieces], [1])

    def finish(self, arrived):
        core, first, second = self.lines
        (others,) = arrived
        offsets = [(one, two) for one in range(first.size) for two in range(second.size)]
        placed = [(core.place, first.behind(one), second.behind(two)) for one, two in offsets]
        far, near = (second, first) if core.crossed else (first, second)
        placed += [(core.behind(1), far.behind(one), near.behind(two)) for one, two in offsets]
        places = [(c * first.size + f) * second.size + s for c, f, s in placed]
        return [jnp.stack(places).astype(jnp.int32), self.pieces, others]


def column_blocks(place, shard_place, *weights):
    count = len(weights)
    rows, columns = weights[0].shape[1:]
    shards = lax.axis_size("shard")
    block = columns // shards

    def body(places_ref, *refs):
        sources, outs = refs[:count], refs[count : 2 * count]
        held, cut, in_sems, out_sems = refs[2 * count :]
        loads = [
            pltpu.make_async_copy(sources[at].at[places_ref[0]], held.at[at], in_sems.at[at])
            for at in range(count)
        ]

        def store(at, z):
            ahead = lax.rem(z + shards - places_ref[1], shards)
            return pltpu.make_async_copy(cut.at[at, z], outs[at].at[ahead], out_sems.at[at, z])

        for load in loads:
            load.start()
        for at in range(count):
            loads[at].wait()
            for z in range(shards):
                cut[at, z] = held[at, :, z * block : (z + 1) * block]
                store(at, z).start()
        for at in range(count):
            for z in range(shards):
                store(at, z).wait()

    return pl.pallas_call(
        body,
        out_shape=[jax.ShapeDtypeStruct((shards, rows, block), jnp.bfloat16)] * count,
        in_specs=[pl.BlockSpec(memory_space=pltpu.SMEM)]
        + [pl.BlockSpec(memory_space=pl.ANY)] * count,
        out_specs=[pl.BlockSpec(memory_space=pl.ANY)] * count,
        scratch_shapes=[
            pltpu.VMEM((count, rows, columns), jnp.bfloat16),
            pltpu.VMEM((count, shards, rows, block), jnp.bfloat16),
            pltpu.SemaphoreType.DMA((count,)),
            pltpu.SemaphoreType.DMA((count, shards)),
        ],
        compiler_params=pltpu.CompilerParams(vmem_limit_bytes=VMEM_LIMIT),
        cost_estimate=COST,
        name="column_blocks",
    )(jnp.stack([place, shard_place]).astype(jnp.int32), *weights)


def place_blocks(order, places, pieces, others):
    half, groups, shards = pieces.shape[:3]

    def body(order_ref, places_ref, pieces_ref, others_ref, *rest):
        def source_of(g, k, r):
            return (pieces_ref if r < half else others_ref).at[r % half, g, k]

        move_blocks(source_of, lambda r: places_ref[r], order_ref, rest[:groups], *rest[groups:])

    return blocks_call(body, 2, 2, groups, shards, 2 * half, pieces.shape[3:])(
        order, places, pieces, others
    )


def place_gathered(order, gathered, groups):
    shards = lax.axis_size("shard")
    reps = gathered.shape[0] // (shards * groups)

    def body(order_ref, source, *rest):
        move_blocks(
            lambda g, k, r: source.at[(r * shards + k) * groups + g],
            lambda r: r,
            order_ref,
            rest[:groups],
            *rest[groups:],
        )

    return blocks_call(body, 1, 1, groups, shards, reps, gathered.shape[1:])(order, gathered)


def move_blocks(source_of, place_of, order_ref, outs, held, in_sems, out_sems):
    groups, shards, reps = in_sems.shape
    slabs = [(g, k) for g in range(groups) for k in range(shards)]

    def load(g, k, r):
        return pltpu.make_async_copy(
            source_of(g, k, r), held.at[g, k, place_of(r)], in_sems.at[g, k, r]
        )

    def store(g, k):
        return pltpu.make_async_copy(held.at[g, k], outs[g].at[order_ref[k]], out_sems.at[g, k])

    for g, k in slabs:
        for r in range(reps):
            load(g, k, r).start()
    for g, k in slabs:
        for r in range(reps):
            load(g, k, r).wait()
        store(g, k).start()
    for g, k in slabs:
        store(g, k).wait()


def blocks_call(body, scalars, sources, groups, shards, reps, block):
    whole = (shards, reps) + block
    return pl.pallas_call(
        body,
        out_shape=[jax.ShapeDtypeStruct(whole, jnp.bfloat16)] * groups,
        in_specs=[pl.BlockSpec(memory_space=pltpu.SMEM)] * scalars
        + [pl.BlockSpec(memory_space=pl.ANY)] * sources,
        out_specs=[pl.BlockSpec(memory_space=pl.ANY)] * groups,
        scratch_shapes=[
            pltpu.VMEM((groups,) + whole, jnp.bfloat16),
            pltpu.SemaphoreType.DMA((groups, shards, reps)),
            pltpu.SemaphoreType.DMA((groups, shards)),
        ],
        compiler_params=pltpu.CompilerParams(vmem_limit_bytes=VMEM_LIMIT),
        cost_estimate=COST,
        name="place_blocks",
    )


def widen_pieces(places, pieces, others):
    half, rows, columns = pieces.shape
    reps = 2 * half
    strip = next(size for size in (16, 8, rows) if rows % size == 0)

    def body(places_ref, pieces_ref, others_ref, out_ref, narrow, wide, in_sems, out_sems):
        loads = [
            pltpu.make_async_copy(
                (pieces_ref if r < half else others_ref).at[r % half], narrow.at[r], in_sems.at[r]
            )
            for r in range(reps)
        ]
        stores = [
            pltpu.make_async_copy(wide.at[r], out_ref.at[places_ref[r]], out_sems.at[r])
            for r in range(reps)
        ]
        for load in loads:
            load.start()
        for r in range(reps):
            loads[r].wait()

            def convert(at, carry):
                cut = pl.ds(pl.multiple_of(at * strip, strip), strip)
                wide[r, cut, :] = narrow[r, cut, :].astype(jnp.float32)
                return carry

            lax.fori_loop(0, rows // strip, convert, 0)
            stores[r].start()
        for store in stores:
            store.wait()

    result = pl.pallas_call(
        body,
        out_shape=jax.ShapeDtypeStruct((reps, rows, columns), jnp.float32),
        in_specs=[pl.BlockSpec(memory_space=pltpu.SMEM)]
        + [pl.BlockSpec(memory_space=pl.ANY)] * 2,
        out_specs=pl.BlockSpec(memory_space=pl.ANY),
        scratch_shapes=[
            pltpu.VMEM((reps, rows, columns), jnp.bfloat16),
            pltpu.VMEM((reps, rows, columns), jnp.float32),
            pltpu.SemaphoreType.DMA((reps,)),
            pltpu.SemaphoreType.DMA((reps,)),
        ],
        compiler_params=pltpu.CompilerParams(vmem_limit_bytes=VMEM_LIMIT),
        cost_estimate=COST,
        name="widen_pieces",
    )(places, pieces, others)
    return (result.reshape(reps * rows, columns),)


def resident(shape):
    return pl.BlockSpec(shape, lambda i: (0, 0), pipeline_mode=pl.Buffered(1))


def feed_forward(rows, cotangents, gate_matrix, up_matrix, down_matrix):
    count, width = rows.shape
    units = gate_matrix.shape[1]
    steps = pl.cdiv(units, TILE)
    slabs = next(size for size in range(min(steps, width // 128), 0, -1) if width % (128 * size) == 0)
    slab = width // slabs

    def body(
        rows_ref,
        cotangents_ref,
        gate_ref,
        up_ref,
        down_ref,
        inner_ref,
        d_gate_ref,
        d_up_ref,
        turned_rows_ref,
        turned_inner_ref,
    ):
        gate = jnp.dot(rows_ref[...], gate_ref[...], preferred_element_type=jnp.float32)
        up = jnp.dot(rows_ref[...], up_ref[...], preferred_element_type=jnp.float32)
        sigmoid = jax.nn.sigmoid(gate)
        silu = gate * sigmoid
        inner = (silu * up).astype(jnp.bfloat16)
        inner_ref[...] = inner
        turned_inner_ref[...] = inner.T
        d_inner = times_transposed(cotangents_ref[...], down_ref[...])
        d_up_ref[...] = (d_inner * silu).astype(jnp.bfloat16)
        d_gate_ref[...] = (d_inner * up * sigmoid * (1.0 + gate * (1.0 - sigmoid))).astype(
            jnp.bfloat16
        )
        for step in range(slabs):

            @pl.when(pl.program_id(0) == step)
            def turn():
                turned_rows_ref[...] = rows_ref[:, step * slab : (step + 1) * slab].T

    columns = pl.BlockSpec((width, TILE), lambda i: (0, i))
    results = pl.BlockSpec((count, TILE), lambda i: (0, i))
    return pl.pallas_call(
        body,
        grid=(steps,),
        out_shape=[jax.ShapeDtypeStruct((count, units), jnp.bfloat16)] * 3
        + [
            jax.ShapeDtypeStruct((width, count), jnp.bfloat16),
            jax.ShapeDtypeStruct((units, count), jnp.bfloat16),
        ],
        in_specs=[
            resident((count, width)),
            resident((count, width)),
            columns,
            columns,
            pl.BlockSpec((TILE, width), lambda i: (i, 0)),
        ],
        out_specs=[results] * 3
        + [
            pl.BlockSpec((slab, count), lambda i: (jnp.minimum(i, slabs - 1), 0)),
            pl.BlockSpec((TILE, count), lambda i: (i, 0)),
        ],
        compiler_params=pltpu.CompilerParams(vmem_limit_bytes=VMEM_LIMIT),
        cost_estimate=COST,
        name="feed_forward",
    )(rows, cotangents, gate_matrix, up_matrix, down_matrix)


def split_gradient(left, right, groups, places, core_place, turned):
    rows, count = left.shape if turned else left.shape[::-1]
    columns = right.shape[1]
    half = rows // (2 * groups)
    part = half // places

    def body(core_ref, left_ref, right_ref, other_ref, own_ref, *scratch):
        if turned:
            rows_ref = left_ref
        else:
            (rows_ref,) = scratch

            @pl.when(pl.program_id(0) == 0)
            def turn():
                rows_ref[...] = left_ref[...].T

        core = core_ref[0]
        for out_ref, which in ((other_ref, 1 - core), (own_ref, core)):
            halves = [
                rows_ref[pl.ds(pl.multiple_of((2 * group + which) * half, 16), half), :]
                for group in range(groups)
            ]
            product = jnp.dot(
                jnp.concatenate(halves, axis=0), right_ref[...], preferred_element_type=jnp.float32
            )
            for group in range(groups):
                for place in range(places):
                    at = group * half + place * part
                    out_ref[place, group] = product[at : at + part].astype(jnp.bfloat16)

    return pl.pallas_call(
        body,
        grid=(pl.cdiv(columns, TILE),),
        out_shape=[jax.ShapeDtypeStruct((places, groups, part, columns), jnp.bfloat16)] * 2,
        in_specs=[
            pl.BlockSpec(memory_space=pltpu.SMEM),
            resident(left.shape),
            pl.BlockSpec((count, TILE), lambda i: (0, i)),
        ],
        out_specs=[pl.BlockSpec((places, groups, part, TILE), lambda i: (0, 0, 0, i))] * 2,
        scratch_shapes=[] if turned else [pltpu.VMEM((rows, count), jnp.bfloat16)],
        compiler_params=pltpu.CompilerParams(vmem_limit_bytes=VMEM_LIMIT),
        cost_estimate=COST,
        name="split_gradient",
    )(core_place.reshape(1).astype(jnp.int32), left, right)


def ordered_gradient(left, right, shards, order):
    reps = len(order)
    rows, count = left.shape
    columns = right.shape[1]
    part = rows // (shards * reps)

    def body(left_ref, right_ref, out_ref):
        product = jnp.dot(left_ref[...], right_ref[...], preferred_element_type=jnp.float32)
        for z in range(shards):
            for r in range(reps):
                at = (z * reps + order[r]) * part
                out_ref[r, z] = product[at : at + part].astype(jnp.bfloat16)

    return pl.pallas_call(
        body,
        grid=(pl.cdiv(columns, TILE),),
        out_shape=[jax.ShapeDtypeStruct((reps, shards, part, columns), jnp.bfloat16)],
        in_specs=[
            resident((rows, count)),
            pl.BlockSpec((count, TILE), lambda i: (0, i)),
        ],
        out_specs=[pl.BlockSpec((reps, shards, part, TILE), lambda i: (0, 0, 0, i))],
        compiler_params=pltpu.CompilerParams(vmem_limit_bytes=VMEM_LIMIT),
        cost_estimate=COST,
        name="ordered_gradient",
    )(left, right)


def rows_product(lefts, rights, turned, blocks):
    count, depth = lefts[0].shape
    columns = rights[0].shape[0 if turned else 1]
    pairs, part = len(lefts), count // blocks

    def body(*refs):
        total = None
        for left_ref, right_ref in zip(refs[:pairs], refs[pairs : 2 * pairs]):
            if turned:
                product = times_transposed(left_ref[...], right_ref[...])
            else:
                product = jnp.dot(
                    left_ref[...], right_ref[...], preferred_element_type=jnp.float32
                )
            total = product if total is None else total + product
        for block in range(blocks):
            refs[2 * pairs + block][...] = total[block * part : (block + 1) * part].astype(
                jnp.bfloat16
            )

    right_spec = (
        pl.BlockSpec((TILE, depth), lambda i: (i, 0))
        if turned
        else pl.BlockSpec((depth, TILE), lambda i: (0, i))
    )
    return pl.pallas_call(
        body,
        grid=(pl.cdiv(columns, TILE),),
        out_shape=[jax.ShapeDtypeStruct((part, columns), jnp.bfloat16)] * blocks,
        in_specs=[resident((count, depth))] * pairs + [right_spec] * pairs,
        out_specs=[pl.BlockSpec((part, TILE), lambda i: (0, i))] * blocks,
        compiler_params=pltpu.CompilerParams(vmem_limit_bytes=VMEM_LIMIT),
        cost_estimate=COST,
        name="rows_product",
    )(*lefts, *rights)


def kept_bias(row_segments, row_index, key_segments, key_index):
    kept = (row_segments == key_segments) & (key_index <= row_index)
    return jnp.where(kept, 0.0, MASKED)


def in_vmem(count):
    return [pl.BlockSpec(memory_space=pltpu.VMEM)] * count


def attention_forward(projected, cosine, signed_sine, pairs, rows, keys):
    count = projected.shape[0]
    per_group = QH // KVH
    scale = 1.0 / math.sqrt(HD)
    shape = (KVH, per_group * count, HD)

    def body(projected_ref, cosine_ref, sine_ref, pairs_ref, rows_ref, keys_ref, queries_ref, out_ref):
        bias = kept_bias(rows_ref[:, 0:1], rows_ref[:, 1:2], keys_ref[0:1, :], keys_ref[1:2, :])
        for k in range(KVH):
            for h in range(per_group):
                at = (k * per_group + h) * HD
                field = projected_ref[:, at : at + HD]
                queries_ref[k, h * count : (h + 1) * count, :] = (
                    field * cosine_ref[...] + pltpu.roll(field, HD // 2, 1) * sine_ref[...]
                ).astype(jnp.bfloat16)
            keys_here = pairs_ref[:, k * HD : (k + 1) * HD]
            values_here = pairs_ref[:, (KVH + k) * HD : (KVH + k + 1) * HD]
            scores = times_transposed(queries_ref[k], keys_here) * scale + bias
            powers = jnp.exp(scores - jnp.max(scores, axis=1, keepdims=True))
            shares = powers * (1.0 / jnp.sum(powers, axis=1, keepdims=True))
            result = jnp.dot(
                shares.astype(jnp.bfloat16), values_here, preferred_element_type=jnp.float32
            ).astype(jnp.bfloat16)
            for h in range(per_group):
                at = (k * per_group + h) * HD
                out_ref[:, at : at + HD] = result[h * count : (h + 1) * count]

    return pl.pallas_call(
        body,
        out_shape=[
            jax.ShapeDtypeStruct(shape, jnp.bfloat16),
            jax.ShapeDtypeStruct((count, QH * HD), jnp.bfloat16),
        ],
        in_specs=in_vmem(6),
        out_specs=in_vmem(2),
        compiler_params=pltpu.CompilerParams(vmem_limit_bytes=VMEM_LIMIT),
        cost_estimate=COST,
        name="attention_forward",
    )(projected, cosine, signed_sine, pairs, rows, keys)


def attention_backward(queries, gradient, pairs, cosine, signed_sine, rows, keys, blocks):
    count = gradient.shape[0]
    per_group = QH // KVH
    scale = 1.0 / math.sqrt(HD)
    group_rows = pairs.shape[0]
    part = group_rows // blocks

    def body(queries_ref, gradient_ref, pairs_ref, cosine_ref, sine_ref, rows_ref, keys_ref, d_ref, *outs):
        block_refs, stacked = outs[:blocks], outs[blocks]
        bias = kept_bias(rows_ref[0:1, :], rows_ref[1:2, :], keys_ref[:, 0:1], keys_ref[:, 1:2])
        for k in range(KVH):
            for h in range(per_group):
                at = (k * per_group + h) * HD
                stacked[h * count : (h + 1) * count, :] = gradient_ref[:, at : at + HD]
            keys_here = pairs_ref[:, k * HD : (k + 1) * HD]
            values_here = pairs_ref[:, (KVH + k) * HD : (KVH + k + 1) * HD]
            scores = times_transposed(keys_here, queries_ref[k]) * scale + bias
            powers = jnp.exp(scores - jnp.max(scores, axis=0, keepdims=True))
            shares = powers * (1.0 / jnp.sum(powers, axis=0, keepdims=True))
            d_shares = times_transposed(values_here, stacked[...])
            dots = jnp.sum(shares * d_shares, axis=0, keepdims=True)
            d_scores = (shares * (d_shares - dots)).astype(jnp.bfloat16)
            d_keys = jnp.dot(d_scores, queries_ref[k], preferred_element_type=jnp.float32) * scale
            d_values = jnp.dot(
                shares.astype(jnp.bfloat16), stacked[...], preferred_element_type=jnp.float32
            )
            for block in range(blocks):
                cut = slice(block * part, (block + 1) * part)
                block_refs[block][:, k * HD : (k + 1) * HD] = d_keys[cut].astype(jnp.bfloat16)
                block_refs[block][:, (KVH + k) * HD : (KVH + k + 1) * HD] = d_values[cut].astype(
                    jnp.bfloat16
                )
            d_queries = transposed_times(d_scores, keys_here) * scale
            for h in range(per_group):
                at = (k * per_group + h) * HD
                field = d_queries[h * count : (h + 1) * count]
                d_ref[:, at : at + HD] = (
                    field * cosine_ref[...] - pltpu.roll(field, HD // 2, 1) * sine_ref[...]
                ).astype(jnp.bfloat16)

    return pl.pallas_call(
        body,
        out_shape=[jax.ShapeDtypeStruct((count, QH * HD), jnp.bfloat16)]
        + [jax.ShapeDtypeStruct((part, 2 * KVH * HD), jnp.bfloat16)] * blocks,
        in_specs=in_vmem(7),
        out_specs=in_vmem(1 + blocks),
        scratch_shapes=[pltpu.VMEM((per_group * count, HD), jnp.bfloat16)],
        compiler_params=pltpu.CompilerParams(vmem_limit_bytes=VMEM_LIMIT),
        cost_estimate=COST,
        name="attention_backward",
    )(queries, gradient, pairs, cosine, signed_sine, rows, keys)


def join_projected(d_queries, pair_terms, cosine, signed_sine):
    count, query_width = d_queries.shape
    pair_width = KVH * HD
    terms = len(pair_terms)

    def body(d_queries_ref, cosine_ref, sine_ref, *refs):
        term_refs, out_ref, sum_ref = refs[:terms], refs[terms], refs[terms + 1]
        out_ref[:, :query_width] = d_queries_ref[...]
        for at in range(0, 2 * pair_width, HD):
            field = total_of([term[:, at : at + HD] for term in term_refs])
            if at < pair_width:
                field = field * cosine_ref[...] - pltpu.roll(field, HD // 2, 1) * sine_ref[...]
            out_ref[:, query_width + at : query_width + at + HD] = field.astype(jnp.bfloat16)
        sum_ref[...] = jnp.sum(out_ref[...].astype(jnp.float32), axis=0, keepdims=True)

    return pl.pallas_call(
        body,
        out_shape=[
            jax.ShapeDtypeStruct((count, query_width + 2 * pair_width), jnp.bfloat16),
            jax.ShapeDtypeStruct((1, query_width + 2 * pair_width), jnp.float32),
        ],
        in_specs=in_vmem(3 + terms),
        out_specs=in_vmem(2),
        cost_estimate=COST,
        name="join_projected",
    )(d_queries, cosine, signed_sine, *pair_terms)


def on_device(
    tokens,
    segment_ids,
    first_gain,
    input_weight,
    input_bias,
    output_weight,
    second_gain,
    gate_weight,
    up_weight,
    down_weight,
    output_cotangent,
):
    bf16, f32 = jnp.bfloat16, jnp.float32
    shards, reps = lax.axis_size("shard"), lax.axis_size("rep")
    shard, core, first, second = make_lines(reps, shards)
    rep_place = (core.place * first.size + first.place) * second.size + second.place
    own_rows, width = tokens.shape
    segments = segment_ids[0]
    per_group = QH // KVH
    query_width = QH * HD
    pair_width = KVH * HD
    first_row = shard.place * own_rows
    part_rows = input_weight.shape[0] // reps
    hidden_units = gate_weight.shape[1]
    block_units = hidden_units // shards
    clock = Clock()
    z_order = jnp.stack([shard.behind(step) for step in range(shards)]).astype(jnp.int32)

    def weight_piece(weight, place):
        return pick(weight.reshape(reps, part_rows, weight.shape[1]), place, 0)

    def spread(piece):
        return Spread(clock, piece, core, first, second)

    def blocks_of(blocks):
        return [pick(blocks, shard.ahead(step), 0) for step in range(shards)]

    steps = range(1, shards)

    def send_blocks(blocks):
        return clock.send(shard, blocks[1:], steps)

    def send_around(value):
        return clock.send(shard, [value] * len(steps), steps)

    def send_back(rows):
        return clock.send(shard, rows, [shards - step for step in steps])

    rep_index = lax.axis_index("rep")
    input_matrix = lax.all_gather(
        weight_piece(input_weight, rep_index), ("shard", "rep"), axis=0, tiled=True
    )
    shard_vectors = jnp.concatenate([first_gain, second_gain, input_bias])
    vector_row = jnp.pad(shard_vectors, (0, output_weight.shape[1] - shard_vectors.shape[0]))
    own_output = jnp.concatenate(
        [weight_piece(output_weight, rep_place), vector_row[None]], axis=0
    )
    output_moving = send_around(own_output)
    gate_blocks, up_blocks = clock.run(
        lambda *weights: column_blocks(rep_index, shard.place, *weights),
        gate_weight.reshape(reps, part_rows, hidden_units),
        up_weight.reshape(reps, part_rows, hidden_units),
    )
    (output_rows,) = clock.wait(output_moving)
    output_rows = [own_output] + output_rows

    output_spread = spread(jnp.stack([rows[:part_rows] for rows in output_rows])[None])
    gate_moving = send_blocks(gate_blocks)
    vector_rows = jnp.stack(in_place_order([rows[part_rows] for rows in output_rows], shard))
    own_gain = first_gain.shape[0]
    gain_one = vector_rows[:, :own_gain].reshape(width).astype(f32)
    gain_two = vector_rows[:, own_gain : 2 * own_gain].reshape(width).astype(f32)
    shift_row = (
        vector_rows[:, 2 * own_gain : shard_vectors.shape[0]].reshape(-1).astype(f32)
    )
    places = positions(segments)
    cosine_table, sine_table = rope_tables(
        lax.dynamic_slice_in_dim(places, first_row, own_rows), HD
    )
    signed_sine = jnp.concatenate(
        [-sine_table[:, : HD // 2], sine_table[:, HD // 2 :]], axis=1
    )
    own_segments = lax.dynamic_slice_in_dim(segments, first_row, own_rows)
    row_index = jnp.arange(own_rows, dtype=jnp.int32)
    key_index = jnp.concatenate([shard.behind(step) * own_rows + row_index for step in range(shards)])
    key_segments = jnp.concatenate(
        [
            lax.dynamic_slice_in_dim(segments, shard.behind(step) * own_rows, own_rows)
            for step in range(shards)
        ]
    )
    key_marks = jnp.stack([key_segments, key_index])
    row_marks = jnp.tile(jnp.stack([own_segments, first_row + row_index]), (1, per_group))
    wide_tokens = tokens.astype(f32)
    inverse_one = lax.rsqrt(jnp.mean(wide_tokens * wide_tokens, axis=-1, keepdims=True) + EPSILON)
    unit_one = wide_tokens * inverse_one
    normed_one = (unit_one * gain_one).astype(bf16)
    (
        normed_one,
        cosine_table,
        sine_table,
        signed_sine,
        key_marks,
        row_marks,
    ) = clock(normed_one, cosine_table, sine_table, signed_sine, key_marks, row_marks)
    output_arrived, gate_rows = clock.wait(output_spread.moving, gate_moving)

    output_spread.along(output_arrived)
    up_moving = send_blocks(up_blocks)
    output_arrived, up_rows = clock.wait(output_spread.moving, up_moving)

    gate_up = jnp.stack(
        [row for pair in zip([gate_blocks[0]] + gate_rows, [up_blocks[0]] + up_rows) for row in pair]
    )
    gate_up = lax.all_gather(clock(gate_up)[0], "rep", axis=0, tiled=True)
    passed = [[output_cotangent] * 2]
    passing = clock.pass_on(shard, *passed[-1])
    output_spread.over(output_arrived)
    input_matrix, normed_one = clock(input_matrix, normed_one)
    projected = jnp.dot(normed_one, input_matrix, preferred_element_type=f32) + shift_row
    key_part = rotate(
        projected[:, query_width : query_width + pair_width].reshape(own_rows, KVH, HD),
        cosine_table,
        sine_table,
    )
    (own_pairs,) = clock(
        jnp.concatenate(
            [key_part.reshape(own_rows, pair_width), projected[:, query_width + pair_width :]],
            axis=1,
        ).astype(bf16)
    )
    arrived, output_arrived = clock.wait(passing, output_spread.moving)
    passed.append(arrived)

    pair_moving = send_around(own_pairs)
    passing = clock.pass_on(shard, *passed[-1]) if shards > 2 else []
    pair_rows, arrived = clock.wait(pair_moving, passing)
    passed.append(arrived)
    pairs = jnp.concatenate([own_pairs] + pair_rows, axis=0)

    passing = clock.pass_on(shard, *passed[-1]) if shards > 3 else []
    (output_matrix,) = clock.run(place_blocks, z_order, *output_spread.finish(output_arrived))
    output_matrix = output_matrix.reshape(width, width)
    queries, attention_low = clock.run(
        attention_forward, projected, cosine_table, signed_sine, pairs, row_marks.T, key_marks
    )
    hidden = wide_tokens + jnp.dot(attention_low, output_matrix, preferred_element_type=f32)
    inverse_two = lax.rsqrt(jnp.mean(hidden * hidden, axis=-1, keepdims=True) + EPSILON)
    unit_two = hidden * inverse_two
    (normed_two,) = clock((unit_two * gain_two).astype(bf16))
    (arrived,) = clock.wait(passing)
    passed.append(arrived)

    normed_moving = send_around(normed_two)
    gate_matrix, up_matrix = clock.run(
        lambda order, gathered: place_gathered(order, gathered, 2), z_order, gate_up
    )
    gate_matrix = gate_matrix.reshape(width, block_units)
    up_matrix = up_matrix.reshape(width, block_units)
    (normed_arrived,) = clock.wait(normed_moving)
    while len(passed) < shards:
        (arrived,) = clock.wait(clock.pass_on(shard, *passed[-1]))
        passed.append(arrived)
    group_normed = jnp.concatenate([normed_two] + normed_arrived, axis=0)
    cotangents = jnp.concatenate(
        [output_cotangent]
        + [
            jnp.where(shard.place >= step, passed[step][0], passed[shards - step][1])
            for step in steps
        ],
        axis=0,
    )

    inner_act, d_gate, d_up, turned_normed, turned_inner = clock.run(
        feed_forward, group_normed, cotangents, gate_matrix, up_matrix, down_weight
    )

    def split_halves(left, right, groups, turned):
        count = first.size * second.size
        halves = clock.run(
            lambda left, right: split_gradient(left, right, groups, count, core.place, turned),
            left,
            right,
        )
        return [half.reshape((first.size, second.size) + half.shape[1:]) for half in halves]

    def side_by_side(rows):
        return clock(jnp.concatenate(in_place_order(rows, shard), axis=1))[0]

    def sum_over_rep(blocks):
        return lax.psum_scatter(blocks, "rep", scatter_dimension=0, tiled=True)

    def row_sum(own, arrived):
        return clock(total_of(own + arrived).astype(bf16))[0]

    def send_some(rows, chosen):
        return clock.send(shard, [rows[k] for k in chosen], [shards - 1 - k for k in chosen])

    edges = sorted({0, shards - 2})
    inside = list(range(1, shards - 2))

    normed_own, *normed_partial = clock.run(
        lambda *operands: rows_product(operands[:2], operands[2:], True, shards),
        d_gate,
        d_up,
        gate_matrix,
        up_matrix,
    )
    up_halves = split_halves(turned_normed, d_up, shards, True)

    up = Halving(clock, *up_halves, core, first, second)
    normed_moving = send_some(normed_partial, edges)
    (gate_blocks,) = clock.run(
        lambda left, right: ordered_gradient(left, right, shards, rep_places(reps)),
        turned_normed,
        d_gate,
    )
    up_arrived, normed_arrived = clock.wait(up.moving, normed_moving)
    gate_piece = sum_over_rep(clock(gate_blocks)[0].reshape(width, block_units))

    up.along_first(up_arrived)
    normed_moving = send_some(normed_partial, inside)
    (down_blocks,) = clock.run(
        lambda left, right: ordered_gradient(left, right, 1, list(range(reps))),
        turned_inner,
        cotangents,
    )
    up_arrived, more_arrived = clock.wait(up.moving, normed_moving)

    up.along_second(up_arrived)
    normed_two_gradient = total_of([normed_own] + normed_arrived + more_arrived)
    gain_two_gradient = jnp.sum(normed_two_gradient * unit_two, axis=0)
    hidden_gradient = output_cotangent.astype(f32) + norm_back(
        normed_two_gradient, unit_two, inverse_two, gain_two
    )
    (branch_gradient,) = clock(hidden_gradient.astype(bf16))
    (attention_gradient,) = clock(times_transposed(branch_gradient, output_matrix).astype(bf16))
    d_queries, pair_own, *pair_partial = clock.run(
        lambda *operands: attention_backward(*operands, shards),
        queries,
        attention_gradient,
        pairs,
        cosine_table,
        signed_sine,
        row_marks,
        key_marks.T,
    )
    output_halves = split_halves(attention_low, branch_gradient, shards, False)
    (up_arrived,) = clock.wait(up.moving)

    pair_moving = send_back(pair_partial)
    output = Halving(clock, *output_halves, core, first, second)
    up_blocks = clock(*blocks_of(up.finish(up_arrived)))
    block_own, *block_partial = clock.run(
        lambda left, right: rows_product((left,), (right,), False, shards), inner_act, down_weight
    )
    pair_arrived, output_arrived = clock.wait(pair_moving, output.moving)

    (gate_piece,) = clock(gate_piece)
    down_piece = sum_over_rep(clock(down_blocks)[0].reshape(block_units, width))
    output.along_first(output_arrived)
    up_moving = send_blocks(up_blocks)
    projected_gradient, bias_sum = clock.run(
        lambda *operands: join_projected(operands[0], operands[3:], *operands[1:3]),
        d_queries,
        cosine_table,
        signed_sine,
        pair_own,
        *pair_arrived,
    )
    projected_halves = split_halves(normed_one, projected_gradient, shards, False)
    output_arrived, up_rows = clock.wait(output.moving, up_moving)

    projected = Halving(clock, *projected_halves, core, first, second)
    output.along_second(output_arrived)
    up_spread = spread(side_by_side(up_blocks[:1] + up_rows))
    block_moving = send_some(block_partial, inside)
    projected_gradient, hidden_gradient = clock(projected_gradient, hidden_gradient)
    normed_one_gradient = times_transposed(projected_gradient, input_matrix)
    gain_one_gradient = jnp.sum(normed_one_gradient * unit_one, axis=0)
    (tokens_gradient,) = clock(
        (
            hidden_gradient + norm_back(normed_one_gradient, unit_one, inverse_one, gain_one)
        ).astype(bf16)
    )
    projected_arrived, output_arrived, up_arrived, block_arrived = clock.wait(
        projected.moving, output.moving, up_spread.moving, block_moving
    )

    projected.along_first(projected_arrived)
    up_spread.along(up_arrived)
    gate_blocks = clock(*blocks_of(gate_piece.reshape(shards, part_rows, block_units)))
    gate_moving = send_blocks(gate_blocks)
    output_blocks = clock(*blocks_of(output.finish(output_arrived)))
    bias_gradient = bias_sum[0]
    bias_split = query_width + pair_width
    small_parts = (
        gain_one_gradient,
        gain_two_gradient,
        bias_gradient[:bias_split],
        bias_gradient[bias_split:],
    )
    (small,) = clock(
        jnp.concatenate([part.reshape(shards, -1) for part in small_parts], axis=1)
    )
    projected_arrived, up_arrived, gate_rows = clock.wait(
        projected.moving, up_spread.moving, gate_moving
    )

    projected.along_second(projected_arrived)
    gate_spread = spread(side_by_side(gate_blocks[:1] + gate_rows))
    output_moving = send_blocks(output_blocks)
    projected_arrived, gate_arrived, output_rows = clock.wait(
        projected.moving, gate_spread.moving, output_moving
    )

    input_blocks = clock(*blocks_of(projected.finish(projected_arrived)))
    input_moving = send_blocks(input_blocks)
    gate_spread.along(gate_arrived)
    output_spread = spread(row_sum(output_blocks[:1], output_rows))
    (down_piece,) = clock(down_piece)
    down_gathered = lax.all_gather(down_piece, "rep", axis=0, tiled=True)
    input_rows, gate_arrived, output_arrived = clock.wait(
        input_moving, gate_spread.moving, output_spread.moving
    )

    input_spread = spread(row_sum(input_blocks[:1], input_rows))
    output_spread.along(output_arrived)
    up_spread.over(up_arrived)
    gate_spread.over(gate_arrived)
    small_moving = clock.send(core, [small], [1])
    input_arrived, output_arrived, up_arrived, gate_arrived, small_arrived = clock.wait(
        input_spread.moving, output_spread.moving, up_spread.moving, gate_spread.moving, small_moving
    )
    small = total_of([small] + small_arrived)

    input_spread.along(input_arrived)
    output_spread.over(output_arrived)
    small_moving = clock.send(first, [small] * (first.size - 1), range(1, first.size))
    block_moving = send_some(block_partial, edges[:1])
    (up_total,) = clock.run(widen_pieces, *up_spread.finish(up_arrived))
    input_arrived, output_arrived, small_arrived, more_arrived = clock.wait(
        input_spread.moving, output_spread.moving, small_moving, block_moving
    )
    small = total_of([small] + small_arrived)
    block_arrived = block_arrived + more_arrived

    input_spread.over(input_arrived)
    small_moving = clock.send(second, [small] * (second.size - 1), range(1, second.size))
    block_moving = send_some(block_partial, edges[1:])
    (gate_total,) = clock.run(widen_pieces, *gate_spread.finish(gate_arrived))
    input_arrived, small_arrived, more_arrived = clock.wait(
        input_spread.moving, small_moving, block_moving
    )
    block_arrived = block_arrived + more_arrived
    small_blocks = clock(*blocks_of(total_of([small] + small_arrived)))

    small_moving = send_blocks(small_blocks)
    (output_total,) = clock.run(widen_pieces, *output_spread.finish(output_arrived))
    (input_total,) = clock.run(widen_pieces, *input_spread.finish(input_arrived))
    (down_gathered,) = clock(down_gathered)
    (down_total,) = clock(down_gathered.astype(f32))
    (block_out,) = clock(total_of([hidden, block_own] + block_arrived).astype(bf16))
    (small_arrived,) = clock.wait(small_moving)
    small = total_of(small_blocks[:1] + small_arrived)

    small = small + clock.token[0, 0]
    small_totals, at = [], 0
    for part in small_parts:
        size = part.shape[0] // shards
        small_totals.append(small[at : at + size])
        at += size
    return (
        block_out,
        tokens_gradient,
        small_totals[0],
        input_total,
        small_totals[2],
        small_totals[3],
        output_total,
        small_totals[1],
        gate_total,
        up_total,
        down_total,
    )


def solution(mesh):
    placed = (
        P(("rep", "shard"), None),
        P("rep", None),
        P("shard"),
        P("shard", None),
        P("shard"),
        P("shard", None),
        P("shard"),
        P("shard", None),
        P("shard", None),
        P("shard", None),
        P(("rep", "shard"), None),
    )
    return jax.shard_map(
        on_device,
        mesh=mesh,
        in_specs=placed,
        out_specs=(
            P(("rep", "shard"), None),
            P(("rep", "shard"), None),
            P("shard"),
            P("shard", None),
            P("shard"),
            P("shard"),
            P("shard", None),
            P("shard"),
            P("shard", None),
            P("shard", None),
            P("shard", None),
        ),
        check_vma=False,
    )
```

```python
import math

import jax
import jax.numpy as jnp
from jax import lax
from jax.experimental import pallas as pl
from jax.experimental.pallas import tpu as pltpu
from jax.sharding import PartitionSpec as P

QH = 12
KVH = 2
HD = 128
SEQS = 3


EPSILON = 1e-06
LOG_THETA = math.log(1000000.0)
MASKED = -1e30
VMEM_LIMIT = 56 * 1024 * 1024
TILE = 512
COST = pl.CostEstimate(flops=1, bytes_accessed=1, transcendentals=0)


def rope_tables(places, head_width):
    half_width = head_width // 2
    frequency = jnp.exp(jnp.arange(half_width, dtype=jnp.float32) * (-2.0 * LOG_THETA / head_width))
    angles = places.astype(jnp.float32)[:, None] * frequency[None, :]
    angles = jnp.concatenate([angles, angles], axis=-1)
    return (jnp.cos(angles), jnp.sin(angles))


def positions(segments):
    labels = jnp.arange(SEQS, dtype=jnp.int32)
    starts = jnp.sum((segments[None, :] < labels[:, None]).astype(jnp.int32), axis=1)
    own_start = jnp.sum(jnp.where(segments[:, None] == labels[None, :], starts[None, :], 0), axis=1)
    return jnp.arange(segments.shape[0], dtype=jnp.int32) - own_start


def rotate(field_rows, cosine_table, sine_table):
    half_width = field_rows.shape[-1] // 2
    turned = jnp.concatenate([-field_rows[..., half_width:], field_rows[..., :half_width]], axis=-1)
    return field_rows * cosine_table[:, None, :] + turned * sine_table[:, None, :]


def transposed_times(left_side, right_side):
    return lax.dot_general(
        left_side, right_side, (((0,), (0,)), ((), ())), preferred_element_type=jnp.float32
    )


def times_transposed(left_side, right_side):
    return lax.dot_general(
        left_side, right_side, (((1,), (1,)), ((), ())), preferred_element_type=jnp.float32
    )


def norm_back(normed_gradient, unit_rows, inverse_rms, gain_row):
    scaled = normed_gradient * gain_row
    return inverse_rms * (scaled - unit_rows * jnp.mean(scaled * unit_rows, axis=-1, keepdims=True))


class Line:
    def __init__(self, name, size, place, pairs, crossed=False):
        self.name, self.size, self.place, self.pairs = name, size, place, pairs
        self.crossed = crossed

    def shift(self, value, step):
        return lax.ppermute(value, self.name, self.pairs(step % self.size))

    def pass_on(self, value, up):
        places = range(self.size - 1)
        pairs = [(at, at + 1) if up else (at + 1, at) for at in places]
        return lax.ppermute(value, self.name, pairs)

    def behind(self, step):
        return lax.rem(self.place + (self.size - step % self.size), self.size)

    def ahead(self, step):
        return lax.rem(self.place + step % self.size, self.size) if step else self.place


def make_lines(reps, shards):
    inner = 2 if reps % 4 == 0 else 1
    outer = reps // (2 * inner)
    square = inner == outer

    def split(index):
        core, b, a = index % 2, (index // 2) % inner, index // (2 * inner)
        return core, b, a

    def join(core, b, a):
        return (a * inner + b) * 2 + core

    def first_pairs(step):
        pairs = []
        for index in range(reps):
            core, b, a = split(index)
            if square and core == 0:
                pairs.append((index, join(core, (b + step) % inner, a)))
            else:
                pairs.append((index, join(core, b, (a + step) % outer)))
        return pairs

    def second_pairs(step):
        pairs = []
        for index in range(reps):
            core, b, a = split(index)
            if square and core == 0:
                pairs.append((index, join(core, b, (a + step) % outer)))
            else:
                pairs.append((index, join(core, (b + step) % inner, a)))
        return pairs

    def core_pairs(step):
        pairs = []
        for index in range(reps):
            core, b, a = split(index)
            pairs.append((index, join((core + step) % 2, b, a)))
        return pairs

    def shard_pairs(step):
        return [(index, (index + step) % shards) for index in range(shards)]

    core, b, a = split(lax.axis_index("rep"))
    first, second = (jnp.where(core == 0, b, a), jnp.where(core == 0, a, b)) if square else (a, b)
    return (
        Line("shard", shards, lax.axis_index("shard"), shard_pairs),
        Line("rep", 2, core, core_pairs, square),
        Line("rep", outer, first, first_pairs),
        Line("rep", inner, second, second_pairs),
    )


def rep_places(reps):
    inner = 2 if reps % 4 == 0 else 1
    outer = reps // (2 * inner)
    places = []
    for index in range(reps):
        core, b, a = index % 2, (index // 2) % inner, index // (2 * inner)
        one, two = (b, a) if inner == outer and core == 0 else (a, b)
        places.append((core * outer + one) * inner + two)
    return places


def pick(array, index, axis):
    return lax.dynamic_index_in_dim(array, index, axis, keepdims=False)


def put(array, piece, index, axis):
    return lax.dynamic_update_index_in_dim(array, piece, index, axis)


def in_place_order(pieces, line):
    ordered = []
    for place in range(line.size):
        chosen = pieces[0]
        for step in range(1, line.size):
            chosen = jnp.where(line.behind(step) == place, pieces[step], chosen)
        ordered.append(chosen)
    return ordered


def tie(*arrays):
    return lax.optimization_barrier(arrays)


def gather_line(value, line):
    return [value] + [line.shift(value, step) for step in range(1, line.size)]


class Clock:
    def __init__(self):
        self.token = jnp.zeros((8, 128), jnp.float32)
        self.open = 0

    def __call__(self, *arrays):
        self.token, *arrays = tie(self.token, *arrays)
        return arrays

    def run(self, step, *arrays):
        return self(*step(*self(*arrays)))

    def send(self, line, values, steps):
        self.open += len(values)
        return [line.shift(value, step) for value, step in zip(self(*values), steps)]

    def pass_on(self, line, lower, upper):
        self.open += 2
        lower, upper = self(lower, upper)
        return [line.pass_on(lower, True), line.pass_on(upper, False)]

    def wait(self, *groups):
        flat = self(*[array for group in groups for array in group])
        self.open -= len(flat)
        parts, at = [], 0
        for group in groups:
            parts.append(flat[at : at + len(group)])
            at += len(group)
        return parts


def total_of(terms):
    total = terms[0].astype(jnp.float32)
    for term in terms[1:]:
        total = total + term.astype(jnp.float32)
    return total


class Halving:
    def __init__(self, clock, sent, own, core, first, second):
        self.clock, self.first, self.second = clock, first, second
        self.terms = [own]
        self.moving = clock.send(core, [sent], [1])

    def along(self, line, arrived):
        self.terms = self.terms + arrived
        steps = range(1, line.size)
        blocks = [
            total_of([pick(term, line.ahead(step), 0) for term in self.terms]).astype(jnp.bfloat16)
            for step in steps
        ]
        self.moving = self.clock.send(line, blocks, steps)
        self.terms = [pick(term, line.place, 0) for term in self.terms]

    def along_first(self, arrived):
        self.along(self.first, arrived)

    def along_second(self, arrived):
        self.along(self.second, arrived)

    def finish(self, arrived):
        return self.clock(total_of(self.terms + arrived).astype(jnp.bfloat16))[0]


class Spread:
    def __init__(self, clock, piece, core, first, second):
        self.clock, self.lines = clock, (core, first, second)
        self.pieces = [piece]
        steps = range(1, second.size)
        self.moving = clock.send(second, [piece] * len(steps), steps)

    def along(self, arrived):
        core, first, second = self.lines
        self.pieces = self.pieces + arrived
        steps = range(1, first.size)
        self.moving = self.clock.send(first, [jnp.stack(self.pieces)] * len(steps), steps)

    def over(self, arrived):
        core, first, second = self.lines
        rows = [jnp.stack(self.pieces)] + arrived
        self.pieces = jnp.concatenate(rows, axis=0)
        self.moving = self.clock.send(core, [self.pieces], [1])

    def finish(self, arrived):
        core, first, second = self.lines
        (others,) = arrived
        offsets = [(one, two) for one in range(first.size) for two in range(second.size)]
        placed = [(core.place, first.behind(one), second.behind(two)) for one, two in offsets]
        far, near = (second, first) if core.crossed else (first, second)
        placed += [(core.behind(1), far.behind(one), near.behind(two)) for one, two in offsets]
        places = [(c * first.size + f) * second.size + s for c, f, s in placed]
        return [jnp.stack(places).astype(jnp.int32), self.pieces, others]


def column_blocks(place, shard_place, *weights):
    count = len(weights)
    rows, columns = weights[0].shape[1:]
    shards = lax.axis_size("shard")
    block = columns // shards

    def body(places_ref, *refs):
        sources, outs = refs[:count], refs[count : 2 * count]
        held, cut, in_sems, out_sems = refs[2 * count :]
        loads = [
            pltpu.make_async_copy(sources[at].at[places_ref[0]], held.at[at], in_sems.at[at])
            for at in range(count)
        ]

        def store(at, z):
            ahead = lax.rem(z + shards - places_ref[1], shards)
            return pltpu.make_async_copy(cut.at[at, z], outs[at].at[ahead], out_sems.at[at, z])

        for load in loads:
            load.start()
        for at in range(count):
            loads[at].wait()
            for z in range(shards):
                cut[at, z] = held[at, :, z * block : (z + 1) * block]
                store(at, z).start()
        for at in range(count):
            for z in range(shards):
                store(at, z).wait()

    return pl.pallas_call(
        body,
        out_shape=[jax.ShapeDtypeStruct((shards, rows, block), jnp.bfloat16)] * count,
        in_specs=[pl.BlockSpec(memory_space=pltpu.SMEM)]
        + [pl.BlockSpec(memory_space=pl.ANY)] * count,
        out_specs=[pl.BlockSpec(memory_space=pl.ANY)] * count,
        scratch_shapes=[
            pltpu.VMEM((count, rows, columns), jnp.bfloat16),
            pltpu.VMEM((count, shards, rows, block), jnp.bfloat16),
            pltpu.SemaphoreType.DMA((count,)),
            pltpu.SemaphoreType.DMA((count, shards)),
        ],
        compiler_params=pltpu.CompilerParams(vmem_limit_bytes=VMEM_LIMIT),
        cost_estimate=COST,
        name="column_blocks",
    )(jnp.stack([place, shard_place]).astype(jnp.int32), *weights)


def place_blocks(order, places, pieces, others):
    half, groups, shards = pieces.shape[:3]

    def body(order_ref, places_ref, pieces_ref, others_ref, *rest):
        def source_of(g, k, r):
            return (pieces_ref if r < half else others_ref).at[r % half, g, k]

        move_blocks(source_of, lambda r: places_ref[r], order_ref, rest[:groups], *rest[groups:])

    return blocks_call(body, 2, 2, groups, shards, 2 * half, pieces.shape[3:])(
        order, places, pieces, others
    )


def place_gathered(order, gathered, groups):
    shards = lax.axis_size("shard")
    reps = gathered.shape[0] // (shards * groups)

    def body(order_ref, source, *rest):
        move_blocks(
            lambda g, k, r: source.at[(r * shards + k) * groups + g],
            lambda r: r,
            order_ref,
            rest[:groups],
            *rest[groups:],
        )

    return blocks_call(body, 1, 1, groups, shards, reps, gathered.shape[1:])(order, gathered)


def move_blocks(source_of, place_of, order_ref, outs, held, in_sems, out_sems):
    groups, shards, reps = in_sems.shape
    slabs = [(g, k) for g in range(groups) for k in range(shards)]

    def load(g, k, r):
        return pltpu.make_async_copy(
            source_of(g, k, r), held.at[g, k, place_of(r)], in_sems.at[g, k, r]
        )

    def store(g, k):
        return pltpu.make_async_copy(held.at[g, k], outs[g].at[order_ref[k]], out_sems.at[g, k])

    for g, k in slabs:
        for r in range(reps):
            load(g, k, r).start()
    for g, k in slabs:
        for r in range(reps):
            load(g, k, r).wait()
        store(g, k).start()
    for g, k in slabs:
        store(g, k).wait()


def blocks_call(body, scalars, sources, groups, shards, reps, block):
    whole = (shards, reps) + block
    return pl.pallas_call(
        body,
        out_shape=[jax.ShapeDtypeStruct(whole, jnp.bfloat16)] * groups,
        in_specs=[pl.BlockSpec(memory_space=pltpu.SMEM)] * scalars
        + [pl.BlockSpec(memory_space=pl.ANY)] * sources,
        out_specs=[pl.BlockSpec(memory_space=pl.ANY)] * groups,
        scratch_shapes=[
            pltpu.VMEM((groups,) + whole, jnp.bfloat16),
            pltpu.SemaphoreType.DMA((groups, shards, reps)),
            pltpu.SemaphoreType.DMA((groups, shards)),
        ],
        compiler_params=pltpu.CompilerParams(vmem_limit_bytes=VMEM_LIMIT),
        cost_estimate=COST,
        name="place_blocks",
    )


def widen_pieces(places, pieces, others):
    half, rows, columns = pieces.shape
    reps = 2 * half
    strip = next(size for size in (16, 8, rows) if rows % size == 0)

    def body(places_ref, pieces_ref, others_ref, out_ref, narrow, wide, in_sems, out_sems):
        loads = [
            pltpu.make_async_copy(
                (pieces_ref if r < half else others_ref).at[r % half], narrow.at[r], in_sems.at[r]
            )
            for r in range(reps)
        ]
        stores = [
            pltpu.make_async_copy(wide.at[r], out_ref.at[places_ref[r]], out_sems.at[r])
            for r in range(reps)
        ]
        for load in loads:
            load.start()
        for r in range(reps):
            loads[r].wait()

            def convert(at, carry):
                cut = pl.ds(pl.multiple_of(at * strip, strip), strip)
                wide[r, cut, :] = narrow[r, cut, :].astype(jnp.float32)
                return carry

            lax.fori_loop(0, rows // strip, convert, 0)
            stores[r].start()
        for store in stores:
            store.wait()

    result = pl.pallas_call(
        body,
        out_shape=jax.ShapeDtypeStruct((reps, rows, columns), jnp.float32),
        in_specs=[pl.BlockSpec(memory_space=pltpu.SMEM)]
        + [pl.BlockSpec(memory_space=pl.ANY)] * 2,
        out_specs=pl.BlockSpec(memory_space=pl.ANY),
        scratch_shapes=[
            pltpu.VMEM((reps, rows, columns), jnp.bfloat16),
            pltpu.VMEM((reps, rows, columns), jnp.float32),
            pltpu.SemaphoreType.DMA((reps,)),
            pltpu.SemaphoreType.DMA((reps,)),
        ],
        compiler_params=pltpu.CompilerParams(vmem_limit_bytes=VMEM_LIMIT),
        cost_estimate=COST,
        name="widen_pieces",
    )(places, pieces, others)
    return (result.reshape(reps * rows, columns),)


def resident(shape):
    return pl.BlockSpec(shape, lambda i: (0, 0), pipeline_mode=pl.Buffered(1))


def feed_forward(rows, cotangents, gate_matrix, up_matrix, down_matrix):
    count, width = rows.shape
    units = gate_matrix.shape[1]
    steps = pl.cdiv(units, TILE)
    slabs = next(size for size in range(min(steps, width // 128), 0, -1) if width % (128 * size) == 0)
    slab = width // slabs

    def body(
        rows_ref,
        cotangents_ref,
        gate_ref,
        up_ref,
        down_ref,
        inner_ref,
        d_gate_ref,
        d_up_ref,
        turned_rows_ref,
        turned_inner_ref,
    ):
        gate = jnp.dot(rows_ref[...], gate_ref[...], preferred_element_type=jnp.float32)
        up = jnp.dot(rows_ref[...], up_ref[...], preferred_element_type=jnp.float32)
        sigmoid = jax.nn.sigmoid(gate)
        silu = gate * sigmoid
        inner = (silu * up).astype(jnp.bfloat16)
        inner_ref[...] = inner
        turned_inner_ref[...] = inner.T
        d_inner = times_transposed(cotangents_ref[...], down_ref[...])
        d_up_ref[...] = (d_inner * silu).astype(jnp.bfloat16)
        d_gate_ref[...] = (d_inner * up * sigmoid * (1.0 + gate * (1.0 - sigmoid))).astype(
            jnp.bfloat16
        )
        for step in range(slabs):

            @pl.when(pl.program_id(0) == step)
            def turn():
                turned_rows_ref[...] = rows_ref[:, step * slab : (step + 1) * slab].T

    columns = pl.BlockSpec((width, TILE), lambda i: (0, i))
    results = pl.BlockSpec((count, TILE), lambda i: (0, i))
    return pl.pallas_call(
        body,
        grid=(steps,),
        out_shape=[jax.ShapeDtypeStruct((count, units), jnp.bfloat16)] * 3
        + [
            jax.ShapeDtypeStruct((width, count), jnp.bfloat16),
            jax.ShapeDtypeStruct((units, count), jnp.bfloat16),
        ],
        in_specs=[
            resident((count, width)),
            resident((count, width)),
            columns,
            columns,
            pl.BlockSpec((TILE, width), lambda i: (i, 0)),
        ],
        out_specs=[results] * 3
        + [
            pl.BlockSpec((slab, count), lambda i: (jnp.minimum(i, slabs - 1), 0)),
            pl.BlockSpec((TILE, count), lambda i: (i, 0)),
        ],
        compiler_params=pltpu.CompilerParams(vmem_limit_bytes=VMEM_LIMIT),
        cost_estimate=COST,
        name="feed_forward",
    )(rows, cotangents, gate_matrix, up_matrix, down_matrix)


def split_gradient(left, right, groups, places, core_place, turned):
    rows, count = left.shape if turned else left.shape[::-1]
    columns = right.shape[1]
    half = rows // (2 * groups)
    part = half // places

    def body(core_ref, left_ref, right_ref, other_ref, own_ref, *scratch):
        if turned:
            rows_ref = left_ref
        else:
            (rows_ref,) = scratch

            @pl.when(pl.program_id(0) == 0)
            def turn():
                rows_ref[...] = left_ref[...].T

        core = core_ref[0]
        for out_ref, which in ((other_ref, 1 - core), (own_ref, core)):
            halves = [
                rows_ref[pl.ds(pl.multiple_of((2 * group + which) * half, 16), half), :]
                for group in range(groups)
            ]
            product = jnp.dot(
                jnp.concatenate(halves, axis=0), right_ref[...], preferred_element_type=jnp.float32
            )
            for group in range(groups):
                for place in range(places):
                    at = group * half + place * part
                    out_ref[place, group] = product[at : at + part].astype(jnp.bfloat16)

    return pl.pallas_call(
        body,
        grid=(pl.cdiv(columns, TILE),),
        out_shape=[jax.ShapeDtypeStruct((places, groups, part, columns), jnp.bfloat16)] * 2,
        in_specs=[
            pl.BlockSpec(memory_space=pltpu.SMEM),
            resident(left.shape),
            pl.BlockSpec((count, TILE), lambda i: (0, i)),
        ],
        out_specs=[pl.BlockSpec((places, groups, part, TILE), lambda i: (0, 0, 0, i))] * 2,
        scratch_shapes=[] if turned else [pltpu.VMEM((rows, count), jnp.bfloat16)],
        compiler_params=pltpu.CompilerParams(vmem_limit_bytes=VMEM_LIMIT),
        cost_estimate=COST,
        name="split_gradient",
    )(core_place.reshape(1).astype(jnp.int32), left, right)


def ordered_gradient(left, right, shards, order):
    reps = len(order)
    rows, count = left.shape
    columns = right.shape[1]
    part = rows // (shards * reps)

    def body(left_ref, right_ref, out_ref):
        product = jnp.dot(left_ref[...], right_ref[...], preferred_element_type=jnp.float32)
        for z in range(shards):
            for r in range(reps):
                at = (z * reps + order[r]) * part
                out_ref[r, z] = product[at : at + part].astype(jnp.bfloat16)

    return pl.pallas_call(
        body,
        grid=(pl.cdiv(columns, TILE),),
        out_shape=[jax.ShapeDtypeStruct((reps, shards, part, columns), jnp.bfloat16)],
        in_specs=[
            resident((rows, count)),
            pl.BlockSpec((count, TILE), lambda i: (0, i)),
        ],
        out_specs=[pl.BlockSpec((reps, shards, part, TILE), lambda i: (0, 0, 0, i))],
        compiler_params=pltpu.CompilerParams(vmem_limit_bytes=VMEM_LIMIT),
        cost_estimate=COST,
        name="ordered_gradient",
    )(left, right)


def rows_product(lefts, rights, turned, blocks):
    count, depth = lefts[0].shape
    columns = rights[0].shape[0 if turned else 1]
    pairs, part = len(lefts), count // blocks

    def body(*refs):
        total = None
        for left_ref, right_ref in zip(refs[:pairs], refs[pairs : 2 * pairs]):
            if turned:
                product = times_transposed(left_ref[...], right_ref[...])
            else:
                product = jnp.dot(
                    left_ref[...], right_ref[...], preferred_element_type=jnp.float32
                )
            total = product if total is None else total + product
        for block in range(blocks):
            refs[2 * pairs + block][...] = total[block * part : (block + 1) * part].astype(
                jnp.bfloat16
            )

    right_spec = (
        pl.BlockSpec((TILE, depth), lambda i: (i, 0))
        if turned
        else pl.BlockSpec((depth, TILE), lambda i: (0, i))
    )
    return pl.pallas_call(
        body,
        grid=(pl.cdiv(columns, TILE),),
        out_shape=[jax.ShapeDtypeStruct((part, columns), jnp.bfloat16)] * blocks,
        in_specs=[resident((count, depth))] * pairs + [right_spec] * pairs,
        out_specs=[pl.BlockSpec((part, TILE), lambda i: (0, i))] * blocks,
        compiler_params=pltpu.CompilerParams(vmem_limit_bytes=VMEM_LIMIT),
        cost_estimate=COST,
        name="rows_product",
    )(*lefts, *rights)


def kept_bias(row_segments, row_index, key_segments, key_index):
    kept = (row_segments == key_segments) & (key_index <= row_index)
    return jnp.where(kept, 0.0, MASKED)


def in_vmem(count):
    return [pl.BlockSpec(memory_space=pltpu.VMEM)] * count


def attention_forward(projected, cosine, signed_sine, pairs, rows, keys):
    count = projected.shape[0]
    per_group = QH // KVH
    scale = 1.0 / math.sqrt(HD)
    shape = (KVH, per_group * count, HD)

    def body(projected_ref, cosine_ref, sine_ref, pairs_ref, rows_ref, keys_ref, queries_ref, out_ref):
        bias = kept_bias(rows_ref[:, 0:1], rows_ref[:, 1:2], keys_ref[0:1, :], keys_ref[1:2, :])
        for k in range(KVH):
            for h in range(per_group):
                at = (k * per_group + h) * HD
                field = projected_ref[:, at : at + HD]
                queries_ref[k, h * count : (h + 1) * count, :] = (
                    field * cosine_ref[...] + pltpu.roll(field, HD // 2, 1) * sine_ref[...]
                ).astype(jnp.bfloat16)
            keys_here = pairs_ref[:, k * HD : (k + 1) * HD]
            values_here = pairs_ref[:, (KVH + k) * HD : (KVH + k + 1) * HD]
            scores = times_transposed(queries_ref[k], keys_here) * scale + bias
            powers = jnp.exp(scores - jnp.max(scores, axis=1, keepdims=True))
            shares = powers * (1.0 / jnp.sum(powers, axis=1, keepdims=True))
            result = jnp.dot(
                shares.astype(jnp.bfloat16), values_here, preferred_element_type=jnp.float32
            ).astype(jnp.bfloat16)
            for h in range(per_group):
                at = (k * per_group + h) * HD
                out_ref[:, at : at + HD] = result[h * count : (h + 1) * count]

    return pl.pallas_call(
        body,
        out_shape=[
            jax.ShapeDtypeStruct(shape, jnp.bfloat16),
            jax.ShapeDtypeStruct((count, QH * HD), jnp.bfloat16),
        ],
        in_specs=in_vmem(6),
        out_specs=in_vmem(2),
        compiler_params=pltpu.CompilerParams(vmem_limit_bytes=VMEM_LIMIT),
        cost_estimate=COST,
        name="attention_forward",
    )(projected, cosine, signed_sine, pairs, rows, keys)


def attention_backward(queries, gradient, pairs, cosine, signed_sine, rows, keys, blocks):
    count = gradient.shape[0]
    per_group = QH // KVH
    scale = 1.0 / math.sqrt(HD)
    group_rows = pairs.shape[0]
    part = group_rows // blocks

    def body(queries_ref, gradient_ref, pairs_ref, cosine_ref, sine_ref, rows_ref, keys_ref, d_ref, *outs):
        block_refs, stacked = outs[:blocks], outs[blocks]
        bias = kept_bias(rows_ref[0:1, :], rows_ref[1:2, :], keys_ref[:, 0:1], keys_ref[:, 1:2])
        for k in range(KVH):
            for h in range(per_group):
                at = (k * per_group + h) * HD
                stacked[h * count : (h + 1) * count, :] = gradient_ref[:, at : at + HD]
            keys_here = pairs_ref[:, k * HD : (k + 1) * HD]
            values_here = pairs_ref[:, (KVH + k) * HD : (KVH + k + 1) * HD]
            scores = times_transposed(keys_here, queries_ref[k]) * scale + bias
            powers = jnp.exp(scores - jnp.max(scores, axis=0, keepdims=True))
            shares = powers * (1.0 / jnp.sum(powers, axis=0, keepdims=True))
            d_shares = times_transposed(values_here, stacked[...])
            dots = jnp.sum(shares * d_shares, axis=0, keepdims=True)
            d_scores = (shares * (d_shares - dots)).astype(jnp.bfloat16)
            d_keys = jnp.dot(d_scores, queries_ref[k], preferred_element_type=jnp.float32) * scale
            d_values = jnp.dot(
                shares.astype(jnp.bfloat16), stacked[...], preferred_element_type=jnp.float32
            )
            for block in range(blocks):
                cut = slice(block * part, (block + 1) * part)
                block_refs[block][:, k * HD : (k + 1) * HD] = d_keys[cut].astype(jnp.bfloat16)
                block_refs[block][:, (KVH + k) * HD : (KVH + k + 1) * HD] = d_values[cut].astype(
                    jnp.bfloat16
                )
            d_queries = transposed_times(d_scores, keys_here) * scale
            for h in range(per_group):
                at = (k * per_group + h) * HD
                field = d_queries[h * count : (h + 1) * count]
                d_ref[:, at : at + HD] = (
                    field * cosine_ref[...] - pltpu.roll(field, HD // 2, 1) * sine_ref[...]
                ).astype(jnp.bfloat16)

    return pl.pallas_call(
        body,
        out_shape=[jax.ShapeDtypeStruct((count, QH * HD), jnp.bfloat16)]
        + [jax.ShapeDtypeStruct((part, 2 * KVH * HD), jnp.bfloat16)] * blocks,
        in_specs=in_vmem(7),
        out_specs=in_vmem(1 + blocks),
        scratch_shapes=[pltpu.VMEM((per_group * count, HD), jnp.bfloat16)],
        compiler_params=pltpu.CompilerParams(vmem_limit_bytes=VMEM_LIMIT),
        cost_estimate=COST,
        name="attention_backward",
    )(queries, gradient, pairs, cosine, signed_sine, rows, keys)


def join_projected(d_queries, pair_terms, cosine, signed_sine):
    count, query_width = d_queries.shape
    pair_width = KVH * HD
    terms = len(pair_terms)

    def body(d_queries_ref, cosine_ref, sine_ref, *refs):
        term_refs, out_ref, sum_ref = refs[:terms], refs[terms], refs[terms + 1]
        out_ref[:, :query_width] = d_queries_ref[...]
        for at in range(0, 2 * pair_width, HD):
            field = total_of([term[:, at : at + HD] for term in term_refs])
            if at < pair_width:
                field = field * cosine_ref[...] - pltpu.roll(field, HD // 2, 1) * sine_ref[...]
            out_ref[:, query_width + at : query_width + at + HD] = field.astype(jnp.bfloat16)
        sum_ref[...] = jnp.sum(out_ref[...].astype(jnp.float32), axis=0, keepdims=True)

    return pl.pallas_call(
        body,
        out_shape=[
            jax.ShapeDtypeStruct((count, query_width + 2 * pair_width), jnp.bfloat16),
            jax.ShapeDtypeStruct((1, query_width + 2 * pair_width), jnp.float32),
        ],
        in_specs=in_vmem(3 + terms),
        out_specs=in_vmem(2),
        cost_estimate=COST,
        name="join_projected",
    )(d_queries, cosine, signed_sine, *pair_terms)


def on_device(
    tokens,
    segment_ids,
    first_gain,
    input_weight,
    input_bias,
    output_weight,
    second_gain,
    gate_weight,
    up_weight,
    down_weight,
    output_cotangent,
):
    bf16, f32 = jnp.bfloat16, jnp.float32
    shards, reps = lax.axis_size("shard"), lax.axis_size("rep")
    shard, core, first, second = make_lines(reps, shards)
    rep_place = (core.place * first.size + first.place) * second.size + second.place
    own_rows, width = tokens.shape
    segments = segment_ids[0]
    per_group = QH // KVH
    query_width = QH * HD
    pair_width = KVH * HD
    first_row = shard.place * own_rows
    part_rows = input_weight.shape[0] // reps
    hidden_units = gate_weight.shape[1]
    block_units = hidden_units // shards
    clock = Clock()
    z_order = jnp.stack([shard.behind(step) for step in range(shards)]).astype(jnp.int32)

    def weight_piece(weight, place):
        return pick(weight.reshape(reps, part_rows, weight.shape[1]), place, 0)

    def spread(piece):
        return Spread(clock, piece, core, first, second)

    def blocks_of(blocks):
        return [pick(blocks, shard.ahead(step), 0) for step in range(shards)]

    steps = range(1, shards)

    def send_blocks(blocks):
        return clock.send(shard, blocks[1:], steps)

    def send_around(value):
        return clock.send(shard, [value] * len(steps), steps)

    def send_back(rows):
        return clock.send(shard, rows, [shards - step for step in steps])

    rep_index = lax.axis_index("rep")
    input_matrix = lax.all_gather(
        weight_piece(input_weight, rep_index), ("shard", "rep"), axis=0, tiled=True
    )
    shard_vectors = jnp.concatenate([first_gain, second_gain, input_bias])
    vector_row = jnp.pad(shard_vectors, (0, output_weight.shape[1] - shard_vectors.shape[0]))
    own_output = jnp.concatenate(
        [weight_piece(output_weight, rep_place), vector_row[None]], axis=0
    )
    output_moving = send_around(own_output)
    gate_blocks, up_blocks = clock.run(
        lambda *weights: column_blocks(rep_index, shard.place, *weights),
        gate_weight.reshape(reps, part_rows, hidden_units),
        up_weight.reshape(reps, part_rows, hidden_units),
    )
    passed = [[output_cotangent] * 2]
    passing = clock.pass_on(shard, *passed[-1])
    output_rows, arrived = clock.wait(output_moving, passing)
    passed.append(arrived)
    output_rows = [own_output] + output_rows

    output_spread = spread(jnp.stack([rows[:part_rows] for rows in output_rows])[None])
    gate_moving = send_blocks(gate_blocks)
    vector_rows = jnp.stack(in_place_order([rows[part_rows] for rows in output_rows], shard))
    own_gain = first_gain.shape[0]
    gain_one = vector_rows[:, :own_gain].reshape(width).astype(f32)
    gain_two = vector_rows[:, own_gain : 2 * own_gain].reshape(width).astype(f32)
    shift_row = (
        vector_rows[:, 2 * own_gain : shard_vectors.shape[0]].reshape(-1).astype(f32)
    )
    places = positions(segments)
    cosine_table, sine_table = rope_tables(
        lax.dynamic_slice_in_dim(places, first_row, own_rows), HD
    )
    signed_sine = jnp.concatenate(
        [-sine_table[:, : HD // 2], sine_table[:, HD // 2 :]], axis=1
    )
    own_segments = lax.dynamic_slice_in_dim(segments, first_row, own_rows)
    row_index = jnp.arange(own_rows, dtype=jnp.int32)
    key_index = jnp.concatenate([shard.behind(step) * own_rows + row_index for step in range(shards)])
    key_segments = jnp.concatenate(
        [
            lax.dynamic_slice_in_dim(segments, shard.behind(step) * own_rows, own_rows)
            for step in range(shards)
        ]
    )
    key_marks = jnp.stack([key_segments, key_index])
    row_marks = jnp.tile(jnp.stack([own_segments, first_row + row_index]), (1, per_group))
    wide_tokens = tokens.astype(f32)
    inverse_one = lax.rsqrt(jnp.mean(wide_tokens * wide_tokens, axis=-1, keepdims=True) + EPSILON)
    unit_one = wide_tokens * inverse_one
    normed_one = (unit_one * gain_one).astype(bf16)
    (
        normed_one,
        cosine_table,
        sine_table,
        signed_sine,
        key_marks,
        row_marks,
    ) = clock(normed_one, cosine_table, sine_table, signed_sine, key_marks, row_marks)
    output_arrived, gate_rows = clock.wait(output_spread.moving, gate_moving)

    output_spread.along(output_arrived)
    up_moving = send_blocks(up_blocks)
    output_arrived, up_rows = clock.wait(output_spread.moving, up_moving)

    gate_up = jnp.stack(
        [row for pair in zip([gate_blocks[0]] + gate_rows, [up_blocks[0]] + up_rows) for row in pair]
    )
    gate_up = lax.all_gather(clock(gate_up)[0], "rep", axis=0, tiled=True)
    input_matrix, normed_one = clock(input_matrix, normed_one)
    projected = jnp.dot(normed_one, input_matrix, preferred_element_type=f32) + shift_row
    key_part = rotate(
        projected[:, query_width : query_width + pair_width].reshape(own_rows, KVH, HD),
        cosine_table,
        sine_table,
    )
    (own_pairs,) = clock(
        jnp.concatenate(
            [key_part.reshape(own_rows, pair_width), projected[:, query_width + pair_width :]],
            axis=1,
        ).astype(bf16)
    )
    pair_moving = send_around(own_pairs)
    passing = clock.pass_on(shard, *passed[-1]) if shards > 2 else []
    pair_rows, arrived = clock.wait(pair_moving, passing)
    passed.append(arrived)
    pairs = jnp.concatenate([own_pairs] + pair_rows, axis=0)

    passing = clock.pass_on(shard, *passed[-1]) if shards > 3 else []
    output_spread.over(output_arrived)
    queries, attention_low = clock.run(
        attention_forward, projected, cosine_table, signed_sine, pairs, row_marks.T, key_marks
    )
    arrived, output_arrived = clock.wait(passing, output_spread.moving)
    passed.append(arrived)

    (output_matrix,) = clock.run(place_blocks, z_order, *output_spread.finish(output_arrived))
    output_matrix = output_matrix.reshape(width, width)
    hidden = wide_tokens + jnp.dot(attention_low, output_matrix, preferred_element_type=f32)
    inverse_two = lax.rsqrt(jnp.mean(hidden * hidden, axis=-1, keepdims=True) + EPSILON)
    unit_two = hidden * inverse_two
    (normed_two,) = clock((unit_two * gain_two).astype(bf16))
    normed_moving = send_around(normed_two)
    gate_matrix, up_matrix = clock.run(
        lambda order, gathered: place_gathered(order, gathered, 2), z_order, gate_up
    )
    gate_matrix = gate_matrix.reshape(width, block_units)
    up_matrix = up_matrix.reshape(width, block_units)
    (normed_arrived,) = clock.wait(normed_moving)
    while len(passed) < shards:
        (arrived,) = clock.wait(clock.pass_on(shard, *passed[-1]))
        passed.append(arrived)
    group_normed = jnp.concatenate([normed_two] + normed_arrived, axis=0)
    cotangents = jnp.concatenate(
        [output_cotangent]
        + [
            jnp.where(shard.place >= step, passed[step][0], passed[shards - step][1])
            for step in steps
        ],
        axis=0,
    )

    inner_act, d_gate, d_up, turned_normed, turned_inner = clock.run(
        feed_forward, group_normed, cotangents, gate_matrix, up_matrix, down_weight
    )

    def split_halves(left, right, groups, turned):
        count = first.size * second.size
        halves = clock.run(
            lambda left, right: split_gradient(left, right, groups, count, core.place, turned),
            left,
            right,
        )
        return [half.reshape((first.size, second.size) + half.shape[1:]) for half in halves]

    def side_by_side(rows):
        return clock(jnp.concatenate(in_place_order(rows, shard), axis=1))[0]

    def sum_over_rep(blocks):
        return lax.psum_scatter(blocks, "rep", scatter_dimension=0, tiled=True)

    def row_sum(own, arrived):
        return clock(total_of(own + arrived).astype(bf16))[0]

    def send_some(rows, chosen):
        return clock.send(shard, [rows[k] for k in chosen], [shards - 1 - k for k in chosen])

    edges = sorted({0, shards - 2})
    inside = list(range(1, shards - 2))

    (gate_blocks,) = clock.run(
        lambda left, right: ordered_gradient(left, right, shards, rep_places(reps)),
        turned_normed,
        d_gate,
    )
    gate_piece = sum_over_rep(gate_blocks.reshape(width, block_units))
    normed_own, *normed_partial = clock.run(
        lambda *operands: rows_product(operands[:2], operands[2:], True, shards),
        d_gate,
        d_up,
        gate_matrix,
        up_matrix,
    )
    up_halves = split_halves(turned_normed, d_up, shards, True)

    up = Halving(clock, *up_halves, core, first, second)
    normed_moving = send_some(normed_partial, edges)
    block_own, *block_partial = clock.run(
        lambda left, right: rows_product((left,), (right,), False, shards), inner_act, down_weight
    )
    up_arrived, normed_arrived = clock.wait(up.moving, normed_moving)

    up.along_first(up_arrived)
    normed_moving = send_some(normed_partial, inside)
    (down_blocks,) = clock.run(
        lambda left, right: ordered_gradient(left, right, 1, list(range(reps))),
        turned_inner,
        cotangents,
    )
    up_arrived, more_arrived = clock.wait(up.moving, normed_moving)

    (gate_piece,) = clock(gate_piece)
    down_piece = sum_over_rep(clock(down_blocks)[0].reshape(block_units, width))
    up.along_second(up_arrived)
    block_moving = send_some(block_partial, inside)
    normed_two_gradient = total_of([normed_own] + normed_arrived + more_arrived)
    gain_two_gradient = jnp.sum(normed_two_gradient * unit_two, axis=0)
    hidden_gradient = output_cotangent.astype(f32) + norm_back(
        normed_two_gradient, unit_two, inverse_two, gain_two
    )
    (branch_gradient,) = clock(hidden_gradient.astype(bf16))
    (attention_gradient,) = clock(times_transposed(branch_gradient, output_matrix).astype(bf16))
    d_queries, pair_own, *pair_partial = clock.run(
        lambda *operands: attention_backward(*operands, shards),
        queries,
        attention_gradient,
        pairs,
        cosine_table,
        signed_sine,
        row_marks,
        key_marks.T,
    )
    output_halves = split_halves(attention_low, branch_gradient, shards, False)
    up_arrived, block_arrived = clock.wait(up.moving, block_moving)

    pair_moving = send_back(pair_partial)
    output = Halving(clock, *output_halves, core, first, second)
    up_blocks = clock(*blocks_of(up.finish(up_arrived)))
    pair_arrived, output_arrived = clock.wait(pair_moving, output.moving)

    output.along_first(output_arrived)
    up_moving = send_blocks(up_blocks)
    projected_gradient, bias_sum = clock.run(
        lambda *operands: join_projected(operands[0], operands[3:], *operands[1:3]),
        d_queries,
        cosine_table,
        signed_sine,
        pair_own,
        *pair_arrived,
    )
    projected_halves = split_halves(normed_one, projected_gradient, shards, False)
    output_arrived, up_rows = clock.wait(output.moving, up_moving)

    projected = Halving(clock, *projected_halves, core, first, second)
    output.along_second(output_arrived)
    up_spread = spread(side_by_side(up_blocks[:1] + up_rows))
    block_moving = send_some(block_partial, edges[:1])
    projected_gradient, hidden_gradient = clock(projected_gradient, hidden_gradient)
    normed_one_gradient = times_transposed(projected_gradient, input_matrix)
    gain_one_gradient = jnp.sum(normed_one_gradient * unit_one, axis=0)
    (tokens_gradient,) = clock(
        (
            hidden_gradient + norm_back(normed_one_gradient, unit_one, inverse_one, gain_one)
        ).astype(bf16)
    )
    projected_arrived, output_arrived, up_arrived, more_arrived = clock.wait(
        projected.moving, output.moving, up_spread.moving, block_moving
    )
    block_arrived = block_arrived + more_arrived

    (down_piece,) = clock(down_piece)
    down_gathered = lax.all_gather(down_piece, "rep", axis=0, tiled=True)
    projected.along_first(projected_arrived)
    up_spread.along(up_arrived)
    gate_blocks = clock(*blocks_of(gate_piece.reshape(shards, part_rows, block_units)))
    gate_moving = send_blocks(gate_blocks)
    (output_blocks,) = clock(output.finish(output_arrived))
    bias_gradient = bias_sum[0]
    bias_split = query_width + pair_width
    small_parts = (
        gain_one_gradient,
        gain_two_gradient,
        bias_gradient[:bias_split],
        bias_gradient[bias_split:],
    )
    (small,) = clock(
        jnp.concatenate([part.reshape(shards, -1) for part in small_parts], axis=1)
    )
    projected_arrived, up_arrived, gate_rows = clock.wait(
        projected.moving, up_spread.moving, gate_moving
    )

    projected.along_second(projected_arrived)
    gate_spread = spread(side_by_side(gate_blocks[:1] + gate_rows))
    up_spread.over(up_arrived)
    output_rows = lax.all_to_all(output_blocks, "shard", 0, 0, tiled=True)
    projected_arrived, gate_arrived, up_arrived = clock.wait(
        projected.moving, gate_spread.moving, up_spread.moving
    )

    input_blocks = clock(*blocks_of(projected.finish(projected_arrived)))
    input_moving = send_blocks(input_blocks)
    gate_spread.along(gate_arrived)
    (up_total,) = clock.run(widen_pieces, *up_spread.finish(up_arrived))
    input_rows, gate_arrived = clock.wait(input_moving, gate_spread.moving)

    (output_rows,) = clock(output_rows)
    input_spread = spread(row_sum(input_blocks[:1], input_rows))
    output_spread = spread(row_sum(list(output_rows), []))
    gate_spread.over(gate_arrived)
    small_moving = clock.send(core, [small], [1])
    (down_gathered,) = clock(down_gathered)
    (down_total,) = clock(down_gathered.astype(f32))
    input_arrived, output_arrived, gate_arrived, small_arrived = clock.wait(
        input_spread.moving, output_spread.moving, gate_spread.moving, small_moving
    )
    small = total_of([small] + small_arrived)

    input_spread.along(input_arrived)
    output_spread.along(output_arrived)
    small_moving = clock.send(first, [small] * (first.size - 1), range(1, first.size))
    block_moving = send_some(block_partial, edges[1:])
    (gate_total,) = clock.run(widen_pieces, *gate_spread.finish(gate_arrived))
    input_arrived, output_arrived, small_arrived, more_arrived = clock.wait(
        input_spread.moving, output_spread.moving, small_moving, block_moving
    )
    small = total_of([small] + small_arrived)
    block_arrived = block_arrived + more_arrived

    input_spread.over(input_arrived)
    output_spread.over(output_arrived)
    small_moving = clock.send(second, [small] * (second.size - 1), range(1, second.size))
    (block_out,) = clock(total_of([hidden, block_own] + block_arrived).astype(bf16))
    input_arrived, output_arrived, small_arrived = clock.wait(
        input_spread.moving, output_spread.moving, small_moving
    )
    small_blocks = clock(*blocks_of(total_of([small] + small_arrived)))

    small_moving = send_blocks(small_blocks)
    (output_total,) = clock.run(widen_pieces, *output_spread.finish(output_arrived))
    (input_total,) = clock.run(widen_pieces, *input_spread.finish(input_arrived))
    (small_arrived,) = clock.wait(small_moving)
    small = total_of(small_blocks[:1] + small_arrived)

    small = small + clock.token[0, 0]
    small_totals, at = [], 0
    for part in small_parts:
        size = part.shape[0] // shards
        small_totals.append(small[at : at + size])
        at += size
    return (
        block_out,
        tokens_gradient,
        small_totals[0],
        input_total,
        small_totals[2],
        small_totals[3],
        output_total,
        small_totals[1],
        gate_total,
        up_total,
        down_total,
    )


def solution(mesh):
    placed = (
        P(("rep", "shard"), None),
        P("rep", None),
        P("shard"),
        P("shard", None),
        P("shard"),
        P("shard", None),
        P("shard"),
        P("shard", None),
        P("shard", None),
        P("shard", None),
        P(("rep", "shard"), None),
    )
    return jax.shard_map(
        on_device,
        mesh=mesh,
        in_specs=placed,
        out_specs=(
            P(("rep", "shard"), None),
            P(("rep", "shard"), None),
            P("shard"),
            P("shard", None),
            P("shard"),
            P("shard"),
            P("shard", None),
            P("shard"),
            P("shard", None),
            P("shard", None),
            P("shard", None),
        ),
        check_vma=False,
    )
```

```python
import math

import jax
import jax.numpy as jnp
from jax import lax
from jax.experimental import pallas as pl
from jax.experimental.pallas import tpu as pltpu
from jax.sharding import PartitionSpec as P

QH = 12
KVH = 2
HD = 128
SEQS = 3


EPSILON = 1e-06
LOG_THETA = math.log(1000000.0)
MASKED = -1e30
VMEM_LIMIT = 56 * 1024 * 1024
TILE = 512
COST = pl.CostEstimate(flops=1, bytes_accessed=1, transcendentals=0)


def rope_tables(places, head_width):
    half_width = head_width // 2
    frequency = jnp.exp(jnp.arange(half_width, dtype=jnp.float32) * (-2.0 * LOG_THETA / head_width))
    angles = places.astype(jnp.float32)[:, None] * frequency[None, :]
    angles = jnp.concatenate([angles, angles], axis=-1)
    return (jnp.cos(angles), jnp.sin(angles))


def positions(segments):
    labels = jnp.arange(SEQS, dtype=jnp.int32)
    starts = jnp.sum((segments[None, :] < labels[:, None]).astype(jnp.int32), axis=1)
    own_start = jnp.sum(jnp.where(segments[:, None] == labels[None, :], starts[None, :], 0), axis=1)
    return jnp.arange(segments.shape[0], dtype=jnp.int32) - own_start


def rotate(field_rows, cosine_table, sine_table):
    half_width = field_rows.shape[-1] // 2
    turned = jnp.concatenate([-field_rows[..., half_width:], field_rows[..., :half_width]], axis=-1)
    return field_rows * cosine_table[:, None, :] + turned * sine_table[:, None, :]


def transposed_times(left_side, right_side):
    return lax.dot_general(
        left_side, right_side, (((0,), (0,)), ((), ())), preferred_element_type=jnp.float32
    )


def times_transposed(left_side, right_side):
    return lax.dot_general(
        left_side, right_side, (((1,), (1,)), ((), ())), preferred_element_type=jnp.float32
    )


def norm_back(normed_gradient, unit_rows, inverse_rms, gain_row):
    scaled = normed_gradient * gain_row
    return inverse_rms * (scaled - unit_rows * jnp.mean(scaled * unit_rows, axis=-1, keepdims=True))


class Line:
    def __init__(self, name, size, place, pairs, crossed=False):
        self.name, self.size, self.place, self.pairs = name, size, place, pairs
        self.crossed = crossed

    def shift(self, value, step):
        return lax.ppermute(value, self.name, self.pairs(step % self.size))

    def pass_on(self, value, up):
        places = range(self.size - 1)
        pairs = [(at, at + 1) if up else (at + 1, at) for at in places]
        return lax.ppermute(value, self.name, pairs)

    def behind(self, step):
        return lax.rem(self.place + (self.size - step % self.size), self.size)

    def ahead(self, step):
        return lax.rem(self.place + step % self.size, self.size) if step else self.place


def make_lines(reps, shards):
    inner = 2 if reps % 4 == 0 else 1
    outer = reps // (2 * inner)
    square = inner == outer

    def split(index):
        core, b, a = index % 2, (index // 2) % inner, index // (2 * inner)
        return core, b, a

    def join(core, b, a):
        return (a * inner + b) * 2 + core

    def first_pairs(step):
        pairs = []
        for index in range(reps):
            core, b, a = split(index)
            if square and core == 0:
                pairs.append((index, join(core, (b + step) % inner, a)))
            else:
                pairs.append((index, join(core, b, (a + step) % outer)))
        return pairs

    def second_pairs(step):
        pairs = []
        for index in range(reps):
            core, b, a = split(index)
            if square and core == 0:
                pairs.append((index, join(core, b, (a + step) % outer)))
            else:
                pairs.append((index, join(core, (b + step) % inner, a)))
        return pairs

    def core_pairs(step):
        pairs = []
        for index in range(reps):
            core, b, a = split(index)
            pairs.append((index, join((core + step) % 2, b, a)))
        return pairs

    def shard_pairs(step):
        return [(index, (index + step) % shards) for index in range(shards)]

    core, b, a = split(lax.axis_index("rep"))
    first, second = (jnp.where(core == 0, b, a), jnp.where(core == 0, a, b)) if square else (a, b)
    return (
        Line("shard", shards, lax.axis_index("shard"), shard_pairs),
        Line("rep", 2, core, core_pairs, square),
        Line("rep", outer, first, first_pairs),
        Line("rep", inner, second, second_pairs),
    )


def rep_places(reps):
    inner = 2 if reps % 4 == 0 else 1
    outer = reps // (2 * inner)
    places = []
    for index in range(reps):
        core, b, a = index % 2, (index // 2) % inner, index // (2 * inner)
        one, two = (b, a) if inner == outer and core == 0 else (a, b)
        places.append((core * outer + one) * inner + two)
    return places


def pick(array, index, axis):
    return lax.dynamic_index_in_dim(array, index, axis, keepdims=False)


def put(array, piece, index, axis):
    return lax.dynamic_update_index_in_dim(array, piece, index, axis)


def in_place_order(pieces, line):
    ordered = []
    for place in range(line.size):
        chosen = pieces[0]
        for step in range(1, line.size):
            chosen = jnp.where(line.behind(step) == place, pieces[step], chosen)
        ordered.append(chosen)
    return ordered


def tie(*arrays):
    return lax.optimization_barrier(arrays)


def gather_line(value, line):
    return [value] + [line.shift(value, step) for step in range(1, line.size)]


class Clock:
    def __init__(self):
        self.token = jnp.zeros((8, 128), jnp.float32)
        self.open = 0

    def __call__(self, *arrays):
        self.token, *arrays = tie(self.token, *arrays)
        return arrays

    def run(self, step, *arrays):
        return self(*step(*self(*arrays)))

    def send(self, line, values, steps):
        self.open += len(values)
        return [line.shift(value, step) for value, step in zip(self(*values), steps)]

    def pass_on(self, line, lower, upper):
        self.open += 2
        lower, upper = self(lower, upper)
        return [line.pass_on(lower, True), line.pass_on(upper, False)]

    def wait(self, *groups):
        flat = self(*[array for group in groups for array in group])
        self.open -= len(flat)
        parts, at = [], 0
        for group in groups:
            parts.append(flat[at : at + len(group)])
            at += len(group)
        return parts


def total_of(terms):
    total = terms[0].astype(jnp.float32)
    for term in terms[1:]:
        total = total + term.astype(jnp.float32)
    return total


class Halving:
    def __init__(self, clock, sent, own, core, first, second):
        self.clock, self.first, self.second = clock, first, second
        self.terms = [own]
        self.moving = clock.send(core, [sent], [1])

    def along(self, line, arrived):
        self.terms = self.terms + arrived
        steps = range(1, line.size)
        blocks = [
            total_of([pick(term, line.ahead(step), 0) for term in self.terms]).astype(jnp.bfloat16)
            for step in steps
        ]
        self.moving = self.clock.send(line, blocks, steps)
        self.terms = [pick(term, line.place, 0) for term in self.terms]

    def along_first(self, arrived):
        self.along(self.first, arrived)

    def along_second(self, arrived):
        self.along(self.second, arrived)

    def finish(self, arrived):
        return self.clock(total_of(self.terms + arrived).astype(jnp.bfloat16))[0]


class Spread:
    def __init__(self, clock, piece, core, first, second):
        self.clock, self.lines = clock, (core, first, second)
        self.pieces = [piece]
        steps = range(1, second.size)
        self.moving = clock.send(second, [piece] * len(steps), steps)

    def along(self, arrived):
        core, first, second = self.lines
        self.pieces = self.pieces + arrived
        steps = range(1, first.size)
        self.moving = self.clock.send(first, [jnp.stack(self.pieces)] * len(steps), steps)

    def over(self, arrived):
        core, first, second = self.lines
        rows = [jnp.stack(self.pieces)] + arrived
        self.pieces = jnp.concatenate(rows, axis=0)
        self.moving = self.clock.send(core, [self.pieces], [1])

    def finish(self, arrived):
        core, first, second = self.lines
        (others,) = arrived
        offsets = [(one, two) for one in range(first.size) for two in range(second.size)]
        placed = [(core.place, first.behind(one), second.behind(two)) for one, two in offsets]
        far, near = (second, first) if core.crossed else (first, second)
        placed += [(core.behind(1), far.behind(one), near.behind(two)) for one, two in offsets]
        places = [(c * first.size + f) * second.size + s for c, f, s in placed]
        return [jnp.stack(places).astype(jnp.int32), self.pieces, others]


def column_blocks(place, shard_place, *weights):
    count = len(weights)
    rows, columns = weights[0].shape[1:]
    shards = lax.axis_size("shard")
    block = columns // shards

    def body(places_ref, *refs):
        sources, outs = refs[:count], refs[count : 2 * count]
        held, cut, in_sems, out_sems = refs[2 * count :]
        loads = [
            pltpu.make_async_copy(sources[at].at[places_ref[0]], held.at[at], in_sems.at[at])
            for at in range(count)
        ]

        def store(at, z):
            ahead = lax.rem(z + shards - places_ref[1], shards)
            return pltpu.make_async_copy(cut.at[at, z], outs[at].at[ahead], out_sems.at[at, z])

        for load in loads:
            load.start()
        for at in range(count):
            loads[at].wait()
            for z in range(shards):
                cut[at, z] = held[at, :, z * block : (z + 1) * block]
                store(at, z).start()
        for at in range(count):
            for z in range(shards):
                store(at, z).wait()

    return pl.pallas_call(
        body,
        out_shape=[jax.ShapeDtypeStruct((shards, rows, block), jnp.bfloat16)] * count,
        in_specs=[pl.BlockSpec(memory_space=pltpu.SMEM)]
        + [pl.BlockSpec(memory_space=pl.ANY)] * count,
        out_specs=[pl.BlockSpec(memory_space=pl.ANY)] * count,
        scratch_shapes=[
            pltpu.VMEM((count, rows, columns), jnp.bfloat16),
            pltpu.VMEM((count, shards, rows, block), jnp.bfloat16),
            pltpu.SemaphoreType.DMA((count,)),
            pltpu.SemaphoreType.DMA((count, shards)),
        ],
        compiler_params=pltpu.CompilerParams(vmem_limit_bytes=VMEM_LIMIT),
        cost_estimate=COST,
        name="column_blocks",
    )(jnp.stack([place, shard_place]).astype(jnp.int32), *weights)


def place_blocks(order, places, pieces, others):
    half, groups, shards = pieces.shape[:3]

    def body(order_ref, places_ref, pieces_ref, others_ref, *rest):
        def source_of(g, k, r):
            return (pieces_ref if r < half else others_ref).at[r % half, g, k]

        move_blocks(source_of, lambda r: places_ref[r], order_ref, rest[:groups], *rest[groups:])

    return blocks_call(body, 2, 2, groups, shards, 2 * half, pieces.shape[3:])(
        order, places, pieces, others
    )


def place_gathered(order, gathered, groups):
    shards = lax.axis_size("shard")
    reps = gathered.shape[0] // (shards * groups)

    def body(order_ref, source, *rest):
        move_blocks(
            lambda g, k, r: source.at[(r * shards + k) * groups + g],
            lambda r: r,
            order_ref,
            rest[:groups],
            *rest[groups:],
        )

    return blocks_call(body, 1, 1, groups, shards, reps, gathered.shape[1:])(order, gathered)


def move_blocks(source_of, place_of, order_ref, outs, held, in_sems, out_sems):
    groups, shards, reps = in_sems.shape
    slabs = [(g, k) for g in range(groups) for k in range(shards)]

    def load(g, k, r):
        return pltpu.make_async_copy(
            source_of(g, k, r), held.at[g, k, place_of(r)], in_sems.at[g, k, r]
        )

    def store(g, k):
        return pltpu.make_async_copy(held.at[g, k], outs[g].at[order_ref[k]], out_sems.at[g, k])

    for g, k in slabs:
        for r in range(reps):
            load(g, k, r).start()
    for g, k in slabs:
        for r in range(reps):
            load(g, k, r).wait()
        store(g, k).start()
    for g, k in slabs:
        store(g, k).wait()


def blocks_call(body, scalars, sources, groups, shards, reps, block):
    whole = (shards, reps) + block
    return pl.pallas_call(
        body,
        out_shape=[jax.ShapeDtypeStruct(whole, jnp.bfloat16)] * groups,
        in_specs=[pl.BlockSpec(memory_space=pltpu.SMEM)] * scalars
        + [pl.BlockSpec(memory_space=pl.ANY)] * sources,
        out_specs=[pl.BlockSpec(memory_space=pl.ANY)] * groups,
        scratch_shapes=[
            pltpu.VMEM((groups,) + whole, jnp.bfloat16),
            pltpu.SemaphoreType.DMA((groups, shards, reps)),
            pltpu.SemaphoreType.DMA((groups, shards)),
        ],
        compiler_params=pltpu.CompilerParams(vmem_limit_bytes=VMEM_LIMIT),
        cost_estimate=COST,
        name="place_blocks",
    )


def widen_pieces(places, pieces, others):
    half, rows, columns = pieces.shape
    reps = 2 * half
    strip = next(size for size in (16, 8, rows) if rows % size == 0)

    def body(places_ref, pieces_ref, others_ref, out_ref, narrow, wide, in_sems, out_sems):
        loads = [
            pltpu.make_async_copy(
                (pieces_ref if r < half else others_ref).at[r % half], narrow.at[r], in_sems.at[r]
            )
            for r in range(reps)
        ]
        stores = [
            pltpu.make_async_copy(wide.at[r], out_ref.at[places_ref[r]], out_sems.at[r])
            for r in range(reps)
        ]
        for load in loads:
            load.start()
        for r in range(reps):
            loads[r].wait()

            def convert(at, carry):
                cut = pl.ds(pl.multiple_of(at * strip, strip), strip)
                wide[r, cut, :] = narrow[r, cut, :].astype(jnp.float32)
                return carry

            lax.fori_loop(0, rows // strip, convert, 0)
            stores[r].start()
        for store in stores:
            store.wait()

    result = pl.pallas_call(
        body,
        out_shape=jax.ShapeDtypeStruct((reps, rows, columns), jnp.float32),
        in_specs=[pl.BlockSpec(memory_space=pltpu.SMEM)]
        + [pl.BlockSpec(memory_space=pl.ANY)] * 2,
        out_specs=pl.BlockSpec(memory_space=pl.ANY),
        scratch_shapes=[
            pltpu.VMEM((reps, rows, columns), jnp.bfloat16),
            pltpu.VMEM((reps, rows, columns), jnp.float32),
            pltpu.SemaphoreType.DMA((reps,)),
            pltpu.SemaphoreType.DMA((reps,)),
        ],
        compiler_params=pltpu.CompilerParams(vmem_limit_bytes=VMEM_LIMIT),
        cost_estimate=COST,
        name="widen_pieces",
    )(places, pieces, others)
    return (result.reshape(reps * rows, columns),)


def widen_gathered(gathered, order):
    reps, rows, columns = gathered.shape
    strip = next(size for size in (16, 8, rows) if rows % size == 0)

    def body(source_ref, out_ref, narrow, wide, in_sems, out_sems):
        loads = [
            pltpu.make_async_copy(source_ref.at[r], narrow.at[r], in_sems.at[r])
            for r in range(reps)
        ]
        stores = [
            pltpu.make_async_copy(wide.at[r], out_ref.at[order[r]], out_sems.at[r])
            for r in range(reps)
        ]
        for load in loads:
            load.start()
        for r in range(reps):
            loads[r].wait()

            def convert(at, carry):
                cut = pl.ds(pl.multiple_of(at * strip, strip), strip)
                wide[r, cut, :] = narrow[r, cut, :].astype(jnp.float32)
                return carry

            lax.fori_loop(0, rows // strip, convert, 0)
            stores[r].start()
        for store in stores:
            store.wait()

    result = pl.pallas_call(
        body,
        out_shape=jax.ShapeDtypeStruct((reps, rows, columns), jnp.float32),
        in_specs=[pl.BlockSpec(memory_space=pl.ANY)],
        out_specs=pl.BlockSpec(memory_space=pl.ANY),
        scratch_shapes=[
            pltpu.VMEM((reps, rows, columns), jnp.bfloat16),
            pltpu.VMEM((reps, rows, columns), jnp.float32),
            pltpu.SemaphoreType.DMA((reps,)),
            pltpu.SemaphoreType.DMA((reps,)),
        ],
        compiler_params=pltpu.CompilerParams(vmem_limit_bytes=VMEM_LIMIT),
        cost_estimate=COST,
        name="widen_gathered",
    )(gathered)
    return (result.reshape(reps * rows, columns),)


def resident(shape):
    return pl.BlockSpec(shape, lambda i: (0, 0), pipeline_mode=pl.Buffered(1))


def feed_forward(rows, cotangents, gate_matrix, up_matrix, down_matrix):
    count, width = rows.shape
    units = gate_matrix.shape[1]
    steps = pl.cdiv(units, TILE)
    slabs = next(size for size in range(min(steps, width // 128), 0, -1) if width % (128 * size) == 0)
    slab = width // slabs

    def body(
        rows_ref,
        cotangents_ref,
        gate_ref,
        up_ref,
        down_ref,
        inner_ref,
        d_gate_ref,
        d_up_ref,
        turned_rows_ref,
        turned_inner_ref,
    ):
        gate = jnp.dot(rows_ref[...], gate_ref[...], preferred_element_type=jnp.float32)
        up = jnp.dot(rows_ref[...], up_ref[...], preferred_element_type=jnp.float32)
        sigmoid = jax.nn.sigmoid(gate)
        silu = gate * sigmoid
        inner = (silu * up).astype(jnp.bfloat16)
        inner_ref[...] = inner
        turned_inner_ref[...] = inner.T
        d_inner = times_transposed(cotangents_ref[...], down_ref[...])
        d_up_ref[...] = (d_inner * silu).astype(jnp.bfloat16)
        d_gate_ref[...] = (d_inner * up * sigmoid * (1.0 + gate * (1.0 - sigmoid))).astype(
            jnp.bfloat16
        )
        for step in range(slabs):

            @pl.when(pl.program_id(0) == step)
            def turn():
                turned_rows_ref[...] = rows_ref[:, step * slab : (step + 1) * slab].T

    columns = pl.BlockSpec((width, TILE), lambda i: (0, i))
    results = pl.BlockSpec((count, TILE), lambda i: (0, i))
    return pl.pallas_call(
        body,
        grid=(steps,),
        out_shape=[jax.ShapeDtypeStruct((count, units), jnp.bfloat16)] * 3
        + [
            jax.ShapeDtypeStruct((width, count), jnp.bfloat16),
            jax.ShapeDtypeStruct((units, count), jnp.bfloat16),
        ],
        in_specs=[
            resident((count, width)),
            resident((count, width)),
            columns,
            columns,
            pl.BlockSpec((TILE, width), lambda i: (i, 0)),
        ],
        out_specs=[results] * 3
        + [
            pl.BlockSpec((slab, count), lambda i: (jnp.minimum(i, slabs - 1), 0)),
            pl.BlockSpec((TILE, count), lambda i: (i, 0)),
        ],
        compiler_params=pltpu.CompilerParams(vmem_limit_bytes=VMEM_LIMIT),
        cost_estimate=COST,
        name="feed_forward",
    )(rows, cotangents, gate_matrix, up_matrix, down_matrix)


def split_gradient(left, right, groups, places, core_place, turned):
    rows, count = left.shape if turned else left.shape[::-1]
    columns = right.shape[1]
    half = rows // (2 * groups)
    part = half // places

    def body(core_ref, left_ref, right_ref, other_ref, own_ref, *scratch):
        if turned:
            rows_ref = left_ref
        else:
            (rows_ref,) = scratch

            @pl.when(pl.program_id(0) == 0)
            def turn():
                rows_ref[...] = left_ref[...].T

        core = core_ref[0]
        for out_ref, which in ((other_ref, 1 - core), (own_ref, core)):
            halves = [
                rows_ref[pl.ds(pl.multiple_of((2 * group + which) * half, 16), half), :]
                for group in range(groups)
            ]
            product = jnp.dot(
                jnp.concatenate(halves, axis=0), right_ref[...], preferred_element_type=jnp.float32
            )
            for group in range(groups):
                for place in range(places):
                    at = group * half + place * part
                    out_ref[place, group] = product[at : at + part].astype(jnp.bfloat16)

    return pl.pallas_call(
        body,
        grid=(pl.cdiv(columns, TILE),),
        out_shape=[jax.ShapeDtypeStruct((places, groups, part, columns), jnp.bfloat16)] * 2,
        in_specs=[
            pl.BlockSpec(memory_space=pltpu.SMEM),
            resident(left.shape),
            pl.BlockSpec((count, TILE), lambda i: (0, i)),
        ],
        out_specs=[pl.BlockSpec((places, groups, part, TILE), lambda i: (0, 0, 0, i))] * 2,
        scratch_shapes=[] if turned else [pltpu.VMEM((rows, count), jnp.bfloat16)],
        compiler_params=pltpu.CompilerParams(vmem_limit_bytes=VMEM_LIMIT),
        cost_estimate=COST,
        name="split_gradient",
    )(core_place.reshape(1).astype(jnp.int32), left, right)


def ordered_gradient(left, right, shards, order):
    reps = len(order)
    rows, count = left.shape
    columns = right.shape[1]
    part = rows // (shards * reps)

    def body(left_ref, right_ref, out_ref):
        product = jnp.dot(left_ref[...], right_ref[...], preferred_element_type=jnp.float32)
        for z in range(shards):
            for r in range(reps):
                at = (z * reps + order[r]) * part
                out_ref[r, z] = product[at : at + part].astype(jnp.bfloat16)

    return pl.pallas_call(
        body,
        grid=(pl.cdiv(columns, TILE),),
        out_shape=[jax.ShapeDtypeStruct((reps, shards, part, columns), jnp.bfloat16)],
        in_specs=[
            resident((rows, count)),
            pl.BlockSpec((count, TILE), lambda i: (0, i)),
        ],
        out_specs=[pl.BlockSpec((reps, shards, part, TILE), lambda i: (0, 0, 0, i))],
        compiler_params=pltpu.CompilerParams(vmem_limit_bytes=VMEM_LIMIT),
        cost_estimate=COST,
        name="ordered_gradient",
    )(left, right)


def rows_product(lefts, rights, turned, blocks):
    count, depth = lefts[0].shape
    columns = rights[0].shape[0 if turned else 1]
    pairs, part = len(lefts), count // blocks

    def body(*refs):
        total = None
        for left_ref, right_ref in zip(refs[:pairs], refs[pairs : 2 * pairs]):
            if turned:
                product = times_transposed(left_ref[...], right_ref[...])
            else:
                product = jnp.dot(
                    left_ref[...], right_ref[...], preferred_element_type=jnp.float32
                )
            total = product if total is None else total + product
        for block in range(blocks):
            refs[2 * pairs + block][...] = total[block * part : (block + 1) * part].astype(
                jnp.bfloat16
            )

    right_spec = (
        pl.BlockSpec((TILE, depth), lambda i: (i, 0))
        if turned
        else pl.BlockSpec((depth, TILE), lambda i: (0, i))
    )
    return pl.pallas_call(
        body,
        grid=(pl.cdiv(columns, TILE),),
        out_shape=[jax.ShapeDtypeStruct((part, columns), jnp.bfloat16)] * blocks,
        in_specs=[resident((count, depth))] * pairs + [right_spec] * pairs,
        out_specs=[pl.BlockSpec((part, TILE), lambda i: (0, i))] * blocks,
        compiler_params=pltpu.CompilerParams(vmem_limit_bytes=VMEM_LIMIT),
        cost_estimate=COST,
        name="rows_product",
    )(*lefts, *rights)


def kept_bias(row_segments, row_index, key_segments, key_index):
    kept = (row_segments == key_segments) & (key_index <= row_index)
    return jnp.where(kept, 0.0, MASKED)


def in_vmem(count):
    return [pl.BlockSpec(memory_space=pltpu.VMEM)] * count


def attention_forward(projected, cosine, signed_sine, pairs, rows, keys):
    count = projected.shape[0]
    per_group = QH // KVH
    scale = 1.0 / math.sqrt(HD)
    shape = (KVH, per_group * count, HD)

    def body(projected_ref, cosine_ref, sine_ref, pairs_ref, rows_ref, keys_ref, queries_ref, out_ref):
        bias = kept_bias(rows_ref[:, 0:1], rows_ref[:, 1:2], keys_ref[0:1, :], keys_ref[1:2, :])
        for k in range(KVH):
            for h in range(per_group):
                at = (k * per_group + h) * HD
                field = projected_ref[:, at : at + HD]
                queries_ref[k, h * count : (h + 1) * count, :] = (
                    field * cosine_ref[...] + pltpu.roll(field, HD // 2, 1) * sine_ref[...]
                ).astype(jnp.bfloat16)
            keys_here = pairs_ref[:, k * HD : (k + 1) * HD]
            values_here = pairs_ref[:, (KVH + k) * HD : (KVH + k + 1) * HD]
            scores = times_transposed(queries_ref[k], keys_here) * scale + bias
            powers = jnp.exp(scores - jnp.max(scores, axis=1, keepdims=True))
            shares = powers * (1.0 / jnp.sum(powers, axis=1, keepdims=True))
            result = jnp.dot(
                shares.astype(jnp.bfloat16), values_here, preferred_element_type=jnp.float32
            ).astype(jnp.bfloat16)
            for h in range(per_group):
                at = (k * per_group + h) * HD
                out_ref[:, at : at + HD] = result[h * count : (h + 1) * count]

    return pl.pallas_call(
        body,
        out_shape=[
            jax.ShapeDtypeStruct(shape, jnp.bfloat16),
            jax.ShapeDtypeStruct((count, QH * HD), jnp.bfloat16),
        ],
        in_specs=in_vmem(6),
        out_specs=in_vmem(2),
        compiler_params=pltpu.CompilerParams(vmem_limit_bytes=VMEM_LIMIT),
        cost_estimate=COST,
        name="attention_forward",
    )(projected, cosine, signed_sine, pairs, rows, keys)


def attention_backward(queries, gradient, pairs, cosine, signed_sine, rows, keys, blocks):
    count = gradient.shape[0]
    per_group = QH // KVH
    scale = 1.0 / math.sqrt(HD)
    group_rows = pairs.shape[0]
    part = group_rows // blocks

    def body(queries_ref, gradient_ref, pairs_ref, cosine_ref, sine_ref, rows_ref, keys_ref, d_ref, *outs):
        block_refs, stacked = outs[:blocks], outs[blocks]
        bias = kept_bias(rows_ref[0:1, :], rows_ref[1:2, :], keys_ref[:, 0:1], keys_ref[:, 1:2])
        for k in range(KVH):
            for h in range(per_group):
                at = (k * per_group + h) * HD
                stacked[h * count : (h + 1) * count, :] = gradient_ref[:, at : at + HD]
            keys_here = pairs_ref[:, k * HD : (k + 1) * HD]
            values_here = pairs_ref[:, (KVH + k) * HD : (KVH + k + 1) * HD]
            scores = times_transposed(keys_here, queries_ref[k]) * scale + bias
            powers = jnp.exp(scores - jnp.max(scores, axis=0, keepdims=True))
            shares = powers * (1.0 / jnp.sum(powers, axis=0, keepdims=True))
            d_shares = times_transposed(values_here, stacked[...])
            dots = jnp.sum(shares * d_shares, axis=0, keepdims=True)
            d_scores = (shares * (d_shares - dots)).astype(jnp.bfloat16)
            d_keys = jnp.dot(d_scores, queries_ref[k], preferred_element_type=jnp.float32) * scale
            d_values = jnp.dot(
                shares.astype(jnp.bfloat16), stacked[...], preferred_element_type=jnp.float32
            )
            for block in range(blocks):
                cut = slice(block * part, (block + 1) * part)
                block_refs[block][:, k * HD : (k + 1) * HD] = d_keys[cut].astype(jnp.bfloat16)
                block_refs[block][:, (KVH + k) * HD : (KVH + k + 1) * HD] = d_values[cut].astype(
                    jnp.bfloat16
                )
            d_queries = transposed_times(d_scores, keys_here) * scale
            for h in range(per_group):
                at = (k * per_group + h) * HD
                field = d_queries[h * count : (h + 1) * count]
                d_ref[:, at : at + HD] = (
                    field * cosine_ref[...] - pltpu.roll(field, HD // 2, 1) * sine_ref[...]
                ).astype(jnp.bfloat16)

    return pl.pallas_call(
        body,
        out_shape=[jax.ShapeDtypeStruct((count, QH * HD), jnp.bfloat16)]
        + [jax.ShapeDtypeStruct((part, 2 * KVH * HD), jnp.bfloat16)] * blocks,
        in_specs=in_vmem(7),
        out_specs=in_vmem(1 + blocks),
        scratch_shapes=[pltpu.VMEM((per_group * count, HD), jnp.bfloat16)],
        compiler_params=pltpu.CompilerParams(vmem_limit_bytes=VMEM_LIMIT),
        cost_estimate=COST,
        name="attention_backward",
    )(queries, gradient, pairs, cosine, signed_sine, rows, keys)


def join_projected(d_queries, pair_terms, cosine, signed_sine):
    count, query_width = d_queries.shape
    pair_width = KVH * HD
    terms = len(pair_terms)

    def body(d_queries_ref, cosine_ref, sine_ref, *refs):
        term_refs, out_ref, sum_ref = refs[:terms], refs[terms], refs[terms + 1]
        out_ref[:, :query_width] = d_queries_ref[...]
        for at in range(0, 2 * pair_width, HD):
            field = total_of([term[:, at : at + HD] for term in term_refs])
            if at < pair_width:
                field = field * cosine_ref[...] - pltpu.roll(field, HD // 2, 1) * sine_ref[...]
            out_ref[:, query_width + at : query_width + at + HD] = field.astype(jnp.bfloat16)
        sum_ref[...] = jnp.sum(out_ref[...].astype(jnp.float32), axis=0, keepdims=True)

    return pl.pallas_call(
        body,
        out_shape=[
            jax.ShapeDtypeStruct((count, query_width + 2 * pair_width), jnp.bfloat16),
            jax.ShapeDtypeStruct((1, query_width + 2 * pair_width), jnp.float32),
        ],
        in_specs=in_vmem(3 + terms),
        out_specs=in_vmem(2),
        cost_estimate=COST,
        name="join_projected",
    )(d_queries, cosine, signed_sine, *pair_terms)


def on_device(
    tokens,
    segment_ids,
    first_gain,
    input_weight,
    input_bias,
    output_weight,
    second_gain,
    gate_weight,
    up_weight,
    down_weight,
    output_cotangent,
):
    bf16, f32 = jnp.bfloat16, jnp.float32
    shards, reps = lax.axis_size("shard"), lax.axis_size("rep")
    shard, core, first, second = make_lines(reps, shards)
    rep_place = (core.place * first.size + first.place) * second.size + second.place
    own_rows, width = tokens.shape
    segments = segment_ids[0]
    per_group = QH // KVH
    query_width = QH * HD
    pair_width = KVH * HD
    first_row = shard.place * own_rows
    part_rows = input_weight.shape[0] // reps
    hidden_units = gate_weight.shape[1]
    block_units = hidden_units // shards
    clock = Clock()
    z_order = jnp.stack([shard.behind(step) for step in range(shards)]).astype(jnp.int32)

    def weight_piece(weight, place):
        return pick(weight.reshape(reps, part_rows, weight.shape[1]), place, 0)

    def spread(piece):
        return Spread(clock, piece, core, first, second)

    def blocks_of(blocks):
        return [pick(blocks, shard.ahead(step), 0) for step in range(shards)]

    steps = range(1, shards)

    def send_blocks(blocks):
        return clock.send(shard, blocks[1:], steps)

    def send_around(value):
        return clock.send(shard, [value] * len(steps), steps)

    def send_back(rows):
        return clock.send(shard, rows, [shards - step for step in steps])

    rep_index = lax.axis_index("rep")
    input_matrix = lax.all_gather(
        weight_piece(input_weight, rep_index), ("shard", "rep"), axis=0, tiled=True
    )
    shard_vectors = jnp.concatenate([first_gain, second_gain, input_bias])
    vector_row = jnp.pad(shard_vectors, (0, output_weight.shape[1] - shard_vectors.shape[0]))
    own_output = jnp.concatenate(
        [weight_piece(output_weight, rep_place), vector_row[None]], axis=0
    )
    output_moving = send_around(own_output)
    gate_blocks, up_blocks = clock.run(
        lambda *weights: column_blocks(rep_index, shard.place, *weights),
        gate_weight.reshape(reps, part_rows, hidden_units),
        up_weight.reshape(reps, part_rows, hidden_units),
    )
    (output_rows,) = clock.wait(output_moving)
    output_rows = [own_output] + output_rows

    output_spread = spread(jnp.stack([rows[:part_rows] for rows in output_rows])[None])
    gate_moving = send_blocks(gate_blocks)
    vector_rows = jnp.stack(in_place_order([rows[part_rows] for rows in output_rows], shard))
    own_gain = first_gain.shape[0]
    gain_one = vector_rows[:, :own_gain].reshape(width).astype(f32)
    gain_two = vector_rows[:, own_gain : 2 * own_gain].reshape(width).astype(f32)
    shift_row = (
        vector_rows[:, 2 * own_gain : shard_vectors.shape[0]].reshape(-1).astype(f32)
    )
    places = positions(segments)
    cosine_table, sine_table = rope_tables(
        lax.dynamic_slice_in_dim(places, first_row, own_rows), HD
    )
    signed_sine = jnp.concatenate(
        [-sine_table[:, : HD // 2], sine_table[:, HD // 2 :]], axis=1
    )
    own_segments = lax.dynamic_slice_in_dim(segments, first_row, own_rows)
    row_index = jnp.arange(own_rows, dtype=jnp.int32)
    key_index = jnp.concatenate([shard.behind(step) * own_rows + row_index for step in range(shards)])
    key_segments = jnp.concatenate(
        [
            lax.dynamic_slice_in_dim(segments, shard.behind(step) * own_rows, own_rows)
            for step in range(shards)
        ]
    )
    key_marks = jnp.stack([key_segments, key_index])
    row_marks = jnp.tile(jnp.stack([own_segments, first_row + row_index]), (1, per_group))
    wide_tokens = tokens.astype(f32)
    inverse_one = lax.rsqrt(jnp.mean(wide_tokens * wide_tokens, axis=-1, keepdims=True) + EPSILON)
    unit_one = wide_tokens * inverse_one
    normed_one = (unit_one * gain_one).astype(bf16)
    (
        normed_one,
        cosine_table,
        sine_table,
        signed_sine,
        key_marks,
        row_marks,
    ) = clock(normed_one, cosine_table, sine_table, signed_sine, key_marks, row_marks)
    output_arrived, gate_rows = clock.wait(output_spread.moving, gate_moving)

    output_spread.along(output_arrived)
    up_moving = send_blocks(up_blocks)
    output_arrived, up_rows = clock.wait(output_spread.moving, up_moving)

    gate_up = jnp.stack(
        [row for pair in zip([gate_blocks[0]] + gate_rows, [up_blocks[0]] + up_rows) for row in pair]
    )
    gate_up = lax.all_gather(clock(gate_up)[0], "rep", axis=0, tiled=True)
    passed = [[output_cotangent] * 2]
    passing = clock.pass_on(shard, *passed[-1])
    output_spread.over(output_arrived)
    input_matrix, normed_one = clock(input_matrix, normed_one)
    projected = jnp.dot(normed_one, input_matrix, preferred_element_type=f32) + shift_row
    key_part = rotate(
        projected[:, query_width : query_width + pair_width].reshape(own_rows, KVH, HD),
        cosine_table,
        sine_table,
    )
    (own_pairs,) = clock(
        jnp.concatenate(
            [key_part.reshape(own_rows, pair_width), projected[:, query_width + pair_width :]],
            axis=1,
        ).astype(bf16)
    )
    arrived, output_arrived = clock.wait(passing, output_spread.moving)
    passed.append(arrived)

    pair_moving = send_around(own_pairs)
    passing = clock.pass_on(shard, *passed[-1]) if shards > 2 else []
    pair_rows, arrived = clock.wait(pair_moving, passing)
    passed.append(arrived)
    pairs = jnp.concatenate([own_pairs] + pair_rows, axis=0)

    passing = clock.pass_on(shard, *passed[-1]) if shards > 3 else []
    (output_matrix,) = clock.run(place_blocks, z_order, *output_spread.finish(output_arrived))
    output_matrix = output_matrix.reshape(width, width)
    queries, attention_low = clock.run(
        attention_forward, projected, cosine_table, signed_sine, pairs, row_marks.T, key_marks
    )
    hidden = wide_tokens + jnp.dot(attention_low, output_matrix, preferred_element_type=f32)
    inverse_two = lax.rsqrt(jnp.mean(hidden * hidden, axis=-1, keepdims=True) + EPSILON)
    unit_two = hidden * inverse_two
    (normed_two,) = clock((unit_two * gain_two).astype(bf16))
    (arrived,) = clock.wait(passing)
    passed.append(arrived)

    normed_moving = send_around(normed_two)
    gate_matrix, up_matrix = clock.run(
        lambda order, gathered: place_gathered(order, gathered, 2), z_order, gate_up
    )
    gate_matrix = gate_matrix.reshape(width, block_units)
    up_matrix = up_matrix.reshape(width, block_units)
    (normed_arrived,) = clock.wait(normed_moving)
    while len(passed) < shards:
        (arrived,) = clock.wait(clock.pass_on(shard, *passed[-1]))
        passed.append(arrived)
    group_normed = jnp.concatenate([normed_two] + normed_arrived, axis=0)
    cotangents = jnp.concatenate(
        [output_cotangent]
        + [
            jnp.where(shard.place >= step, passed[step][0], passed[shards - step][1])
            for step in steps
        ],
        axis=0,
    )

    inner_act, d_gate, d_up, turned_normed, turned_inner = clock.run(
        feed_forward, group_normed, cotangents, gate_matrix, up_matrix, down_weight
    )

    def split_halves(left, right, groups, turned):
        count = first.size * second.size
        halves = clock.run(
            lambda left, right: split_gradient(left, right, groups, count, core.place, turned),
            left,
            right,
        )
        return [half.reshape((first.size, second.size) + half.shape[1:]) for half in halves]

    def side_by_side(rows):
        return clock(jnp.concatenate(in_place_order(rows, shard), axis=1))[0]

    def sum_over_rep(blocks):
        return lax.psum_scatter(blocks, "rep", scatter_dimension=0, tiled=True)

    def row_sum(own, arrived):
        return clock(total_of(own + arrived).astype(bf16))[0]

    def send_some(rows, chosen):
        return clock.send(shard, [rows[k] for k in chosen], [shards - 1 - k for k in chosen])

    edges = sorted({0, shards - 2})
    inside = list(range(1, shards - 2))

    def gather_rep(piece):
        return lax.all_gather(piece[None], "rep", axis=0, tiled=True)

    up_halves = split_halves(turned_normed, d_up, shards, True)

    up = Halving(clock, *up_halves, core, first, second)
    (gate_blocks,) = clock.run(
        lambda left, right: ordered_gradient(left, right, shards, rep_places(reps)),
        turned_normed,
        d_gate,
    )
    (up_arrived,) = clock.wait(up.moving)

    gate_piece = sum_over_rep(clock(gate_blocks)[0].reshape(width, block_units))
    up.along_first(up_arrived)
    normed_own, *normed_partial = clock.run(
        lambda *operands: rows_product(operands[:2], operands[2:], True, shards),
        d_gate,
        d_up,
        gate_matrix,
        up_matrix,
    )
    normed_moving = send_some(normed_partial, edges)
    down_halves = split_halves(turned_inner, cotangents, 1, True)
    up_arrived, normed_arrived = clock.wait(up.moving, normed_moving)

    up.along_second(up_arrived)
    down = Halving(clock, *down_halves, core, first, second)
    normed_moving = send_some(normed_partial, inside)
    block_own, *block_partial = clock.run(
        lambda left, right: rows_product((left,), (right,), False, shards), inner_act, down_weight
    )
    up_arrived, down_arrived, more_arrived = clock.wait(up.moving, down.moving, normed_moving)

    down.along_first(down_arrived)
    up_blocks = clock(*blocks_of(up.finish(up_arrived)))
    up_moving = send_blocks(up_blocks)
    normed_two_gradient = total_of([normed_own] + normed_arrived + more_arrived)
    gain_two_gradient = jnp.sum(normed_two_gradient * unit_two, axis=0)
    hidden_gradient = output_cotangent.astype(f32) + norm_back(
        normed_two_gradient, unit_two, inverse_two, gain_two
    )
    (branch_gradient,) = clock(hidden_gradient.astype(bf16))
    (attention_gradient,) = clock(times_transposed(branch_gradient, output_matrix).astype(bf16))
    d_queries, pair_own, *pair_partial = clock.run(
        lambda *operands: attention_backward(*operands, shards),
        queries,
        attention_gradient,
        pairs,
        cosine_table,
        signed_sine,
        row_marks,
        key_marks.T,
    )
    output_halves = split_halves(attention_low, branch_gradient, shards, False)
    down_arrived, up_rows = clock.wait(down.moving, up_moving)

    pair_moving = send_back(pair_partial)
    output = Halving(clock, *output_halves, core, first, second)
    down.along_second(down_arrived)
    up_piece = side_by_side(up_blocks[:1] + up_rows)
    pair_arrived, output_arrived, down_arrived = clock.wait(
        pair_moving, output.moving, down.moving
    )

    (gate_piece,) = clock(gate_piece)
    down_gathered = gather_rep(down.finish(down_arrived)[0])
    output.along_first(output_arrived)
    gate_blocks = clock(*blocks_of(gate_piece.reshape(shards, part_rows, block_units)))
    gate_moving = send_blocks(gate_blocks)
    projected_gradient, bias_sum = clock.run(
        lambda *operands: join_projected(operands[0], operands[3:], *operands[1:3]),
        d_queries,
        cosine_table,
        signed_sine,
        pair_own,
        *pair_arrived,
    )
    projected_halves = split_halves(normed_one, projected_gradient, shards, False)
    output_arrived, gate_rows = clock.wait(output.moving, gate_moving)

    projected = Halving(clock, *projected_halves, core, first, second)
    output.along_second(output_arrived)
    gate_spread = spread(side_by_side(gate_blocks[:1] + gate_rows))
    block_moving = send_some(block_partial, edges[:1])
    projected_gradient, hidden_gradient = clock(projected_gradient, hidden_gradient)
    normed_one_gradient = times_transposed(projected_gradient, input_matrix)
    gain_one_gradient = jnp.sum(normed_one_gradient * unit_one, axis=0)
    (tokens_gradient,) = clock(
        (
            hidden_gradient + norm_back(normed_one_gradient, unit_one, inverse_one, gain_one)
        ).astype(bf16)
    )
    projected_arrived, output_arrived, gate_arrived, block_arrived = clock.wait(
        projected.moving, output.moving, gate_spread.moving, block_moving
    )

    projected.along_first(projected_arrived)
    gate_spread.along(gate_arrived)
    output_blocks = clock(*blocks_of(output.finish(output_arrived)))
    output_moving = send_blocks(output_blocks)
    bias_gradient = bias_sum[0]
    bias_split = query_width + pair_width
    small_parts = (
        gain_one_gradient,
        gain_two_gradient,
        bias_gradient[:bias_split],
        bias_gradient[bias_split:],
    )
    (small,) = clock(
        jnp.concatenate([part.reshape(shards, -1) for part in small_parts], axis=1)
    )
    projected_arrived, gate_arrived, output_rows = clock.wait(
        projected.moving, gate_spread.moving, output_moving
    )

    projected.along_second(projected_arrived)
    gate_spread.over(gate_arrived)
    output_spread = spread(row_sum(output_blocks[:1], output_rows))
    block_moving = send_some(block_partial, inside)
    (down_gathered,) = clock(down_gathered)
    up_gathered = gather_rep(clock(up_piece)[0])
    projected_arrived, gate_arrived, output_arrived, more_arrived = clock.wait(
        projected.moving, gate_spread.moving, output_spread.moving, block_moving
    )
    block_arrived = block_arrived + more_arrived

    input_blocks = clock(*blocks_of(projected.finish(projected_arrived)))
    input_moving = send_blocks(input_blocks)
    output_spread.along(output_arrived)
    (gate_total,) = clock.run(widen_pieces, *gate_spread.finish(gate_arrived))
    input_rows, output_arrived = clock.wait(input_moving, output_spread.moving)

    input_spread = spread(row_sum(input_blocks[:1], input_rows))
    output_spread.over(output_arrived)
    small_moving = clock.send(core, [small], [1])
    block_moving = send_some(block_partial, edges[1:])
    (down_total,) = clock.run(lambda gathered: widen_gathered(gathered, rep_places(reps)), down_gathered)
    input_arrived, output_arrived, small_arrived, more_arrived = clock.wait(
        input_spread.moving, output_spread.moving, small_moving, block_moving
    )
    small = total_of([small] + small_arrived)
    block_arrived = block_arrived + more_arrived

    input_spread.along(input_arrived)
    small_moving = clock.send(first, [small] * (first.size - 1), range(1, first.size))
    (output_total,) = clock.run(widen_pieces, *output_spread.finish(output_arrived))
    (block_out,) = clock(total_of([hidden, block_own] + block_arrived).astype(bf16))
    input_arrived, small_arrived = clock.wait(input_spread.moving, small_moving)
    small = total_of([small] + small_arrived)

    input_spread.over(input_arrived)
    small_moving = clock.send(second, [small] * (second.size - 1), range(1, second.size))
    input_arrived, small_arrived = clock.wait(input_spread.moving, small_moving)
    small_blocks = clock(*blocks_of(total_of([small] + small_arrived)))

    small_moving = send_blocks(small_blocks)
    (input_total,) = clock.run(widen_pieces, *input_spread.finish(input_arrived))
    (up_gathered,) = clock(up_gathered)
    (up_total,) = clock.run(lambda gathered: widen_gathered(gathered, rep_places(reps)), up_gathered)
    (small_arrived,) = clock.wait(small_moving)
    small = total_of(small_blocks[:1] + small_arrived)

    small = small + clock.token[0, 0]
    small_totals, at = [], 0
    for part in small_parts:
        size = part.shape[0] // shards
        small_totals.append(small[at : at + size])
        at += size
    return (
        block_out,
        tokens_gradient,
        small_totals[0],
        input_total,
        small_totals[2],
        small_totals[3],
        output_total,
        small_totals[1],
        gate_total,
        up_total,
        down_total,
    )


def solution(mesh):
    placed = (
        P(("rep", "shard"), None),
        P("rep", None),
        P("shard"),
        P("shard", None),
        P("shard"),
        P("shard", None),
        P("shard"),
        P("shard", None),
        P("shard", None),
        P("shard", None),
        P(("rep", "shard"), None),
    )
    return jax.shard_map(
        on_device,
        mesh=mesh,
        in_specs=placed,
        out_specs=(
            P(("rep", "shard"), None),
            P(("rep", "shard"), None),
            P("shard"),
            P("shard", None),
            P("shard"),
            P("shard"),
            P("shard", None),
            P("shard"),
            P("shard", None),
            P("shard", None),
            P("shard", None),
        ),
        check_vma=False,
    )
```

```python
import math

import jax
import jax.numpy as jnp
from jax import lax
from jax.experimental import pallas as pl
from jax.experimental.pallas import tpu as pltpu
from jax.sharding import PartitionSpec as P

QH = 12
KVH = 2
HD = 128
SEQS = 3


EPSILON = 1e-06
LOG_THETA = math.log(1000000.0)
MASKED = -1e30
VMEM_LIMIT = 56 * 1024 * 1024
TILE = 512
COST = pl.CostEstimate(flops=1, bytes_accessed=1, transcendentals=0)


def rope_tables(places, head_width):
    half_width = head_width // 2
    frequency = jnp.exp(jnp.arange(half_width, dtype=jnp.float32) * (-2.0 * LOG_THETA / head_width))
    angles = places.astype(jnp.float32)[:, None] * frequency[None, :]
    angles = jnp.concatenate([angles, angles], axis=-1)
    return (jnp.cos(angles), jnp.sin(angles))


def positions(segments):
    labels = jnp.arange(SEQS, dtype=jnp.int32)
    starts = jnp.sum((segments[None, :] < labels[:, None]).astype(jnp.int32), axis=1)
    own_start = jnp.sum(jnp.where(segments[:, None] == labels[None, :], starts[None, :], 0), axis=1)
    return jnp.arange(segments.shape[0], dtype=jnp.int32) - own_start


def rotate(field_rows, cosine_table, sine_table):
    half_width = field_rows.shape[-1] // 2
    turned = jnp.concatenate([-field_rows[..., half_width:], field_rows[..., :half_width]], axis=-1)
    return field_rows * cosine_table[:, None, :] + turned * sine_table[:, None, :]


def transposed_times(left_side, right_side):
    return lax.dot_general(
        left_side, right_side, (((0,), (0,)), ((), ())), preferred_element_type=jnp.float32
    )


def times_transposed(left_side, right_side):
    return lax.dot_general(
        left_side, right_side, (((1,), (1,)), ((), ())), preferred_element_type=jnp.float32
    )


def norm_back(normed_gradient, unit_rows, inverse_rms, gain_row):
    scaled = normed_gradient * gain_row
    return inverse_rms * (scaled - unit_rows * jnp.mean(scaled * unit_rows, axis=-1, keepdims=True))


class Line:
    def __init__(self, name, size, place, pairs, crossed=False):
        self.name, self.size, self.place, self.pairs = name, size, place, pairs
        self.crossed = crossed

    def shift(self, value, step):
        return lax.ppermute(value, self.name, self.pairs(step % self.size))

    def pass_on(self, value, up):
        places = range(self.size - 1)
        pairs = [(at, at + 1) if up else (at + 1, at) for at in places]
        return lax.ppermute(value, self.name, pairs)

    def behind(self, step):
        return lax.rem(self.place + (self.size - step % self.size), self.size)

    def ahead(self, step):
        return lax.rem(self.place + step % self.size, self.size) if step else self.place


def make_lines(reps, shards):
    inner = 2 if reps % 4 == 0 else 1
    outer = reps // (2 * inner)
    square = inner == outer

    def split(index):
        core, b, a = index % 2, (index // 2) % inner, index // (2 * inner)
        return core, b, a

    def join(core, b, a):
        return (a * inner + b) * 2 + core

    def first_pairs(step):
        pairs = []
        for index in range(reps):
            core, b, a = split(index)
            if square and core == 0:
                pairs.append((index, join(core, (b + step) % inner, a)))
            else:
                pairs.append((index, join(core, b, (a + step) % outer)))
        return pairs

    def second_pairs(step):
        pairs = []
        for index in range(reps):
            core, b, a = split(index)
            if square and core == 0:
                pairs.append((index, join(core, b, (a + step) % outer)))
            else:
                pairs.append((index, join(core, (b + step) % inner, a)))
        return pairs

    def core_pairs(step):
        pairs = []
        for index in range(reps):
            core, b, a = split(index)
            pairs.append((index, join((core + step) % 2, b, a)))
        return pairs

    def shard_pairs(step):
        return [(index, (index + step) % shards) for index in range(shards)]

    core, b, a = split(lax.axis_index("rep"))
    first, second = (jnp.where(core == 0, b, a), jnp.where(core == 0, a, b)) if square else (a, b)
    return (
        Line("shard", shards, lax.axis_index("shard"), shard_pairs),
        Line("rep", 2, core, core_pairs, square),
        Line("rep", outer, first, first_pairs),
        Line("rep", inner, second, second_pairs),
    )


def rep_places(reps):
    inner = 2 if reps % 4 == 0 else 1
    outer = reps // (2 * inner)
    places = []
    for index in range(reps):
        core, b, a = index % 2, (index // 2) % inner, index // (2 * inner)
        one, two = (b, a) if inner == outer and core == 0 else (a, b)
        places.append((core * outer + one) * inner + two)
    return places


def pick(array, index, axis):
    return lax.dynamic_index_in_dim(array, index, axis, keepdims=False)


def put(array, piece, index, axis):
    return lax.dynamic_update_index_in_dim(array, piece, index, axis)


def in_place_order(pieces, line):
    ordered = []
    for place in range(line.size):
        chosen = pieces[0]
        for step in range(1, line.size):
            chosen = jnp.where(line.behind(step) == place, pieces[step], chosen)
        ordered.append(chosen)
    return ordered


def tie(*arrays):
    return lax.optimization_barrier(arrays)


def gather_line(value, line):
    return [value] + [line.shift(value, step) for step in range(1, line.size)]


class Clock:
    def __init__(self):
        self.token = jnp.zeros((8, 128), jnp.float32)
        self.open = 0

    def __call__(self, *arrays):
        self.token, *arrays = tie(self.token, *arrays)
        return arrays

    def run(self, step, *arrays):
        return self(*step(*self(*arrays)))

    def send(self, line, values, steps):
        self.open += len(values)
        return [line.shift(value, step) for value, step in zip(self(*values), steps)]

    def pass_on(self, line, lower, upper):
        self.open += 2
        lower, upper = self(lower, upper)
        return [line.pass_on(lower, True), line.pass_on(upper, False)]

    def wait(self, *groups):
        flat = self(*[array for group in groups for array in group])
        self.open -= len(flat)
        parts, at = [], 0
        for group in groups:
            parts.append(flat[at : at + len(group)])
            at += len(group)
        return parts


def total_of(terms):
    total = terms[0].astype(jnp.float32)
    for term in terms[1:]:
        total = total + term.astype(jnp.float32)
    return total


class Halving:
    def __init__(self, clock, sent, own, core, first, second):
        self.clock, self.first, self.second = clock, first, second
        self.terms = [own]
        self.moving = clock.send(core, [sent], [1])

    def along(self, line, arrived):
        self.terms = self.terms + arrived
        steps = range(1, line.size)
        blocks = [
            total_of([pick(term, line.ahead(step), 0) for term in self.terms]).astype(jnp.bfloat16)
            for step in steps
        ]
        self.moving = self.clock.send(line, blocks, steps)
        self.terms = [pick(term, line.place, 0) for term in self.terms]

    def along_first(self, arrived):
        self.along(self.first, arrived)

    def along_second(self, arrived):
        self.along(self.second, arrived)

    def finish(self, arrived):
        return self.clock(total_of(self.terms + arrived).astype(jnp.bfloat16))[0]


class Spread:
    def __init__(self, clock, piece, core, first, second):
        self.clock, self.lines = clock, (core, first, second)
        self.pieces = [piece]
        steps = range(1, second.size)
        self.moving = clock.send(second, [piece] * len(steps), steps)

    def along(self, arrived):
        core, first, second = self.lines
        self.pieces = self.pieces + arrived
        steps = range(1, first.size)
        self.moving = self.clock.send(first, [jnp.stack(self.pieces)] * len(steps), steps)

    def over(self, arrived):
        core, first, second = self.lines
        rows = [jnp.stack(self.pieces)] + arrived
        self.pieces = jnp.concatenate(rows, axis=0)
        self.moving = self.clock.send(core, [self.pieces], [1])

    def finish(self, arrived):
        core, first, second = self.lines
        (others,) = arrived
        offsets = [(one, two) for one in range(first.size) for two in range(second.size)]
        placed = [(core.place, first.behind(one), second.behind(two)) for one, two in offsets]
        far, near = (second, first) if core.crossed else (first, second)
        placed += [(core.behind(1), far.behind(one), near.behind(two)) for one, two in offsets]
        places = [(c * first.size + f) * second.size + s for c, f, s in placed]
        return [jnp.stack(places).astype(jnp.int32), self.pieces, others]


def column_blocks(place, shard_place, *weights):
    count = len(weights)
    rows, columns = weights[0].shape[1:]
    shards = lax.axis_size("shard")
    block = columns // shards

    def body(places_ref, *refs):
        sources, outs = refs[:count], refs[count : 2 * count]
        held, cut, in_sems, out_sems = refs[2 * count :]
        loads = [
            pltpu.make_async_copy(sources[at].at[places_ref[0]], held.at[at], in_sems.at[at])
            for at in range(count)
        ]

        def store(at, z):
            ahead = lax.rem(z + shards - places_ref[1], shards)
            return pltpu.make_async_copy(cut.at[at, z], outs[at].at[ahead], out_sems.at[at, z])

        for load in loads:
            load.start()
        for at in range(count):
            loads[at].wait()
            for z in range(shards):
                cut[at, z] = held[at, :, z * block : (z + 1) * block]
                store(at, z).start()
        for at in range(count):
            for z in range(shards):
                store(at, z).wait()

    return pl.pallas_call(
        body,
        out_shape=[jax.ShapeDtypeStruct((shards, rows, block), jnp.bfloat16)] * count,
        in_specs=[pl.BlockSpec(memory_space=pltpu.SMEM)]
        + [pl.BlockSpec(memory_space=pl.ANY)] * count,
        out_specs=[pl.BlockSpec(memory_space=pl.ANY)] * count,
        scratch_shapes=[
            pltpu.VMEM((count, rows, columns), jnp.bfloat16),
            pltpu.VMEM((count, shards, rows, block), jnp.bfloat16),
            pltpu.SemaphoreType.DMA((count,)),
            pltpu.SemaphoreType.DMA((count, shards)),
        ],
        compiler_params=pltpu.CompilerParams(vmem_limit_bytes=VMEM_LIMIT),
        cost_estimate=COST,
        name="column_blocks",
    )(jnp.stack([place, shard_place]).astype(jnp.int32), *weights)


def place_blocks(order, places, pieces, others):
    half, groups, shards = pieces.shape[:3]

    def body(order_ref, places_ref, pieces_ref, others_ref, *rest):
        def source_of(g, k, r):
            return (pieces_ref if r < half else others_ref).at[r % half, g, k]

        move_blocks(source_of, lambda r: places_ref[r], order_ref, rest[:groups], *rest[groups:])

    return blocks_call(body, 2, 2, groups, shards, 2 * half, pieces.shape[3:])(
        order, places, pieces, others
    )


def place_gathered(order, gathered, groups):
    shards = lax.axis_size("shard")
    reps = gathered.shape[0] // (shards * groups)

    def body(order_ref, source, *rest):
        move_blocks(
            lambda g, k, r: source.at[(r * shards + k) * groups + g],
            lambda r: r,
            order_ref,
            rest[:groups],
            *rest[groups:],
        )

    return blocks_call(body, 1, 1, groups, shards, reps, gathered.shape[1:])(order, gathered)


def move_blocks(source_of, place_of, order_ref, outs, held, in_sems, out_sems):
    groups, shards, reps = in_sems.shape
    slabs = [(g, k) for g in range(groups) for k in range(shards)]

    def load(g, k, r):
        return pltpu.make_async_copy(
            source_of(g, k, r), held.at[g, k, place_of(r)], in_sems.at[g, k, r]
        )

    def store(g, k):
        return pltpu.make_async_copy(held.at[g, k], outs[g].at[order_ref[k]], out_sems.at[g, k])

    for g, k in slabs:
        for r in range(reps):
            load(g, k, r).start()
    for g, k in slabs:
        for r in range(reps):
            load(g, k, r).wait()
        store(g, k).start()
    for g, k in slabs:
        store(g, k).wait()


def blocks_call(body, scalars, sources, groups, shards, reps, block):
    whole = (shards, reps) + block
    return pl.pallas_call(
        body,
        out_shape=[jax.ShapeDtypeStruct(whole, jnp.bfloat16)] * groups,
        in_specs=[pl.BlockSpec(memory_space=pltpu.SMEM)] * scalars
        + [pl.BlockSpec(memory_space=pl.ANY)] * sources,
        out_specs=[pl.BlockSpec(memory_space=pl.ANY)] * groups,
        scratch_shapes=[
            pltpu.VMEM((groups,) + whole, jnp.bfloat16),
            pltpu.SemaphoreType.DMA((groups, shards, reps)),
            pltpu.SemaphoreType.DMA((groups, shards)),
        ],
        compiler_params=pltpu.CompilerParams(vmem_limit_bytes=VMEM_LIMIT),
        cost_estimate=COST,
        name="place_blocks",
    )


def widen_pieces(places, pieces, others):
    half, rows, columns = pieces.shape
    reps = 2 * half
    strip = next(size for size in (16, 8, rows) if rows % size == 0)

    def body(places_ref, pieces_ref, others_ref, out_ref, narrow, wide, in_sems, out_sems):
        loads = [
            pltpu.make_async_copy(
                (pieces_ref if r < half else others_ref).at[r % half], narrow.at[r], in_sems.at[r]
            )
            for r in range(reps)
        ]
        stores = [
            pltpu.make_async_copy(wide.at[r], out_ref.at[places_ref[r]], out_sems.at[r])
            for r in range(reps)
        ]
        for load in loads:
            load.start()
        for r in range(reps):
            loads[r].wait()

            def convert(at, carry):
                cut = pl.ds(pl.multiple_of(at * strip, strip), strip)
                wide[r, cut, :] = narrow[r, cut, :].astype(jnp.float32)
                return carry

            lax.fori_loop(0, rows // strip, convert, 0)
            stores[r].start()
        for store in stores:
            store.wait()

    result = pl.pallas_call(
        body,
        out_shape=jax.ShapeDtypeStruct((reps, rows, columns), jnp.float32),
        in_specs=[pl.BlockSpec(memory_space=pltpu.SMEM)]
        + [pl.BlockSpec(memory_space=pl.ANY)] * 2,
        out_specs=pl.BlockSpec(memory_space=pl.ANY),
        scratch_shapes=[
            pltpu.VMEM((reps, rows, columns), jnp.bfloat16),
            pltpu.VMEM((reps, rows, columns), jnp.float32),
            pltpu.SemaphoreType.DMA((reps,)),
            pltpu.SemaphoreType.DMA((reps,)),
        ],
        compiler_params=pltpu.CompilerParams(vmem_limit_bytes=VMEM_LIMIT),
        cost_estimate=COST,
        name="widen_pieces",
    )(places, pieces, others)
    return (result.reshape(reps * rows, columns),)


def widen_gathered(gathered, order):
    reps, rows, columns = gathered.shape
    strip = next(size for size in (16, 8, rows) if rows % size == 0)

    def body(source_ref, out_ref, narrow, wide, in_sems, out_sems):
        loads = [
            pltpu.make_async_copy(source_ref.at[r], narrow.at[r], in_sems.at[r])
            for r in range(reps)
        ]
        stores = [
            pltpu.make_async_copy(wide.at[r], out_ref.at[order[r]], out_sems.at[r])
            for r in range(reps)
        ]
        for load in loads:
            load.start()
        for r in range(reps):
            loads[r].wait()

            def convert(at, carry):
                cut = pl.ds(pl.multiple_of(at * strip, strip), strip)
                wide[r, cut, :] = narrow[r, cut, :].astype(jnp.float32)
                return carry

            lax.fori_loop(0, rows // strip, convert, 0)
            stores[r].start()
        for store in stores:
            store.wait()

    result = pl.pallas_call(
        body,
        out_shape=jax.ShapeDtypeStruct((reps, rows, columns), jnp.float32),
        in_specs=[pl.BlockSpec(memory_space=pl.ANY)],
        out_specs=pl.BlockSpec(memory_space=pl.ANY),
        scratch_shapes=[
            pltpu.VMEM((reps, rows, columns), jnp.bfloat16),
            pltpu.VMEM((reps, rows, columns), jnp.float32),
            pltpu.SemaphoreType.DMA((reps,)),
            pltpu.SemaphoreType.DMA((reps,)),
        ],
        compiler_params=pltpu.CompilerParams(vmem_limit_bytes=VMEM_LIMIT),
        cost_estimate=COST,
        name="widen_gathered",
    )(gathered)
    return (result.reshape(reps * rows, columns),)


def resident(shape):
    return pl.BlockSpec(shape, lambda i: (0, 0), pipeline_mode=pl.Buffered(1))


def feed_forward(rows, cotangents, gate_matrix, up_matrix, down_matrix):
    count, width = rows.shape
    units = gate_matrix.shape[1]
    steps = pl.cdiv(units, TILE)
    slabs = next(size for size in range(min(steps, width // 128), 0, -1) if width % (128 * size) == 0)
    slab = width // slabs

    def body(
        rows_ref,
        cotangents_ref,
        gate_ref,
        up_ref,
        down_ref,
        inner_ref,
        d_gate_ref,
        d_up_ref,
        turned_rows_ref,
        turned_inner_ref,
    ):
        gate = jnp.dot(rows_ref[...], gate_ref[...], preferred_element_type=jnp.float32)
        up = jnp.dot(rows_ref[...], up_ref[...], preferred_element_type=jnp.float32)
        sigmoid = jax.nn.sigmoid(gate)
        silu = gate * sigmoid
        inner = (silu * up).astype(jnp.bfloat16)
        inner_ref[...] = inner
        turned_inner_ref[...] = inner.T
        d_inner = times_transposed(cotangents_ref[...], down_ref[...])
        d_up_ref[...] = (d_inner * silu).astype(jnp.bfloat16)
        d_gate_ref[...] = (d_inner * up * sigmoid * (1.0 + gate * (1.0 - sigmoid))).astype(
            jnp.bfloat16
        )
        for step in range(slabs):

            @pl.when(pl.program_id(0) == step)
            def turn():
                turned_rows_ref[...] = rows_ref[:, step * slab : (step + 1) * slab].T

    columns = pl.BlockSpec((width, TILE), lambda i: (0, i))
    results = pl.BlockSpec((count, TILE), lambda i: (0, i))
    return pl.pallas_call(
        body,
        grid=(steps,),
        out_shape=[jax.ShapeDtypeStruct((count, units), jnp.bfloat16)] * 3
        + [
            jax.ShapeDtypeStruct((width, count), jnp.bfloat16),
            jax.ShapeDtypeStruct((units, count), jnp.bfloat16),
        ],
        in_specs=[
            resident((count, width)),
            resident((count, width)),
            columns,
            columns,
            pl.BlockSpec((TILE, width), lambda i: (i, 0)),
        ],
        out_specs=[results] * 3
        + [
            pl.BlockSpec((slab, count), lambda i: (jnp.minimum(i, slabs - 1), 0)),
            pl.BlockSpec((TILE, count), lambda i: (i, 0)),
        ],
        compiler_params=pltpu.CompilerParams(vmem_limit_bytes=VMEM_LIMIT),
        cost_estimate=COST,
        name="feed_forward",
    )(rows, cotangents, gate_matrix, up_matrix, down_matrix)


def split_gradient(left, right, groups, places, core_place, turned):
    rows, count = left.shape if turned else left.shape[::-1]
    columns = right.shape[1]
    half = rows // (2 * groups)
    part = half // places

    def body(core_ref, left_ref, right_ref, other_ref, own_ref, *scratch):
        if turned:
            rows_ref = left_ref
        else:
            (rows_ref,) = scratch

            @pl.when(pl.program_id(0) == 0)
            def turn():
                rows_ref[...] = left_ref[...].T

        core = core_ref[0]
        for out_ref, which in ((other_ref, 1 - core), (own_ref, core)):
            halves = [
                rows_ref[pl.ds(pl.multiple_of((2 * group + which) * half, 16), half), :]
                for group in range(groups)
            ]
            product = jnp.dot(
                jnp.concatenate(halves, axis=0), right_ref[...], preferred_element_type=jnp.float32
            )
            for group in range(groups):
                for place in range(places):
                    at = group * half + place * part
                    out_ref[place, group] = product[at : at + part].astype(jnp.bfloat16)

    return pl.pallas_call(
        body,
        grid=(pl.cdiv(columns, TILE),),
        out_shape=[jax.ShapeDtypeStruct((places, groups, part, columns), jnp.bfloat16)] * 2,
        in_specs=[
            pl.BlockSpec(memory_space=pltpu.SMEM),
            resident(left.shape),
            pl.BlockSpec((count, TILE), lambda i: (0, i)),
        ],
        out_specs=[pl.BlockSpec((places, groups, part, TILE), lambda i: (0, 0, 0, i))] * 2,
        scratch_shapes=[] if turned else [pltpu.VMEM((rows, count), jnp.bfloat16)],
        compiler_params=pltpu.CompilerParams(vmem_limit_bytes=VMEM_LIMIT),
        cost_estimate=COST,
        name="split_gradient",
    )(core_place.reshape(1).astype(jnp.int32), left, right)


def ordered_gradient(left, right, shards, order):
    reps = len(order)
    rows, count = left.shape
    columns = right.shape[1]
    part = rows // (shards * reps)

    def body(left_ref, right_ref, out_ref):
        product = jnp.dot(left_ref[...], right_ref[...], preferred_element_type=jnp.float32)
        for z in range(shards):
            for r in range(reps):
                at = (z * reps + order[r]) * part
                out_ref[r, z] = product[at : at + part].astype(jnp.bfloat16)

    return pl.pallas_call(
        body,
        grid=(pl.cdiv(columns, TILE),),
        out_shape=[jax.ShapeDtypeStruct((reps, shards, part, columns), jnp.bfloat16)],
        in_specs=[
            resident((rows, count)),
            pl.BlockSpec((count, TILE), lambda i: (0, i)),
        ],
        out_specs=[pl.BlockSpec((reps, shards, part, TILE), lambda i: (0, 0, 0, i))],
        compiler_params=pltpu.CompilerParams(vmem_limit_bytes=VMEM_LIMIT),
        cost_estimate=COST,
        name="ordered_gradient",
    )(left, right)


def rows_product(lefts, rights, turned, blocks):
    count, depth = lefts[0].shape
    columns = rights[0].shape[0 if turned else 1]
    pairs, part = len(lefts), count // blocks

    def body(*refs):
        total = None
        for left_ref, right_ref in zip(refs[:pairs], refs[pairs : 2 * pairs]):
            if turned:
                product = times_transposed(left_ref[...], right_ref[...])
            else:
                product = jnp.dot(
                    left_ref[...], right_ref[...], preferred_element_type=jnp.float32
                )
            total = product if total is None else total + product
        for block in range(blocks):
            refs[2 * pairs + block][...] = total[block * part : (block + 1) * part].astype(
                jnp.bfloat16
            )

    right_spec = (
        pl.BlockSpec((TILE, depth), lambda i: (i, 0))
        if turned
        else pl.BlockSpec((depth, TILE), lambda i: (0, i))
    )
    return pl.pallas_call(
        body,
        grid=(pl.cdiv(columns, TILE),),
        out_shape=[jax.ShapeDtypeStruct((part, columns), jnp.bfloat16)] * blocks,
        in_specs=[resident((count, depth))] * pairs + [right_spec] * pairs,
        out_specs=[pl.BlockSpec((part, TILE), lambda i: (0, i))] * blocks,
        compiler_params=pltpu.CompilerParams(vmem_limit_bytes=VMEM_LIMIT),
        cost_estimate=COST,
        name="rows_product",
    )(*lefts, *rights)


def kept_bias(row_segments, row_index, key_segments, key_index):
    kept = (row_segments == key_segments) & (key_index <= row_index)
    return jnp.where(kept, 0.0, MASKED)


def in_vmem(count):
    return [pl.BlockSpec(memory_space=pltpu.VMEM)] * count


def attention_forward(projected, cosine, signed_sine, pairs, rows, keys):
    count = projected.shape[0]
    per_group = QH // KVH
    scale = 1.0 / math.sqrt(HD)
    shape = (KVH, per_group * count, HD)

    def body(projected_ref, cosine_ref, sine_ref, pairs_ref, rows_ref, keys_ref, queries_ref, out_ref):
        bias = kept_bias(rows_ref[:, 0:1], rows_ref[:, 1:2], keys_ref[0:1, :], keys_ref[1:2, :])
        for k in range(KVH):
            for h in range(per_group):
                at = (k * per_group + h) * HD
                field = projected_ref[:, at : at + HD]
                queries_ref[k, h * count : (h + 1) * count, :] = (
                    field * cosine_ref[...] + pltpu.roll(field, HD // 2, 1) * sine_ref[...]
                ).astype(jnp.bfloat16)
            keys_here = pairs_ref[:, k * HD : (k + 1) * HD]
            values_here = pairs_ref[:, (KVH + k) * HD : (KVH + k + 1) * HD]
            scores = times_transposed(queries_ref[k], keys_here) * scale + bias
            powers = jnp.exp(scores - jnp.max(scores, axis=1, keepdims=True))
            shares = powers * (1.0 / jnp.sum(powers, axis=1, keepdims=True))
            result = jnp.dot(
                shares.astype(jnp.bfloat16), values_here, preferred_element_type=jnp.float32
            ).astype(jnp.bfloat16)
            for h in range(per_group):
                at = (k * per_group + h) * HD
                out_ref[:, at : at + HD] = result[h * count : (h + 1) * count]

    return pl.pallas_call(
        body,
        out_shape=[
            jax.ShapeDtypeStruct(shape, jnp.bfloat16),
            jax.ShapeDtypeStruct((count, QH * HD), jnp.bfloat16),
        ],
        in_specs=in_vmem(6),
        out_specs=in_vmem(2),
        compiler_params=pltpu.CompilerParams(vmem_limit_bytes=VMEM_LIMIT),
        cost_estimate=COST,
        name="attention_forward",
    )(projected, cosine, signed_sine, pairs, rows, keys)


def attention_backward(queries, gradient, pairs, cosine, signed_sine, rows, keys, blocks):
    count = gradient.shape[0]
    per_group = QH // KVH
    scale = 1.0 / math.sqrt(HD)
    group_rows = pairs.shape[0]
    part = group_rows // blocks

    def body(queries_ref, gradient_ref, pairs_ref, cosine_ref, sine_ref, rows_ref, keys_ref, d_ref, *outs):
        block_refs, stacked = outs[:blocks], outs[blocks]
        bias = kept_bias(rows_ref[0:1, :], rows_ref[1:2, :], keys_ref[:, 0:1], keys_ref[:, 1:2])
        for k in range(KVH):
            for h in range(per_group):
                at = (k * per_group + h) * HD
                stacked[h * count : (h + 1) * count, :] = gradient_ref[:, at : at + HD]
            keys_here = pairs_ref[:, k * HD : (k + 1) * HD]
            values_here = pairs_ref[:, (KVH + k) * HD : (KVH + k + 1) * HD]
            scores = times_transposed(keys_here, queries_ref[k]) * scale + bias
            powers = jnp.exp(scores - jnp.max(scores, axis=0, keepdims=True))
            shares = powers * (1.0 / jnp.sum(powers, axis=0, keepdims=True))
            d_shares = times_transposed(values_here, stacked[...])
            dots = jnp.sum(shares * d_shares, axis=0, keepdims=True)
            d_scores = (shares * (d_shares - dots)).astype(jnp.bfloat16)
            d_keys = jnp.dot(d_scores, queries_ref[k], preferred_element_type=jnp.float32) * scale
            d_values = jnp.dot(
                shares.astype(jnp.bfloat16), stacked[...], preferred_element_type=jnp.float32
            )
            for block in range(blocks):
                cut = slice(block * part, (block + 1) * part)
                block_refs[block][:, k * HD : (k + 1) * HD] = d_keys[cut].astype(jnp.bfloat16)
                block_refs[block][:, (KVH + k) * HD : (KVH + k + 1) * HD] = d_values[cut].astype(
                    jnp.bfloat16
                )
            d_queries = transposed_times(d_scores, keys_here) * scale
            for h in range(per_group):
                at = (k * per_group + h) * HD
                field = d_queries[h * count : (h + 1) * count]
                d_ref[:, at : at + HD] = (
                    field * cosine_ref[...] - pltpu.roll(field, HD // 2, 1) * sine_ref[...]
                ).astype(jnp.bfloat16)

    return pl.pallas_call(
        body,
        out_shape=[jax.ShapeDtypeStruct((count, QH * HD), jnp.bfloat16)]
        + [jax.ShapeDtypeStruct((part, 2 * KVH * HD), jnp.bfloat16)] * blocks,
        in_specs=in_vmem(7),
        out_specs=in_vmem(1 + blocks),
        scratch_shapes=[pltpu.VMEM((per_group * count, HD), jnp.bfloat16)],
        compiler_params=pltpu.CompilerParams(vmem_limit_bytes=VMEM_LIMIT),
        cost_estimate=COST,
        name="attention_backward",
    )(queries, gradient, pairs, cosine, signed_sine, rows, keys)


def join_projected(d_queries, pair_terms, cosine, signed_sine):
    count, query_width = d_queries.shape
    pair_width = KVH * HD
    terms = len(pair_terms)

    def body(d_queries_ref, cosine_ref, sine_ref, *refs):
        term_refs, out_ref, sum_ref = refs[:terms], refs[terms], refs[terms + 1]
        out_ref[:, :query_width] = d_queries_ref[...]
        for at in range(0, 2 * pair_width, HD):
            field = total_of([term[:, at : at + HD] for term in term_refs])
            if at < pair_width:
                field = field * cosine_ref[...] - pltpu.roll(field, HD // 2, 1) * sine_ref[...]
            out_ref[:, query_width + at : query_width + at + HD] = field.astype(jnp.bfloat16)
        sum_ref[...] = jnp.sum(out_ref[...].astype(jnp.float32), axis=0, keepdims=True)

    return pl.pallas_call(
        body,
        out_shape=[
            jax.ShapeDtypeStruct((count, query_width + 2 * pair_width), jnp.bfloat16),
            jax.ShapeDtypeStruct((1, query_width + 2 * pair_width), jnp.float32),
        ],
        in_specs=in_vmem(3 + terms),
        out_specs=in_vmem(2),
        cost_estimate=COST,
        name="join_projected",
    )(d_queries, cosine, signed_sine, *pair_terms)


def on_device(
    tokens,
    segment_ids,
    first_gain,
    input_weight,
    input_bias,
    output_weight,
    second_gain,
    gate_weight,
    up_weight,
    down_weight,
    output_cotangent,
):
    bf16, f32 = jnp.bfloat16, jnp.float32
    shards, reps = lax.axis_size("shard"), lax.axis_size("rep")
    shard, core, first, second = make_lines(reps, shards)
    rep_place = (core.place * first.size + first.place) * second.size + second.place
    own_rows, width = tokens.shape
    segments = segment_ids[0]
    per_group = QH // KVH
    query_width = QH * HD
    pair_width = KVH * HD
    first_row = shard.place * own_rows
    part_rows = input_weight.shape[0] // reps
    hidden_units = gate_weight.shape[1]
    block_units = hidden_units // shards
    clock = Clock()
    z_order = jnp.stack([shard.behind(step) for step in range(shards)]).astype(jnp.int32)

    def weight_piece(weight, place):
        return pick(weight.reshape(reps, part_rows, weight.shape[1]), place, 0)

    def spread(piece):
        return Spread(clock, piece, core, first, second)

    def blocks_of(blocks):
        return [pick(blocks, shard.ahead(step), 0) for step in range(shards)]

    steps = range(1, shards)

    def send_blocks(blocks):
        return clock.send(shard, blocks[1:], steps)

    def send_around(value):
        return clock.send(shard, [value] * len(steps), steps)

    def send_back(rows):
        return clock.send(shard, rows, [shards - step for step in steps])

    rep_index = lax.axis_index("rep")
    input_matrix = lax.all_gather(
        weight_piece(input_weight, rep_index), ("shard", "rep"), axis=0, tiled=True
    )
    shard_vectors = jnp.concatenate([first_gain, second_gain, input_bias])
    vector_row = jnp.pad(shard_vectors, (0, output_weight.shape[1] - shard_vectors.shape[0]))
    own_output = jnp.concatenate(
        [weight_piece(output_weight, rep_place), vector_row[None]], axis=0
    )
    output_moving = send_around(own_output)
    gate_blocks, up_blocks = clock.run(
        lambda *weights: column_blocks(rep_index, shard.place, *weights),
        gate_weight.reshape(reps, part_rows, hidden_units),
        up_weight.reshape(reps, part_rows, hidden_units),
    )
    (output_rows,) = clock.wait(output_moving)
    output_rows = [own_output] + output_rows

    output_spread = spread(jnp.stack([rows[:part_rows] for rows in output_rows])[None])
    gate_moving = send_blocks(gate_blocks)
    vector_rows = jnp.stack(in_place_order([rows[part_rows] for rows in output_rows], shard))
    own_gain = first_gain.shape[0]
    gain_one = vector_rows[:, :own_gain].reshape(width).astype(f32)
    gain_two = vector_rows[:, own_gain : 2 * own_gain].reshape(width).astype(f32)
    shift_row = (
        vector_rows[:, 2 * own_gain : shard_vectors.shape[0]].reshape(-1).astype(f32)
    )
    places = positions(segments)
    cosine_table, sine_table = rope_tables(
        lax.dynamic_slice_in_dim(places, first_row, own_rows), HD
    )
    signed_sine = jnp.concatenate(
        [-sine_table[:, : HD // 2], sine_table[:, HD // 2 :]], axis=1
    )
    own_segments = lax.dynamic_slice_in_dim(segments, first_row, own_rows)
    row_index = jnp.arange(own_rows, dtype=jnp.int32)
    key_index = jnp.concatenate([shard.behind(step) * own_rows + row_index for step in range(shards)])
    key_segments = jnp.concatenate(
        [
            lax.dynamic_slice_in_dim(segments, shard.behind(step) * own_rows, own_rows)
            for step in range(shards)
        ]
    )
    key_marks = jnp.stack([key_segments, key_index])
    row_marks = jnp.tile(jnp.stack([own_segments, first_row + row_index]), (1, per_group))
    wide_tokens = tokens.astype(f32)
    inverse_one = lax.rsqrt(jnp.mean(wide_tokens * wide_tokens, axis=-1, keepdims=True) + EPSILON)
    unit_one = wide_tokens * inverse_one
    normed_one = (unit_one * gain_one).astype(bf16)
    (
        normed_one,
        cosine_table,
        sine_table,
        signed_sine,
        key_marks,
        row_marks,
    ) = clock(normed_one, cosine_table, sine_table, signed_sine, key_marks, row_marks)
    output_arrived, gate_rows = clock.wait(output_spread.moving, gate_moving)

    output_spread.along(output_arrived)
    up_moving = send_blocks(up_blocks)
    output_arrived, up_rows = clock.wait(output_spread.moving, up_moving)

    gate_up = jnp.stack(
        [row for pair in zip([gate_blocks[0]] + gate_rows, [up_blocks[0]] + up_rows) for row in pair]
    )
    gate_up = lax.all_gather(clock(gate_up)[0], "rep", axis=0, tiled=True)
    passed = [[output_cotangent] * 2]
    passing = clock.pass_on(shard, *passed[-1])
    output_spread.over(output_arrived)
    input_matrix, normed_one = clock(input_matrix, normed_one)
    projected = jnp.dot(normed_one, input_matrix, preferred_element_type=f32) + shift_row
    key_part = rotate(
        projected[:, query_width : query_width + pair_width].reshape(own_rows, KVH, HD),
        cosine_table,
        sine_table,
    )
    (own_pairs,) = clock(
        jnp.concatenate(
            [key_part.reshape(own_rows, pair_width), projected[:, query_width + pair_width :]],
            axis=1,
        ).astype(bf16)
    )
    arrived, output_arrived = clock.wait(passing, output_spread.moving)
    passed.append(arrived)

    pair_moving = send_around(own_pairs)
    passing = clock.pass_on(shard, *passed[-1]) if shards > 2 else []
    pair_rows, arrived = clock.wait(pair_moving, passing)
    passed.append(arrived)
    pairs = jnp.concatenate([own_pairs] + pair_rows, axis=0)

    passing = clock.pass_on(shard, *passed[-1]) if shards > 3 else []
    (output_matrix,) = clock.run(place_blocks, z_order, *output_spread.finish(output_arrived))
    output_matrix = output_matrix.reshape(width, width)
    queries, attention_low = clock.run(
        attention_forward, projected, cosine_table, signed_sine, pairs, row_marks.T, key_marks
    )
    hidden = wide_tokens + jnp.dot(attention_low, output_matrix, preferred_element_type=f32)
    inverse_two = lax.rsqrt(jnp.mean(hidden * hidden, axis=-1, keepdims=True) + EPSILON)
    unit_two = hidden * inverse_two
    (normed_two,) = clock((unit_two * gain_two).astype(bf16))
    (arrived,) = clock.wait(passing)
    passed.append(arrived)

    normed_moving = send_around(normed_two)
    gate_matrix, up_matrix = clock.run(
        lambda order, gathered: place_gathered(order, gathered, 2), z_order, gate_up
    )
    gate_matrix = gate_matrix.reshape(width, block_units)
    up_matrix = up_matrix.reshape(width, block_units)
    (normed_arrived,) = clock.wait(normed_moving)
    while len(passed) < shards:
        (arrived,) = clock.wait(clock.pass_on(shard, *passed[-1]))
        passed.append(arrived)
    group_normed = jnp.concatenate([normed_two] + normed_arrived, axis=0)
    cotangents = jnp.concatenate(
        [output_cotangent]
        + [
            jnp.where(shard.place >= step, passed[step][0], passed[shards - step][1])
            for step in steps
        ],
        axis=0,
    )

    inner_act, d_gate, d_up, turned_normed, turned_inner = clock.run(
        feed_forward, group_normed, cotangents, gate_matrix, up_matrix, down_weight
    )

    def split_halves(left, right, groups, turned):
        count = first.size * second.size
        halves = clock.run(
            lambda left, right: split_gradient(left, right, groups, count, core.place, turned),
            left,
            right,
        )
        return [half.reshape((first.size, second.size) + half.shape[1:]) for half in halves]

    def side_by_side(rows):
        return clock(jnp.concatenate(in_place_order(rows, shard), axis=1))[0]

    def sum_over_rep(blocks):
        return lax.psum_scatter(blocks, "rep", scatter_dimension=0, tiled=True)

    def row_sum(own, arrived):
        return clock(total_of(own + arrived).astype(bf16))[0]

    def send_some(rows, chosen):
        return clock.send(shard, [rows[k] for k in chosen], [shards - 1 - k for k in chosen])

    edges = sorted({0, shards - 2})
    inside = list(range(1, shards - 2))

    def gather_rep(piece):
        return lax.all_gather(piece[None], "rep", axis=0, tiled=True)

    up_halves = split_halves(turned_normed, d_up, shards, True)

    up = Halving(clock, *up_halves, core, first, second)
    (gate_blocks,) = clock.run(
        lambda left, right: ordered_gradient(left, right, shards, rep_places(reps)),
        turned_normed,
        d_gate,
    )
    (up_arrived,) = clock.wait(up.moving)

    gate_piece = sum_over_rep(clock(gate_blocks)[0].reshape(width, block_units))
    up.along_first(up_arrived)
    normed_own, *normed_partial = clock.run(
        lambda *operands: rows_product(operands[:2], operands[2:], True, shards),
        d_gate,
        d_up,
        gate_matrix,
        up_matrix,
    )
    normed_moving = send_some(normed_partial, edges)
    down_halves = split_halves(turned_inner, cotangents, 1, True)
    up_arrived, normed_arrived = clock.wait(up.moving, normed_moving)

    up.along_second(up_arrived)
    down = Halving(clock, *down_halves, core, first, second)
    normed_moving = send_some(normed_partial, inside)
    block_own, *block_partial = clock.run(
        lambda left, right: rows_product((left,), (right,), False, shards), inner_act, down_weight
    )
    up_arrived, down_arrived, more_arrived = clock.wait(up.moving, down.moving, normed_moving)

    down.along_first(down_arrived)
    up_blocks = clock(*blocks_of(up.finish(up_arrived)))
    up_moving = send_blocks(up_blocks)
    normed_two_gradient = total_of([normed_own] + normed_arrived + more_arrived)
    gain_two_gradient = jnp.sum(normed_two_gradient * unit_two, axis=0)
    hidden_gradient = output_cotangent.astype(f32) + norm_back(
        normed_two_gradient, unit_two, inverse_two, gain_two
    )
    (branch_gradient,) = clock(hidden_gradient.astype(bf16))
    (attention_gradient,) = clock(times_transposed(branch_gradient, output_matrix).astype(bf16))
    d_queries, pair_own, *pair_partial = clock.run(
        lambda *operands: attention_backward(*operands, shards),
        queries,
        attention_gradient,
        pairs,
        cosine_table,
        signed_sine,
        row_marks,
        key_marks.T,
    )
    output_halves = split_halves(attention_low, branch_gradient, shards, False)
    down_arrived, up_rows = clock.wait(down.moving, up_moving)

    pair_moving = send_back(pair_partial)
    output = Halving(clock, *output_halves, core, first, second)
    down.along_second(down_arrived)
    up_piece = side_by_side(up_blocks[:1] + up_rows)
    pair_arrived, output_arrived, down_arrived = clock.wait(
        pair_moving, output.moving, down.moving
    )

    (gate_piece,) = clock(gate_piece)
    down_gathered = gather_rep(down.finish(down_arrived)[0])
    projected_gradient, bias_sum = clock.run(
        lambda *operands: join_projected(operands[0], operands[3:], *operands[1:3]),
        d_queries,
        cosine_table,
        signed_sine,
        pair_own,
        *pair_arrived,
    )
    projected_halves = split_halves(normed_one, projected_gradient, shards, False)

    projected = Halving(clock, *projected_halves, core, first, second)
    output.along_first(output_arrived)
    gate_blocks = clock(*blocks_of(gate_piece.reshape(shards, part_rows, block_units)))
    gate_moving = send_blocks(gate_blocks)
    projected_gradient, hidden_gradient = clock(projected_gradient, hidden_gradient)
    normed_one_gradient = times_transposed(projected_gradient, input_matrix)
    gain_one_gradient = jnp.sum(normed_one_gradient * unit_one, axis=0)
    (tokens_gradient,) = clock(
        (
            hidden_gradient + norm_back(normed_one_gradient, unit_one, inverse_one, gain_one)
        ).astype(bf16)
    )
    projected_arrived, output_arrived, gate_rows = clock.wait(
        projected.moving, output.moving, gate_moving
    )

    projected.along_first(projected_arrived)
    output.along_second(output_arrived)
    gate_spread = spread(side_by_side(gate_blocks[:1] + gate_rows))
    block_moving = send_some(block_partial, inside)
    bias_gradient = bias_sum[0]
    bias_split = query_width + pair_width
    small_parts = (
        gain_one_gradient,
        gain_two_gradient,
        bias_gradient[:bias_split],
        bias_gradient[bias_split:],
    )
    (small,) = clock(
        jnp.concatenate([part.reshape(shards, -1) for part in small_parts], axis=1)
    )
    projected_arrived, output_arrived, gate_arrived, block_arrived = clock.wait(
        projected.moving, output.moving, gate_spread.moving, block_moving
    )

    projected.along_second(projected_arrived)
    gate_spread.along(gate_arrived)
    output_blocks = clock(*blocks_of(output.finish(output_arrived)))
    output_moving = send_blocks(output_blocks)
    (down_gathered,) = clock(down_gathered)
    up_gathered = gather_rep(clock(up_piece)[0])
    projected_arrived, gate_arrived, output_rows = clock.wait(
        projected.moving, gate_spread.moving, output_moving
    )

    input_blocks = clock(*blocks_of(projected.finish(projected_arrived)))
    input_moving = send_blocks(input_blocks)
    output_spread = spread(row_sum(output_blocks[:1], output_rows))
    gate_spread.over(gate_arrived)
    input_rows, output_arrived, gate_arrived = clock.wait(
        input_moving, output_spread.moving, gate_spread.moving
    )

    input_spread = spread(row_sum(input_blocks[:1], input_rows))
    output_spread.along(output_arrived)
    small_moving = clock.send(core, [small], [1])
    block_moving = send_some(block_partial, edges[:1])
    (gate_total,) = clock.run(widen_pieces, *gate_spread.finish(gate_arrived))
    input_arrived, output_arrived, small_arrived, more_arrived = clock.wait(
        input_spread.moving, output_spread.moving, small_moving, block_moving
    )
    small = total_of([small] + small_arrived)
    block_arrived = block_arrived + more_arrived

    input_spread.along(input_arrived)
    output_spread.over(output_arrived)
    small_moving = clock.send(first, [small] * (first.size - 1), range(1, first.size))
    block_moving = send_some(block_partial, edges[1:])
    (down_total,) = clock.run(lambda gathered: widen_gathered(gathered, rep_places(reps)), down_gathered)
    input_arrived, output_arrived, small_arrived, more_arrived = clock.wait(
        input_spread.moving, output_spread.moving, small_moving, block_moving
    )
    small = total_of([small] + small_arrived)
    block_arrived = block_arrived + more_arrived

    input_spread.over(input_arrived)
    small_moving = clock.send(second, [small] * (second.size - 1), range(1, second.size))
    (output_total,) = clock.run(widen_pieces, *output_spread.finish(output_arrived))
    (block_out,) = clock(total_of([hidden, block_own] + block_arrived).astype(bf16))
    input_arrived, small_arrived = clock.wait(input_spread.moving, small_moving)
    small_blocks = clock(*blocks_of(total_of([small] + small_arrived)))

    small_moving = send_blocks(small_blocks)
    (up_gathered,) = clock(up_gathered)
    (up_total,) = clock.run(lambda gathered: widen_gathered(gathered, rep_places(reps)), up_gathered)
    (input_total,) = clock.run(widen_pieces, *input_spread.finish(input_arrived))
    (small_arrived,) = clock.wait(small_moving)
    small = total_of(small_blocks[:1] + small_arrived)

    small = small + clock.token[0, 0]
    small_totals, at = [], 0
    for part in small_parts:
        size = part.shape[0] // shards
        small_totals.append(small[at : at + size])
        at += size
    return (
        block_out,
        tokens_gradient,
        small_totals[0],
        input_total,
        small_totals[2],
        small_totals[3],
        output_total,
        small_totals[1],
        gate_total,
        up_total,
        down_total,
    )


def solution(mesh):
    placed = (
        P(("rep", "shard"), None),
        P("rep", None),
        P("shard"),
        P("shard", None),
        P("shard"),
        P("shard", None),
        P("shard"),
        P("shard", None),
        P("shard", None),
        P("shard", None),
        P(("rep", "shard"), None),
    )
    return jax.shard_map(
        on_device,
        mesh=mesh,
        in_specs=placed,
        out_specs=(
            P(("rep", "shard"), None),
            P(("rep", "shard"), None),
            P("shard"),
            P("shard", None),
            P("shard"),
            P("shard"),
            P("shard", None),
            P("shard"),
            P("shard", None),
            P("shard", None),
            P("shard", None),
        ),
        check_vma=False,
    )
```

```python
import math

import jax
import jax.numpy as jnp
from jax import lax
from jax.experimental import pallas as pl
from jax.experimental.pallas import tpu as pltpu
from jax.sharding import PartitionSpec as P

QH = 12
KVH = 2
HD = 128
SEQS = 3


EPSILON = 1e-06
LOG_THETA = math.log(1000000.0)
MASKED = -1e30
VMEM_LIMIT = 56 * 1024 * 1024
TILE = 512
COST = pl.CostEstimate(flops=1, bytes_accessed=1, transcendentals=0)


def rope_tables(places, head_width):
    half_width = head_width // 2
    frequency = jnp.exp(jnp.arange(half_width, dtype=jnp.float32) * (-2.0 * LOG_THETA / head_width))
    angles = places.astype(jnp.float32)[:, None] * frequency[None, :]
    angles = jnp.concatenate([angles, angles], axis=-1)
    return (jnp.cos(angles), jnp.sin(angles))


def positions(segments):
    labels = jnp.arange(SEQS, dtype=jnp.int32)
    starts = jnp.sum((segments[None, :] < labels[:, None]).astype(jnp.int32), axis=1)
    own_start = jnp.sum(jnp.where(segments[:, None] == labels[None, :], starts[None, :], 0), axis=1)
    return jnp.arange(segments.shape[0], dtype=jnp.int32) - own_start


def rotate(field_rows, cosine_table, sine_table):
    half_width = field_rows.shape[-1] // 2
    turned = jnp.concatenate([-field_rows[..., half_width:], field_rows[..., :half_width]], axis=-1)
    return field_rows * cosine_table[:, None, :] + turned * sine_table[:, None, :]


def transposed_times(left_side, right_side):
    return lax.dot_general(
        left_side, right_side, (((0,), (0,)), ((), ())), preferred_element_type=jnp.float32
    )


def times_transposed(left_side, right_side):
    return lax.dot_general(
        left_side, right_side, (((1,), (1,)), ((), ())), preferred_element_type=jnp.float32
    )


def norm_back(normed_gradient, unit_rows, inverse_rms, gain_row):
    scaled = normed_gradient * gain_row
    return inverse_rms * (scaled - unit_rows * jnp.mean(scaled * unit_rows, axis=-1, keepdims=True))


class Line:
    def __init__(self, name, size, place, pairs, crossed=False):
        self.name, self.size, self.place, self.pairs = name, size, place, pairs
        self.crossed = crossed

    def shift(self, value, step):
        return lax.ppermute(value, self.name, self.pairs(step % self.size))

    def pass_on(self, value, up):
        places = range(self.size - 1)
        pairs = [(at, at + 1) if up else (at + 1, at) for at in places]
        return lax.ppermute(value, self.name, pairs)

    def behind(self, step):
        return lax.rem(self.place + (self.size - step % self.size), self.size)

    def ahead(self, step):
        return lax.rem(self.place + step % self.size, self.size) if step else self.place


def make_lines(reps, shards):
    inner = 2 if reps % 4 == 0 else 1
    outer = reps // (2 * inner)
    square = inner == outer

    def split(index):
        core, b, a = index % 2, (index // 2) % inner, index // (2 * inner)
        return core, b, a

    def join(core, b, a):
        return (a * inner + b) * 2 + core

    def first_pairs(step):
        pairs = []
        for index in range(reps):
            core, b, a = split(index)
            if square and core == 0:
                pairs.append((index, join(core, (b + step) % inner, a)))
            else:
                pairs.append((index, join(core, b, (a + step) % outer)))
        return pairs

    def second_pairs(step):
        pairs = []
        for index in range(reps):
            core, b, a = split(index)
            if square and core == 0:
                pairs.append((index, join(core, b, (a + step) % outer)))
            else:
                pairs.append((index, join(core, (b + step) % inner, a)))
        return pairs

    def core_pairs(step):
        pairs = []
        for index in range(reps):
            core, b, a = split(index)
            pairs.append((index, join((core + step) % 2, b, a)))
        return pairs

    def shard_pairs(step):
        return [(index, (index + step) % shards) for index in range(shards)]

    core, b, a = split(lax.axis_index("rep"))
    first, second = (jnp.where(core == 0, b, a), jnp.where(core == 0, a, b)) if square else (a, b)
    return (
        Line("shard", shards, lax.axis_index("shard"), shard_pairs),
        Line("rep", 2, core, core_pairs, square),
        Line("rep", outer, first, first_pairs),
        Line("rep", inner, second, second_pairs),
    )


def rep_places(reps):
    inner = 2 if reps % 4 == 0 else 1
    outer = reps // (2 * inner)
    places = []
    for index in range(reps):
        core, b, a = index % 2, (index // 2) % inner, index // (2 * inner)
        one, two = (b, a) if inner == outer and core == 0 else (a, b)
        places.append((core * outer + one) * inner + two)
    return places


def pick(array, index, axis):
    return lax.dynamic_index_in_dim(array, index, axis, keepdims=False)


def put(array, piece, index, axis):
    return lax.dynamic_update_index_in_dim(array, piece, index, axis)


def in_place_order(pieces, line):
    ordered = []
    for place in range(line.size):
        chosen = pieces[0]
        for step in range(1, line.size):
            chosen = jnp.where(line.behind(step) == place, pieces[step], chosen)
        ordered.append(chosen)
    return ordered


def tie(*arrays):
    return lax.optimization_barrier(arrays)


def gather_line(value, line):
    return [value] + [line.shift(value, step) for step in range(1, line.size)]


class Clock:
    def __init__(self):
        self.token = jnp.zeros((8, 128), jnp.float32)
        self.open = 0

    def __call__(self, *arrays):
        self.token, *arrays = tie(self.token, *arrays)
        return arrays

    def run(self, step, *arrays):
        return self(*step(*self(*arrays)))

    def send(self, line, values, steps):
        self.open += len(values)
        return [line.shift(value, step) for value, step in zip(self(*values), steps)]

    def pass_on(self, line, lower, upper):
        self.open += 2
        lower, upper = self(lower, upper)
        return [line.pass_on(lower, True), line.pass_on(upper, False)]

    def wait(self, *groups):
        flat = self(*[array for group in groups for array in group])
        self.open -= len(flat)
        parts, at = [], 0
        for group in groups:
            parts.append(flat[at : at + len(group)])
            at += len(group)
        return parts


def total_of(terms):
    total = terms[0].astype(jnp.float32)
    for term in terms[1:]:
        total = total + term.astype(jnp.float32)
    return total


class Halving:
    def __init__(self, clock, sent, own, core, first, second):
        self.clock, self.first, self.second = clock, first, second
        self.terms = [own]
        self.moving = clock.send(core, [sent], [1])

    def along(self, line, arrived):
        self.terms = self.terms + arrived
        steps = range(1, line.size)
        blocks = [
            total_of([pick(term, line.ahead(step), 0) for term in self.terms]).astype(jnp.bfloat16)
            for step in steps
        ]
        self.moving = self.clock.send(line, blocks, steps)
        self.terms = [pick(term, line.place, 0) for term in self.terms]

    def along_first(self, arrived):
        self.along(self.first, arrived)

    def along_second(self, arrived):
        self.along(self.second, arrived)

    def finish(self, arrived):
        return self.clock(total_of(self.terms + arrived).astype(jnp.bfloat16))[0]


class Spread:
    def __init__(self, clock, piece, core, first, second):
        self.clock, self.lines = clock, (core, first, second)
        self.pieces = [piece]
        steps = range(1, second.size)
        self.moving = clock.send(second, [piece] * len(steps), steps)

    def along(self, arrived):
        core, first, second = self.lines
        self.pieces = self.pieces + arrived
        steps = range(1, first.size)
        self.moving = self.clock.send(first, [jnp.stack(self.pieces)] * len(steps), steps)

    def over(self, arrived):
        core, first, second = self.lines
        rows = [jnp.stack(self.pieces)] + arrived
        self.pieces = jnp.concatenate(rows, axis=0)
        self.moving = self.clock.send(core, [self.pieces], [1])

    def finish(self, arrived):
        core, first, second = self.lines
        (others,) = arrived
        offsets = [(one, two) for one in range(first.size) for two in range(second.size)]
        placed = [(core.place, first.behind(one), second.behind(two)) for one, two in offsets]
        far, near = (second, first) if core.crossed else (first, second)
        placed += [(core.behind(1), far.behind(one), near.behind(two)) for one, two in offsets]
        places = [(c * first.size + f) * second.size + s for c, f, s in placed]
        return [jnp.stack(places).astype(jnp.int32), self.pieces, others]


def column_blocks(place, shard_place, *weights):
    count = len(weights)
    rows, columns = weights[0].shape[1:]
    shards = lax.axis_size("shard")
    block = columns // shards

    def body(places_ref, *refs):
        sources, outs = refs[:count], refs[count : 2 * count]
        held, cut, in_sems, out_sems = refs[2 * count :]
        loads = [
            pltpu.make_async_copy(sources[at].at[places_ref[0]], held.at[at], in_sems.at[at])
            for at in range(count)
        ]

        def store(at, z):
            ahead = lax.rem(z + shards - places_ref[1], shards)
            return pltpu.make_async_copy(cut.at[at, z], outs[at].at[ahead], out_sems.at[at, z])

        for load in loads:
            load.start()
        for at in range(count):
            loads[at].wait()
            for z in range(shards):
                cut[at, z] = held[at, :, z * block : (z + 1) * block]
                store(at, z).start()
        for at in range(count):
            for z in range(shards):
                store(at, z).wait()

    return pl.pallas_call(
        body,
        out_shape=[jax.ShapeDtypeStruct((shards, rows, block), jnp.bfloat16)] * count,
        in_specs=[pl.BlockSpec(memory_space=pltpu.SMEM)]
        + [pl.BlockSpec(memory_space=pl.ANY)] * count,
        out_specs=[pl.BlockSpec(memory_space=pl.ANY)] * count,
        scratch_shapes=[
            pltpu.VMEM((count, rows, columns), jnp.bfloat16),
            pltpu.VMEM((count, shards, rows, block), jnp.bfloat16),
            pltpu.SemaphoreType.DMA((count,)),
            pltpu.SemaphoreType.DMA((count, shards)),
        ],
        compiler_params=pltpu.CompilerParams(vmem_limit_bytes=VMEM_LIMIT),
        cost_estimate=COST,
        name="column_blocks",
    )(jnp.stack([place, shard_place]).astype(jnp.int32), *weights)


def place_blocks(order, places, pieces, others):
    half, groups, shards = pieces.shape[:3]

    def body(order_ref, places_ref, pieces_ref, others_ref, *rest):
        def source_of(g, k, r):
            return (pieces_ref if r < half else others_ref).at[r % half, g, k]

        move_blocks(source_of, lambda r: places_ref[r], order_ref, rest[:groups], *rest[groups:])

    return blocks_call(body, 2, 2, groups, shards, 2 * half, pieces.shape[3:])(
        order, places, pieces, others
    )


def place_gathered(order, gathered, groups):
    shards = lax.axis_size("shard")
    reps = gathered.shape[0] // (shards * groups)

    def body(order_ref, source, *rest):
        move_blocks(
            lambda g, k, r: source.at[(r * shards + k) * groups + g],
            lambda r: r,
            order_ref,
            rest[:groups],
            *rest[groups:],
        )

    return blocks_call(body, 1, 1, groups, shards, reps, gathered.shape[1:])(order, gathered)


def move_blocks(source_of, place_of, order_ref, outs, held, in_sems, out_sems):
    groups, shards, reps = in_sems.shape
    slabs = [(g, k) for g in range(groups) for k in range(shards)]

    def load(g, k, r):
        return pltpu.make_async_copy(
            source_of(g, k, r), held.at[g, k, place_of(r)], in_sems.at[g, k, r]
        )

    def store(g, k):
        return pltpu.make_async_copy(held.at[g, k], outs[g].at[order_ref[k]], out_sems.at[g, k])

    for g, k in slabs:
        for r in range(reps):
            load(g, k, r).start()
    for g, k in slabs:
        for r in range(reps):
            load(g, k, r).wait()
        store(g, k).start()
    for g, k in slabs:
        store(g, k).wait()


def blocks_call(body, scalars, sources, groups, shards, reps, block):
    whole = (shards, reps) + block
    return pl.pallas_call(
        body,
        out_shape=[jax.ShapeDtypeStruct(whole, jnp.bfloat16)] * groups,
        in_specs=[pl.BlockSpec(memory_space=pltpu.SMEM)] * scalars
        + [pl.BlockSpec(memory_space=pl.ANY)] * sources,
        out_specs=[pl.BlockSpec(memory_space=pl.ANY)] * groups,
        scratch_shapes=[
            pltpu.VMEM((groups,) + whole, jnp.bfloat16),
            pltpu.SemaphoreType.DMA((groups, shards, reps)),
            pltpu.SemaphoreType.DMA((groups, shards)),
        ],
        compiler_params=pltpu.CompilerParams(vmem_limit_bytes=VMEM_LIMIT),
        cost_estimate=COST,
        name="place_blocks",
    )


def widen_pieces(places, pieces, others):
    half, rows, columns = pieces.shape
    reps = 2 * half
    strip = next(size for size in (16, 8, rows) if rows % size == 0)

    def body(places_ref, pieces_ref, others_ref, out_ref, narrow, wide, in_sems, out_sems):
        loads = [
            pltpu.make_async_copy(
                (pieces_ref if r < half else others_ref).at[r % half], narrow.at[r], in_sems.at[r]
            )
            for r in range(reps)
        ]
        stores = [
            pltpu.make_async_copy(wide.at[r], out_ref.at[places_ref[r]], out_sems.at[r])
            for r in range(reps)
        ]
        for load in loads:
            load.start()
        for r in range(reps):
            loads[r].wait()

            def convert(at, carry):
                cut = pl.ds(pl.multiple_of(at * strip, strip), strip)
                wide[r, cut, :] = narrow[r, cut, :].astype(jnp.float32)
                return carry

            lax.fori_loop(0, rows // strip, convert, 0)
            stores[r].start()
        for store in stores:
            store.wait()

    result = pl.pallas_call(
        body,
        out_shape=jax.ShapeDtypeStruct((reps, rows, columns), jnp.float32),
        in_specs=[pl.BlockSpec(memory_space=pltpu.SMEM)]
        + [pl.BlockSpec(memory_space=pl.ANY)] * 2,
        out_specs=pl.BlockSpec(memory_space=pl.ANY),
        scratch_shapes=[
            pltpu.VMEM((reps, rows, columns), jnp.bfloat16),
            pltpu.VMEM((reps, rows, columns), jnp.float32),
            pltpu.SemaphoreType.DMA((reps,)),
            pltpu.SemaphoreType.DMA((reps,)),
        ],
        compiler_params=pltpu.CompilerParams(vmem_limit_bytes=VMEM_LIMIT),
        cost_estimate=COST,
        name="widen_pieces",
    )(places, pieces, others)
    return (result.reshape(reps * rows, columns),)


def widen_gathered(gathered, order):
    reps, rows, columns = gathered.shape
    strip = next(size for size in (16, 8, rows) if rows % size == 0)

    def body(source_ref, out_ref, narrow, wide, in_sems, out_sems):
        loads = [
            pltpu.make_async_copy(source_ref.at[r], narrow.at[r], in_sems.at[r])
            for r in range(reps)
        ]
        stores = [
            pltpu.make_async_copy(wide.at[r], out_ref.at[order[r]], out_sems.at[r])
            for r in range(reps)
        ]
        for load in loads:
            load.start()
        for r in range(reps):
            loads[r].wait()

            def convert(at, carry):
                cut = pl.ds(pl.multiple_of(at * strip, strip), strip)
                wide[r, cut, :] = narrow[r, cut, :].astype(jnp.float32)
                return carry

            lax.fori_loop(0, rows // strip, convert, 0)
            stores[r].start()
        for store in stores:
            store.wait()

    result = pl.pallas_call(
        body,
        out_shape=jax.ShapeDtypeStruct((reps, rows, columns), jnp.float32),
        in_specs=[pl.BlockSpec(memory_space=pl.ANY)],
        out_specs=pl.BlockSpec(memory_space=pl.ANY),
        scratch_shapes=[
            pltpu.VMEM((reps, rows, columns), jnp.bfloat16),
            pltpu.VMEM((reps, rows, columns), jnp.float32),
            pltpu.SemaphoreType.DMA((reps,)),
            pltpu.SemaphoreType.DMA((reps,)),
        ],
        compiler_params=pltpu.CompilerParams(vmem_limit_bytes=VMEM_LIMIT),
        cost_estimate=COST,
        name="widen_gathered",
    )(gathered)
    return (result.reshape(reps * rows, columns),)


def resident(shape):
    return pl.BlockSpec(shape, lambda i: (0, 0), pipeline_mode=pl.Buffered(1))


def feed_forward(rows, cotangents, gate_matrix, up_matrix, down_matrix):
    count, width = rows.shape
    units = gate_matrix.shape[1]
    steps = pl.cdiv(units, TILE)
    slabs = next(size for size in range(min(steps, width // 128), 0, -1) if width % (128 * size) == 0)
    slab = width // slabs

    def body(
        rows_ref,
        cotangents_ref,
        gate_ref,
        up_ref,
        down_ref,
        inner_ref,
        d_gate_ref,
        d_up_ref,
        turned_rows_ref,
        turned_inner_ref,
    ):
        gate = jnp.dot(rows_ref[...], gate_ref[...], preferred_element_type=jnp.float32)
        up = jnp.dot(rows_ref[...], up_ref[...], preferred_element_type=jnp.float32)
        sigmoid = jax.nn.sigmoid(gate)
        silu = gate * sigmoid
        inner = (silu * up).astype(jnp.bfloat16)
        inner_ref[...] = inner
        turned_inner_ref[...] = inner.T
        d_inner = times_transposed(cotangents_ref[...], down_ref[...])
        d_up_ref[...] = (d_inner * silu).astype(jnp.bfloat16)
        d_gate_ref[...] = (d_inner * up * sigmoid * (1.0 + gate * (1.0 - sigmoid))).astype(
            jnp.bfloat16
        )
        for step in range(slabs):

            @pl.when(pl.program_id(0) == step)
            def turn():
                turned_rows_ref[...] = rows_ref[:, step * slab : (step + 1) * slab].T

    columns = pl.BlockSpec((width, TILE), lambda i: (0, i))
    results = pl.BlockSpec((count, TILE), lambda i: (0, i))
    return pl.pallas_call(
        body,
        grid=(steps,),
        out_shape=[jax.ShapeDtypeStruct((count, units), jnp.bfloat16)] * 3
        + [
            jax.ShapeDtypeStruct((width, count), jnp.bfloat16),
            jax.ShapeDtypeStruct((units, count), jnp.bfloat16),
        ],
        in_specs=[
            resident((count, width)),
            resident((count, width)),
            columns,
            columns,
            pl.BlockSpec((TILE, width), lambda i: (i, 0)),
        ],
        out_specs=[results] * 3
        + [
            pl.BlockSpec((slab, count), lambda i: (jnp.minimum(i, slabs - 1), 0)),
            pl.BlockSpec((TILE, count), lambda i: (i, 0)),
        ],
        compiler_params=pltpu.CompilerParams(vmem_limit_bytes=VMEM_LIMIT),
        cost_estimate=COST,
        name="feed_forward",
    )(rows, cotangents, gate_matrix, up_matrix, down_matrix)


def split_gradient(left, right, groups, places, core_place, turned):
    rows, count = left.shape if turned else left.shape[::-1]
    columns = right.shape[1]
    half = rows // (2 * groups)
    part = half // places

    def body(core_ref, left_ref, right_ref, other_ref, own_ref, *scratch):
        if turned:
            rows_ref = left_ref
        else:
            (rows_ref,) = scratch

            @pl.when(pl.program_id(0) == 0)
            def turn():
                rows_ref[...] = left_ref[...].T

        core = core_ref[0]
        for out_ref, which in ((other_ref, 1 - core), (own_ref, core)):
            halves = [
                rows_ref[pl.ds(pl.multiple_of((2 * group + which) * half, 16), half), :]
                for group in range(groups)
            ]
            product = jnp.dot(
                jnp.concatenate(halves, axis=0), right_ref[...], preferred_element_type=jnp.float32
            )
            for group in range(groups):
                for place in range(places):
                    at = group * half + place * part
                    out_ref[place, group] = product[at : at + part].astype(jnp.bfloat16)

    return pl.pallas_call(
        body,
        grid=(pl.cdiv(columns, TILE),),
        out_shape=[jax.ShapeDtypeStruct((places, groups, part, columns), jnp.bfloat16)] * 2,
        in_specs=[
            pl.BlockSpec(memory_space=pltpu.SMEM),
            resident(left.shape),
            pl.BlockSpec((count, TILE), lambda i: (0, i)),
        ],
        out_specs=[pl.BlockSpec((places, groups, part, TILE), lambda i: (0, 0, 0, i))] * 2,
        scratch_shapes=[] if turned else [pltpu.VMEM((rows, count), jnp.bfloat16)],
        compiler_params=pltpu.CompilerParams(vmem_limit_bytes=VMEM_LIMIT),
        cost_estimate=COST,
        name="split_gradient",
    )(core_place.reshape(1).astype(jnp.int32), left, right)


def ordered_gradient(left, right, shards, order):
    reps = len(order)
    rows, count = left.shape
    columns = right.shape[1]
    part = rows // (shards * reps)

    def body(left_ref, right_ref, out_ref):
        product = jnp.dot(left_ref[...], right_ref[...], preferred_element_type=jnp.float32)
        for z in range(shards):
            for r in range(reps):
                at = (z * reps + order[r]) * part
                out_ref[r, z] = product[at : at + part].astype(jnp.bfloat16)

    return pl.pallas_call(
        body,
        grid=(pl.cdiv(columns, TILE),),
        out_shape=[jax.ShapeDtypeStruct((reps, shards, part, columns), jnp.bfloat16)],
        in_specs=[
            resident((rows, count)),
            pl.BlockSpec((count, TILE), lambda i: (0, i)),
        ],
        out_specs=[pl.BlockSpec((reps, shards, part, TILE), lambda i: (0, 0, 0, i))],
        compiler_params=pltpu.CompilerParams(vmem_limit_bytes=VMEM_LIMIT),
        cost_estimate=COST,
        name="ordered_gradient",
    )(left, right)


def rows_product(lefts, rights, turned, blocks):
    count, depth = lefts[0].shape
    columns = rights[0].shape[0 if turned else 1]
    pairs, part = len(lefts), count // blocks

    def body(*refs):
        total = None
        for left_ref, right_ref in zip(refs[:pairs], refs[pairs : 2 * pairs]):
            if turned:
                product = times_transposed(left_ref[...], right_ref[...])
            else:
                product = jnp.dot(
                    left_ref[...], right_ref[...], preferred_element_type=jnp.float32
                )
            total = product if total is None else total + product
        for block in range(blocks):
            refs[2 * pairs + block][...] = total[block * part : (block + 1) * part].astype(
                jnp.bfloat16
            )

    right_spec = (
        pl.BlockSpec((TILE, depth), lambda i: (i, 0))
        if turned
        else pl.BlockSpec((depth, TILE), lambda i: (0, i))
    )
    return pl.pallas_call(
        body,
        grid=(pl.cdiv(columns, TILE),),
        out_shape=[jax.ShapeDtypeStruct((part, columns), jnp.bfloat16)] * blocks,
        in_specs=[resident((count, depth))] * pairs + [right_spec] * pairs,
        out_specs=[pl.BlockSpec((part, TILE), lambda i: (0, i))] * blocks,
        compiler_params=pltpu.CompilerParams(vmem_limit_bytes=VMEM_LIMIT),
        cost_estimate=COST,
        name="rows_product",
    )(*lefts, *rights)


def kept_bias(row_segments, row_index, key_segments, key_index):
    kept = (row_segments == key_segments) & (key_index <= row_index)
    return jnp.where(kept, 0.0, MASKED)


def in_vmem(count):
    return [pl.BlockSpec(memory_space=pltpu.VMEM)] * count


def attention_forward(projected, cosine, signed_sine, pairs, rows, keys):
    count = projected.shape[0]
    per_group = QH // KVH
    scale = 1.0 / math.sqrt(HD)
    shape = (KVH, per_group * count, HD)

    def body(projected_ref, cosine_ref, sine_ref, pairs_ref, rows_ref, keys_ref, queries_ref, out_ref):
        bias = kept_bias(rows_ref[:, 0:1], rows_ref[:, 1:2], keys_ref[0:1, :], keys_ref[1:2, :])
        for k in range(KVH):
            for h in range(per_group):
                at = (k * per_group + h) * HD
                field = projected_ref[:, at : at + HD]
                queries_ref[k, h * count : (h + 1) * count, :] = (
                    field * cosine_ref[...] + pltpu.roll(field, HD // 2, 1) * sine_ref[...]
                ).astype(jnp.bfloat16)
            keys_here = pairs_ref[:, k * HD : (k + 1) * HD]
            values_here = pairs_ref[:, (KVH + k) * HD : (KVH + k + 1) * HD]
            scores = times_transposed(queries_ref[k], keys_here) * scale + bias
            powers = jnp.exp(scores - jnp.max(scores, axis=1, keepdims=True))
            shares = powers * (1.0 / jnp.sum(powers, axis=1, keepdims=True))
            result = jnp.dot(
                shares.astype(jnp.bfloat16), values_here, preferred_element_type=jnp.float32
            ).astype(jnp.bfloat16)
            for h in range(per_group):
                at = (k * per_group + h) * HD
                out_ref[:, at : at + HD] = result[h * count : (h + 1) * count]

    return pl.pallas_call(
        body,
        out_shape=[
            jax.ShapeDtypeStruct(shape, jnp.bfloat16),
            jax.ShapeDtypeStruct((count, QH * HD), jnp.bfloat16),
        ],
        in_specs=in_vmem(6),
        out_specs=in_vmem(2),
        compiler_params=pltpu.CompilerParams(vmem_limit_bytes=VMEM_LIMIT),
        cost_estimate=COST,
        name="attention_forward",
    )(projected, cosine, signed_sine, pairs, rows, keys)


def attention_backward(queries, gradient, pairs, cosine, signed_sine, rows, keys, blocks):
    count = gradient.shape[0]
    per_group = QH // KVH
    scale = 1.0 / math.sqrt(HD)
    group_rows = pairs.shape[0]
    part = group_rows // blocks

    def body(queries_ref, gradient_ref, pairs_ref, cosine_ref, sine_ref, rows_ref, keys_ref, d_ref, *outs):
        block_refs, stacked = outs[:blocks], outs[blocks]
        bias = kept_bias(rows_ref[0:1, :], rows_ref[1:2, :], keys_ref[:, 0:1], keys_ref[:, 1:2])
        for k in range(KVH):
            for h in range(per_group):
                at = (k * per_group + h) * HD
                stacked[h * count : (h + 1) * count, :] = gradient_ref[:, at : at + HD]
            keys_here = pairs_ref[:, k * HD : (k + 1) * HD]
            values_here = pairs_ref[:, (KVH + k) * HD : (KVH + k + 1) * HD]
            scores = times_transposed(keys_here, queries_ref[k]) * scale + bias
            powers = jnp.exp(scores - jnp.max(scores, axis=0, keepdims=True))
            shares = powers * (1.0 / jnp.sum(powers, axis=0, keepdims=True))
            d_shares = times_transposed(values_here, stacked[...])
            dots = jnp.sum(shares * d_shares, axis=0, keepdims=True)
            d_scores = (shares * (d_shares - dots)).astype(jnp.bfloat16)
            d_keys = jnp.dot(d_scores, queries_ref[k], preferred_element_type=jnp.float32) * scale
            d_values = jnp.dot(
                shares.astype(jnp.bfloat16), stacked[...], preferred_element_type=jnp.float32
            )
            for block in range(blocks):
                cut = slice(block * part, (block + 1) * part)
                block_refs[block][:, k * HD : (k + 1) * HD] = d_keys[cut].astype(jnp.bfloat16)
                block_refs[block][:, (KVH + k) * HD : (KVH + k + 1) * HD] = d_values[cut].astype(
                    jnp.bfloat16
                )
            d_queries = transposed_times(d_scores, keys_here) * scale
            for h in range(per_group):
                at = (k * per_group + h) * HD
                field = d_queries[h * count : (h + 1) * count]
                d_ref[:, at : at + HD] = (
                    field * cosine_ref[...] - pltpu.roll(field, HD // 2, 1) * sine_ref[...]
                ).astype(jnp.bfloat16)

    return pl.pallas_call(
        body,
        out_shape=[jax.ShapeDtypeStruct((count, QH * HD), jnp.bfloat16)]
        + [jax.ShapeDtypeStruct((part, 2 * KVH * HD), jnp.bfloat16)] * blocks,
        in_specs=in_vmem(7),
        out_specs=in_vmem(1 + blocks),
        scratch_shapes=[pltpu.VMEM((per_group * count, HD), jnp.bfloat16)],
        compiler_params=pltpu.CompilerParams(vmem_limit_bytes=VMEM_LIMIT),
        cost_estimate=COST,
        name="attention_backward",
    )(queries, gradient, pairs, cosine, signed_sine, rows, keys)


def join_projected(d_queries, pair_terms, cosine, signed_sine):
    count, query_width = d_queries.shape
    pair_width = KVH * HD
    terms = len(pair_terms)

    def body(d_queries_ref, cosine_ref, sine_ref, *refs):
        term_refs, out_ref, sum_ref = refs[:terms], refs[terms], refs[terms + 1]
        out_ref[:, :query_width] = d_queries_ref[...]
        for at in range(0, 2 * pair_width, HD):
            field = total_of([term[:, at : at + HD] for term in term_refs])
            if at < pair_width:
                field = field * cosine_ref[...] - pltpu.roll(field, HD // 2, 1) * sine_ref[...]
            out_ref[:, query_width + at : query_width + at + HD] = field.astype(jnp.bfloat16)
        sum_ref[...] = jnp.sum(out_ref[...].astype(jnp.float32), axis=0, keepdims=True)

    return pl.pallas_call(
        body,
        out_shape=[
            jax.ShapeDtypeStruct((count, query_width + 2 * pair_width), jnp.bfloat16),
            jax.ShapeDtypeStruct((1, query_width + 2 * pair_width), jnp.float32),
        ],
        in_specs=in_vmem(3 + terms),
        out_specs=in_vmem(2),
        cost_estimate=COST,
        name="join_projected",
    )(d_queries, cosine, signed_sine, *pair_terms)


def on_device(
    tokens,
    segment_ids,
    first_gain,
    input_weight,
    input_bias,
    output_weight,
    second_gain,
    gate_weight,
    up_weight,
    down_weight,
    output_cotangent,
):
    bf16, f32 = jnp.bfloat16, jnp.float32
    shards, reps = lax.axis_size("shard"), lax.axis_size("rep")
    shard, core, first, second = make_lines(reps, shards)
    rep_place = (core.place * first.size + first.place) * second.size + second.place
    own_rows, width = tokens.shape
    segments = segment_ids[0]
    per_group = QH // KVH
    query_width = QH * HD
    pair_width = KVH * HD
    first_row = shard.place * own_rows
    part_rows = input_weight.shape[0] // reps
    hidden_units = gate_weight.shape[1]
    block_units = hidden_units // shards
    clock = Clock()
    z_order = jnp.stack([shard.behind(step) for step in range(shards)]).astype(jnp.int32)

    def weight_piece(weight, place):
        return pick(weight.reshape(reps, part_rows, weight.shape[1]), place, 0)

    def spread(piece):
        return Spread(clock, piece, core, first, second)

    def blocks_of(blocks):
        return [pick(blocks, shard.ahead(step), 0) for step in range(shards)]

    steps = range(1, shards)

    def send_blocks(blocks):
        return clock.send(shard, blocks[1:], steps)

    def send_around(value):
        return clock.send(shard, [value] * len(steps), steps)

    def send_back(rows):
        return clock.send(shard, rows, [shards - step for step in steps])

    rep_index = lax.axis_index("rep")
    input_matrix = lax.all_gather(
        weight_piece(input_weight, rep_index), ("shard", "rep"), axis=0, tiled=True
    )
    shard_vectors = jnp.concatenate([first_gain, second_gain, input_bias])
    vector_row = jnp.pad(shard_vectors, (0, output_weight.shape[1] - shard_vectors.shape[0]))
    own_output = jnp.concatenate(
        [weight_piece(output_weight, rep_place), vector_row[None]], axis=0
    )
    output_moving = send_around(own_output)
    gate_blocks, up_blocks = clock.run(
        lambda *weights: column_blocks(rep_index, shard.place, *weights),
        gate_weight.reshape(reps, part_rows, hidden_units),
        up_weight.reshape(reps, part_rows, hidden_units),
    )
    (output_rows,) = clock.wait(output_moving)
    output_rows = [own_output] + output_rows

    output_spread = spread(jnp.stack([rows[:part_rows] for rows in output_rows])[None])
    gate_moving = send_blocks(gate_blocks)
    vector_rows = jnp.stack(in_place_order([rows[part_rows] for rows in output_rows], shard))
    own_gain = first_gain.shape[0]
    gain_one = vector_rows[:, :own_gain].reshape(width).astype(f32)
    gain_two = vector_rows[:, own_gain : 2 * own_gain].reshape(width).astype(f32)
    shift_row = (
        vector_rows[:, 2 * own_gain : shard_vectors.shape[0]].reshape(-1).astype(f32)
    )
    places = positions(segments)
    cosine_table, sine_table = rope_tables(
        lax.dynamic_slice_in_dim(places, first_row, own_rows), HD
    )
    signed_sine = jnp.concatenate(
        [-sine_table[:, : HD // 2], sine_table[:, HD // 2 :]], axis=1
    )
    own_segments = lax.dynamic_slice_in_dim(segments, first_row, own_rows)
    row_index = jnp.arange(own_rows, dtype=jnp.int32)
    key_index = jnp.concatenate([shard.behind(step) * own_rows + row_index for step in range(shards)])
    key_segments = jnp.concatenate(
        [
            lax.dynamic_slice_in_dim(segments, shard.behind(step) * own_rows, own_rows)
            for step in range(shards)
        ]
    )
    key_marks = jnp.stack([key_segments, key_index])
    row_marks = jnp.tile(jnp.stack([own_segments, first_row + row_index]), (1, per_group))
    wide_tokens = tokens.astype(f32)
    inverse_one = lax.rsqrt(jnp.mean(wide_tokens * wide_tokens, axis=-1, keepdims=True) + EPSILON)
    unit_one = wide_tokens * inverse_one
    normed_one = (unit_one * gain_one).astype(bf16)
    (
        normed_one,
        cosine_table,
        sine_table,
        signed_sine,
        key_marks,
        row_marks,
    ) = clock(normed_one, cosine_table, sine_table, signed_sine, key_marks, row_marks)
    output_arrived, gate_rows = clock.wait(output_spread.moving, gate_moving)

    output_spread.along(output_arrived)
    up_moving = send_blocks(up_blocks)
    output_arrived, up_rows = clock.wait(output_spread.moving, up_moving)

    gate_up = jnp.stack(
        [row for pair in zip([gate_blocks[0]] + gate_rows, [up_blocks[0]] + up_rows) for row in pair]
    )
    gate_up = lax.all_gather(clock(gate_up)[0], "rep", axis=0, tiled=True)
    passed = [[output_cotangent] * 2]
    passing = clock.pass_on(shard, *passed[-1])
    output_spread.over(output_arrived)
    input_matrix, normed_one = clock(input_matrix, normed_one)
    projected = jnp.dot(normed_one, input_matrix, preferred_element_type=f32) + shift_row
    key_part = rotate(
        projected[:, query_width : query_width + pair_width].reshape(own_rows, KVH, HD),
        cosine_table,
        sine_table,
    )
    (own_pairs,) = clock(
        jnp.concatenate(
            [key_part.reshape(own_rows, pair_width), projected[:, query_width + pair_width :]],
            axis=1,
        ).astype(bf16)
    )
    arrived, output_arrived = clock.wait(passing, output_spread.moving)
    passed.append(arrived)

    pair_moving = send_around(own_pairs)
    passing = clock.pass_on(shard, *passed[-1]) if shards > 2 else []
    pair_rows, arrived = clock.wait(pair_moving, passing)
    passed.append(arrived)
    pairs = jnp.concatenate([own_pairs] + pair_rows, axis=0)

    passing = clock.pass_on(shard, *passed[-1]) if shards > 3 else []
    (output_matrix,) = clock.run(place_blocks, z_order, *output_spread.finish(output_arrived))
    output_matrix = output_matrix.reshape(width, width)
    queries, attention_low = clock.run(
        attention_forward, projected, cosine_table, signed_sine, pairs, row_marks.T, key_marks
    )
    hidden = wide_tokens + jnp.dot(attention_low, output_matrix, preferred_element_type=f32)
    inverse_two = lax.rsqrt(jnp.mean(hidden * hidden, axis=-1, keepdims=True) + EPSILON)
    unit_two = hidden * inverse_two
    (normed_two,) = clock((unit_two * gain_two).astype(bf16))
    (arrived,) = clock.wait(passing)
    passed.append(arrived)

    normed_moving = send_around(normed_two)
    gate_matrix, up_matrix = clock.run(
        lambda order, gathered: place_gathered(order, gathered, 2), z_order, gate_up
    )
    gate_matrix = gate_matrix.reshape(width, block_units)
    up_matrix = up_matrix.reshape(width, block_units)
    (normed_arrived,) = clock.wait(normed_moving)
    while len(passed) < shards:
        (arrived,) = clock.wait(clock.pass_on(shard, *passed[-1]))
        passed.append(arrived)
    group_normed = jnp.concatenate([normed_two] + normed_arrived, axis=0)
    cotangents = jnp.concatenate(
        [output_cotangent]
        + [
            jnp.where(shard.place >= step, passed[step][0], passed[shards - step][1])
            for step in steps
        ],
        axis=0,
    )

    inner_act, d_gate, d_up, turned_normed, turned_inner = clock.run(
        feed_forward, group_normed, cotangents, gate_matrix, up_matrix, down_weight
    )

    def split_halves(left, right, groups, turned):
        count = first.size * second.size
        halves = clock.run(
            lambda left, right: split_gradient(left, right, groups, count, core.place, turned),
            left,
            right,
        )
        return [half.reshape((first.size, second.size) + half.shape[1:]) for half in halves]

    def side_by_side(rows):
        return clock(jnp.concatenate(in_place_order(rows, shard), axis=1))[0]

    def sum_over_rep(blocks):
        return lax.psum_scatter(blocks, "rep", scatter_dimension=0, tiled=True)

    def row_sum(own, arrived):
        return clock(total_of(own + arrived).astype(bf16))[0]

    def send_some(rows, chosen):
        return clock.send(shard, [rows[k] for k in chosen], [shards - 1 - k for k in chosen])

    edges = sorted({0, shards - 2})
    inside = list(range(1, shards - 2))

    def gather_rep(piece):
        return lax.all_gather(piece[None], "rep", axis=0, tiled=True)

    up_halves = split_halves(turned_normed, d_up, shards, True)

    up = Halving(clock, *up_halves, core, first, second)
    (gate_blocks,) = clock.run(
        lambda left, right: ordered_gradient(left, right, shards, rep_places(reps)),
        turned_normed,
        d_gate,
    )
    (up_arrived,) = clock.wait(up.moving)

    gate_piece = sum_over_rep(clock(gate_blocks)[0].reshape(width, block_units))
    up.along_first(up_arrived)
    normed_own, *normed_partial = clock.run(
        lambda *operands: rows_product(operands[:2], operands[2:], True, shards),
        d_gate,
        d_up,
        gate_matrix,
        up_matrix,
    )
    normed_moving = send_some(normed_partial, edges)
    down_halves = split_halves(turned_inner, cotangents, 1, True)
    up_arrived, normed_arrived = clock.wait(up.moving, normed_moving)

    up.along_second(up_arrived)
    down = Halving(clock, *down_halves, core, first, second)
    normed_moving = send_some(normed_partial, inside)
    block_own, *block_partial = clock.run(
        lambda left, right: rows_product((left,), (right,), False, shards), inner_act, down_weight
    )
    up_arrived, down_arrived, more_arrived = clock.wait(up.moving, down.moving, normed_moving)

    down.along_first(down_arrived)
    up_blocks = clock(*blocks_of(up.finish(up_arrived)))
    up_moving = send_blocks(up_blocks)
    normed_two_gradient = total_of([normed_own] + normed_arrived + more_arrived)
    gain_two_gradient = jnp.sum(normed_two_gradient * unit_two, axis=0)
    hidden_gradient = output_cotangent.astype(f32) + norm_back(
        normed_two_gradient, unit_two, inverse_two, gain_two
    )
    (branch_gradient,) = clock(hidden_gradient.astype(bf16))
    (attention_gradient,) = clock(times_transposed(branch_gradient, output_matrix).astype(bf16))
    d_queries, pair_own, *pair_partial = clock.run(
        lambda *operands: attention_backward(*operands, shards),
        queries,
        attention_gradient,
        pairs,
        cosine_table,
        signed_sine,
        row_marks,
        key_marks.T,
    )
    output_halves = split_halves(attention_low, branch_gradient, shards, False)
    down_arrived, up_rows = clock.wait(down.moving, up_moving)

    pair_moving = send_back(pair_partial)
    output = Halving(clock, *output_halves, core, first, second)
    down.along_second(down_arrived)
    up_piece = side_by_side(up_blocks[:1] + up_rows)
    pair_arrived, output_arrived, down_arrived = clock.wait(
        pair_moving, output.moving, down.moving
    )

    (gate_piece,) = clock(gate_piece)
    down_gathered = gather_rep(down.finish(down_arrived)[0])
    projected_gradient, bias_sum = clock.run(
        lambda *operands: join_projected(operands[0], operands[3:], *operands[1:3]),
        d_queries,
        cosine_table,
        signed_sine,
        pair_own,
        *pair_arrived,
    )
    projected_halves = split_halves(normed_one, projected_gradient, shards, False)

    projected = Halving(clock, *projected_halves, core, first, second)
    output.along_first(output_arrived)
    gate_blocks = clock(*blocks_of(gate_piece.reshape(shards, part_rows, block_units)))
    gate_moving = send_blocks(gate_blocks)
    projected_gradient, hidden_gradient = clock(projected_gradient, hidden_gradient)
    normed_one_gradient = times_transposed(projected_gradient, input_matrix)
    gain_one_gradient = jnp.sum(normed_one_gradient * unit_one, axis=0)
    (tokens_gradient,) = clock(
        (
            hidden_gradient + norm_back(normed_one_gradient, unit_one, inverse_one, gain_one)
        ).astype(bf16)
    )
    projected_arrived, output_arrived, gate_rows = clock.wait(
        projected.moving, output.moving, gate_moving
    )

    projected.along_first(projected_arrived)
    output.along_second(output_arrived)
    gate_spread = spread(side_by_side(gate_blocks[:1] + gate_rows))
    block_moving = send_some(block_partial, inside)
    bias_gradient = bias_sum[0]
    bias_split = query_width + pair_width
    small_parts = (
        gain_one_gradient,
        gain_two_gradient,
        bias_gradient[:bias_split],
        bias_gradient[bias_split:],
    )
    (small,) = clock(
        jnp.concatenate([part.reshape(shards, -1) for part in small_parts], axis=1)
    )
    (down_gathered,) = clock(down_gathered)
    up_gathered = gather_rep(clock(up_piece)[0])
    (down_total,) = clock.run(lambda gathered: widen_gathered(gathered, rep_places(reps)), down_gathered)
    projected_arrived, output_arrived, gate_arrived, block_arrived = clock.wait(
        projected.moving, output.moving, gate_spread.moving, block_moving
    )

    projected.along_second(projected_arrived)
    gate_spread.along(gate_arrived)
    output_blocks = clock(*blocks_of(output.finish(output_arrived)))
    output_moving = send_blocks(output_blocks)
    projected_arrived, gate_arrived, output_rows = clock.wait(
        projected.moving, gate_spread.moving, output_moving
    )

    input_blocks = clock(*blocks_of(projected.finish(projected_arrived)))
    input_moving = send_blocks(input_blocks)
    output_spread = spread(row_sum(output_blocks[:1], output_rows))
    gate_spread.over(gate_arrived)
    input_rows, output_arrived, gate_arrived = clock.wait(
        input_moving, output_spread.moving, gate_spread.moving
    )

    input_spread = spread(row_sum(input_blocks[:1], input_rows))
    output_spread.along(output_arrived)
    small_moving = clock.send(core, [small], [1])
    block_moving = send_some(block_partial, edges[:1])
    (up_gathered,) = clock(up_gathered)
    (up_total,) = clock.run(lambda gathered: widen_gathered(gathered, rep_places(reps)), up_gathered)
    input_arrived, output_arrived, small_arrived, more_arrived = clock.wait(
        input_spread.moving, output_spread.moving, small_moving, block_moving
    )
    small = total_of([small] + small_arrived)
    block_arrived = block_arrived + more_arrived

    input_spread.along(input_arrived)
    output_spread.over(output_arrived)
    small_moving = clock.send(first, [small] * (first.size - 1), range(1, first.size))
    block_moving = send_some(block_partial, edges[1:])
    (gate_total,) = clock.run(widen_pieces, *gate_spread.finish(gate_arrived))
    input_arrived, output_arrived, small_arrived, more_arrived = clock.wait(
        input_spread.moving, output_spread.moving, small_moving, block_moving
    )
    small = total_of([small] + small_arrived)
    block_arrived = block_arrived + more_arrived

    input_spread.over(input_arrived)
    small_moving = clock.send(second, [small] * (second.size - 1), range(1, second.size))
    (output_total,) = clock.run(widen_pieces, *output_spread.finish(output_arrived))
    (block_out,) = clock(total_of([hidden, block_own] + block_arrived).astype(bf16))
    input_arrived, small_arrived = clock.wait(input_spread.moving, small_moving)
    small_blocks = clock(*blocks_of(total_of([small] + small_arrived)))

    small_moving = send_blocks(small_blocks)
    (input_total,) = clock.run(widen_pieces, *input_spread.finish(input_arrived))
    (small_arrived,) = clock.wait(small_moving)
    small = total_of(small_blocks[:1] + small_arrived)

    small = small + clock.token[0, 0]
    small_totals, at = [], 0
    for part in small_parts:
        size = part.shape[0] // shards
        small_totals.append(small[at : at + size])
        at += size
    return (
        block_out,
        tokens_gradient,
        small_totals[0],
        input_total,
        small_totals[2],
        small_totals[3],
        output_total,
        small_totals[1],
        gate_total,
        up_total,
        down_total,
    )


def solution(mesh):
    placed = (
        P(("rep", "shard"), None),
        P("rep", None),
        P("shard"),
        P("shard", None),
        P("shard"),
        P("shard", None),
        P("shard"),
        P("shard", None),
        P("shard", None),
        P("shard", None),
        P(("rep", "shard"), None),
    )
    return jax.shard_map(
        on_device,
        mesh=mesh,
        in_specs=placed,
        out_specs=(
            P(("rep", "shard"), None),
            P(("rep", "shard"), None),
            P("shard"),
            P("shard", None),
            P("shard"),
            P("shard"),
            P("shard", None),
            P("shard"),
            P("shard", None),
            P("shard", None),
            P("shard", None),
        ),
        check_vma=False,
    )
```

```python
import math

import jax
import jax.numpy as jnp
from jax import lax
from jax.experimental import pallas as pl
from jax.experimental.pallas import tpu as pltpu
from jax.sharding import PartitionSpec as P

QH = 12
KVH = 2
HD = 128
SEQS = 3


EPSILON = 1e-06
LOG_THETA = math.log(1000000.0)
MASKED = -1e30
VMEM_LIMIT = 56 * 1024 * 1024
TILE = 512
COST = pl.CostEstimate(flops=1, bytes_accessed=1, transcendentals=0)


def rope_tables(places, head_width):
    half_width = head_width // 2
    frequency = jnp.exp(jnp.arange(half_width, dtype=jnp.float32) * (-2.0 * LOG_THETA / head_width))
    angles = places.astype(jnp.float32)[:, None] * frequency[None, :]
    angles = jnp.concatenate([angles, angles], axis=-1)
    return (jnp.cos(angles), jnp.sin(angles))


def positions(segments):
    labels = jnp.arange(SEQS, dtype=jnp.int32)
    starts = jnp.sum((segments[None, :] < labels[:, None]).astype(jnp.int32), axis=1)
    own_start = jnp.sum(jnp.where(segments[:, None] == labels[None, :], starts[None, :], 0), axis=1)
    return jnp.arange(segments.shape[0], dtype=jnp.int32) - own_start


def rotate(field_rows, cosine_table, sine_table):
    half_width = field_rows.shape[-1] // 2
    turned = jnp.concatenate([-field_rows[..., half_width:], field_rows[..., :half_width]], axis=-1)
    return field_rows * cosine_table[:, None, :] + turned * sine_table[:, None, :]


def transposed_times(left_side, right_side):
    return lax.dot_general(
        left_side, right_side, (((0,), (0,)), ((), ())), preferred_element_type=jnp.float32
    )


def times_transposed(left_side, right_side):
    return lax.dot_general(
        left_side, right_side, (((1,), (1,)), ((), ())), preferred_element_type=jnp.float32
    )


def norm_back(normed_gradient, unit_rows, inverse_rms, gain_row):
    scaled = normed_gradient * gain_row
    return inverse_rms * (scaled - unit_rows * jnp.mean(scaled * unit_rows, axis=-1, keepdims=True))


class Line:
    def __init__(self, name, size, place, pairs, crossed=False):
        self.name, self.size, self.place, self.pairs = name, size, place, pairs
        self.crossed = crossed

    def shift(self, value, step):
        return lax.ppermute(value, self.name, self.pairs(step % self.size))

    def pass_on(self, value, up):
        places = range(self.size - 1)
        pairs = [(at, at + 1) if up else (at + 1, at) for at in places]
        return lax.ppermute(value, self.name, pairs)

    def behind(self, step):
        return lax.rem(self.place + (self.size - step % self.size), self.size)

    def ahead(self, step):
        return lax.rem(self.place + step % self.size, self.size) if step else self.place


def make_lines(reps, shards):
    inner = 2 if reps % 4 == 0 else 1
    outer = reps // (2 * inner)
    square = inner == outer

    def split(index):
        core, b, a = index % 2, (index // 2) % inner, index // (2 * inner)
        return core, b, a

    def join(core, b, a):
        return (a * inner + b) * 2 + core

    def first_pairs(step):
        pairs = []
        for index in range(reps):
            core, b, a = split(index)
            if square and core == 0:
                pairs.append((index, join(core, (b + step) % inner, a)))
            else:
                pairs.append((index, join(core, b, (a + step) % outer)))
        return pairs

    def second_pairs(step):
        pairs = []
        for index in range(reps):
            core, b, a = split(index)
            if square and core == 0:
                pairs.append((index, join(core, b, (a + step) % outer)))
            else:
                pairs.append((index, join(core, (b + step) % inner, a)))
        return pairs

    def core_pairs(step):
        pairs = []
        for index in range(reps):
            core, b, a = split(index)
            pairs.append((index, join((core + step) % 2, b, a)))
        return pairs

    def shard_pairs(step):
        return [(index, (index + step) % shards) for index in range(shards)]

    core, b, a = split(lax.axis_index("rep"))
    first, second = (jnp.where(core == 0, b, a), jnp.where(core == 0, a, b)) if square else (a, b)
    return (
        Line("shard", shards, lax.axis_index("shard"), shard_pairs),
        Line("rep", 2, core, core_pairs, square),
        Line("rep", outer, first, first_pairs),
        Line("rep", inner, second, second_pairs),
    )


def rep_places(reps):
    inner = 2 if reps % 4 == 0 else 1
    outer = reps // (2 * inner)
    places = []
    for index in range(reps):
        core, b, a = index % 2, (index // 2) % inner, index // (2 * inner)
        one, two = (b, a) if inner == outer and core == 0 else (a, b)
        places.append((core * outer + one) * inner + two)
    return places


def pick(array, index, axis):
    return lax.dynamic_index_in_dim(array, index, axis, keepdims=False)


def put(array, piece, index, axis):
    return lax.dynamic_update_index_in_dim(array, piece, index, axis)


def in_place_order(pieces, line):
    ordered = []
    for place in range(line.size):
        chosen = pieces[0]
        for step in range(1, line.size):
            chosen = jnp.where(line.behind(step) == place, pieces[step], chosen)
        ordered.append(chosen)
    return ordered


def tie(*arrays):
    return lax.optimization_barrier(arrays)


def gather_line(value, line):
    return [value] + [line.shift(value, step) for step in range(1, line.size)]


class Clock:
    def __init__(self):
        self.token = jnp.zeros((8, 128), jnp.float32)
        self.open = 0

    def __call__(self, *arrays):
        self.token, *arrays = tie(self.token, *arrays)
        return arrays

    def run(self, step, *arrays):
        return self(*step(*self(*arrays)))

    def send(self, line, values, steps):
        self.open += len(values)
        return [line.shift(value, step) for value, step in zip(self(*values), steps)]

    def pass_on(self, line, lower, upper):
        self.open += 2
        lower, upper = self(lower, upper)
        return [line.pass_on(lower, True), line.pass_on(upper, False)]

    def wait(self, *groups):
        flat = self(*[array for group in groups for array in group])
        self.open -= len(flat)
        parts, at = [], 0
        for group in groups:
            parts.append(flat[at : at + len(group)])
            at += len(group)
        return parts


def total_of(terms):
    total = terms[0].astype(jnp.float32)
    for term in terms[1:]:
        total = total + term.astype(jnp.float32)
    return total


class Halving:
    def __init__(self, clock, sent, own, core, first, second):
        self.clock, self.first, self.second = clock, first, second
        self.terms = [own]
        self.moving = clock.send(core, [sent], [1])

    def along(self, line, arrived):
        self.terms = self.terms + arrived
        steps = range(1, line.size)
        blocks = [
            total_of([pick(term, line.ahead(step), 0) for term in self.terms]).astype(jnp.bfloat16)
            for step in steps
        ]
        self.moving = self.clock.send(line, blocks, steps)
        self.terms = [pick(term, line.place, 0) for term in self.terms]

    def along_first(self, arrived):
        self.along(self.first, arrived)

    def along_second(self, arrived):
        self.along(self.second, arrived)

    def finish(self, arrived):
        return self.clock(total_of(self.terms + arrived).astype(jnp.bfloat16))[0]


class Spread:
    def __init__(self, clock, piece, core, first, second):
        self.clock, self.lines = clock, (core, first, second)
        self.pieces = [piece]
        steps = range(1, second.size)
        self.moving = clock.send(second, [piece] * len(steps), steps)

    def along(self, arrived):
        core, first, second = self.lines
        self.pieces = self.pieces + arrived
        steps = range(1, first.size)
        self.moving = self.clock.send(first, [jnp.stack(self.pieces)] * len(steps), steps)

    def over(self, arrived):
        core, first, second = self.lines
        rows = [jnp.stack(self.pieces)] + arrived
        self.pieces = jnp.concatenate(rows, axis=0)
        self.moving = self.clock.send(core, [self.pieces], [1])

    def finish(self, arrived):
        core, first, second = self.lines
        (others,) = arrived
        offsets = [(one, two) for one in range(first.size) for two in range(second.size)]
        placed = [(core.place, first.behind(one), second.behind(two)) for one, two in offsets]
        far, near = (second, first) if core.crossed else (first, second)
        placed += [(core.behind(1), far.behind(one), near.behind(two)) for one, two in offsets]
        places = [(c * first.size + f) * second.size + s for c, f, s in placed]
        return [jnp.stack(places).astype(jnp.int32), self.pieces, others]


def column_blocks(place, shard_place, *weights):
    count = len(weights)
    rows, columns = weights[0].shape[1:]
    shards = lax.axis_size("shard")
    block = columns // shards

    def body(places_ref, *refs):
        sources, outs = refs[:count], refs[count : 2 * count]
        held, cut, in_sems, out_sems = refs[2 * count :]
        loads = [
            pltpu.make_async_copy(sources[at].at[places_ref[0]], held.at[at], in_sems.at[at])
            for at in range(count)
        ]

        def store(at, z):
            ahead = lax.rem(z + shards - places_ref[1], shards)
            return pltpu.make_async_copy(cut.at[at, z], outs[at].at[ahead], out_sems.at[at, z])

        for load in loads:
            load.start()
        for at in range(count):
            loads[at].wait()
            for z in range(shards):
                cut[at, z] = held[at, :, z * block : (z + 1) * block]
                store(at, z).start()
        for at in range(count):
            for z in range(shards):
                store(at, z).wait()

    return pl.pallas_call(
        body,
        out_shape=[jax.ShapeDtypeStruct((shards, rows, block), jnp.bfloat16)] * count,
        in_specs=[pl.BlockSpec(memory_space=pltpu.SMEM)]
        + [pl.BlockSpec(memory_space=pl.ANY)] * count,
        out_specs=[pl.BlockSpec(memory_space=pl.ANY)] * count,
        scratch_shapes=[
            pltpu.VMEM((count, rows, columns), jnp.bfloat16),
            pltpu.VMEM((count, shards, rows, block), jnp.bfloat16),
            pltpu.SemaphoreType.DMA((count,)),
            pltpu.SemaphoreType.DMA((count, shards)),
        ],
        compiler_params=pltpu.CompilerParams(vmem_limit_bytes=VMEM_LIMIT),
        cost_estimate=COST,
        name="column_blocks",
    )(jnp.stack([place, shard_place]).astype(jnp.int32), *weights)


def place_blocks(order, places, pieces, others):
    half, groups, shards = pieces.shape[:3]

    def body(order_ref, places_ref, pieces_ref, others_ref, *rest):
        def source_of(g, k, r):
            return (pieces_ref if r < half else others_ref).at[r % half, g, k]

        move_blocks(source_of, lambda r: places_ref[r], order_ref, rest[:groups], *rest[groups:])

    return blocks_call(body, 2, 2, groups, shards, 2 * half, pieces.shape[3:])(
        order, places, pieces, others
    )


def place_gathered(order, gathered, groups):
    shards = lax.axis_size("shard")
    reps = gathered.shape[0] // (shards * groups)

    def body(order_ref, source, *rest):
        move_blocks(
            lambda g, k, r: source.at[(r * shards + k) * groups + g],
            lambda r: r,
            order_ref,
            rest[:groups],
            *rest[groups:],
        )

    return blocks_call(body, 1, 1, groups, shards, reps, gathered.shape[1:])(order, gathered)


def move_blocks(source_of, place_of, order_ref, outs, held, in_sems, out_sems):
    groups, shards, reps = in_sems.shape
    slabs = [(g, k) for g in range(groups) for k in range(shards)]

    def load(g, k, r):
        return pltpu.make_async_copy(
            source_of(g, k, r), held.at[g, k, place_of(r)], in_sems.at[g, k, r]
        )

    def store(g, k):
        return pltpu.make_async_copy(held.at[g, k], outs[g].at[order_ref[k]], out_sems.at[g, k])

    for g, k in slabs:
        for r in range(reps):
            load(g, k, r).start()
    for g, k in slabs:
        for r in range(reps):
            load(g, k, r).wait()
        store(g, k).start()
    for g, k in slabs:
        store(g, k).wait()


def blocks_call(body, scalars, sources, groups, shards, reps, block):
    whole = (shards, reps) + block
    return pl.pallas_call(
        body,
        out_shape=[jax.ShapeDtypeStruct(whole, jnp.bfloat16)] * groups,
        in_specs=[pl.BlockSpec(memory_space=pltpu.SMEM)] * scalars
        + [pl.BlockSpec(memory_space=pl.ANY)] * sources,
        out_specs=[pl.BlockSpec(memory_space=pl.ANY)] * groups,
        scratch_shapes=[
            pltpu.VMEM((groups,) + whole, jnp.bfloat16),
            pltpu.SemaphoreType.DMA((groups, shards, reps)),
            pltpu.SemaphoreType.DMA((groups, shards)),
        ],
        compiler_params=pltpu.CompilerParams(vmem_limit_bytes=VMEM_LIMIT),
        cost_estimate=COST,
        name="place_blocks",
    )


def widen_pieces(places, pieces, others):
    half, rows, columns = pieces.shape
    reps = 2 * half
    strip = next(size for size in (16, 8, rows) if rows % size == 0)

    def body(places_ref, pieces_ref, others_ref, out_ref, narrow, wide, in_sems, out_sems):
        loads = [
            pltpu.make_async_copy(
                (pieces_ref if r < half else others_ref).at[r % half], narrow.at[r], in_sems.at[r]
            )
            for r in range(reps)
        ]
        stores = [
            pltpu.make_async_copy(wide.at[r], out_ref.at[places_ref[r]], out_sems.at[r])
            for r in range(reps)
        ]
        for load in loads:
            load.start()
        for r in range(reps):
            loads[r].wait()

            def convert(at, carry):
                cut = pl.ds(pl.multiple_of(at * strip, strip), strip)
                wide[r, cut, :] = narrow[r, cut, :].astype(jnp.float32)
                return carry

            lax.fori_loop(0, rows // strip, convert, 0)
            stores[r].start()
        for store in stores:
            store.wait()

    result = pl.pallas_call(
        body,
        out_shape=jax.ShapeDtypeStruct((reps, rows, columns), jnp.float32),
        in_specs=[pl.BlockSpec(memory_space=pltpu.SMEM)]
        + [pl.BlockSpec(memory_space=pl.ANY)] * 2,
        out_specs=pl.BlockSpec(memory_space=pl.ANY),
        scratch_shapes=[
            pltpu.VMEM((reps, rows, columns), jnp.bfloat16),
            pltpu.VMEM((reps, rows, columns), jnp.float32),
            pltpu.SemaphoreType.DMA((reps,)),
            pltpu.SemaphoreType.DMA((reps,)),
        ],
        compiler_params=pltpu.CompilerParams(vmem_limit_bytes=VMEM_LIMIT),
        cost_estimate=COST,
        name="widen_pieces",
    )(places, pieces, others)
    return (result.reshape(reps * rows, columns),)


def widen_gathered(gathered, order):
    reps, rows, columns = gathered.shape
    strip = next(size for size in (16, 8, rows) if rows % size == 0)

    def body(source_ref, out_ref, narrow, wide, in_sems, out_sems):
        loads = [
            pltpu.make_async_copy(source_ref.at[r], narrow.at[r], in_sems.at[r])
            for r in range(reps)
        ]
        stores = [
            pltpu.make_async_copy(wide.at[r], out_ref.at[order[r]], out_sems.at[r])
            for r in range(reps)
        ]
        for load in loads:
            load.start()
        for r in range(reps):
            loads[r].wait()

            def convert(at, carry):
                cut = pl.ds(pl.multiple_of(at * strip, strip), strip)
                wide[r, cut, :] = narrow[r, cut, :].astype(jnp.float32)
                return carry

            lax.fori_loop(0, rows // strip, convert, 0)
            stores[r].start()
        for store in stores:
            store.wait()

    result = pl.pallas_call(
        body,
        out_shape=jax.ShapeDtypeStruct((reps, rows, columns), jnp.float32),
        in_specs=[pl.BlockSpec(memory_space=pl.ANY)],
        out_specs=pl.BlockSpec(memory_space=pl.ANY),
        scratch_shapes=[
            pltpu.VMEM((reps, rows, columns), jnp.bfloat16),
            pltpu.VMEM((reps, rows, columns), jnp.float32),
            pltpu.SemaphoreType.DMA((reps,)),
            pltpu.SemaphoreType.DMA((reps,)),
        ],
        compiler_params=pltpu.CompilerParams(vmem_limit_bytes=VMEM_LIMIT),
        cost_estimate=COST,
        name="widen_gathered",
    )(gathered)
    return (result.reshape(reps * rows, columns),)


def resident(shape):
    return pl.BlockSpec(shape, lambda i: (0, 0), pipeline_mode=pl.Buffered(1))


def feed_forward(rows, cotangents, gate_matrix, up_matrix, down_matrix):
    count, width = rows.shape
    units = gate_matrix.shape[1]
    steps = pl.cdiv(units, TILE)
    slabs = next(size for size in range(min(steps, width // 128), 0, -1) if width % (128 * size) == 0)
    slab = width // slabs

    def body(
        rows_ref,
        cotangents_ref,
        gate_ref,
        up_ref,
        down_ref,
        inner_ref,
        d_gate_ref,
        d_up_ref,
        turned_rows_ref,
        turned_inner_ref,
    ):
        gate = jnp.dot(rows_ref[...], gate_ref[...], preferred_element_type=jnp.float32)
        up = jnp.dot(rows_ref[...], up_ref[...], preferred_element_type=jnp.float32)
        sigmoid = jax.nn.sigmoid(gate)
        silu = gate * sigmoid
        inner = (silu * up).astype(jnp.bfloat16)
        inner_ref[...] = inner
        turned_inner_ref[...] = inner.T
        d_inner = times_transposed(cotangents_ref[...], down_ref[...])
        d_up_ref[...] = (d_inner * silu).astype(jnp.bfloat16)
        d_gate_ref[...] = (d_inner * up * sigmoid * (1.0 + gate * (1.0 - sigmoid))).astype(
            jnp.bfloat16
        )
        for step in range(slabs):

            @pl.when(pl.program_id(0) == step)
            def turn():
                turned_rows_ref[...] = rows_ref[:, step * slab : (step + 1) * slab].T

    columns = pl.BlockSpec((width, TILE), lambda i: (0, i))
    results = pl.BlockSpec((count, TILE), lambda i: (0, i))
    return pl.pallas_call(
        body,
        grid=(steps,),
        out_shape=[jax.ShapeDtypeStruct((count, units), jnp.bfloat16)] * 3
        + [
            jax.ShapeDtypeStruct((width, count), jnp.bfloat16),
            jax.ShapeDtypeStruct((units, count), jnp.bfloat16),
        ],
        in_specs=[
            resident((count, width)),
            resident((count, width)),
            columns,
            columns,
            pl.BlockSpec((TILE, width), lambda i: (i, 0)),
        ],
        out_specs=[results] * 3
        + [
            pl.BlockSpec((slab, count), lambda i: (jnp.minimum(i, slabs - 1), 0)),
            pl.BlockSpec((TILE, count), lambda i: (i, 0)),
        ],
        compiler_params=pltpu.CompilerParams(vmem_limit_bytes=VMEM_LIMIT),
        cost_estimate=COST,
        name="feed_forward",
    )(rows, cotangents, gate_matrix, up_matrix, down_matrix)


def split_gradient(left, right, groups, places, core_place, turned):
    rows, count = left.shape if turned else left.shape[::-1]
    columns = right.shape[1]
    half = rows // (2 * groups)
    part = half // places

    def body(core_ref, left_ref, right_ref, other_ref, own_ref, *scratch):
        if turned:
            rows_ref = left_ref
        else:
            (rows_ref,) = scratch

            @pl.when(pl.program_id(0) == 0)
            def turn():
                rows_ref[...] = left_ref[...].T

        core = core_ref[0]
        for out_ref, which in ((other_ref, 1 - core), (own_ref, core)):
            halves = [
                rows_ref[pl.ds(pl.multiple_of((2 * group + which) * half, 16), half), :]
                for group in range(groups)
            ]
            product = jnp.dot(
                jnp.concatenate(halves, axis=0), right_ref[...], preferred_element_type=jnp.float32
            )
            for group in range(groups):
                for place in range(places):
                    at = group * half + place * part
                    out_ref[place, group] = product[at : at + part].astype(jnp.bfloat16)

    return pl.pallas_call(
        body,
        grid=(pl.cdiv(columns, TILE),),
        out_shape=[jax.ShapeDtypeStruct((places, groups, part, columns), jnp.bfloat16)] * 2,
        in_specs=[
            pl.BlockSpec(memory_space=pltpu.SMEM),
            resident(left.shape),
            pl.BlockSpec((count, TILE), lambda i: (0, i)),
        ],
        out_specs=[pl.BlockSpec((places, groups, part, TILE), lambda i: (0, 0, 0, i))] * 2,
        scratch_shapes=[] if turned else [pltpu.VMEM((rows, count), jnp.bfloat16)],
        compiler_params=pltpu.CompilerParams(vmem_limit_bytes=VMEM_LIMIT),
        cost_estimate=COST,
        name="split_gradient",
    )(core_place.reshape(1).astype(jnp.int32), left, right)


def ordered_gradient(left, right, shards, order):
    reps = len(order)
    rows, count = left.shape
    columns = right.shape[1]
    part = rows // (shards * reps)

    def body(left_ref, right_ref, out_ref):
        product = jnp.dot(left_ref[...], right_ref[...], preferred_element_type=jnp.float32)
        for z in range(shards):
            for r in range(reps):
                at = (z * reps + order[r]) * part
                out_ref[r, z] = product[at : at + part].astype(jnp.bfloat16)

    return pl.pallas_call(
        body,
        grid=(pl.cdiv(columns, TILE),),
        out_shape=[jax.ShapeDtypeStruct((reps, shards, part, columns), jnp.bfloat16)],
        in_specs=[
            resident((rows, count)),
            pl.BlockSpec((count, TILE), lambda i: (0, i)),
        ],
        out_specs=[pl.BlockSpec((reps, shards, part, TILE), lambda i: (0, 0, 0, i))],
        compiler_params=pltpu.CompilerParams(vmem_limit_bytes=VMEM_LIMIT),
        cost_estimate=COST,
        name="ordered_gradient",
    )(left, right)


def rows_product(lefts, rights, turned, blocks):
    count, depth = lefts[0].shape
    columns = rights[0].shape[0 if turned else 1]
    pairs, part = len(lefts), count // blocks

    def body(*refs):
        total = None
        for left_ref, right_ref in zip(refs[:pairs], refs[pairs : 2 * pairs]):
            if turned:
                product = times_transposed(left_ref[...], right_ref[...])
            else:
                product = jnp.dot(
                    left_ref[...], right_ref[...], preferred_element_type=jnp.float32
                )
            total = product if total is None else total + product
        for block in range(blocks):
            refs[2 * pairs + block][...] = total[block * part : (block + 1) * part].astype(
                jnp.bfloat16
            )

    right_spec = (
        pl.BlockSpec((TILE, depth), lambda i: (i, 0))
        if turned
        else pl.BlockSpec((depth, TILE), lambda i: (0, i))
    )
    return pl.pallas_call(
        body,
        grid=(pl.cdiv(columns, TILE),),
        out_shape=[jax.ShapeDtypeStruct((part, columns), jnp.bfloat16)] * blocks,
        in_specs=[resident((count, depth))] * pairs + [right_spec] * pairs,
        out_specs=[pl.BlockSpec((part, TILE), lambda i: (0, i))] * blocks,
        compiler_params=pltpu.CompilerParams(vmem_limit_bytes=VMEM_LIMIT),
        cost_estimate=COST,
        name="rows_product",
    )(*lefts, *rights)


def kept_bias(row_segments, row_index, key_segments, key_index):
    kept = (row_segments == key_segments) & (key_index <= row_index)
    return jnp.where(kept, 0.0, MASKED)


def in_vmem(count):
    return [pl.BlockSpec(memory_space=pltpu.VMEM)] * count


def attention_forward(projected, cosine, signed_sine, pairs, rows, keys):
    count = projected.shape[0]
    per_group = QH // KVH
    scale = 1.0 / math.sqrt(HD)
    shape = (KVH, per_group * count, HD)

    def body(projected_ref, cosine_ref, sine_ref, pairs_ref, rows_ref, keys_ref, queries_ref, out_ref):
        bias = kept_bias(rows_ref[:, 0:1], rows_ref[:, 1:2], keys_ref[0:1, :], keys_ref[1:2, :])
        for k in range(KVH):
            for h in range(per_group):
                at = (k * per_group + h) * HD
                field = projected_ref[:, at : at + HD]
                queries_ref[k, h * count : (h + 1) * count, :] = (
                    field * cosine_ref[...] + pltpu.roll(field, HD // 2, 1) * sine_ref[...]
                ).astype(jnp.bfloat16)
            keys_here = pairs_ref[:, k * HD : (k + 1) * HD]
            values_here = pairs_ref[:, (KVH + k) * HD : (KVH + k + 1) * HD]
            scores = times_transposed(queries_ref[k], keys_here) * scale + bias
            powers = jnp.exp(scores - jnp.max(scores, axis=1, keepdims=True))
            shares = powers * (1.0 / jnp.sum(powers, axis=1, keepdims=True))
            result = jnp.dot(
                shares.astype(jnp.bfloat16), values_here, preferred_element_type=jnp.float32
            ).astype(jnp.bfloat16)
            for h in range(per_group):
                at = (k * per_group + h) * HD
                out_ref[:, at : at + HD] = result[h * count : (h + 1) * count]

    return pl.pallas_call(
        body,
        out_shape=[
            jax.ShapeDtypeStruct(shape, jnp.bfloat16),
            jax.ShapeDtypeStruct((count, QH * HD), jnp.bfloat16),
        ],
        in_specs=in_vmem(6),
        out_specs=in_vmem(2),
        compiler_params=pltpu.CompilerParams(vmem_limit_bytes=VMEM_LIMIT),
        cost_estimate=COST,
        name="attention_forward",
    )(projected, cosine, signed_sine, pairs, rows, keys)


def attention_backward(queries, gradient, pairs, cosine, signed_sine, rows, keys, blocks):
    count = gradient.shape[0]
    per_group = QH // KVH
    scale = 1.0 / math.sqrt(HD)
    group_rows = pairs.shape[0]
    part = group_rows // blocks

    def body(queries_ref, gradient_ref, pairs_ref, cosine_ref, sine_ref, rows_ref, keys_ref, d_ref, *outs):
        block_refs, stacked = outs[:blocks], outs[blocks]
        bias = kept_bias(rows_ref[0:1, :], rows_ref[1:2, :], keys_ref[:, 0:1], keys_ref[:, 1:2])
        for k in range(KVH):
            for h in range(per_group):
                at = (k * per_group + h) * HD
                stacked[h * count : (h + 1) * count, :] = gradient_ref[:, at : at + HD]
            keys_here = pairs_ref[:, k * HD : (k + 1) * HD]
            values_here = pairs_ref[:, (KVH + k) * HD : (KVH + k + 1) * HD]
            scores = times_transposed(keys_here, queries_ref[k]) * scale + bias
            powers = jnp.exp(scores - jnp.max(scores, axis=0, keepdims=True))
            shares = powers * (1.0 / jnp.sum(powers, axis=0, keepdims=True))
            d_shares = times_transposed(values_here, stacked[...])
            dots = jnp.sum(shares * d_shares, axis=0, keepdims=True)
            d_scores = (shares * (d_shares - dots)).astype(jnp.bfloat16)
            d_keys = jnp.dot(d_scores, queries_ref[k], preferred_element_type=jnp.float32) * scale
            d_values = jnp.dot(
                shares.astype(jnp.bfloat16), stacked[...], preferred_element_type=jnp.float32
            )
            for block in range(blocks):
                cut = slice(block * part, (block + 1) * part)
                block_refs[block][:, k * HD : (k + 1) * HD] = d_keys[cut].astype(jnp.bfloat16)
                block_refs[block][:, (KVH + k) * HD : (KVH + k + 1) * HD] = d_values[cut].astype(
                    jnp.bfloat16
                )
            d_queries = transposed_times(d_scores, keys_here) * scale
            for h in range(per_group):
                at = (k * per_group + h) * HD
                field = d_queries[h * count : (h + 1) * count]
                d_ref[:, at : at + HD] = (
                    field * cosine_ref[...] - pltpu.roll(field, HD // 2, 1) * sine_ref[...]
                ).astype(jnp.bfloat16)

    return pl.pallas_call(
        body,
        out_shape=[jax.ShapeDtypeStruct((count, QH * HD), jnp.bfloat16)]
        + [jax.ShapeDtypeStruct((part, 2 * KVH * HD), jnp.bfloat16)] * blocks,
        in_specs=in_vmem(7),
        out_specs=in_vmem(1 + blocks),
        scratch_shapes=[pltpu.VMEM((per_group * count, HD), jnp.bfloat16)],
        compiler_params=pltpu.CompilerParams(vmem_limit_bytes=VMEM_LIMIT),
        cost_estimate=COST,
        name="attention_backward",
    )(queries, gradient, pairs, cosine, signed_sine, rows, keys)


def join_projected(d_queries, pair_terms, cosine, signed_sine):
    count, query_width = d_queries.shape
    pair_width = KVH * HD
    terms = len(pair_terms)

    def body(d_queries_ref, cosine_ref, sine_ref, *refs):
        term_refs, out_ref, sum_ref = refs[:terms], refs[terms], refs[terms + 1]
        out_ref[:, :query_width] = d_queries_ref[...]
        for at in range(0, 2 * pair_width, HD):
            field = total_of([term[:, at : at + HD] for term in term_refs])
            if at < pair_width:
                field = field * cosine_ref[...] - pltpu.roll(field, HD // 2, 1) * sine_ref[...]
            out_ref[:, query_width + at : query_width + at + HD] = field.astype(jnp.bfloat16)
        sum_ref[...] = jnp.sum(out_ref[...].astype(jnp.float32), axis=0, keepdims=True)

    return pl.pallas_call(
        body,
        out_shape=[
            jax.ShapeDtypeStruct((count, query_width + 2 * pair_width), jnp.bfloat16),
            jax.ShapeDtypeStruct((1, query_width + 2 * pair_width), jnp.float32),
        ],
        in_specs=in_vmem(3 + terms),
        out_specs=in_vmem(2),
        cost_estimate=COST,
        name="join_projected",
    )(d_queries, cosine, signed_sine, *pair_terms)


def on_device(
    tokens,
    segment_ids,
    first_gain,
    input_weight,
    input_bias,
    output_weight,
    second_gain,
    gate_weight,
    up_weight,
    down_weight,
    output_cotangent,
):
    bf16, f32 = jnp.bfloat16, jnp.float32
    shards, reps = lax.axis_size("shard"), lax.axis_size("rep")
    shard, core, first, second = make_lines(reps, shards)
    rep_place = (core.place * first.size + first.place) * second.size + second.place
    own_rows, width = tokens.shape
    segments = segment_ids[0]
    per_group = QH // KVH
    query_width = QH * HD
    pair_width = KVH * HD
    first_row = shard.place * own_rows
    part_rows = input_weight.shape[0] // reps
    hidden_units = gate_weight.shape[1]
    block_units = hidden_units // shards
    clock = Clock()
    z_order = jnp.stack([shard.behind(step) for step in range(shards)]).astype(jnp.int32)

    def weight_piece(weight, place):
        return pick(weight.reshape(reps, part_rows, weight.shape[1]), place, 0)

    def spread(piece):
        return Spread(clock, piece, core, first, second)

    def blocks_of(blocks):
        return [pick(blocks, shard.ahead(step), 0) for step in range(shards)]

    steps = range(1, shards)

    def send_blocks(blocks):
        return clock.send(shard, blocks[1:], steps)

    def send_around(value):
        return clock.send(shard, [value] * len(steps), steps)

    def send_back(rows):
        return clock.send(shard, rows, [shards - step for step in steps])

    rep_index = lax.axis_index("rep")
    input_matrix = lax.all_gather(
        weight_piece(input_weight, rep_index), ("shard", "rep"), axis=0, tiled=True
    )
    shard_vectors = jnp.concatenate([first_gain, second_gain, input_bias])
    vector_row = jnp.pad(shard_vectors, (0, output_weight.shape[1] - shard_vectors.shape[0]))
    own_output = jnp.concatenate(
        [weight_piece(output_weight, rep_place), vector_row[None]], axis=0
    )
    output_moving = send_around(own_output)
    gate_blocks, up_blocks = clock.run(
        lambda *weights: column_blocks(rep_index, shard.place, *weights),
        gate_weight.reshape(reps, part_rows, hidden_units),
        up_weight.reshape(reps, part_rows, hidden_units),
    )
    (output_rows,) = clock.wait(output_moving)
    output_rows = [own_output] + output_rows

    output_spread = spread(jnp.stack([rows[:part_rows] for rows in output_rows])[None])
    gate_moving = send_blocks(gate_blocks)
    vector_rows = jnp.stack(in_place_order([rows[part_rows] for rows in output_rows], shard))
    own_gain = first_gain.shape[0]
    gain_one = vector_rows[:, :own_gain].reshape(width).astype(f32)
    gain_two = vector_rows[:, own_gain : 2 * own_gain].reshape(width).astype(f32)
    shift_row = (
        vector_rows[:, 2 * own_gain : shard_vectors.shape[0]].reshape(-1).astype(f32)
    )
    places = positions(segments)
    cosine_table, sine_table = rope_tables(
        lax.dynamic_slice_in_dim(places, first_row, own_rows), HD
    )
    signed_sine = jnp.concatenate(
        [-sine_table[:, : HD // 2], sine_table[:, HD // 2 :]], axis=1
    )
    own_segments = lax.dynamic_slice_in_dim(segments, first_row, own_rows)
    row_index = jnp.arange(own_rows, dtype=jnp.int32)
    key_index = jnp.concatenate([shard.behind(step) * own_rows + row_index for step in range(shards)])
    key_segments = jnp.concatenate(
        [
            lax.dynamic_slice_in_dim(segments, shard.behind(step) * own_rows, own_rows)
            for step in range(shards)
        ]
    )
    key_marks = jnp.stack([key_segments, key_index])
    row_marks = jnp.tile(jnp.stack([own_segments, first_row + row_index]), (1, per_group))
    wide_tokens = tokens.astype(f32)
    inverse_one = lax.rsqrt(jnp.mean(wide_tokens * wide_tokens, axis=-1, keepdims=True) + EPSILON)
    unit_one = wide_tokens * inverse_one
    normed_one = (unit_one * gain_one).astype(bf16)
    (
        normed_one,
        cosine_table,
        sine_table,
        signed_sine,
        key_marks,
        row_marks,
    ) = clock(normed_one, cosine_table, sine_table, signed_sine, key_marks, row_marks)
    output_arrived, gate_rows = clock.wait(output_spread.moving, gate_moving)

    output_spread.along(output_arrived)
    up_moving = send_blocks(up_blocks)
    output_arrived, up_rows = clock.wait(output_spread.moving, up_moving)

    gate_up = jnp.stack(
        [row for pair in zip([gate_blocks[0]] + gate_rows, [up_blocks[0]] + up_rows) for row in pair]
    )
    gate_up = lax.all_gather(clock(gate_up)[0], "rep", axis=0, tiled=True)
    passed = [[output_cotangent] * 2]
    passing = clock.pass_on(shard, *passed[-1])
    output_spread.over(output_arrived)
    input_matrix, normed_one = clock(input_matrix, normed_one)
    projected = jnp.dot(normed_one, input_matrix, preferred_element_type=f32) + shift_row
    key_part = rotate(
        projected[:, query_width : query_width + pair_width].reshape(own_rows, KVH, HD),
        cosine_table,
        sine_table,
    )
    (own_pairs,) = clock(
        jnp.concatenate(
            [key_part.reshape(own_rows, pair_width), projected[:, query_width + pair_width :]],
            axis=1,
        ).astype(bf16)
    )
    arrived, output_arrived = clock.wait(passing, output_spread.moving)
    passed.append(arrived)

    pair_moving = send_around(own_pairs)
    passing = clock.pass_on(shard, *passed[-1]) if shards > 2 else []
    pair_rows, arrived = clock.wait(pair_moving, passing)
    passed.append(arrived)
    pairs = jnp.concatenate([own_pairs] + pair_rows, axis=0)

    passing = clock.pass_on(shard, *passed[-1]) if shards > 3 else []
    (output_matrix,) = clock.run(place_blocks, z_order, *output_spread.finish(output_arrived))
    output_matrix = output_matrix.reshape(width, width)
    queries, attention_low = clock.run(
        attention_forward, projected, cosine_table, signed_sine, pairs, row_marks.T, key_marks
    )
    hidden = wide_tokens + jnp.dot(attention_low, output_matrix, preferred_element_type=f32)
    inverse_two = lax.rsqrt(jnp.mean(hidden * hidden, axis=-1, keepdims=True) + EPSILON)
    unit_two = hidden * inverse_two
    (normed_two,) = clock((unit_two * gain_two).astype(bf16))
    (arrived,) = clock.wait(passing)
    passed.append(arrived)

    normed_moving = send_around(normed_two)
    gate_matrix, up_matrix = clock.run(
        lambda order, gathered: place_gathered(order, gathered, 2), z_order, gate_up
    )
    gate_matrix = gate_matrix.reshape(width, block_units)
    up_matrix = up_matrix.reshape(width, block_units)
    (normed_arrived,) = clock.wait(normed_moving)
    while len(passed) < shards:
        (arrived,) = clock.wait(clock.pass_on(shard, *passed[-1]))
        passed.append(arrived)
    group_normed = jnp.concatenate([normed_two] + normed_arrived, axis=0)
    cotangents = jnp.concatenate(
        [output_cotangent]
        + [
            jnp.where(shard.place >= step, passed[step][0], passed[shards - step][1])
            for step in steps
        ],
        axis=0,
    )

    inner_act, d_gate, d_up, turned_normed, turned_inner = clock.run(
        feed_forward, group_normed, cotangents, gate_matrix, up_matrix, down_weight
    )

    def split_halves(left, right, groups, turned):
        count = first.size * second.size
        halves = clock.run(
            lambda left, right: split_gradient(left, right, groups, count, core.place, turned),
            left,
            right,
        )
        return [half.reshape((first.size, second.size) + half.shape[1:]) for half in halves]

    def side_by_side(rows):
        return clock(jnp.concatenate(in_place_order(rows, shard), axis=1))[0]

    def sum_over_rep(blocks):
        return lax.psum_scatter(blocks, "rep", scatter_dimension=0, tiled=True)

    def row_sum(own, arrived):
        return clock(total_of(own + arrived).astype(bf16))[0]

    def send_some(rows, chosen):
        return clock.send(shard, [rows[k] for k in chosen], [shards - 1 - k for k in chosen])

    edges = sorted({0, shards - 2})
    inside = list(range(1, shards - 2))

    def gather_rep(piece):
        return lax.all_gather(piece[None], "rep", axis=0, tiled=True)

    up_halves = split_halves(turned_normed, d_up, shards, True)

    up = Halving(clock, *up_halves, core, first, second)
    (gate_blocks,) = clock.run(
        lambda left, right: ordered_gradient(left, right, shards, rep_places(reps)),
        turned_normed,
        d_gate,
    )
    (up_arrived,) = clock.wait(up.moving)

    gate_piece = sum_over_rep(clock(gate_blocks)[0].reshape(width, block_units))
    up.along_first(up_arrived)
    normed_own, *normed_partial = clock.run(
        lambda *operands: rows_product(operands[:2], operands[2:], True, shards),
        d_gate,
        d_up,
        gate_matrix,
        up_matrix,
    )
    normed_moving = send_some(normed_partial, edges)
    down_halves = split_halves(turned_inner, cotangents, 1, True)
    up_arrived, normed_arrived = clock.wait(up.moving, normed_moving)

    up.along_second(up_arrived)
    down = Halving(clock, *down_halves, core, first, second)
    normed_moving = send_some(normed_partial, inside)
    block_own, *block_partial = clock.run(
        lambda left, right: rows_product((left,), (right,), False, shards), inner_act, down_weight
    )
    up_arrived, down_arrived, more_arrived = clock.wait(up.moving, down.moving, normed_moving)

    down.along_first(down_arrived)
    up_blocks = clock(*blocks_of(up.finish(up_arrived)))
    up_moving = send_blocks(up_blocks)
    normed_two_gradient = total_of([normed_own] + normed_arrived + more_arrived)
    gain_two_gradient = jnp.sum(normed_two_gradient * unit_two, axis=0)
    hidden_gradient = output_cotangent.astype(f32) + norm_back(
        normed_two_gradient, unit_two, inverse_two, gain_two
    )
    (branch_gradient,) = clock(hidden_gradient.astype(bf16))
    (attention_gradient,) = clock(times_transposed(branch_gradient, output_matrix).astype(bf16))
    d_queries, pair_own, *pair_partial = clock.run(
        lambda *operands: attention_backward(*operands, shards),
        queries,
        attention_gradient,
        pairs,
        cosine_table,
        signed_sine,
        row_marks,
        key_marks.T,
    )
    output_halves = split_halves(attention_low, branch_gradient, shards, False)
    down_arrived, up_rows = clock.wait(down.moving, up_moving)

    pair_moving = send_back(pair_partial)
    output = Halving(clock, *output_halves, core, first, second)
    down.along_second(down_arrived)
    up_piece = side_by_side(up_blocks[:1] + up_rows)
    pair_arrived, output_arrived, down_arrived = clock.wait(
        pair_moving, output.moving, down.moving
    )

    (gate_piece,) = clock(gate_piece)
    down_gathered = gather_rep(down.finish(down_arrived)[0])
    projected_gradient, bias_sum = clock.run(
        lambda *operands: join_projected(operands[0], operands[3:], *operands[1:3]),
        d_queries,
        cosine_table,
        signed_sine,
        pair_own,
        *pair_arrived,
    )
    projected_halves = split_halves(normed_one, projected_gradient, shards, False)

    projected = Halving(clock, *projected_halves, core, first, second)
    output.along_first(output_arrived)
    gate_blocks = clock(*blocks_of(gate_piece.reshape(shards, part_rows, block_units)))
    gate_moving = send_blocks(gate_blocks)
    projected_gradient, hidden_gradient = clock(projected_gradient, hidden_gradient)
    normed_one_gradient = times_transposed(projected_gradient, input_matrix)
    gain_one_gradient = jnp.sum(normed_one_gradient * unit_one, axis=0)
    (tokens_gradient,) = clock(
        (
            hidden_gradient + norm_back(normed_one_gradient, unit_one, inverse_one, gain_one)
        ).astype(bf16)
    )
    projected_arrived, output_arrived, gate_rows = clock.wait(
        projected.moving, output.moving, gate_moving
    )

    projected.along_first(projected_arrived)
    output.along_second(output_arrived)
    gate_spread = spread(side_by_side(gate_blocks[:1] + gate_rows))
    block_moving = send_some(block_partial, inside)
    bias_gradient = bias_sum[0]
    bias_split = query_width + pair_width
    small_parts = (
        gain_one_gradient,
        gain_two_gradient,
        bias_gradient[:bias_split],
        bias_gradient[bias_split:],
    )
    (small,) = clock(
        jnp.concatenate([part.reshape(shards, -1) for part in small_parts], axis=1)
    )
    (down_gathered,) = clock(down_gathered)
    (down_total,) = clock.run(lambda gathered: widen_gathered(gathered, rep_places(reps)), down_gathered)
    projected_arrived, output_arrived, gate_arrived, block_arrived = clock.wait(
        projected.moving, output.moving, gate_spread.moving, block_moving
    )

    projected.along_second(projected_arrived)
    gate_spread.along(gate_arrived)
    output_blocks = clock(*blocks_of(output.finish(output_arrived)))
    output_moving = send_blocks(output_blocks)
    up_gathered = gather_rep(clock(up_piece)[0])
    projected_arrived, gate_arrived, output_rows = clock.wait(
        projected.moving, gate_spread.moving, output_moving
    )

    input_blocks = clock(*blocks_of(projected.finish(projected_arrived)))
    input_moving = send_blocks(input_blocks)
    output_spread = spread(row_sum(output_blocks[:1], output_rows))
    gate_spread.over(gate_arrived)
    input_rows, output_arrived, gate_arrived = clock.wait(
        input_moving, output_spread.moving, gate_spread.moving
    )

    input_spread = spread(row_sum(input_blocks[:1], input_rows))
    output_spread.along(output_arrived)
    small_moving = clock.send(core, [small], [1])
    block_moving = send_some(block_partial, edges[:1])
    (up_gathered,) = clock(up_gathered)
    (up_total,) = clock.run(lambda gathered: widen_gathered(gathered, rep_places(reps)), up_gathered)
    input_arrived, output_arrived, small_arrived, more_arrived = clock.wait(
        input_spread.moving, output_spread.moving, small_moving, block_moving
    )
    small = total_of([small] + small_arrived)
    block_arrived = block_arrived + more_arrived

    input_spread.along(input_arrived)
    output_spread.over(output_arrived)
    small_moving = clock.send(first, [small] * (first.size - 1), range(1, first.size))
    block_moving = send_some(block_partial, edges[1:])
    (gate_total,) = clock.run(widen_pieces, *gate_spread.finish(gate_arrived))
    input_arrived, output_arrived, small_arrived, more_arrived = clock.wait(
        input_spread.moving, output_spread.moving, small_moving, block_moving
    )
    small = total_of([small] + small_arrived)
    block_arrived = block_arrived + more_arrived

    input_spread.over(input_arrived)
    small_moving = clock.send(second, [small] * (second.size - 1), range(1, second.size))
    (output_total,) = clock.run(widen_pieces, *output_spread.finish(output_arrived))
    (block_out,) = clock(total_of([hidden, block_own] + block_arrived).astype(bf16))
    input_arrived, small_arrived = clock.wait(input_spread.moving, small_moving)
    small_blocks = clock(*blocks_of(total_of([small] + small_arrived)))

    small_moving = send_blocks(small_blocks)
    (input_total,) = clock.run(widen_pieces, *input_spread.finish(input_arrived))
    (small_arrived,) = clock.wait(small_moving)
    small = total_of(small_blocks[:1] + small_arrived)

    small = small + clock.token[0, 0]
    small_totals, at = [], 0
    for part in small_parts:
        size = part.shape[0] // shards
        small_totals.append(small[at : at + size])
        at += size
    return (
        block_out,
        tokens_gradient,
        small_totals[0],
        input_total,
        small_totals[2],
        small_totals[3],
        output_total,
        small_totals[1],
        gate_total,
        up_total,
        down_total,
    )


def solution(mesh):
    placed = (
        P(("rep", "shard"), None),
        P("rep", None),
        P("shard"),
        P("shard", None),
        P("shard"),
        P("shard", None),
        P("shard"),
        P("shard", None),
        P("shard", None),
        P("shard", None),
        P(("rep", "shard"), None),
    )
    return jax.shard_map(
        on_device,
        mesh=mesh,
        in_specs=placed,
        out_specs=(
            P(("rep", "shard"), None),
            P(("rep", "shard"), None),
            P("shard"),
            P("shard", None),
            P("shard"),
            P("shard"),
            P("shard", None),
            P("shard"),
            P("shard", None),
            P("shard", None),
            P("shard", None),
        ),
        check_vma=False,
    )
```

```python
import math

import jax
import jax.numpy as jnp
from jax import lax
from jax.experimental import pallas as pl
from jax.experimental.pallas import tpu as pltpu
from jax.sharding import PartitionSpec as P

QH = 12
KVH = 2
HD = 128
SEQS = 3


EPSILON = 1e-06
LOG_THETA = math.log(1000000.0)
MASKED = -1e30
VMEM_LIMIT = 56 * 1024 * 1024
TILE = 512
COST = pl.CostEstimate(flops=1, bytes_accessed=1, transcendentals=0)


def rope_tables(places, head_width):
    half_width = head_width // 2
    frequency = jnp.exp(jnp.arange(half_width, dtype=jnp.float32) * (-2.0 * LOG_THETA / head_width))
    angles = places.astype(jnp.float32)[:, None] * frequency[None, :]
    angles = jnp.concatenate([angles, angles], axis=-1)
    return (jnp.cos(angles), jnp.sin(angles))


def positions(segments):
    labels = jnp.arange(SEQS, dtype=jnp.int32)
    starts = jnp.sum((segments[None, :] < labels[:, None]).astype(jnp.int32), axis=1)
    own_start = jnp.sum(jnp.where(segments[:, None] == labels[None, :], starts[None, :], 0), axis=1)
    return jnp.arange(segments.shape[0], dtype=jnp.int32) - own_start


def rotate(field_rows, cosine_table, sine_table):
    half_width = field_rows.shape[-1] // 2
    turned = jnp.concatenate([-field_rows[..., half_width:], field_rows[..., :half_width]], axis=-1)
    return field_rows * cosine_table[:, None, :] + turned * sine_table[:, None, :]


def transposed_times(left_side, right_side):
    return lax.dot_general(
        left_side, right_side, (((0,), (0,)), ((), ())), preferred_element_type=jnp.float32
    )


def times_transposed(left_side, right_side):
    return lax.dot_general(
        left_side, right_side, (((1,), (1,)), ((), ())), preferred_element_type=jnp.float32
    )


def norm_back(normed_gradient, unit_rows, inverse_rms, gain_row):
    scaled = normed_gradient * gain_row
    return inverse_rms * (scaled - unit_rows * jnp.mean(scaled * unit_rows, axis=-1, keepdims=True))


class Line:
    def __init__(self, name, size, place, pairs, crossed=False):
        self.name, self.size, self.place, self.pairs = name, size, place, pairs
        self.crossed = crossed

    def shift(self, value, step):
        return lax.ppermute(value, self.name, self.pairs(step % self.size))

    def pass_on(self, value, up):
        places = range(self.size - 1)
        pairs = [(at, at + 1) if up else (at + 1, at) for at in places]
        return lax.ppermute(value, self.name, pairs)

    def behind(self, step):
        return lax.rem(self.place + (self.size - step % self.size), self.size)

    def ahead(self, step):
        return lax.rem(self.place + step % self.size, self.size) if step else self.place


def make_lines(reps, shards):
    inner = 2 if reps % 4 == 0 else 1
    outer = reps // (2 * inner)
    square = inner == outer

    def split(index):
        core, b, a = index % 2, (index // 2) % inner, index // (2 * inner)
        return core, b, a

    def join(core, b, a):
        return (a * inner + b) * 2 + core

    def first_pairs(step):
        pairs = []
        for index in range(reps):
            core, b, a = split(index)
            if square and core == 0:
                pairs.append((index, join(core, (b + step) % inner, a)))
            else:
                pairs.append((index, join(core, b, (a + step) % outer)))
        return pairs

    def second_pairs(step):
        pairs = []
        for index in range(reps):
            core, b, a = split(index)
            if square and core == 0:
                pairs.append((index, join(core, b, (a + step) % outer)))
            else:
                pairs.append((index, join(core, (b + step) % inner, a)))
        return pairs

    def core_pairs(step):
        pairs = []
        for index in range(reps):
            core, b, a = split(index)
            pairs.append((index, join((core + step) % 2, b, a)))
        return pairs

    def shard_pairs(step):
        return [(index, (index + step) % shards) for index in range(shards)]

    core, b, a = split(lax.axis_index("rep"))
    first, second = (jnp.where(core == 0, b, a), jnp.where(core == 0, a, b)) if square else (a, b)
    return (
        Line("shard", shards, lax.axis_index("shard"), shard_pairs),
        Line("rep", 2, core, core_pairs, square),
        Line("rep", outer, first, first_pairs),
        Line("rep", inner, second, second_pairs),
    )


def rep_places(reps):
    inner = 2 if reps % 4 == 0 else 1
    outer = reps // (2 * inner)
    places = []
    for index in range(reps):
        core, b, a = index % 2, (index // 2) % inner, index // (2 * inner)
        one, two = (b, a) if inner == outer and core == 0 else (a, b)
        places.append((core * outer + one) * inner + two)
    return places


def pick(array, index, axis):
    return lax.dynamic_index_in_dim(array, index, axis, keepdims=False)


def put(array, piece, index, axis):
    return lax.dynamic_update_index_in_dim(array, piece, index, axis)


def in_place_order(pieces, line):
    ordered = []
    for place in range(line.size):
        chosen = pieces[0]
        for step in range(1, line.size):
            chosen = jnp.where(line.behind(step) == place, pieces[step], chosen)
        ordered.append(chosen)
    return ordered


def tie(*arrays):
    return lax.optimization_barrier(arrays)


def gather_line(value, line):
    return [value] + [line.shift(value, step) for step in range(1, line.size)]


class Clock:
    def __init__(self):
        self.token = jnp.zeros((8, 128), jnp.float32)
        self.open = 0

    def __call__(self, *arrays):
        self.token, *arrays = tie(self.token, *arrays)
        return arrays

    def run(self, step, *arrays):
        return self(*step(*self(*arrays)))

    def send(self, line, values, steps):
        self.open += len(values)
        return [line.shift(value, step) for value, step in zip(self(*values), steps)]

    def pass_on(self, line, lower, upper):
        self.open += 2
        lower, upper = self(lower, upper)
        return [line.pass_on(lower, True), line.pass_on(upper, False)]

    def wait(self, *groups):
        flat = self(*[array for group in groups for array in group])
        self.open -= len(flat)
        parts, at = [], 0
        for group in groups:
            parts.append(flat[at : at + len(group)])
            at += len(group)
        return parts


def total_of(terms):
    total = terms[0].astype(jnp.float32)
    for term in terms[1:]:
        total = total + term.astype(jnp.float32)
    return total


class Halving:
    def __init__(self, clock, sent, own, core, first, second):
        self.clock, self.first, self.second = clock, first, second
        self.terms = [own]
        self.moving = clock.send(core, [sent], [1])

    def along(self, line, arrived):
        self.terms = self.terms + arrived
        steps = range(1, line.size)
        blocks = [
            total_of([pick(term, line.ahead(step), 0) for term in self.terms]).astype(jnp.bfloat16)
            for step in steps
        ]
        self.moving = self.clock.send(line, blocks, steps)
        self.terms = [pick(term, line.place, 0) for term in self.terms]

    def along_first(self, arrived):
        self.along(self.first, arrived)

    def along_second(self, arrived):
        self.along(self.second, arrived)

    def finish(self, arrived):
        return self.clock(total_of(self.terms + arrived).astype(jnp.bfloat16))[0]


class Spread:
    def __init__(self, clock, piece, core, first, second):
        self.clock, self.lines = clock, (core, first, second)
        self.pieces = [piece]
        steps = range(1, second.size)
        self.moving = clock.send(second, [piece] * len(steps), steps)

    def along(self, arrived):
        core, first, second = self.lines
        self.pieces = self.pieces + arrived
        steps = range(1, first.size)
        self.moving = self.clock.send(first, [jnp.stack(self.pieces)] * len(steps), steps)

    def over(self, arrived):
        core, first, second = self.lines
        rows = [jnp.stack(self.pieces)] + arrived
        self.pieces = jnp.concatenate(rows, axis=0)
        self.moving = self.clock.send(core, [self.pieces], [1])

    def finish(self, arrived):
        core, first, second = self.lines
        (others,) = arrived
        offsets = [(one, two) for one in range(first.size) for two in range(second.size)]
        placed = [(core.place, first.behind(one), second.behind(two)) for one, two in offsets]
        far, near = (second, first) if core.crossed else (first, second)
        placed += [(core.behind(1), far.behind(one), near.behind(two)) for one, two in offsets]
        places = [(c * first.size + f) * second.size + s for c, f, s in placed]
        return [jnp.stack(places).astype(jnp.int32), self.pieces, others]


def column_blocks(place, shard_place, *weights):
    count = len(weights)
    rows, columns = weights[0].shape[1:]
    shards = lax.axis_size("shard")
    block = columns // shards

    def body(places_ref, *refs):
        sources, outs = refs[:count], refs[count : 2 * count]
        held, cut, in_sems, out_sems = refs[2 * count :]
        loads = [
            pltpu.make_async_copy(sources[at].at[places_ref[0]], held.at[at], in_sems.at[at])
            for at in range(count)
        ]

        def store(at, z):
            ahead = lax.rem(z + shards - places_ref[1], shards)
            return pltpu.make_async_copy(cut.at[at, z], outs[at].at[ahead], out_sems.at[at, z])

        for load in loads:
            load.start()
        for at in range(count):
            loads[at].wait()
            for z in range(shards):
                cut[at, z] = held[at, :, z * block : (z + 1) * block]
                store(at, z).start()
        for at in range(count):
            for z in range(shards):
                store(at, z).wait()

    return pl.pallas_call(
        body,
        out_shape=[jax.ShapeDtypeStruct((shards, rows, block), jnp.bfloat16)] * count,
        in_specs=[pl.BlockSpec(memory_space=pltpu.SMEM)]
        + [pl.BlockSpec(memory_space=pl.ANY)] * count,
        out_specs=[pl.BlockSpec(memory_space=pl.ANY)] * count,
        scratch_shapes=[
            pltpu.VMEM((count, rows, columns), jnp.bfloat16),
            pltpu.VMEM((count, shards, rows, block), jnp.bfloat16),
            pltpu.SemaphoreType.DMA((count,)),
            pltpu.SemaphoreType.DMA((count, shards)),
        ],
        compiler_params=pltpu.CompilerParams(vmem_limit_bytes=VMEM_LIMIT),
        cost_estimate=COST,
        name="column_blocks",
    )(jnp.stack([place, shard_place]).astype(jnp.int32), *weights)


def place_blocks(order, places, pieces, others):
    half, groups, shards = pieces.shape[:3]

    def body(order_ref, places_ref, pieces_ref, others_ref, *rest):
        def source_of(g, k, r):
            return (pieces_ref if r < half else others_ref).at[r % half, g, k]

        move_blocks(source_of, lambda r: places_ref[r], order_ref, rest[:groups], *rest[groups:])

    return blocks_call(body, 2, 2, groups, shards, 2 * half, pieces.shape[3:])(
        order, places, pieces, others
    )


def place_gathered(order, gathered, groups):
    shards = lax.axis_size("shard")
    reps = gathered.shape[0] // (shards * groups)

    def body(order_ref, source, *rest):
        move_blocks(
            lambda g, k, r: source.at[(r * shards + k) * groups + g],
            lambda r: r,
            order_ref,
            rest[:groups],
            *rest[groups:],
        )

    return blocks_call(body, 1, 1, groups, shards, reps, gathered.shape[1:])(order, gathered)


def move_blocks(source_of, place_of, order_ref, outs, held, in_sems, out_sems):
    groups, shards, reps = in_sems.shape
    slabs = [(g, k) for g in range(groups) for k in range(shards)]

    def load(g, k, r):
        return pltpu.make_async_copy(
            source_of(g, k, r), held.at[g, k, place_of(r)], in_sems.at[g, k, r]
        )

    def store(g, k):
        return pltpu.make_async_copy(held.at[g, k], outs[g].at[order_ref[k]], out_sems.at[g, k])

    for g, k in slabs:
        for r in range(reps):
            load(g, k, r).start()
    for g, k in slabs:
        for r in range(reps):
            load(g, k, r).wait()
        store(g, k).start()
    for g, k in slabs:
        store(g, k).wait()


def blocks_call(body, scalars, sources, groups, shards, reps, block):
    whole = (shards, reps) + block
    return pl.pallas_call(
        body,
        out_shape=[jax.ShapeDtypeStruct(whole, jnp.bfloat16)] * groups,
        in_specs=[pl.BlockSpec(memory_space=pltpu.SMEM)] * scalars
        + [pl.BlockSpec(memory_space=pl.ANY)] * sources,
        out_specs=[pl.BlockSpec(memory_space=pl.ANY)] * groups,
        scratch_shapes=[
            pltpu.VMEM((groups,) + whole, jnp.bfloat16),
            pltpu.SemaphoreType.DMA((groups, shards, reps)),
            pltpu.SemaphoreType.DMA((groups, shards)),
        ],
        compiler_params=pltpu.CompilerParams(vmem_limit_bytes=VMEM_LIMIT),
        cost_estimate=COST,
        name="place_blocks",
    )


def widen_pieces(places, pieces, others):
    half, rows, columns = pieces.shape
    reps = 2 * half
    strip = 16 if rows % 16 == 0 else rows

    def body(places_ref, pieces_ref, others_ref, out_ref, narrow, wide, in_sems, out_sems):
        loads = [
            pltpu.make_async_copy(
                (pieces_ref if r < half else others_ref).at[r % half], narrow.at[r], in_sems.at[r]
            )
            for r in range(reps)
        ]
        stores = [
            pltpu.make_async_copy(wide.at[r], out_ref.at[places_ref[r]], out_sems.at[r])
            for r in range(reps)
        ]
        for load in loads:
            load.start()
        for r in range(reps):
            loads[r].wait()

            def convert(at, carry):
                cut = pl.ds(pl.multiple_of(at * strip, strip), strip)
                wide[r, cut, :] = narrow[r, cut, :].astype(jnp.float32)
                return carry

            if strip == rows:
                wide[r] = narrow[r].astype(jnp.float32)
            else:
                lax.fori_loop(0, rows // strip, convert, 0)
            stores[r].start()
        for store in stores:
            store.wait()

    result = pl.pallas_call(
        body,
        out_shape=jax.ShapeDtypeStruct((reps, rows, columns), jnp.float32),
        in_specs=[pl.BlockSpec(memory_space=pltpu.SMEM)]
        + [pl.BlockSpec(memory_space=pl.ANY)] * 2,
        out_specs=pl.BlockSpec(memory_space=pl.ANY),
        scratch_shapes=[
            pltpu.VMEM((reps, rows, columns), jnp.bfloat16),
            pltpu.VMEM((reps, rows, columns), jnp.float32),
            pltpu.SemaphoreType.DMA((reps,)),
            pltpu.SemaphoreType.DMA((reps,)),
        ],
        compiler_params=pltpu.CompilerParams(vmem_limit_bytes=VMEM_LIMIT),
        cost_estimate=COST,
        name="widen_pieces",
    )(places, pieces, others)
    return (result.reshape(reps * rows, columns),)


def widen_gathered(gathered, order):
    reps, rows, columns = gathered.shape
    strip = 16 if rows % 16 == 0 else rows

    def body(source_ref, out_ref, narrow, wide, in_sems, out_sems):
        loads = [
            pltpu.make_async_copy(source_ref.at[r], narrow.at[r], in_sems.at[r])
            for r in range(reps)
        ]
        stores = [
            pltpu.make_async_copy(wide.at[r], out_ref.at[order[r]], out_sems.at[r])
            for r in range(reps)
        ]
        for load in loads:
            load.start()
        for r in range(reps):
            loads[r].wait()

            def convert(at, carry):
                cut = pl.ds(pl.multiple_of(at * strip, strip), strip)
                wide[r, cut, :] = narrow[r, cut, :].astype(jnp.float32)
                return carry

            if strip == rows:
                wide[r] = narrow[r].astype(jnp.float32)
            else:
                lax.fori_loop(0, rows // strip, convert, 0)
            stores[r].start()
        for store in stores:
            store.wait()

    result = pl.pallas_call(
        body,
        out_shape=jax.ShapeDtypeStruct((reps, rows, columns), jnp.float32),
        in_specs=[pl.BlockSpec(memory_space=pl.ANY)],
        out_specs=pl.BlockSpec(memory_space=pl.ANY),
        scratch_shapes=[
            pltpu.VMEM((reps, rows, columns), jnp.bfloat16),
            pltpu.VMEM((reps, rows, columns), jnp.float32),
            pltpu.SemaphoreType.DMA((reps,)),
            pltpu.SemaphoreType.DMA((reps,)),
        ],
        compiler_params=pltpu.CompilerParams(vmem_limit_bytes=VMEM_LIMIT),
        cost_estimate=COST,
        name="widen_gathered",
    )(gathered)
    return (result.reshape(reps * rows, columns),)


def resident(shape):
    return pl.BlockSpec(shape, lambda i: (0, 0), pipeline_mode=pl.Buffered(1))


def feed_forward(rows, cotangents, gate_matrix, up_matrix, down_matrix):
    count, width = rows.shape
    units = gate_matrix.shape[1]
    steps = pl.cdiv(units, TILE)
    slabs = next(size for size in range(min(steps, width // 128), 0, -1) if width % (128 * size) == 0)
    slab = width // slabs

    def body(
        rows_ref,
        cotangents_ref,
        gate_ref,
        up_ref,
        down_ref,
        inner_ref,
        d_gate_ref,
        d_up_ref,
        turned_rows_ref,
        turned_inner_ref,
    ):
        gate = jnp.dot(rows_ref[...], gate_ref[...], preferred_element_type=jnp.float32)
        up = jnp.dot(rows_ref[...], up_ref[...], preferred_element_type=jnp.float32)
        sigmoid = jax.nn.sigmoid(gate)
        silu = gate * sigmoid
        inner = (silu * up).astype(jnp.bfloat16)
        inner_ref[...] = inner
        turned_inner_ref[...] = inner.T
        d_inner = times_transposed(cotangents_ref[...], down_ref[...])
        d_up_ref[...] = (d_inner * silu).astype(jnp.bfloat16)
        d_gate_ref[...] = (d_inner * up * sigmoid * (1.0 + gate * (1.0 - sigmoid))).astype(
            jnp.bfloat16
        )
        for step in range(slabs):

            @pl.when(pl.program_id(0) == step)
            def turn():
                turned_rows_ref[...] = rows_ref[:, step * slab : (step + 1) * slab].T

    columns = pl.BlockSpec((width, TILE), lambda i: (0, i))
    results = pl.BlockSpec((count, TILE), lambda i: (0, i))
    return pl.pallas_call(
        body,
        grid=(steps,),
        out_shape=[jax.ShapeDtypeStruct((count, units), jnp.bfloat16)] * 3
        + [
            jax.ShapeDtypeStruct((width, count), jnp.bfloat16),
            jax.ShapeDtypeStruct((units, count), jnp.bfloat16),
        ],
        in_specs=[
            resident((count, width)),
            resident((count, width)),
            columns,
            columns,
            pl.BlockSpec((TILE, width), lambda i: (i, 0)),
        ],
        out_specs=[results] * 3
        + [
            pl.BlockSpec((slab, count), lambda i: (jnp.minimum(i, slabs - 1), 0)),
            pl.BlockSpec((TILE, count), lambda i: (i, 0)),
        ],
        compiler_params=pltpu.CompilerParams(vmem_limit_bytes=VMEM_LIMIT),
        cost_estimate=COST,
        name="feed_forward",
    )(rows, cotangents, gate_matrix, up_matrix, down_matrix)


def split_gradient(left, right, groups, places, core_place, turned):
    rows, count = left.shape if turned else left.shape[::-1]
    columns = right.shape[1]
    half = rows // (2 * groups)
    part = half // places

    def body(core_ref, left_ref, right_ref, other_ref, own_ref, *scratch):
        if turned:
            rows_ref = left_ref
        else:
            (rows_ref,) = scratch

            @pl.when(pl.program_id(0) == 0)
            def turn():
                rows_ref[...] = left_ref[...].T

        core = core_ref[0]
        for out_ref, which in ((other_ref, 1 - core), (own_ref, core)):
            halves = [
                rows_ref[pl.ds(pl.multiple_of((2 * group + which) * half, 16), half), :]
                for group in range(groups)
            ]
            product = jnp.dot(
                jnp.concatenate(halves, axis=0), right_ref[...], preferred_element_type=jnp.float32
            )
            for group in range(groups):
                for place in range(places):
                    at = group * half + place * part
                    out_ref[place, group] = product[at : at + part].astype(jnp.bfloat16)

    return pl.pallas_call(
        body,
        grid=(pl.cdiv(columns, TILE),),
        out_shape=[jax.ShapeDtypeStruct((places, groups, part, columns), jnp.bfloat16)] * 2,
        in_specs=[
            pl.BlockSpec(memory_space=pltpu.SMEM),
            resident(left.shape),
            pl.BlockSpec((count, TILE), lambda i: (0, i)),
        ],
        out_specs=[pl.BlockSpec((places, groups, part, TILE), lambda i: (0, 0, 0, i))] * 2,
        scratch_shapes=[] if turned else [pltpu.VMEM((rows, count), jnp.bfloat16)],
        compiler_params=pltpu.CompilerParams(vmem_limit_bytes=VMEM_LIMIT),
        cost_estimate=COST,
        name="split_gradient",
    )(core_place.reshape(1).astype(jnp.int32), left, right)


def ordered_gradient(left, right, shards, order):
    reps = len(order)
    rows, count = left.shape
    columns = right.shape[1]
    part = rows // (shards * reps)

    def body(left_ref, right_ref, out_ref):
        product = jnp.dot(left_ref[...], right_ref[...], preferred_element_type=jnp.float32)
        for z in range(shards):
            for r in range(reps):
                at = (z * reps + order[r]) * part
                out_ref[r, z] = product[at : at + part].astype(jnp.bfloat16)

    return pl.pallas_call(
        body,
        grid=(pl.cdiv(columns, TILE),),
        out_shape=[jax.ShapeDtypeStruct((reps, shards, part, columns), jnp.bfloat16)],
        in_specs=[
            resident((rows, count)),
            pl.BlockSpec((count, TILE), lambda i: (0, i)),
        ],
        out_specs=[pl.BlockSpec((reps, shards, part, TILE), lambda i: (0, 0, 0, i))],
        compiler_params=pltpu.CompilerParams(vmem_limit_bytes=VMEM_LIMIT),
        cost_estimate=COST,
        name="ordered_gradient",
    )(left, right)


def rows_product(lefts, rights, turned, blocks):
    count, depth = lefts[0].shape
    columns = rights[0].shape[0 if turned else 1]
    pairs, part = len(lefts), count // blocks

    def body(*refs):
        total = None
        for left_ref, right_ref in zip(refs[:pairs], refs[pairs : 2 * pairs]):
            if turned:
                product = times_transposed(left_ref[...], right_ref[...])
            else:
                product = jnp.dot(
                    left_ref[...], right_ref[...], preferred_element_type=jnp.float32
                )
            total = product if total is None else total + product
        for block in range(blocks):
            refs[2 * pairs + block][...] = total[block * part : (block + 1) * part].astype(
                jnp.bfloat16
            )

    right_spec = (
        pl.BlockSpec((TILE, depth), lambda i: (i, 0))
        if turned
        else pl.BlockSpec((depth, TILE), lambda i: (0, i))
    )
    return pl.pallas_call(
        body,
        grid=(pl.cdiv(columns, TILE),),
        out_shape=[jax.ShapeDtypeStruct((part, columns), jnp.bfloat16)] * blocks,
        in_specs=[resident((count, depth))] * pairs + [right_spec] * pairs,
        out_specs=[pl.BlockSpec((part, TILE), lambda i: (0, i))] * blocks,
        compiler_params=pltpu.CompilerParams(vmem_limit_bytes=VMEM_LIMIT),
        cost_estimate=COST,
        name="rows_product",
    )(*lefts, *rights)


def kept_bias(row_segments, row_index, key_segments, key_index):
    kept = (row_segments == key_segments) & (key_index <= row_index)
    return jnp.where(kept, 0.0, MASKED)


def in_vmem(count):
    return [pl.BlockSpec(memory_space=pltpu.VMEM)] * count


def attention_forward(projected, cosine, signed_sine, pairs, rows, keys):
    count = projected.shape[0]
    per_group = QH // KVH
    scale = 1.0 / math.sqrt(HD)
    shape = (KVH, per_group * count, HD)

    def body(projected_ref, cosine_ref, sine_ref, pairs_ref, rows_ref, keys_ref, queries_ref, out_ref):
        bias = kept_bias(rows_ref[:, 0:1], rows_ref[:, 1:2], keys_ref[0:1, :], keys_ref[1:2, :])
        for k in range(KVH):
            for h in range(per_group):
                at = (k * per_group + h) * HD
                field = projected_ref[:, at : at + HD]
                queries_ref[k, h * count : (h + 1) * count, :] = (
                    field * cosine_ref[...] + pltpu.roll(field, HD // 2, 1) * sine_ref[...]
                ).astype(jnp.bfloat16)
            keys_here = pairs_ref[:, k * HD : (k + 1) * HD]
            values_here = pairs_ref[:, (KVH + k) * HD : (KVH + k + 1) * HD]
            scores = times_transposed(queries_ref[k], keys_here) * scale + bias
            powers = jnp.exp(scores - jnp.max(scores, axis=1, keepdims=True))
            shares = powers * (1.0 / jnp.sum(powers, axis=1, keepdims=True))
            result = jnp.dot(
                shares.astype(jnp.bfloat16), values_here, preferred_element_type=jnp.float32
            ).astype(jnp.bfloat16)
            for h in range(per_group):
                at = (k * per_group + h) * HD
                out_ref[:, at : at + HD] = result[h * count : (h + 1) * count]

    return pl.pallas_call(
        body,
        out_shape=[
            jax.ShapeDtypeStruct(shape, jnp.bfloat16),
            jax.ShapeDtypeStruct((count, QH * HD), jnp.bfloat16),
        ],
        in_specs=in_vmem(6),
        out_specs=in_vmem(2),
        compiler_params=pltpu.CompilerParams(vmem_limit_bytes=VMEM_LIMIT),
        cost_estimate=COST,
        name="attention_forward",
    )(projected, cosine, signed_sine, pairs, rows, keys)


def attention_backward(queries, gradient, pairs, cosine, signed_sine, rows, keys, blocks):
    count = gradient.shape[0]
    per_group = QH // KVH
    scale = 1.0 / math.sqrt(HD)
    group_rows = pairs.shape[0]
    part = group_rows // blocks

    def body(queries_ref, gradient_ref, pairs_ref, cosine_ref, sine_ref, rows_ref, keys_ref, d_ref, *outs):
        block_refs, stacked = outs[:blocks], outs[blocks]
        bias = kept_bias(rows_ref[0:1, :], rows_ref[1:2, :], keys_ref[:, 0:1], keys_ref[:, 1:2])
        for k in range(KVH):
            for h in range(per_group):
                at = (k * per_group + h) * HD
                stacked[h * count : (h + 1) * count, :] = gradient_ref[:, at : at + HD]
            keys_here = pairs_ref[:, k * HD : (k + 1) * HD]
            values_here = pairs_ref[:, (KVH + k) * HD : (KVH + k + 1) * HD]
            scores = times_transposed(keys_here, queries_ref[k]) * scale + bias
            powers = jnp.exp(scores - jnp.max(scores, axis=0, keepdims=True))
            shares = powers * (1.0 / jnp.sum(powers, axis=0, keepdims=True))
            d_shares = times_transposed(values_here, stacked[...])
            dots = jnp.sum(shares * d_shares, axis=0, keepdims=True)
            d_scores = (shares * (d_shares - dots)).astype(jnp.bfloat16)
            d_keys = jnp.dot(d_scores, queries_ref[k], preferred_element_type=jnp.float32) * scale
            d_values = jnp.dot(
                shares.astype(jnp.bfloat16), stacked[...], preferred_element_type=jnp.float32
            )
            for block in range(blocks):
                cut = slice(block * part, (block + 1) * part)
                block_refs[block][:, k * HD : (k + 1) * HD] = d_keys[cut].astype(jnp.bfloat16)
                block_refs[block][:, (KVH + k) * HD : (KVH + k + 1) * HD] = d_values[cut].astype(
                    jnp.bfloat16
                )
            d_queries = transposed_times(d_scores, keys_here) * scale
            for h in range(per_group):
                at = (k * per_group + h) * HD
                field = d_queries[h * count : (h + 1) * count]
                d_ref[:, at : at + HD] = (
                    field * cosine_ref[...] - pltpu.roll(field, HD // 2, 1) * sine_ref[...]
                ).astype(jnp.bfloat16)

    return pl.pallas_call(
        body,
        out_shape=[jax.ShapeDtypeStruct((count, QH * HD), jnp.bfloat16)]
        + [jax.ShapeDtypeStruct((part, 2 * KVH * HD), jnp.bfloat16)] * blocks,
        in_specs=in_vmem(7),
        out_specs=in_vmem(1 + blocks),
        scratch_shapes=[pltpu.VMEM((per_group * count, HD), jnp.bfloat16)],
        compiler_params=pltpu.CompilerParams(vmem_limit_bytes=VMEM_LIMIT),
        cost_estimate=COST,
        name="attention_backward",
    )(queries, gradient, pairs, cosine, signed_sine, rows, keys)


def join_projected(d_queries, pair_terms, cosine, signed_sine):
    count, query_width = d_queries.shape
    pair_width = KVH * HD
    terms = len(pair_terms)

    def body(d_queries_ref, cosine_ref, sine_ref, *refs):
        term_refs, out_ref, sum_ref = refs[:terms], refs[terms], refs[terms + 1]
        out_ref[:, :query_width] = d_queries_ref[...]
        for at in range(0, 2 * pair_width, HD):
            field = total_of([term[:, at : at + HD] for term in term_refs])
            if at < pair_width:
                field = field * cosine_ref[...] - pltpu.roll(field, HD // 2, 1) * sine_ref[...]
            out_ref[:, query_width + at : query_width + at + HD] = field.astype(jnp.bfloat16)
        sum_ref[...] = jnp.sum(out_ref[...].astype(jnp.float32), axis=0, keepdims=True)

    return pl.pallas_call(
        body,
        out_shape=[
            jax.ShapeDtypeStruct((count, query_width + 2 * pair_width), jnp.bfloat16),
            jax.ShapeDtypeStruct((1, query_width + 2 * pair_width), jnp.float32),
        ],
        in_specs=in_vmem(3 + terms),
        out_specs=in_vmem(2),
        cost_estimate=COST,
        name="join_projected",
    )(d_queries, cosine, signed_sine, *pair_terms)


def on_device(
    tokens,
    segment_ids,
    first_gain,
    input_weight,
    input_bias,
    output_weight,
    second_gain,
    gate_weight,
    up_weight,
    down_weight,
    output_cotangent,
):
    bf16, f32 = jnp.bfloat16, jnp.float32
    shards, reps = lax.axis_size("shard"), lax.axis_size("rep")
    shard, core, first, second = make_lines(reps, shards)
    rep_place = (core.place * first.size + first.place) * second.size + second.place
    own_rows, width = tokens.shape
    segments = segment_ids[0]
    per_group = QH // KVH
    query_width = QH * HD
    pair_width = KVH * HD
    first_row = shard.place * own_rows
    part_rows = input_weight.shape[0] // reps
    hidden_units = gate_weight.shape[1]
    block_units = hidden_units // shards
    clock = Clock()
    z_order = jnp.stack([shard.behind(step) for step in range(shards)]).astype(jnp.int32)

    def weight_piece(weight, place):
        return pick(weight.reshape(reps, part_rows, weight.shape[1]), place, 0)

    def spread(piece):
        return Spread(clock, piece, core, first, second)

    def blocks_of(blocks):
        return [pick(blocks, shard.ahead(step), 0) for step in range(shards)]

    steps = range(1, shards)

    def send_blocks(blocks):
        return clock.send(shard, blocks[1:], steps)

    def send_around(value):
        return clock.send(shard, [value] * len(steps), steps)

    def send_back(rows):
        return clock.send(shard, rows, [shards - step for step in steps])

    rep_index = lax.axis_index("rep")
    input_matrix = lax.all_gather(
        weight_piece(input_weight, rep_index), ("shard", "rep"), axis=0, tiled=True
    )
    shard_vectors = jnp.concatenate([first_gain, second_gain, input_bias])
    vector_row = jnp.pad(shard_vectors, (0, output_weight.shape[1] - shard_vectors.shape[0]))
    own_output = jnp.concatenate(
        [weight_piece(output_weight, rep_place), vector_row[None]], axis=0
    )
    output_moving = send_around(own_output)
    gate_blocks, up_blocks = clock.run(
        lambda *weights: column_blocks(rep_index, shard.place, *weights),
        gate_weight.reshape(reps, part_rows, hidden_units),
        up_weight.reshape(reps, part_rows, hidden_units),
    )
    (output_rows,) = clock.wait(output_moving)
    output_rows = [own_output] + output_rows

    output_spread = spread(jnp.stack([rows[:part_rows] for rows in output_rows])[None])
    gate_moving = send_blocks(gate_blocks)
    vector_rows = jnp.stack(in_place_order([rows[part_rows] for rows in output_rows], shard))
    own_gain = first_gain.shape[0]
    gain_one = vector_rows[:, :own_gain].reshape(width).astype(f32)
    gain_two = vector_rows[:, own_gain : 2 * own_gain].reshape(width).astype(f32)
    shift_row = (
        vector_rows[:, 2 * own_gain : shard_vectors.shape[0]].reshape(-1).astype(f32)
    )
    places = positions(segments)
    cosine_table, sine_table = rope_tables(
        lax.dynamic_slice_in_dim(places, first_row, own_rows), HD
    )
    signed_sine = jnp.concatenate(
        [-sine_table[:, : HD // 2], sine_table[:, HD // 2 :]], axis=1
    )
    own_segments = lax.dynamic_slice_in_dim(segments, first_row, own_rows)
    row_index = jnp.arange(own_rows, dtype=jnp.int32)
    key_index = jnp.concatenate([shard.behind(step) * own_rows + row_index for step in range(shards)])
    key_segments = jnp.concatenate(
        [
            lax.dynamic_slice_in_dim(segments, shard.behind(step) * own_rows, own_rows)
            for step in range(shards)
        ]
    )
    key_marks = jnp.stack([key_segments, key_index])
    row_marks = jnp.tile(jnp.stack([own_segments, first_row + row_index]), (1, per_group))
    wide_tokens = tokens.astype(f32)
    inverse_one = lax.rsqrt(jnp.mean(wide_tokens * wide_tokens, axis=-1, keepdims=True) + EPSILON)
    unit_one = wide_tokens * inverse_one
    normed_one = (unit_one * gain_one).astype(bf16)
    (
        normed_one,
        cosine_table,
        sine_table,
        signed_sine,
        key_marks,
        row_marks,
    ) = clock(normed_one, cosine_table, sine_table, signed_sine, key_marks, row_marks)
    output_arrived, gate_rows = clock.wait(output_spread.moving, gate_moving)

    output_spread.along(output_arrived)
    up_moving = send_blocks(up_blocks)
    output_arrived, up_rows = clock.wait(output_spread.moving, up_moving)

    gate_up = jnp.stack(
        [row for pair in zip([gate_blocks[0]] + gate_rows, [up_blocks[0]] + up_rows) for row in pair]
    )
    gate_up = lax.all_gather(clock(gate_up)[0], "rep", axis=0, tiled=True)
    passed = [[output_cotangent] * 2]
    passing = clock.pass_on(shard, *passed[-1])
    output_spread.over(output_arrived)
    input_matrix, normed_one = clock(input_matrix, normed_one)
    projected = jnp.dot(normed_one, input_matrix, preferred_element_type=f32) + shift_row
    key_part = rotate(
        projected[:, query_width : query_width + pair_width].reshape(own_rows, KVH, HD),
        cosine_table,
        sine_table,
    )
    (own_pairs,) = clock(
        jnp.concatenate(
            [key_part.reshape(own_rows, pair_width), projected[:, query_width + pair_width :]],
            axis=1,
        ).astype(bf16)
    )
    arrived, output_arrived = clock.wait(passing, output_spread.moving)
    passed.append(arrived)

    pair_moving = send_around(own_pairs)
    passing = clock.pass_on(shard, *passed[-1]) if shards > 2 else []
    pair_rows, arrived = clock.wait(pair_moving, passing)
    passed.append(arrived)
    pairs = jnp.concatenate([own_pairs] + pair_rows, axis=0)

    passing = clock.pass_on(shard, *passed[-1]) if shards > 3 else []
    (output_matrix,) = clock.run(place_blocks, z_order, *output_spread.finish(output_arrived))
    output_matrix = output_matrix.reshape(width, width)
    queries, attention_low = clock.run(
        attention_forward, projected, cosine_table, signed_sine, pairs, row_marks.T, key_marks
    )
    hidden = wide_tokens + jnp.dot(attention_low, output_matrix, preferred_element_type=f32)
    inverse_two = lax.rsqrt(jnp.mean(hidden * hidden, axis=-1, keepdims=True) + EPSILON)
    unit_two = hidden * inverse_two
    (normed_two,) = clock((unit_two * gain_two).astype(bf16))
    (arrived,) = clock.wait(passing)
    passed.append(arrived)

    normed_moving = send_around(normed_two)
    gate_matrix, up_matrix = clock.run(
        lambda order, gathered: place_gathered(order, gathered, 2), z_order, gate_up
    )
    gate_matrix = gate_matrix.reshape(width, block_units)
    up_matrix = up_matrix.reshape(width, block_units)
    (normed_arrived,) = clock.wait(normed_moving)
    while len(passed) < shards:
        (arrived,) = clock.wait(clock.pass_on(shard, *passed[-1]))
        passed.append(arrived)
    group_normed = jnp.concatenate([normed_two] + normed_arrived, axis=0)
    cotangents = jnp.concatenate(
        [output_cotangent]
        + [
            jnp.where(shard.place >= step, passed[step][0], passed[shards - step][1])
            for step in steps
        ],
        axis=0,
    )

    inner_act, d_gate, d_up, turned_normed, turned_inner = clock.run(
        feed_forward, group_normed, cotangents, gate_matrix, up_matrix, down_weight
    )

    def split_halves(left, right, groups, turned):
        count = first.size * second.size
        halves = clock.run(
            lambda left, right: split_gradient(left, right, groups, count, core.place, turned),
            left,
            right,
        )
        return [half.reshape((first.size, second.size) + half.shape[1:]) for half in halves]

    def side_by_side(rows):
        return clock(jnp.concatenate(in_place_order(rows, shard), axis=1))[0]

    def sum_over_rep(blocks):
        return lax.psum_scatter(blocks, "rep", scatter_dimension=0, tiled=True)

    def row_sum(own, arrived):
        return clock(total_of(own + arrived).astype(bf16))[0]

    def send_some(rows, chosen):
        return clock.send(shard, [rows[k] for k in chosen], [shards - 1 - k for k in chosen])

    edges = sorted({0, shards - 2})
    inside = list(range(1, shards - 2))

    def gather_rep(piece):
        return lax.all_gather(piece[None], "rep", axis=0, tiled=True)

    up_halves = split_halves(turned_normed, d_up, shards, True)

    up = Halving(clock, *up_halves, core, first, second)
    (gate_blocks,) = clock.run(
        lambda left, right: ordered_gradient(left, right, shards, rep_places(reps)),
        turned_normed,
        d_gate,
    )
    (up_arrived,) = clock.wait(up.moving)

    gate_piece = sum_over_rep(clock(gate_blocks)[0].reshape(width, block_units))
    up.along_first(up_arrived)
    normed_own, *normed_partial = clock.run(
        lambda *operands: rows_product(operands[:2], operands[2:], True, shards),
        d_gate,
        d_up,
        gate_matrix,
        up_matrix,
    )
    normed_moving = send_some(normed_partial, edges)
    down_halves = split_halves(turned_inner, cotangents, 1, True)
    up_arrived, normed_arrived = clock.wait(up.moving, normed_moving)

    up.along_second(up_arrived)
    down = Halving(clock, *down_halves, core, first, second)
    normed_moving = send_some(normed_partial, inside)
    block_own, *block_partial = clock.run(
        lambda left, right: rows_product((left,), (right,), False, shards), inner_act, down_weight
    )
    up_arrived, down_arrived, more_arrived = clock.wait(up.moving, down.moving, normed_moving)

    down.along_first(down_arrived)
    up_blocks = clock(*blocks_of(up.finish(up_arrived)))
    up_moving = send_blocks(up_blocks)
    normed_two_gradient = total_of([normed_own] + normed_arrived + more_arrived)
    gain_two_gradient = jnp.sum(normed_two_gradient * unit_two, axis=0)
    hidden_gradient = output_cotangent.astype(f32) + norm_back(
        normed_two_gradient, unit_two, inverse_two, gain_two
    )
    (branch_gradient,) = clock(hidden_gradient.astype(bf16))
    (attention_gradient,) = clock(times_transposed(branch_gradient, output_matrix).astype(bf16))
    d_queries, pair_own, *pair_partial = clock.run(
        lambda *operands: attention_backward(*operands, shards),
        queries,
        attention_gradient,
        pairs,
        cosine_table,
        signed_sine,
        row_marks,
        key_marks.T,
    )
    output_halves = split_halves(attention_low, branch_gradient, shards, False)
    down_arrived, up_rows = clock.wait(down.moving, up_moving)

    pair_moving = send_back(pair_partial)
    output = Halving(clock, *output_halves, core, first, second)
    down.along_second(down_arrived)
    up_piece = side_by_side(up_blocks[:1] + up_rows)
    pair_arrived, output_arrived, down_arrived = clock.wait(
        pair_moving, output.moving, down.moving
    )

    (gate_piece,) = clock(gate_piece)
    down_gathered = gather_rep(down.finish(down_arrived)[0])
    projected_gradient, bias_sum = clock.run(
        lambda *operands: join_projected(operands[0], operands[3:], *operands[1:3]),
        d_queries,
        cosine_table,
        signed_sine,
        pair_own,
        *pair_arrived,
    )
    projected_halves = split_halves(normed_one, projected_gradient, shards, False)

    projected = Halving(clock, *projected_halves, core, first, second)
    output.along_first(output_arrived)
    gate_blocks = clock(*blocks_of(gate_piece.reshape(shards, part_rows, block_units)))
    gate_moving = send_blocks(gate_blocks)
    projected_gradient, hidden_gradient = clock(projected_gradient, hidden_gradient)
    normed_one_gradient = times_transposed(projected_gradient, input_matrix)
    gain_one_gradient = jnp.sum(normed_one_gradient * unit_one, axis=0)
    (tokens_gradient,) = clock(
        (
            hidden_gradient + norm_back(normed_one_gradient, unit_one, inverse_one, gain_one)
        ).astype(bf16)
    )
    projected_arrived, output_arrived, gate_rows = clock.wait(
        projected.moving, output.moving, gate_moving
    )

    projected.along_first(projected_arrived)
    output.along_second(output_arrived)
    gate_spread = spread(side_by_side(gate_blocks[:1] + gate_rows))
    block_moving = send_some(block_partial, inside)
    bias_gradient = bias_sum[0]
    bias_split = query_width + pair_width
    small_parts = (
        gain_one_gradient,
        gain_two_gradient,
        bias_gradient[:bias_split],
        bias_gradient[bias_split:],
    )
    (small,) = clock(
        jnp.concatenate([part.reshape(shards, -1) for part in small_parts], axis=1)
    )
    (down_gathered,) = clock(down_gathered)
    (down_total,) = clock.run(lambda gathered: widen_gathered(gathered, rep_places(reps)), down_gathered)
    projected_arrived, output_arrived, gate_arrived, block_arrived = clock.wait(
        projected.moving, output.moving, gate_spread.moving, block_moving
    )

    projected.along_second(projected_arrived)
    gate_spread.along(gate_arrived)
    output_blocks = clock(*blocks_of(output.finish(output_arrived)))
    output_moving = send_blocks(output_blocks)
    up_gathered = gather_rep(clock(up_piece)[0])
    projected_arrived, gate_arrived, output_rows = clock.wait(
        projected.moving, gate_spread.moving, output_moving
    )

    input_blocks = clock(*blocks_of(projected.finish(projected_arrived)))
    input_moving = send_blocks(input_blocks)
    output_spread = spread(row_sum(output_blocks[:1], output_rows))
    gate_spread.over(gate_arrived)
    input_rows, output_arrived, gate_arrived = clock.wait(
        input_moving, output_spread.moving, gate_spread.moving
    )

    input_spread = spread(row_sum(input_blocks[:1], input_rows))
    output_spread.along(output_arrived)
    small_moving = clock.send(core, [small], [1])
    block_moving = send_some(block_partial, edges[:1])
    (up_gathered,) = clock(up_gathered)
    (up_total,) = clock.run(lambda gathered: widen_gathered(gathered, rep_places(reps)), up_gathered)
    input_arrived, output_arrived, small_arrived, more_arrived = clock.wait(
        input_spread.moving, output_spread.moving, small_moving, block_moving
    )
    small = total_of([small] + small_arrived)
    block_arrived = block_arrived + more_arrived

    input_spread.along(input_arrived)
    output_spread.over(output_arrived)
    small_moving = clock.send(first, [small] * (first.size - 1), range(1, first.size))
    block_moving = send_some(block_partial, edges[1:])
    (gate_total,) = clock.run(widen_pieces, *gate_spread.finish(gate_arrived))
    input_arrived, output_arrived, small_arrived, more_arrived = clock.wait(
        input_spread.moving, output_spread.moving, small_moving, block_moving
    )
    small = total_of([small] + small_arrived)
    block_arrived = block_arrived + more_arrived

    input_spread.over(input_arrived)
    small_moving = clock.send(second, [small] * (second.size - 1), range(1, second.size))
    (output_total,) = clock.run(widen_pieces, *output_spread.finish(output_arrived))
    (block_out,) = clock(total_of([hidden, block_own] + block_arrived).astype(bf16))
    input_arrived, small_arrived = clock.wait(input_spread.moving, small_moving)
    small_blocks = clock(*blocks_of(total_of([small] + small_arrived)))

    small_moving = send_blocks(small_blocks)
    (input_total,) = clock.run(widen_pieces, *input_spread.finish(input_arrived))
    (small_arrived,) = clock.wait(small_moving)
    small = total_of(small_blocks[:1] + small_arrived)

    small = small + clock.token[0, 0]
    small_totals, at = [], 0
    for part in small_parts:
        size = part.shape[0] // shards
        small_totals.append(small[at : at + size])
        at += size
    return (
        block_out,
        tokens_gradient,
        small_totals[0],
        input_total,
        small_totals[2],
        small_totals[3],
        output_total,
        small_totals[1],
        gate_total,
        up_total,
        down_total,
    )


def solution(mesh):
    placed = (
        P(("rep", "shard"), None),
        P("rep", None),
        P("shard"),
        P("shard", None),
        P("shard"),
        P("shard", None),
        P("shard"),
        P("shard", None),
        P("shard", None),
        P("shard", None),
        P(("rep", "shard"), None),
    )
    return jax.shard_map(
        on_device,
        mesh=mesh,
        in_specs=placed,
        out_specs=(
            P(("rep", "shard"), None),
            P(("rep", "shard"), None),
            P("shard"),
            P("shard", None),
            P("shard"),
            P("shard"),
            P("shard", None),
            P("shard"),
            P("shard", None),
            P("shard", None),
            P("shard", None),
        ),
        check_vma=False,
    )
```
